32 devices in a mesh: wide: 8 (over z, x), narrow: 4 (over y, core).
Axes of the slice: x: 2, y: 2, z: 4, core: 2. Of those that a mesh axis runs over, the one named last changes fastest.
Arguments:
- tokens: bfloat16 [2, 8, 1024, 768], P(None, 'wide', 'narrow'), may hold values from -6 to 6
- lengths: int32 [2, 8], P(None, 'wide'), may hold values from 256 to 1024, as said below
- norm_one: float32 [768], replicated, may hold values from 0.25 to 1.75
- w_query: bfloat16 [768, 768], P('wide', 'narrow'), may hold values from -0.02734375 to 0.02734375
- w_key: bfloat16 [768, 768], P('wide', 'narrow'), may hold values from -0.21875 to 0.21875
- w_value: bfloat16 [768, 768], P('wide', 'narrow'), may hold values from -0.21875 to 0.21875
- w_out: bfloat16 [768, 768], P('narrow', 'wide'), may hold values from -6 to 6
- norm_two: float32 [768], replicated, may hold values from 0.25 to 1.75
- w_gate: bfloat16 [768, 2048], P('wide', 'narrow'), may hold values from -0.21875 to 0.21875
- w_up: bfloat16 [768, 2048], P('wide', 'narrow'), may hold values from -0.21875 to 0.21875
- w_down: bfloat16 [2048, 768], P('narrow', 'wide'), may hold values from -0.125 to 0.125
- cotangent: bfloat16 [2, 8, 1024, 768], P(None, 'wide', 'narrow'), may hold values from -6 to 6
Outputs:
- output: bfloat16 [2, 8, 1024, 768], P(None, 'wide', 'narrow')
- input_grad: bfloat16 [2, 8, 1024, 768], P(None, 'wide', 'narrow')
- grad_norm_one: float32 [768], replicated
- grad_query: float32 [768, 768], P('wide', 'narrow')
- grad_key: float32 [768, 768], P('wide', 'narrow')
- grad_value: float32 [768, 768], P('wide', 'narrow')
- grad_out: float32 [768, 768], P('narrow', 'wide')
- grad_norm_two: float32 [768], replicated
- grad_gate: float32 [768, 2048], P('wide', 'narrow')
- grad_up: float32 [768, 2048], P('wide', 'narrow')
- grad_down: float32 [2048, 768], P('narrow', 'wide')
The draws below stay inside these ranges and needn't reach their ends.
Inputs may be any that keep to these rules, and one draw needn't show every extreme that they name: The first lengths[m, i] slots of an item are real patches, the rest padding; in every micro-batch some item fills all 1024 slots.
All inputs are finite; a program needn't handle non-finite values.
Results may differ from the reference program's by a relative error of at most 0.023.
Values may be sent and summed in bfloat16 or wider, within the bound.
No kernel may reach another device: no remote copies, remote signals or barrier semaphores. Data moves between devices by JAX's collectives and lax.ppermute only.
A program may use at most 192 MiB of HBM per device.

```python
import jax
import jax.numpy as jnp
from jax import lax

D = 768
H = 12
HD = 64
FF = 2048
BUCKET = 1024
MICRO = 2
ITEMS = 8


def draw_lengths(key, part):
    key = jax.random.fold_in(key, 7)
    first_key, second_key = jax.random.split(key)
    spread = jax.random.randint(first_key, (MICRO, ITEMS), BUCKET // 4, BUCKET + 1)
    chosen = jax.random.randint(second_key, (MICRO, 1), 0, ITEMS)
    filled = jnp.where(jnp.arange(ITEMS)[None, :] == chosen, BUCKET, spread)
    return filled.astype(jnp.int32)


def with_spikes(entries, key, source, target, shards_of, factor):
    owner, partner = [(jnp.arange(entries.shape[position]) // (entries.shape[position] // shards_of)).reshape([-1 if axis == position else 1 for axis in range(entries.ndim)]) for position in (source, target)]
    chosen = jax.random.permutation(key, shards_of)[partner]
    strong = (owner == chosen) | (owner == (partner + shards_of // 2) % shards_of)
    return jnp.where(strong, factor * entries, entries)


def levels(key, extent, cuts, smallest, high):
    gain, own = 1.0, jax.random.fold_in(key, 6)
    for position, parts in cuts:
        heights = jnp.exp(jax.random.uniform(jax.random.fold_in(own, position), (parts,), jnp.float32, smallest / len(cuts), high / len(cuts)))
        gain = gain * jnp.repeat(heights, extent[position] // parts).reshape([-1 if axis == position else 1 for axis in range(len(extent))])
    return gain


def gaussian(rng, extent, scale, reach, pieces=(), kind=jnp.bfloat16):
    array = scale * jax.random.normal(rng, extent, jnp.float32)
    if pieces:
        array = array * levels(rng, extent, pieces, -0.22, 0.18)
    return jnp.clip(array, -reach, reach).astype(kind)


def heavy_noise(stream_key, extent, deviation, most, cuts, heavy, held_as=jnp.bfloat16):
    entries = deviation * jax.random.normal(stream_key, extent, jnp.float32)
    if cuts:
        entries = entries * levels(stream_key, extent, cuts, -0.22, 0.18)
    return jnp.clip(with_spikes(entries, jax.random.fold_in(stream_key, 3), *heavy), -most, most).astype(held_as)


def setup_inputs(seed: int = 0) -> dict:
    key_list = jax.random.split(jax.random.key(seed), 13)
    return {
        "tokens": heavy_noise(key_list[0], (MICRO, ITEMS, BUCKET, D), 1.0, 6.0, ((1, 8), (2, 4)), (1, 3, 8, 2.0)),
        "lengths": draw_lengths(jax.random.fold_in(key_list[12], 71), 0),
        "norm_one": jnp.clip(1.0 + 0.15 * jax.random.normal(key_list[2], (D,), jnp.float32), 0.25, 1.75),
        "w_query": gaussian(key_list[3], (D, H * HD), (D * HD) ** -0.5, 0.02734375, ((0, 8), (1, 4))),
        "w_key": gaussian(key_list[4], (D, H * HD), D ** -0.5, 0.21875, ((0, 8), (1, 4))),
        "w_value": gaussian(key_list[5], (D, H * HD), D ** -0.5, 0.21875, ((0, 8), (1, 4))),
        "w_out": gaussian(key_list[6], (H * HD, D), (max(2 * D // BUCKET, 1)) ** -0.5, 6.0, ((0, 4), (1, 8))),
        "norm_two": jnp.clip(1.0 + 0.15 * jax.random.normal(key_list[7], (D,), jnp.float32), 0.25, 1.75),
        "w_gate": gaussian(key_list[8], (D, FF), D ** -0.5, 0.21875, ((0, 8), (1, 4))),
        "w_up": gaussian(key_list[9], (D, FF), D ** -0.5, 0.21875, ((0, 8), (1, 4))),
        "w_down": gaussian(key_list[10], (FF, D), FF ** -0.5, 0.125, ((0, 4), (1, 8))),
        "cotangent": heavy_noise(key_list[11], (MICRO, ITEMS, BUCKET, D), 1.0, 6.0, ((1, 8), (2, 4)), (1, 3, 8, 2.0)),
    }


EPSILON = 1e-06
PRECISE = lax.Precision.HIGHEST

@jax.custom_vjp
def low(v):
    return lax.optimization_barrier(v.astype(jnp.bfloat16)).astype(jnp.float32)

@jax.custom_vjp
def low_back(v):
    return v

def low_keep(v):
    return (low(v), None)

def low_pass(kept, grad):
    return (grad,)

def back_keep(v):
    return (v, None)

def back_low(kept, grad):
    return (low(grad),)
low.defvjp(low_keep, low_pass)
low_back.defvjp(back_keep, back_low)

def product(left, right):
    return jnp.dot(left, right, precision=PRECISE, preferred_element_type=jnp.float32)

def root_norm(values, scaling):
    inverse = lax.rsqrt(lax.optimization_barrier(jnp.mean(values * values, axis=-1, keepdims=True)) + EPSILON)
    return values * inverse * scaling

def attention(normed, w_query, w_key, w_value, w_out, usable):
    queries = low(low_back(product(normed, w_query))).reshape(BUCKET, H, HD)
    key_rows = low(low_back(product(normed, w_key))).reshape(BUCKET, H, HD)
    value_rows = low(low_back(product(normed, w_value))).reshape(BUCKET, H, HD)
    scores = jnp.einsum('qhd,khd->hqk', queries, key_rows, precision=PRECISE)
    scores = low_back(jnp.where(usable[None, None, :], scores, -1e+30))
    probs = low(jax.nn.softmax(scores, axis=-1))
    context = jnp.einsum('hqk,khd->qhd', probs, value_rows, precision=PRECISE).reshape(BUCKET, H * HD)
    context = low(low_back(context))
    return low_back(product(context, w_out))

def block_forward(rows_in, norm_one, w_query, w_key, w_value, w_out, norm_two, w_gate, w_up, w_down, usable):
    normed = low(root_norm(rows_in, norm_one))
    middle = rows_in + attention(normed, w_query, w_key, w_value, w_out, usable)
    middle_low = low(middle)
    normed_two = low(root_norm(middle_low, norm_two))
    gate_rows = low_back(product(normed_two, w_gate))
    up_rows = low_back(product(normed_two, w_up))
    hidden = low(jax.nn.gelu(gate_rows, approximate=True) * up_rows)
    return middle + low_back(product(hidden, w_down))

def reference(tokens, lengths, norm_one, w_query, w_key, w_value, w_out, norm_two, w_gate, w_up, w_down, cotangent):
    params = tuple((p.astype(jnp.float32) for p in (norm_one, w_query, w_key, w_value, w_out, norm_two, w_gate, w_up, w_down)))
    flat_tokens = tokens.reshape(MICRO * ITEMS, BUCKET, D)
    flat_cot = cotangent.reshape(MICRO * ITEMS, BUCKET, D)
    flat_lengths = lengths.reshape(MICRO * ITEMS)
    positions = jnp.arange(BUCKET, dtype=jnp.int32)

    def scan_step(totals, packed):
        rows_in, cot_rows, length = packed
        usable = positions < length

        def forward(values, *weights):
            return block_forward(values, *weights, usable)
        result, pull_back = jax.vjp(forward, rows_in.astype(jnp.float32), *params)
        grads = pull_back(cot_rows.astype(jnp.float32))
        totals = tuple((a + b for a, b in zip(totals, grads[1:])))
        return (totals, (result.astype(jnp.bfloat16), grads[0].astype(jnp.bfloat16)))
    start = tuple((jnp.zeros(p.shape, jnp.float32) for p in params))
    totals, (results, input_grads) = lax.scan(scan_step, start, (flat_tokens, flat_cot, flat_lengths))
    shape = (MICRO, ITEMS, BUCKET, D)
    return (results.reshape(shape), input_grads.reshape(shape), totals[0], totals[1], totals[2], totals[3], totals[4], totals[5], totals[6], totals[7], totals[8])
```

```python
import functools

import jax
import jax.numpy as jnp
from jax import lax
from jax.experimental import pallas as pl
from jax.experimental.pallas import tpu as pltpu
from jax.sharding import PartitionSpec as P

HD = 64
EPSILON = 1e-06
MASKED = -1e30
TILE = 256
VMEM_LIMIT = 60 * 1024 * 1024
BF = jnp.bfloat16
F32 = jnp.float32


def mm(left, right):
    return jnp.dot(left, right, preferred_element_type=F32)


def mm_nt(left, right):
    return lax.dot_general(left, right, (((1,), (1,)), ((), ())), preferred_element_type=F32)


def identity(size):
    rows = lax.broadcasted_iota(jnp.int32, (size, size), 0)
    cols = lax.broadcasted_iota(jnp.int32, (size, size), 1)
    return jnp.where(rows == cols, 1.0, 0.0).astype(BF)


def flipped(values):
    return mm_nt(identity(values.shape[1]), values).astype(BF)


def flip_into(dest, values):
    eye = identity(TILE)
    for start in range(0, values.shape[1], TILE):
        dest[start : start + TILE, :] = mm_nt(eye, values[:, start : start + TILE]).astype(BF)


def inverse_rms(features):
    return lax.rsqrt(jnp.mean(features * features, axis=-1, keepdims=True) + EPSILON)


def assemble(meta, pieces, dest, sems, width):
    copies = []
    for index, piece in enumerate(pieces):
        rows = piece.shape[0]
        start = pl.multiple_of(meta[index], 16) if len(pieces) > 1 else 0
        copy = pltpu.make_async_copy(
            piece.at[:, pl.ds(0, width)], dest.at[pl.ds(start, rows), :], sems.at[index]
        )
        copy.start()
        copies.append(copy)
    return copies


def disperse(meta, source, groups, sems, base):
    copies = []
    count = sum(group.shape[0] for group in groups)
    index = 0
    for group in groups:
        rows = group.shape[1]
        for place in range(group.shape[0]):
            start = pl.multiple_of(meta[index], 16) if count > 1 else 0
            copy = pltpu.make_async_copy(
                source.at[pl.ds(start, rows), :], group.at[place], sems.at[base + index]
            )
            copy.start()
            copies.append(copy)
            index += 1
    return copies


def wait_all(copies):
    for copy in copies:
        copy.wait()


def forward_kernel(heads, n_pieces, first, meta, *refs):
    refs = list(refs)
    take = lambda count: [refs.pop(0) for _ in range(count)]
    width = heads * HD
    if first:
        rows_in = take(4)
        (gain,) = take(1)
        pieces = take(n_pieces)
        normed, proj, expo, inverse, context = take(5)
        weight, q_ext, k_ext, v_flip, sems = take(5)
    else:
        (normed, context_first) = take(2)
        pieces_first = take(n_pieces)
        pieces = take(n_pieces)
        proj, expo, inverse, context, partial = take(5)
        weight, q_ext, k_ext, v_flip, out_first, sems, sems_first = take(7)
    step = pl.program_id(0)

    @pl.when(step == 0)
    def _():
        copies = assemble(meta, pieces, weight, sems, weight.shape[1])
        if not first:
            copies += assemble(meta, pieces_first, out_first, sems_first, out_first.shape[1])
        if first:
            for block in range(4):
                features = rows_in[block][...].astype(F32)
                normed[block * TILE : (block + 1) * TILE, :] = (
                    features * inverse_rms(features) * gain[...]
                ).astype(BF)
        wait_all(copies)
        lanes = lax.broadcasted_iota(jnp.int32, (TILE, HD), 1)
        index = lax.broadcasted_iota(jnp.int32, (TILE, HD), 0)
        for block in range(4):
            rows = slice(block * TILE, (block + 1) * TILE)
            tile = mm(normed[rows, :], weight[...]).astype(BF)
            proj[rows, :] = tile
            usable = meta[8 + block] + index < meta[12]
            bias = jnp.where((lanes == 0) & ~usable, MASKED, 0.0).astype(BF)
            ones = jnp.where(lanes == 0, 1.0, 0.0).astype(BF)
            for head in range(heads):
                at = width + head * HD
                q_ext[head, rows, 0:HD] = tile[:, at : at + HD]
                q_ext[head, rows, HD : 2 * HD] = ones
                at = 2 * width + head * HD
                k_ext[head, rows, 0:HD] = tile[:, at : at + HD]
                k_ext[head, rows, HD : 2 * HD] = bias
        total = proj.shape[0]
        below = lax.broadcasted_iota(jnp.int32, (16, total), 0)
        for head in range(heads):
            at = 3 * width + head * HD
            v_flip[head, 0:HD, :] = flipped(proj[:, at : at + HD])
            v_flip[head, HD : HD + 16, :] = jnp.where(below == 0, 1.0, 0.0).astype(BF)

    rows = pl.ds(pl.multiple_of(step * TILE, TILE), TILE)
    eye = identity(TILE)
    inverse[...] = jnp.ones_like(inverse)
    for head in range(heads):
        scores = mm_nt(k_ext[head], q_ext[head, rows, :])
        top = jnp.max(scores, axis=0, keepdims=True)
        raised = jnp.exp(scores - top).astype(BF)
        expo[head] = raised
        mixed = mm(v_flip[head], raised)
        inv = 1.0 / mixed[HD : HD + 1, :]
        inverse[head : head + 1, :] = inv
        low = (mixed[0:HD, :] * inv).astype(BF)
        context[:, head * HD : (head + 1) * HD] = mm_nt(eye, low).astype(BF)
    if not first:
        partial[...] = (
            mm_nt(context_first[...], out_first[:, 0:width])
            + mm_nt(context[...], weight[:, 0:width])
        ).astype(BF)


def whole(shape):
    return pl.BlockSpec(shape, lambda step: (0,) * len(shape))


ANY = pl.BlockSpec(memory_space=pl.ANY)
SMEM = pl.BlockSpec(memory_space=pltpu.SMEM)


def params():
    return pltpu.CompilerParams(
        vmem_limit_bytes=VMEM_LIMIT, dimension_semantics=("arbitrary",)
    )


def attention_forward(meta, heads, pieces, rows_in=None, gain=None, normed=None, before=None):
    first = before is None
    width = pieces[0].shape[1]
    model = rows_in[0].shape[1] if first else normed.shape[1]
    total = 4 * TILE
    n_pieces = len(pieces)
    head_width = heads * HD
    out_shape = [
        jax.ShapeDtypeStruct((total, width), BF),
        jax.ShapeDtypeStruct((heads, total, total), BF),
        jax.ShapeDtypeStruct((8, total), F32),
        jax.ShapeDtypeStruct((total, head_width), BF),
    ]
    out_specs = [
        whole((total, width)),
        pl.BlockSpec((heads, total, TILE), lambda step: (0, 0, step)),
        pl.BlockSpec((8, TILE), lambda step: (0, step)),
        pl.BlockSpec((TILE, head_width), lambda step: (step, 0)),
    ]
    scratch = [
        pltpu.VMEM((model, width), BF),
        pltpu.VMEM((heads, total, 2 * HD), BF),
        pltpu.VMEM((heads, total, 2 * HD), BF),
        pltpu.VMEM((heads, HD + 16, total), BF),
    ]
    if first:
        operands = [meta, *rows_in, gain, *pieces]
        in_specs = [SMEM] + [whole((TILE, model))] * 4 + [whole((1, model))] + [ANY] * n_pieces
        out_shape = [jax.ShapeDtypeStruct((total, model), BF)] + out_shape
        out_specs = [whole((total, model))] + out_specs
        scratch += [pltpu.SemaphoreType.DMA((n_pieces,))]
    else:
        pieces_first, context_first = before
        operands = [meta, normed, context_first, *pieces_first, *pieces]
        in_specs = [
            SMEM,
            whole((total, model)),
            pl.BlockSpec((TILE, head_width), lambda step: (step, 0)),
        ] + [ANY] * (2 * n_pieces)
        out_shape = out_shape + [jax.ShapeDtypeStruct((total, model), BF)]
        out_specs = out_specs + [pl.BlockSpec((TILE, model), lambda step: (step, 0))]
        scratch += [
            pltpu.VMEM((model, 256), BF),
            pltpu.SemaphoreType.DMA((n_pieces,)),
            pltpu.SemaphoreType.DMA((n_pieces,)),
        ]
    return pl.pallas_call(
        functools.partial(forward_kernel, heads, n_pieces, first),
        grid=(4,),
        in_specs=in_specs,
        out_specs=out_specs,
        out_shape=out_shape,
        scratch_shapes=scratch,
        compiler_params=params(),
        cost_estimate=pl.CostEstimate(
            flops=16 * 10**9, bytes_accessed=12 * 10**6, transcendentals=3 * 10**6
        ),
        name="attention_forward",
    )(*operands)


def gelu_terms(gate):
    scale = 0.7978845608028654
    cube = 0.044715
    square = gate * gate
    bent = jnp.tanh(scale * gate * (1.0 + cube * square))
    half = 0.5 * (1.0 + bent)
    slope = half + 0.5 * gate * (1.0 - bent * bent) * (scale * (1.0 + 3.0 * cube * square))
    return gate * half, slope


def feed_kernel(n_pieces, groups_near, groups_far, meta, *refs):
    refs = list(refs)
    take = lambda count: [refs.pop(0) for _ in range(count)]
    rows_in = take(4)
    part_mine, part_other, gain = take(3)
    cots = take(4)
    pieces_near = take(n_pieces)
    pieces_far = take(n_pieces)
    mine, other, d_normed = take(3)
    near = take(groups_near)
    far = take(groups_far)
    (weight, hidden, d_gate, d_up, normed_all, cot_all, flip_n, flip_c, grad, sems, sems_out) = take(11)
    units = weight.shape[2] // 3
    step = pl.program_id(0)
    copies = []

    @pl.when(step == 0)
    def _():
        made = assemble(meta, pieces_near, weight.at[0], sems.at[0], weight.shape[2])
        made += assemble(meta, pieces_far, weight.at[1], sems.at[1], weight.shape[2])
        wait_all(made)

    def tile(block):
        rows = slice(block * TILE, (block + 1) * TILE)
        swapped = slice(((block + 2) % 4) * TILE, ((block + 2) % 4 + 1) * TILE)
        features = (
            rows_in[block][...].astype(F32)
            + part_mine[rows, :].astype(F32)
            + part_other[swapped, :].astype(F32)
        )
        features = features.astype(BF).astype(F32)
        normed = (features * inverse_rms(features) * gain[...]).astype(BF)
        normed_all[rows, :] = normed
        cot = cots[block][...]
        cot_all[rows, :] = cot
        result = None
        back = None
        for part in range(2):
            pre = mm(normed, weight[part, :, 0 : 2 * units])
            act, slope = gelu_terms(pre[:, :units])
            up = pre[:, units:]
            low = (act * up).astype(BF)
            hidden[part, rows, :] = low
            d_hidden = mm(cot, weight[part, :, 2 * units :])
            gate_low = (d_hidden * up * slope).astype(BF)
            up_low = (d_hidden * act).astype(BF)
            d_gate[part, rows, :] = gate_low
            d_up[part, rows, :] = up_low
            down = mm_nt(low, weight[part, :, 2 * units :])
            through = mm_nt(gate_low, weight[part, :, 0:units]) + mm_nt(
                up_low, weight[part, :, units : 2 * units]
            )
            result = down if result is None else result + down
            back = through if back is None else back + through
        if block < 2:
            mine[rows, :] = result.astype(BF)
        else:
            other[(block - 2) * TILE : (block - 1) * TILE, :] = result.astype(BF)
        d_normed[rows, :] = back.astype(BF)

    for block in range(4):
        pl.when(step == block)(functools.partial(tile, block))

    @pl.when(step == 3)
    def _():
        flip_into(flip_n, normed_all)
        flip_into(flip_c, cot_all)
        made = []
        for part, groups in ((1, far), (0, near)):
            grad[part, :, 0:units] = mm(flip_n[...], d_gate[part]).astype(BF)
            grad[part, :, units : 2 * units] = mm(flip_n[...], d_up[part]).astype(BF)
            grad[part, :, 2 * units :] = mm(flip_c[...], hidden[part]).astype(BF)
            made += disperse(meta, grad.at[part], groups, sems_out.at[part], 0)
        wait_all(made)


def feed_forward(meta, rows_in, part_mine, part_other, gain, cots, near, far, shapes_near, shapes_far):
    n_pieces = len(near)
    width = near[0].shape[1]
    model = part_mine.shape[1]
    total = 4 * TILE
    units = width // 3
    out_shape = [
        jax.ShapeDtypeStruct((2 * TILE, model), BF),
        jax.ShapeDtypeStruct((2 * TILE, model), BF),
        jax.ShapeDtypeStruct((total, model), BF),
    ] + [jax.ShapeDtypeStruct((*shape, width), BF) for shape in (*shapes_near, *shapes_far)]
    return pl.pallas_call(
        functools.partial(feed_kernel, n_pieces, len(shapes_near), len(shapes_far)),
        grid=(4,),
        in_specs=[SMEM]
        + [whole((TILE, model))] * 4
        + [whole((total, model))] * 2
        + [whole((1, model))]
        + [whole((TILE, model))] * 4
        + [ANY] * (2 * n_pieces),
        out_specs=[whole((2 * TILE, model))] * 2
        + [whole((total, model))]
        + [ANY] * (len(shapes_near) + len(shapes_far)),
        out_shape=out_shape,
        scratch_shapes=[
            pltpu.VMEM((2, model, width), BF),
            pltpu.VMEM((2, total, units), BF),
            pltpu.VMEM((2, total, units), BF),
            pltpu.VMEM((2, total, units), BF),
            pltpu.VMEM((total, model), BF),
            pltpu.VMEM((total, model), BF),
            pltpu.VMEM((model, total), BF),
            pltpu.VMEM((model, total), BF),
            pltpu.VMEM((2, model, width), BF),
            pltpu.SemaphoreType.DMA((2, n_pieces)),
            pltpu.SemaphoreType.DMA((2, n_pieces)),
        ],
        compiler_params=params(),
        cost_estimate=pl.CostEstimate(
            flops=16 * 10**9, bytes_accessed=20 * 10**6, transcendentals=10**6
        ),
        name="feed_forward",
    )(meta, *rows_in, part_mine, part_other, gain, *cots, *near, *far)


def middle_kernel(heads, n_pieces, meta, *refs):
    refs = list(refs)
    take = lambda count: [refs.pop(0) for _ in range(count)]
    rows_in = take(4)
    part_mine, part_other, gain = take(3)
    cots = take(4)
    d_mine, d_other, context_near, context_far = take(4)
    pieces_near = take(n_pieces)
    pieces_far = take(n_pieces)
    d_middle, d_context_near, d_context_far, grad_near, grad_far, d_gain = take(6)
    weight, d_all, flip_d, sems = take(4)
    width = heads * HD
    step = pl.program_id(0)

    @pl.when(step == 0)
    def _():
        made = assemble(meta, pieces_near, weight.at[0], sems.at[0], weight.shape[2])
        made += assemble(meta, pieces_far, weight.at[1], sems.at[1], weight.shape[2])
        d_gain[...] = jnp.zeros_like(d_gain)
        wait_all(made)

    def tile(block):
        rows = slice(block * TILE, (block + 1) * TILE)
        swapped = slice(((block + 2) % 4) * TILE, ((block + 2) % 4 + 1) * TILE)
        features = (
            rows_in[block][...].astype(F32)
            + part_mine[rows, :].astype(F32)
            + part_other[swapped, :].astype(F32)
        )
        features = features.astype(BF).astype(F32)
        inverse = inverse_rms(features)
        back = d_mine[rows, :].astype(F32) + d_other[swapped, :].astype(F32)
        scaled = back * gain[...]
        inner = jnp.mean(scaled * features, axis=-1, keepdims=True)
        result = (
            cots[block][...].astype(F32)
            + inverse * scaled
            - features * (inverse * inverse * inverse * inner)
        )
        low = result.astype(BF)
        d_all[rows, :] = low
        if block < 2:
            d_middle[rows, :] = result
            d_gain[0:1, :] += jnp.sum(back * features * inverse, axis=0, keepdims=True)
        d_context_near[rows, :] = mm(low, weight[0, :, 0:width]).astype(BF)
        d_context_far[rows, :] = mm(low, weight[1, :, 0:width]).astype(BF)

    for block in range(4):
        pl.when(step == block)(functools.partial(tile, block))

    @pl.when(step == 3)
    def _():
        flip_into(flip_d, d_all)
        grad_near[...] = mm(flip_d[...], context_near[...]).astype(BF)
        grad_far[...] = mm(flip_d[...], context_far[...]).astype(BF)


def middle_backward(
    meta, heads, rows_in, part_mine, part_other, gain, cots, d_mine, d_other, contexts, near, far
):
    n_pieces = len(near)
    model = part_mine.shape[1]
    total = 4 * TILE
    width = heads * HD
    return pl.pallas_call(
        functools.partial(middle_kernel, heads, n_pieces),
        grid=(4,),
        in_specs=[SMEM]
        + [whole((TILE, model))] * 4
        + [whole((total, model))] * 2
        + [whole((1, model))]
        + [whole((TILE, model))] * 4
        + [whole((total, model))] * 2
        + [whole((total, width))] * 2
        + [ANY] * (2 * n_pieces),
        out_specs=[
            whole((2 * TILE, model)),
            whole((total, width)),
            whole((total, width)),
            whole((model, width)),
            whole((model, width)),
            whole((8, model)),
        ],
        out_shape=[
            jax.ShapeDtypeStruct((2 * TILE, model), F32),
            jax.ShapeDtypeStruct((total, width), BF),
            jax.ShapeDtypeStruct((total, width), BF),
            jax.ShapeDtypeStruct((model, width), BF),
            jax.ShapeDtypeStruct((model, width), BF),
            jax.ShapeDtypeStruct((8, model), F32),
        ],
        scratch_shapes=[
            pltpu.VMEM((2, model, 256), BF),
            pltpu.VMEM((total, model), BF),
            pltpu.VMEM((model, total), BF),
            pltpu.SemaphoreType.DMA((2, n_pieces)),
        ],
        compiler_params=params(),
        cost_estimate=pl.CostEstimate(
            flops=3 * 10**9, bytes_accessed=15 * 10**6, transcendentals=1000
        ),
        name="middle_backward",
    )(meta, *rows_in, part_mine, part_other, gain, *cots, d_mine, d_other, *contexts, *near, *far)


def backward_kernel(heads, n_pieces, n_groups, last, meta, *refs):
    refs = list(refs)
    take = lambda count: [refs.pop(0) for _ in range(count)]
    normed, proj, expo, inverse, context, d_context, grad_out = take(7)
    pieces = take(n_pieces)
    if last:
        (before,) = take(1)
        mine, other = take(2)
    else:
        (result,) = take(1)
    groups = take(n_groups)
    weight, do_ext, v_ext, k_flip, d_keys, d_proj, flip_n, grad, sems, sems_out = take(10)
    width = heads * HD
    total = 4 * TILE
    step = pl.program_id(0)

    @pl.when(step == 0)
    def _():
        assemble(meta, pieces, weight, sems, weight.shape[1])
        lanes = lax.broadcasted_iota(jnp.int32, (total, HD), 1)
        columns = inverse[...].T
        for head in range(heads):
            at = head * HD
            scaled = (
                d_context[:, at : at + HD].astype(F32) * columns[:, head : head + 1]
            ).astype(BF)
            inner = -jnp.sum(
                scaled.astype(F32) * context[:, at : at + HD].astype(F32), axis=-1, keepdims=True
            )
            high = inner.astype(BF).astype(F32)
            do_ext[head, :, 0:HD] = scaled
            do_ext[head, :, HD : 2 * HD] = jnp.where(
                lanes == 0, high, jnp.where(lanes == 1, inner - high, 0.0)
            ).astype(BF)
            v_ext[head, :, 0:HD] = proj[:, 3 * width + at : 3 * width + at + HD]
            v_ext[head, :, HD : 2 * HD] = jnp.where(lanes < 2, 1.0, 0.0).astype(BF)
            k_flip[head] = flipped(proj[:, 2 * width + at : 2 * width + at + HD])
        d_keys[...] = jnp.zeros_like(d_keys)
        d_proj[:, 0:width] = jnp.zeros((total, width), BF)
        flip_into(flip_n, normed)

    rows = pl.ds(pl.multiple_of(step * TILE, TILE), TILE)
    eye = identity(TILE)
    for head in range(heads):
        at = head * HD
        raised = expo[head]
        d_out = do_ext[head, rows, :]
        d_probs = mm_nt(v_ext[head], d_out)
        d_scores = (raised.astype(F32) * d_probs).astype(BF)
        d_keys[head, :, 0:HD] += mm(d_scores, proj[rows, width + at : width + at + HD])
        d_keys[head, :, HD : 2 * HD] += mm(raised, d_out[:, 0:HD])
        d_query = mm(k_flip[head], d_scores).astype(BF)
        d_proj[rows, width + at : width + at + HD] = mm_nt(eye, d_query).astype(BF)

    @pl.when(step == 3)
    def _():
        for head in range(heads):
            at = head * HD
            d_proj[:, 2 * width + at : 2 * width + at + HD] = d_keys[head, :, 0:HD].astype(BF)
            d_proj[:, 3 * width + at : 3 * width + at + HD] = d_keys[head, :, HD : 2 * HD].astype(
                BF
            )
        for index in range(n_pieces):
            piece = pieces[index]
            start = pl.multiple_of(meta[index], 16) if n_pieces > 1 else 0
            pltpu.make_async_copy(
                piece.at[:, pl.ds(0, weight.shape[1])],
                weight.at[pl.ds(start, piece.shape[0]), :],
                sems.at[index],
            ).wait()
        grad[...] = mm(flip_n[...], d_proj[...]).astype(BF)
        grad[:, 0:width] = grad_out[...]
        made = disperse(meta, grad, groups, sems_out, 0)
        through = mm_nt(d_proj[...], weight[...])
        if last:
            through = through + before[...].astype(F32)
            mine[...] = through[0 : 2 * TILE].astype(BF)
            other[...] = through[2 * TILE :].astype(BF)
        else:
            result[...] = through.astype(BF)
        wait_all(made)


def attention_backward(
    meta, heads, normed, proj, expo, inverse, context, d_context, grad_out, pieces, shapes, before=None
):
    last = before is not None
    n_pieces = len(pieces)
    model = normed.shape[1]
    width = proj.shape[1]
    total = 4 * TILE
    head_width = heads * HD
    operands = [meta, normed, proj, expo, inverse, context, d_context, grad_out, *pieces]
    in_specs = [
        SMEM,
        whole((total, model)),
        whole((total, width)),
        pl.BlockSpec((heads, total, TILE), lambda step: (0, 0, step)),
        whole((8, total)),
        whole((total, head_width)),
        whole((total, head_width)),
        whole((model, head_width)),
    ] + [ANY] * n_pieces
    if last:
        operands += [before]
        in_specs += [whole((total, model))]
        out_shape = [jax.ShapeDtypeStruct((2 * TILE, model), BF)] * 2
        out_specs = [whole((2 * TILE, model))] * 2
    else:
        out_shape = [jax.ShapeDtypeStruct((total, model), BF)]
        out_specs = [whole((total, model))]
    out_shape += [jax.ShapeDtypeStruct((*shape, width), BF) for shape in shapes]
    out_specs += [ANY] * len(shapes)
    return pl.pallas_call(
        functools.partial(backward_kernel, heads, n_pieces, len(shapes), last),
        grid=(4,),
        in_specs=in_specs,
        out_specs=out_specs,
        out_shape=out_shape,
        scratch_shapes=[
            pltpu.VMEM((model, width), BF),
            pltpu.VMEM((heads, total, 2 * HD), BF),
            pltpu.VMEM((heads, total, 2 * HD), BF),
            pltpu.VMEM((heads, HD, total), BF),
            pltpu.VMEM((heads, total, 2 * HD), F32),
            pltpu.VMEM((total, width), BF),
            pltpu.VMEM((model, total), BF),
            pltpu.VMEM((model, width), BF),
            pltpu.SemaphoreType.DMA((n_pieces,)),
            pltpu.SemaphoreType.DMA((n_pieces,)),
        ],
        compiler_params=params(),
        cost_estimate=pl.CostEstimate(
            flops=24 * 10**9, bytes_accessed=12 * 10**6, transcendentals=1000
        ),
        name="attention_backward",
    )(*operands)


class Links:
    def __init__(self, wide, narrow):
        self.wide, self.narrow = wide, narrow
        self.planes = wide // 2
        self.staged = wide == 8

    def y(self, values):
        return lax.ppermute(values, "narrow", [(i, (i + 2) % 4) for i in range(4)])

    def core(self, values):
        return lax.ppermute(values, "narrow", [(i, i ^ 1) for i in range(4)])

    def x(self, values):
        return lax.ppermute(values, "wide", [(i, i ^ 1) for i in range(self.wide)])

    def z(self, values, ahead):
        turn = lambda i: ((i // 2 + ahead) % self.planes) * 2 + i % 2
        return lax.ppermute(values, "wide", [(i, turn(i)) for i in range(self.wide)])

    def gather(self, piece):
        if not self.staged:
            near = lax.all_gather(piece, "wide", axis=0, tiled=True)
            return [near], [self.y(near)]
        column = [piece] + [self.z(piece, self.planes - k) for k in range(1, self.planes)]
        over_x = [self.x(block) for block in column]
        over_y = [self.y(block) for block in column]
        half = self.planes // 2
        both = [self.y(block) for block in over_x[:half]] + [self.x(block) for block in over_y[half:]]
        return column + over_x, over_y + both

    def shapes(self, model):
        if not self.staged:
            return [(1, model)], [(1, model)]
        rows = model // self.wide
        half = self.planes // 2
        near = [(half, rows), (half, rows), (half, rows), (half, rows)]
        return near, near

    def reduce(self, near, far):
        if not self.staged:
            return lax.psum_scatter(near[0][0], "wide", scatter_dimension=0, tiled=True).astype(
                F32
            ) + lax.psum_scatter(self.y(far[0][0]), "wide", scatter_dimension=0, tiled=True).astype(F32)
        add = lambda *terms: sum(term.astype(F32) for term in terms)
        own_low, own_high, x_low, x_high = near
        y_low, y_high, xy_low, xy_high = far
        from_xy = self.y(xy_low)
        from_yx = self.x(xy_high)
        from_x_high = self.x(x_high)
        from_y_low = self.y(y_low)
        from_x_low = self.x(add(x_low, from_xy).astype(BF))
        from_y_high = self.y(add(y_high, from_yx).astype(BF))
        low = add(own_low, from_x_low, from_y_low)
        high = add(own_high, from_x_high, from_y_high)
        blocks = [low[i] for i in range(low.shape[0])] + [high[i] for i in range(high.shape[0])]
        parts = [self.z(blocks[k].astype(BF), k) for k in range(1, self.planes)]
        return add(blocks[0], *parts)

    def everywhere(self, values):
        values = values + self.core(values)
        if not self.staged:
            return lax.psum(values + self.y(values), "wide")
        over_x, over_y = self.x(values), self.y(values)
        values = values + over_x + (over_y + self.x(over_y))
        return values + sum(self.z(values, k) for k in range(1, self.planes))


def on_device(
    tokens,
    lengths,
    norm_one,
    w_query,
    w_key,
    w_value,
    w_out,
    norm_two,
    w_gate,
    w_up,
    w_down,
    cotangent,
):
    model = tokens.shape[-1]
    wide, narrow = lax.axis_size("wide"), lax.axis_size("narrow")
    links = Links(wide, narrow)
    heads = w_query.shape[1] // HD
    head_width = heads * HD
    units = w_gate.shape[1]
    at_wide, at_narrow = lax.axis_index("wide"), lax.axis_index("narrow")
    y, c = at_narrow // 2, at_narrow % 2
    x, z = at_wide % 2, at_wide // 2

    places = [
        ((z + k) % links.planes) * 2 + (x ^ side) for side in range(2) for k in range(4)
    ]
    offsets = [place * (model // wide) for place in places]
    blocks = [((y ^ far) * 2 + (c ^ side)) * TILE for side in range(2) for far in range(2)]
    length = lax.dynamic_index_in_dim(lengths, y, 0, keepdims=False)[0]
    meta = jnp.stack([jnp.asarray(v, jnp.int32) for v in (*offsets, *blocks, length)])

    gain_one = norm_one.reshape(1, model)
    gain_two = norm_two.reshape(1, model)

    def spread(rows):
        flat = rows.reshape(2, TILE, model)
        keep = lax.dynamic_index_in_dim(flat, y, 0, keepdims=False)
        give = lax.dynamic_index_in_dim(flat, 1 - y, 0, keepdims=False)
        got = links.y(give)
        return [keep, got, links.core(keep), links.core(got)]

    def bring_back(rows):
        mine, theirs = rows[:TILE], rows[TILE:]
        got = links.y(theirs)
        stacked = jnp.where(y == 0, jnp.stack([mine, got]), jnp.stack([got, mine]))
        return stacked.reshape(tokens.shape)

    rows_in = spread(tokens)
    attn_piece = jnp.concatenate([w_out.T, w_query, w_key, w_value], axis=1)
    feed_piece = jnp.concatenate([w_gate, w_up, w_down.T], axis=1)
    attn_near, attn_far = links.gather(attn_piece)
    cots = spread(cotangent)
    feed_near, feed_far = links.gather(feed_piece)

    normed, proj_near, expo_near, inv_near, context_near = attention_forward(
        meta, heads, attn_near, rows_in=rows_in, gain=gain_one
    )
    proj_far, expo_far, inv_far, context_far, part_mine = attention_forward(
        meta, heads, attn_far, normed=normed, before=(attn_near, context_near)
    )
    part_other = links.core(part_mine)

    shapes_near, shapes_far = links.shapes(model)
    mlp_mine, mlp_other, d_mine, *grads = feed_forward(
        meta, rows_in, part_mine, part_other, gain_two, cots, feed_near, feed_far, shapes_near, shapes_far
    )
    d_other = links.core(d_mine)
    feed_grad = links.reduce(grads[: len(shapes_near)], grads[len(shapes_near) :])

    half = 2 * TILE
    own_rows = jnp.concatenate(rows_in[:2], axis=0).astype(F32)
    result = (
        own_rows
        + part_mine[:half].astype(F32)
        + part_other[half:].astype(F32)
        + mlp_mine.astype(F32)
        + links.core(mlp_other).astype(F32)
    ).astype(BF)
    output = bring_back(result)

    d_middle, d_context_near, d_context_far, out_near, out_far, gain_rows = middle_backward(
        meta,
        heads,
        rows_in,
        part_mine,
        part_other,
        gain_two,
        cots,
        d_mine,
        d_other,
        (context_near, context_far),
        attn_near,
        attn_far,
    )
    d_first, *far = attention_backward(
        meta, heads, normed, proj_far, expo_far, inv_far, context_far, d_context_far, out_far,
        attn_far, shapes_far,
    )
    last_mine, last_other, *near = attention_backward(
        meta, heads, normed, proj_near, expo_near, inv_near, context_near, d_context_near, out_near,
        attn_near, shapes_near, before=d_first,
    )
    attn_grad = links.reduce(near, far)

    d_normed = last_mine.astype(F32) + links.core(last_other).astype(F32)
    inverse = inverse_rms(own_rows)
    scaled = d_normed * gain_one
    inner = jnp.mean(scaled * own_rows, axis=-1, keepdims=True)
    d_tokens = (
        d_middle + inverse * scaled - own_rows * (inverse * inverse * inverse * inner)
    ).astype(BF)
    input_grad = bring_back(d_tokens)
    gain_first = jnp.sum(d_normed * own_rows * inverse, axis=0)
    gains = links.everywhere(jnp.stack([gain_first, gain_rows[0]]))
    return (
        output,
        input_grad,
        gains[0],
        attn_grad[:, head_width : 2 * head_width],
        attn_grad[:, 2 * head_width : 3 * head_width],
        attn_grad[:, 3 * head_width :],
        attn_grad[:, :head_width].T,
        gains[1],
        feed_grad[:, :units],
        feed_grad[:, units : 2 * units],
        feed_grad[:, 2 * units :].T,
    )


def solution(mesh):
    in_specs = (
        P(None, "wide", "narrow", None),
        P(None, "wide"),
        P(),
        P("wide", "narrow"),
        P("wide", "narrow"),
        P("wide", "narrow"),
        P("narrow", "wide"),
        P(),
        P("wide", "narrow"),
        P("wide", "narrow"),
        P("narrow", "wide"),
        P(None, "wide", "narrow", None),
    )
    out_specs = (
        P(None, "wide", "narrow", None),
        P(None, "wide", "narrow", None),
        P(),
        P("wide", "narrow"),
        P("wide", "narrow"),
        P("wide", "narrow"),
        P("narrow", "wide"),
        P(),
        P("wide", "narrow"),
        P("wide", "narrow"),
        P("narrow", "wide"),
    )
    return jax.shard_map(
        on_device, mesh=mesh, in_specs=in_specs, out_specs=out_specs, check_vma=False
    )
```

```python
import functools

import jax
import jax.numpy as jnp
from jax import lax
from jax.experimental import pallas as pl
from jax.experimental.pallas import tpu as pltpu
from jax.sharding import PartitionSpec as P

HD = 64
EPSILON = 1e-06
MASKED = -1e30
TILE = 256
FEED_ROWS = 1024
FEED_LIMIT = 40 * 1024 * 1024
VMEM_LIMIT = 60 * 1024 * 1024
BF = jnp.bfloat16
F32 = jnp.float32


def mm(left, right):
    return jnp.dot(left, right, preferred_element_type=F32)


def mm_nt(left, right):
    return lax.dot_general(left, right, (((1,), (1,)), ((), ())), preferred_element_type=F32)


def mm_tn(left, right):
    return lax.dot_general(left, right, (((0,), (0,)), ((), ())), preferred_element_type=F32)


def inverse_rms(features):
    return lax.rsqrt(jnp.mean(features * features, axis=-1, keepdims=True) + EPSILON)


def assemble(meta, pieces, dest, sems, width):
    copies = []
    for index, piece in enumerate(pieces):
        rows = piece.shape[0]
        start = pl.multiple_of(meta[index], 16) if len(pieces) > 1 else 0
        copy = pltpu.make_async_copy(
            piece.at[:, pl.ds(0, width)], dest.at[pl.ds(start, rows), :], sems.at[index]
        )
        copy.start()
        copies.append(copy)
    return copies


def disperse(meta, source, groups, sems, base):
    copies = []
    count = sum(group.shape[0] for group in groups)
    index = 0
    for group in groups:
        rows = group.shape[1]
        for place in range(group.shape[0]):
            start = pl.multiple_of(meta[index], 16) if count > 1 else 0
            copy = pltpu.make_async_copy(
                source.at[pl.ds(start, rows), :], group.at[place], sems.at[base + index]
            )
            copy.start()
            copies.append(copy)
            index += 1
    return copies


def wait_all(copies):
    for copy in copies:
        copy.wait()


def forward_kernel(heads, n_pieces, first, meta, *refs):
    refs = list(refs)
    take = lambda count: [refs.pop(0) for _ in range(count)]
    width = heads * HD
    if first:
        rows_in = take(4)
        (gain,) = take(1)
        pieces = take(n_pieces)
        normed, proj, expo, inverse, context = take(5)
        weight, q_ext, k_ext, v_flip, sems = take(5)
    else:
        (normed, context_first) = take(2)
        pieces_first = take(n_pieces)
        pieces = take(n_pieces)
        proj, expo, inverse, context, partial = take(5)
        weight, q_ext, k_ext, v_flip, out_first, sems, sems_first = take(7)
    step = pl.program_id(0)

    @pl.when(step == 0)
    def _():
        copies = assemble(meta, pieces, weight, sems, weight.shape[1])
        if not first:
            copies += assemble(meta, pieces_first, out_first, sems_first, out_first.shape[1])
        if first:
            for block in range(4):
                features = rows_in[block][...].astype(F32)
                normed[block * TILE : (block + 1) * TILE, :] = (
                    features * inverse_rms(features) * gain[...]
                ).astype(BF)
        wait_all(copies)
        lanes = lax.broadcasted_iota(jnp.int32, (TILE, HD), 1)
        index = lax.broadcasted_iota(jnp.int32, (TILE, HD), 0)
        for block in range(4):
            rows = slice(block * TILE, (block + 1) * TILE)
            tile = mm(normed[rows, :], weight[...]).astype(BF)
            proj[rows, :] = tile
            usable = meta[8 + block] + index < meta[12]
            bias = jnp.where((lanes == 0) & ~usable, MASKED, 0.0).astype(BF)
            ones = jnp.where(lanes == 0, 1.0, 0.0).astype(BF)
            for head in range(heads):
                at = width + head * HD
                q_ext[head, rows, 0:HD] = tile[:, at : at + HD]
                q_ext[head, rows, HD : 2 * HD] = ones
                at = 2 * width + head * HD
                k_ext[head, rows, 0:HD] = tile[:, at : at + HD]
                k_ext[head, rows, HD : 2 * HD] = bias
        total = proj.shape[0]
        below = lax.broadcasted_iota(jnp.int32, (16, total), 0)
        for head in range(heads):
            at = 3 * width + head * HD
            v_flip[head, 0:HD, :] = proj[:, at : at + HD].T
            v_flip[head, HD : HD + 16, :] = jnp.where(below == 0, 1.0, 0.0).astype(BF)

    rows = pl.ds(pl.multiple_of(step * TILE, TILE), TILE)
    inverse[...] = jnp.ones_like(inverse)
    for head in range(heads):
        scores = mm_nt(k_ext[head], q_ext[head, rows, :])
        top = jnp.max(scores, axis=0, keepdims=True)
        raised = jnp.exp(scores - top).astype(BF)
        expo[head] = raised
        mixed = mm(v_flip[head], raised)
        inv = 1.0 / mixed[HD : HD + 1, :]
        inverse[head : head + 1, :] = inv
        low = (mixed[0:HD, :] * inv).astype(BF)
        context[:, head * HD : (head + 1) * HD] = low.T
    if not first:
        partial[...] = (
            mm_nt(context_first[...], out_first[:, 0:width])
            + mm_nt(context[...], weight[:, 0:width])
        ).astype(BF)


def whole(shape):
    return pl.BlockSpec(shape, lambda step: (0,) * len(shape))


ANY = pl.BlockSpec(memory_space=pl.ANY)
SMEM = pl.BlockSpec(memory_space=pltpu.SMEM)


def params():
    return pltpu.CompilerParams(
        vmem_limit_bytes=VMEM_LIMIT, dimension_semantics=("arbitrary",)
    )


def attention_forward(meta, heads, pieces, rows_in=None, gain=None, normed=None, before=None):
    first = before is None
    width = pieces[0].shape[1]
    model = rows_in[0].shape[1] if first else normed.shape[1]
    total = 4 * TILE
    n_pieces = len(pieces)
    head_width = heads * HD
    out_shape = [
        jax.ShapeDtypeStruct((total, width), BF),
        jax.ShapeDtypeStruct((heads, total, total), BF),
        jax.ShapeDtypeStruct((8, total), F32),
        jax.ShapeDtypeStruct((total, head_width), BF),
    ]
    out_specs = [
        whole((total, width)),
        pl.BlockSpec((heads, total, TILE), lambda step: (0, 0, step)),
        pl.BlockSpec((8, TILE), lambda step: (0, step)),
        pl.BlockSpec((TILE, head_width), lambda step: (step, 0)),
    ]
    scratch = [
        pltpu.VMEM((model, width), BF),
        pltpu.VMEM((heads, total, 2 * HD), BF),
        pltpu.VMEM((heads, total, 2 * HD), BF),
        pltpu.VMEM((heads, HD + 16, total), BF),
    ]
    if first:
        operands = [meta, *rows_in, gain, *pieces]
        in_specs = [SMEM] + [whole((TILE, model))] * 4 + [whole((1, model))] + [ANY] * n_pieces
        out_shape = [jax.ShapeDtypeStruct((total, model), BF)] + out_shape
        out_specs = [whole((total, model))] + out_specs
        scratch += [pltpu.SemaphoreType.DMA((n_pieces,))]
    else:
        pieces_first, context_first = before
        operands = [meta, normed, context_first, *pieces_first, *pieces]
        in_specs = [
            SMEM,
            whole((total, model)),
            pl.BlockSpec((TILE, head_width), lambda step: (step, 0)),
        ] + [ANY] * (2 * n_pieces)
        out_shape = out_shape + [jax.ShapeDtypeStruct((total, model), BF)]
        out_specs = out_specs + [pl.BlockSpec((TILE, model), lambda step: (step, 0))]
        scratch += [
            pltpu.VMEM((model, 256), BF),
            pltpu.SemaphoreType.DMA((n_pieces,)),
            pltpu.SemaphoreType.DMA((n_pieces,)),
        ]
    return pl.pallas_call(
        functools.partial(forward_kernel, heads, n_pieces, first),
        grid=(4,),
        in_specs=in_specs,
        out_specs=out_specs,
        out_shape=out_shape,
        scratch_shapes=scratch,
        compiler_params=params(),
        cost_estimate=pl.CostEstimate(
            flops=16 * 10**9, bytes_accessed=12 * 10**6, transcendentals=3 * 10**6
        ),
        name="attention_forward",
    )(*operands)


def gelu_terms(gate):
    scale = 0.7978845608028654
    cube = 0.044715
    square = gate * gate
    bent = jnp.tanh(scale * gate * (1.0 + cube * square))
    half = 0.5 * (1.0 + bent)
    slope = half + 0.5 * gate * (1.0 - bent * bent) * (scale * (1.0 + 3.0 * cube * square))
    return gate * half, slope


def feed_kernel(n_pieces, n_groups, first, meta, *refs):
    refs = list(refs)
    take = lambda count: [refs.pop(0) for _ in range(count)]
    if first:
        rows_in = take(4)
        part_mine, part_other, gain = take(3)
    else:
        normed, result_before, back_before = take(3)
    cots = take(4)
    pieces = take(n_pieces)
    if first:
        normed, result, back = take(3)
    else:
        mine, other, back = take(3)
    groups = take(n_groups)
    weight, hidden, d_gate, d_up, cot, grad, sems, sems_out = take(8)
    units = weight.shape[1] // 3
    copies = assemble(meta, pieces, weight, sems, weight.shape[1])
    for block in range(4):
        rows = slice(block * TILE, (block + 1) * TILE)
        cot[rows, :] = cots[block][...]
        if first:
            swapped = slice(((block + 2) % 4) * TILE, ((block + 2) % 4 + 1) * TILE)
            features = (
                rows_in[block][...].astype(F32)
                + part_mine[rows, :].astype(F32)
                + part_other[swapped, :].astype(F32)
            )
            features = features.astype(BF).astype(F32)
            normed[rows, :] = (features * inverse_rms(features) * gain[...]).astype(BF)
    wait_all(copies)
    for start in range(0, 4 * TILE, FEED_ROWS):
        rows = slice(start, start + FEED_ROWS)
        pre = mm(normed[rows, :], weight[:, 0 : 2 * units])
        act, slope = gelu_terms(pre[:, :units])
        up = pre[:, units:]
        low = (act * up).astype(BF)
        hidden[rows, :] = low
        d_hidden = mm(cot[rows, :], weight[:, 2 * units :])
        gate_low = (d_hidden * up * slope).astype(BF)
        up_low = (d_hidden * act).astype(BF)
        d_gate[rows, :] = gate_low
        d_up[rows, :] = up_low
        down = mm_nt(low, weight[:, 2 * units :])
        through = mm_nt(gate_low, weight[:, 0:units]) + mm_nt(up_low, weight[:, units : 2 * units])
        if first:
            result[rows, :] = down.astype(BF)
            back[rows, :] = through.astype(BF)
        else:
            down = (down + result_before[rows, :].astype(F32)).astype(BF)
            if start < 2 * TILE:
                mine[rows, :] = down[: 2 * TILE - start]
            if start + FEED_ROWS > 2 * TILE:
                begin = max(start - 2 * TILE, 0)
                other[begin : start + FEED_ROWS - 2 * TILE, :] = down[begin + 2 * TILE - start :]
            back[rows, :] = (through + back_before[rows, :].astype(F32)).astype(BF)
    grad[:, 2 * units :] = mm_tn(cot[...], hidden[...]).astype(BF)
    grad[:, 0:units] = mm_tn(normed[...], d_gate[...]).astype(BF)
    grad[:, units : 2 * units] = mm_tn(normed[...], d_up[...]).astype(BF)
    wait_all(disperse(meta, grad, groups, sems_out, 0))


def feed_forward(meta, cots, pieces, shapes, start=None, before=None):
    first = before is None
    n_pieces = len(pieces)
    width = pieces[0].shape[1]
    model = cots[0].shape[1]
    total = 4 * TILE
    units = width // 3
    full = jax.ShapeDtypeStruct((total, model), BF)
    half = jax.ShapeDtypeStruct((2 * TILE, model), BF)
    operands = [*start, *cots, *pieces] if first else [*before, *cots, *pieces]
    out_shape = [full, full, full] if first else [half, half, full]
    vmem = pl.BlockSpec(memory_space=pltpu.VMEM)
    return pl.pallas_call(
        functools.partial(feed_kernel, n_pieces, len(shapes), first),
        in_specs=[SMEM] + [vmem] * (len(operands) - n_pieces) + [ANY] * n_pieces,
        out_specs=[vmem] * 3 + [ANY] * len(shapes),
        out_shape=out_shape
        + [jax.ShapeDtypeStruct((*shape, width), BF) for shape in shapes],
        scratch_shapes=[
            pltpu.VMEM((model, width), BF),
            pltpu.VMEM((total, units), BF),
            pltpu.VMEM((total, units), BF),
            pltpu.VMEM((total, units), BF),
            pltpu.VMEM((total, model), BF),
            pltpu.VMEM((model, width), BF),
            pltpu.SemaphoreType.DMA((n_pieces,)),
            pltpu.SemaphoreType.DMA((n_pieces,)),
        ],
        compiler_params=pltpu.CompilerParams(vmem_limit_bytes=FEED_LIMIT),
        cost_estimate=pl.CostEstimate(
            flops=8 * 10**9, bytes_accessed=15 * 10**6, transcendentals=10**6
        ),
        name="feed_forward",
    )(meta, *operands)


def middle_kernel(heads, n_pieces, meta, *refs):
    refs = list(refs)
    take = lambda count: [refs.pop(0) for _ in range(count)]
    rows_in = take(4)
    part_mine, part_other, gain = take(3)
    cots = take(4)
    d_mine, d_other, context_near, context_far = take(4)
    pieces_near = take(n_pieces)
    pieces_far = take(n_pieces)
    d_middle, d_context_near, d_context_far, grad_near, grad_far, d_gain = take(6)
    weight, d_all, sems = take(3)
    width = heads * HD
    step = pl.program_id(0)

    @pl.when(step == 0)
    def _():
        made = assemble(meta, pieces_near, weight.at[0], sems.at[0], weight.shape[2])
        made += assemble(meta, pieces_far, weight.at[1], sems.at[1], weight.shape[2])
        d_gain[...] = jnp.zeros_like(d_gain)
        wait_all(made)

    def tile(block):
        rows = slice(block * TILE, (block + 1) * TILE)
        swapped = slice(((block + 2) % 4) * TILE, ((block + 2) % 4 + 1) * TILE)
        features = (
            rows_in[block][...].astype(F32)
            + part_mine[rows, :].astype(F32)
            + part_other[swapped, :].astype(F32)
        )
        features = features.astype(BF).astype(F32)
        inverse = inverse_rms(features)
        back = d_mine[rows, :].astype(F32) + d_other[swapped, :].astype(F32)
        scaled = back * gain[...]
        inner = jnp.mean(scaled * features, axis=-1, keepdims=True)
        result = (
            cots[block][...].astype(F32)
            + inverse * scaled
            - features * (inverse * inverse * inverse * inner)
        )
        low = result.astype(BF)
        d_all[rows, :] = low
        if block < 2:
            d_middle[rows, :] = result
            d_gain[0:1, :] += jnp.sum(back * features * inverse, axis=0, keepdims=True)
        d_context_near[rows, :] = mm(low, weight[0, :, 0:width]).astype(BF)
        d_context_far[rows, :] = mm(low, weight[1, :, 0:width]).astype(BF)

    for block in range(4):
        pl.when(step == block)(functools.partial(tile, block))

    @pl.when(step == 3)
    def _():
        grad_near[...] = mm_tn(d_all[...], context_near[...]).astype(BF)
        grad_far[...] = mm_tn(d_all[...], context_far[...]).astype(BF)


def middle_backward(
    meta, heads, rows_in, part_mine, part_other, gain, cots, d_mine, d_other, contexts, near, far
):
    n_pieces = len(near)
    model = part_mine.shape[1]
    total = 4 * TILE
    width = heads * HD
    return pl.pallas_call(
        functools.partial(middle_kernel, heads, n_pieces),
        grid=(4,),
        in_specs=[SMEM]
        + [whole((TILE, model))] * 4
        + [whole((total, model))] * 2
        + [whole((1, model))]
        + [whole((TILE, model))] * 4
        + [whole((total, model))] * 2
        + [whole((total, width))] * 2
        + [ANY] * (2 * n_pieces),
        out_specs=[
            whole((2 * TILE, model)),
            whole((total, width)),
            whole((total, width)),
            whole((model, width)),
            whole((model, width)),
            whole((8, model)),
        ],
        out_shape=[
            jax.ShapeDtypeStruct((2 * TILE, model), F32),
            jax.ShapeDtypeStruct((total, width), BF),
            jax.ShapeDtypeStruct((total, width), BF),
            jax.ShapeDtypeStruct((model, width), BF),
            jax.ShapeDtypeStruct((model, width), BF),
            jax.ShapeDtypeStruct((8, model), F32),
        ],
        scratch_shapes=[
            pltpu.VMEM((2, model, 256), BF),
            pltpu.VMEM((total, model), BF),
            pltpu.SemaphoreType.DMA((2, n_pieces)),
        ],
        compiler_params=params(),
        cost_estimate=pl.CostEstimate(
            flops=3 * 10**9, bytes_accessed=15 * 10**6, transcendentals=1000
        ),
        name="middle_backward",
    )(meta, *rows_in, part_mine, part_other, gain, *cots, d_mine, d_other, *contexts, *near, *far)


def backward_kernel(heads, n_pieces, n_groups, last, meta, *refs):
    refs = list(refs)
    take = lambda count: [refs.pop(0) for _ in range(count)]
    normed, proj, expo, inverse, context, d_context, grad_out = take(7)
    pieces = take(n_pieces)
    if last:
        (before,) = take(1)
        mine, other = take(2)
    else:
        (result,) = take(1)
    groups = take(n_groups)
    weight, do_ext, v_ext, k_flip, d_keys, d_proj, grad, sems, sems_out = take(9)
    width = heads * HD
    total = 4 * TILE
    step = pl.program_id(0)

    @pl.when(step == 0)
    def _():
        assemble(meta, pieces, weight, sems, weight.shape[1])
        lanes = lax.broadcasted_iota(jnp.int32, (total, HD), 1)
        columns = inverse[...].T
        for head in range(heads):
            at = head * HD
            scaled = (
                d_context[:, at : at + HD].astype(F32) * columns[:, head : head + 1]
            ).astype(BF)
            inner = -jnp.sum(
                scaled.astype(F32) * context[:, at : at + HD].astype(F32), axis=-1, keepdims=True
            )
            high = inner.astype(BF).astype(F32)
            do_ext[head, :, 0:HD] = scaled
            do_ext[head, :, HD : 2 * HD] = jnp.where(
                lanes == 0, high, jnp.where(lanes == 1, inner - high, 0.0)
            ).astype(BF)
            v_ext[head, :, 0:HD] = proj[:, 3 * width + at : 3 * width + at + HD]
            v_ext[head, :, HD : 2 * HD] = jnp.where(lanes < 2, 1.0, 0.0).astype(BF)
            k_flip[head] = proj[:, 2 * width + at : 2 * width + at + HD].T
        d_keys[...] = jnp.zeros_like(d_keys)
        d_proj[:, 0:width] = jnp.zeros((total, width), BF)

    rows = pl.ds(pl.multiple_of(step * TILE, TILE), TILE)
    for head in range(heads):
        at = head * HD
        raised = expo[head]
        d_out = do_ext[head, rows, :]
        d_probs = mm_nt(v_ext[head], d_out)
        d_scores = (raised.astype(F32) * d_probs).astype(BF)
        d_keys[head, :, 0:HD] += mm(d_scores, proj[rows, width + at : width + at + HD])
        d_keys[head, :, HD : 2 * HD] += mm(raised, d_out[:, 0:HD])
        d_query = mm(k_flip[head], d_scores).astype(BF)
        d_proj[rows, width + at : width + at + HD] = d_query.T

    @pl.when(step == 3)
    def _():
        for head in range(heads):
            at = head * HD
            d_proj[:, 2 * width + at : 2 * width + at + HD] = d_keys[head, :, 0:HD].astype(BF)
            d_proj[:, 3 * width + at : 3 * width + at + HD] = d_keys[head, :, HD : 2 * HD].astype(
                BF
            )
        for index in range(n_pieces):
            piece = pieces[index]
            start = pl.multiple_of(meta[index], 16) if n_pieces > 1 else 0
            pltpu.make_async_copy(
                piece.at[:, pl.ds(0, weight.shape[1])],
                weight.at[pl.ds(start, piece.shape[0]), :],
                sems.at[index],
            ).wait()
        grad[...] = mm_tn(normed[...], d_proj[...]).astype(BF)
        grad[:, 0:width] = grad_out[...]
        made = disperse(meta, grad, groups, sems_out, 0)
        through = mm_nt(d_proj[...], weight[...])
        if last:
            through = through + before[...].astype(F32)
            mine[...] = through[0 : 2 * TILE].astype(BF)
            other[...] = through[2 * TILE :].astype(BF)
        else:
            result[...] = through.astype(BF)
        wait_all(made)


def attention_backward(
    meta, heads, normed, proj, expo, inverse, context, d_context, grad_out, pieces, shapes, before=None
):
    last = before is not None
    n_pieces = len(pieces)
    model = normed.shape[1]
    width = proj.shape[1]
    total = 4 * TILE
    head_width = heads * HD
    operands = [meta, normed, proj, expo, inverse, context, d_context, grad_out, *pieces]
    in_specs = [
        SMEM,
        whole((total, model)),
        whole((total, width)),
        pl.BlockSpec((heads, total, TILE), lambda step: (0, 0, step)),
        whole((8, total)),
        whole((total, head_width)),
        whole((total, head_width)),
        whole((model, head_width)),
    ] + [ANY] * n_pieces
    if last:
        operands += [before]
        in_specs += [whole((total, model))]
        out_shape = [jax.ShapeDtypeStruct((2 * TILE, model), BF)] * 2
        out_specs = [whole((2 * TILE, model))] * 2
    else:
        out_shape = [jax.ShapeDtypeStruct((total, model), BF)]
        out_specs = [whole((total, model))]
    out_shape += [jax.ShapeDtypeStruct((*shape, width), BF) for shape in shapes]
    out_specs += [ANY] * len(shapes)
    return pl.pallas_call(
        functools.partial(backward_kernel, heads, n_pieces, len(shapes), last),
        grid=(4,),
        in_specs=in_specs,
        out_specs=out_specs,
        out_shape=out_shape,
        scratch_shapes=[
            pltpu.VMEM((model, width), BF),
            pltpu.VMEM((heads, total, 2 * HD), BF),
            pltpu.VMEM((heads, total, 2 * HD), BF),
            pltpu.VMEM((heads, HD, total), BF),
            pltpu.VMEM((heads, total, 2 * HD), F32),
            pltpu.VMEM((total, width), BF),
            pltpu.VMEM((model, width), BF),
            pltpu.SemaphoreType.DMA((n_pieces,)),
            pltpu.SemaphoreType.DMA((n_pieces,)),
        ],
        compiler_params=params(),
        cost_estimate=pl.CostEstimate(
            flops=24 * 10**9, bytes_accessed=12 * 10**6, transcendentals=1000
        ),
        name="attention_backward",
    )(*operands)


def add(*terms):
    return sum(term.astype(F32) for term in terms)


def hold(values, *others):
    values, others = lax.optimization_barrier((values, others))
    return values, *others


class Links:
    def __init__(self, wide, narrow):
        self.wide, self.narrow = wide, narrow
        self.planes = wide // 2
        self.staged = wide == 8

    def y(self, values):
        return lax.ppermute(values, "narrow", [(i, (i + 2) % 4) for i in range(4)])

    def core(self, values):
        return lax.ppermute(values, "narrow", [(i, i ^ 1) for i in range(4)])

    def x(self, values):
        return lax.ppermute(values, "wide", [(i, i ^ 1) for i in range(self.wide)])

    def z(self, values, ahead):
        turn = lambda i: ((i // 2 + ahead) % self.planes) * 2 + i % 2
        return lax.ppermute(values, "wide", [(i, turn(i)) for i in range(self.wide)])

    def shapes(self, model):
        if not self.staged:
            return [(1, model)], [(1, model)]
        rows = model // self.wide
        half = self.planes // 2
        near = [(half, rows), (half, rows), (half, rows), (half, rows)]
        return near, near

    def whole_reduce(self, near, far):
        return lax.psum_scatter(near[0][0], "wide", scatter_dimension=0, tiled=True).astype(
            F32
        ) + lax.psum_scatter(self.y(far[0][0]), "wide", scatter_dimension=0, tiled=True).astype(F32)

    def everywhere(self, values):
        values = values + self.core(values)
        if not self.staged:
            return lax.psum(values + self.y(values), "wide")
        over_x, over_y = self.x(values), self.y(values)
        values = values + over_x + (over_y + self.x(over_y))
        return values + sum(self.z(values, k) for k in range(1, self.planes))


def on_device(
    tokens,
    lengths,
    norm_one,
    w_query,
    w_key,
    w_value,
    w_out,
    norm_two,
    w_gate,
    w_up,
    w_down,
    cotangent,
):
    model = tokens.shape[-1]
    wide, narrow = lax.axis_size("wide"), lax.axis_size("narrow")
    links = Links(wide, narrow)
    heads = w_query.shape[1] // HD
    head_width = heads * HD
    units = w_gate.shape[1]
    at_wide, at_narrow = lax.axis_index("wide"), lax.axis_index("narrow")
    y, c = at_narrow // 2, at_narrow % 2
    x, z = at_wide % 2, at_wide // 2

    places = [
        ((z + k) % links.planes) * 2 + (x ^ side) for side in range(2) for k in range(4)
    ]
    offsets = [place * (model // wide) for place in places]
    blocks = [((y ^ far) * 2 + (c ^ side)) * TILE for side in range(2) for far in range(2)]
    length = lax.dynamic_index_in_dim(lengths, y, 0, keepdims=False)[0]
    meta = jnp.stack([jnp.asarray(v, jnp.int32) for v in (*offsets, *blocks, length)])

    gain_one = norm_one.reshape(1, model)
    gain_two = norm_two.reshape(1, model)

    def keep_give(rows):
        flat = rows.reshape(2, TILE, model)
        return (
            lax.dynamic_index_in_dim(flat, y, 0, keepdims=False),
            lax.dynamic_index_in_dim(flat, 1 - y, 0, keepdims=False),
        )

    def bring_back(rows):
        mine, theirs = rows[:TILE], rows[TILE:]
        got = links.y(theirs)
        stacked = jnp.where(y == 0, jnp.stack([mine, got]), jnp.stack([got, mine]))
        return stacked.reshape(tokens.shape)

    staged = links.staged
    planes = links.planes
    half = planes // 2
    attn_piece = jnp.concatenate([w_out.T, w_query, w_key, w_value], axis=1)
    feed_piece = jnp.concatenate([w_gate, w_up, w_down.T], axis=1)
    keep, give = keep_give(tokens)
    keep_cot, give_cot = keep_give(cotangent)
    shapes_near, shapes_far = links.shapes(model)

    got = links.y(give)
    if staged:
        column = [attn_piece] + [links.z(attn_piece, planes - k) for k in range(1, planes)]
        over_x = [links.x(block) for block in column]
        attn_near = column + over_x
    else:
        attn_near = [lax.all_gather(attn_piece, "wide", axis=0, tiled=True)]
    rows_in = [keep, got, links.core(keep), links.core(got)]
    if staged:
        over_y = [links.y(block) for block in column]
        both = [links.y(block) for block in over_x[:half]] + [
            links.x(block) for block in over_y[half:]
        ]
        attn_far = over_y + both
        feed_column = [links.z(feed_piece, planes - k) for k in range(1, planes)]
        feed_x_own = links.x(feed_piece)
        feed_y_own = links.y(feed_piece)
    else:
        attn_far = [links.y(attn_near[0])]
        feed_near = [lax.all_gather(feed_piece, "wide", axis=0, tiled=True)]
        feed_far = [links.y(feed_near[0])]
    got_cot = links.y(give_cot)

    normed, proj_near, expo_near, inv_near, context_near = attention_forward(
        meta, heads, attn_near, rows_in=rows_in, gain=gain_one
    )
    if staged:
        normed, feed_column, feed_x_own, feed_y_own, got_cot = hold(
            normed, feed_column, feed_x_own, feed_y_own, got_cot
        )
        rest = jnp.stack(feed_column)
        feed_x = links.x(rest)
        feed_y = links.y(rest)
        feed_xy_own = links.y(feed_x_own)
    cots = [keep_cot, got_cot, links.core(keep_cot), links.core(got_cot)]

    proj_far, expo_far, inv_far, context_far, part_mine = attention_forward(
        meta, heads, attn_far, normed=normed, before=(attn_near, context_near)
    )
    if staged:
        part_mine, feed_x, feed_y, feed_xy_own = hold(part_mine, feed_x, feed_y, feed_xy_own)
    part_other = links.core(part_mine)
    if staged:
        feed_xy_one = links.y(feed_x[0])
        feed_xy_two = links.x(feed_y[1:])
        feed_near = [feed_piece, *feed_column, feed_x_own, *(feed_x[k] for k in range(planes - 1))]
        feed_far = [
            feed_y_own,
            *(feed_y[k] for k in range(planes - 1)),
            feed_xy_own,
            feed_xy_one,
            *(feed_xy_two[k] for k in range(planes - 2)),
        ]

    normed_two, down_near, back_near, *near = feed_forward(
        meta, cots, feed_near, shapes_near, start=(*rows_in, part_mine, part_other, gain_two)
    )
    if staged:
        own_low, own_high, x_low, x_high = near
        from_x_high = links.x(x_high)
    mlp_mine, mlp_other, d_mine, *far = feed_forward(
        meta, cots, feed_far, shapes_far, before=(normed_two, down_near, back_near)
    )
    if staged:
        d_mine, from_x_high = hold(d_mine, from_x_high)
        y_low, y_high, xy_low, xy_high = far
        from_xy_high = links.x(xy_high)
        from_xy_low = links.x(xy_low)
    else:
        feed_grad = links.whole_reduce(near, far)
    d_other = links.core(d_mine)
    half_rows = 2 * TILE
    own_rows = jnp.concatenate(rows_in[:2], axis=0).astype(F32)
    output = bring_back(
        (
            own_rows
            + part_mine[:half_rows].astype(F32)
            + part_other[half_rows:].astype(F32)
            + mlp_mine.astype(F32)
            + links.core(mlp_other).astype(F32)
        ).astype(BF)
    )
    d_middle, d_context_near, d_context_far, out_near, out_far, gain_rows = middle_backward(
        meta,
        heads,
        rows_in,
        part_mine,
        part_other,
        gain_two,
        cots,
        d_mine,
        d_other,
        (context_near, context_far),
        attn_near,
        attn_far,
    )
    if staged:
        d_context_far, from_xy_high, output = hold(d_context_far, from_xy_high, output)
        from_y_high = links.y(add(y_high, from_xy_high).astype(BF))
        from_x_low = links.x(x_low)
    d_first, *attn_far_grad = attention_backward(
        meta, heads, normed, proj_far, expo_far, inv_far, context_far, d_context_far, out_far,
        attn_far, shapes_far,
    )
    if staged:
        d_first, from_xy_low, from_y_high, from_x_low = hold(
            d_first, from_xy_low, from_y_high, from_x_low
        )
        from_y_low = links.y(add(y_low, from_xy_low).astype(BF))
        high = add(own_high, from_x_high, from_y_high)
        feed_parts = [links.z(high[k - half].astype(BF), k) for k in range(half, planes)]
        y_low, y_high, xy_low, xy_high = attn_far_grad
        from_xy = links.y(xy_low)
        from_yx = links.x(xy_high)
    last_mine, last_other, *attn_near_grad = attention_backward(
        meta, heads, normed, proj_near, expo_near, inv_near, context_near, d_context_near, out_near,
        attn_near, shapes_near, before=d_first,
    )
    if staged:
        last_mine, from_xy, from_yx, from_y_low, feed_parts = hold(
            last_mine, from_xy, from_yx, from_y_low, feed_parts
        )
        low = add(own_low, from_x_low, from_y_low)
        feed_parts += [links.z(low[k].astype(BF), k) for k in range(1, half)]
        own_low, own_high, x_low, x_high = attn_near_grad
        from_x_low = links.x(add(x_low, from_xy).astype(BF))
        from_x_high = links.x(x_high)
        from_y_low = links.y(y_low)
        from_y_high = links.y(add(y_high, from_yx).astype(BF))
        feed_grad = add(low[0], *feed_parts)
        low = add(own_low, from_x_low, from_y_low)
        high = add(own_high, from_x_high, from_y_high)
        blocks = [low[k] for k in range(half)] + [high[k] for k in range(half)]
        attn_grad = add(
            blocks[0], *(links.z(blocks[k].astype(BF), k) for k in range(1, planes))
        )
    else:
        attn_grad = links.whole_reduce(attn_near_grad, attn_far_grad)

    d_normed = last_mine.astype(F32) + links.core(last_other).astype(F32)
    inverse = inverse_rms(own_rows)
    scaled = d_normed * gain_one
    inner = jnp.mean(scaled * own_rows, axis=-1, keepdims=True)
    d_tokens = (
        d_middle + inverse * scaled - own_rows * (inverse * inverse * inverse * inner)
    ).astype(BF)
    input_grad = bring_back(d_tokens)
    gain_first = jnp.sum(d_normed * own_rows * inverse, axis=0)
    gains = links.everywhere(jnp.stack([gain_first, gain_rows[0]]))
    return (
        output,
        input_grad,
        gains[0],
        attn_grad[:, head_width : 2 * head_width],
        attn_grad[:, 2 * head_width : 3 * head_width],
        attn_grad[:, 3 * head_width :],
        attn_grad[:, :head_width].T,
        gains[1],
        feed_grad[:, :units],
        feed_grad[:, units : 2 * units],
        feed_grad[:, 2 * units :].T,
    )


def solution(mesh):
    in_specs = (
        P(None, "wide", "narrow", None),
        P(None, "wide"),
        P(),
        P("wide", "narrow"),
        P("wide", "narrow"),
        P("wide", "narrow"),
        P("narrow", "wide"),
        P(),
        P("wide", "narrow"),
        P("wide", "narrow"),
        P("narrow", "wide"),
        P(None, "wide", "narrow", None),
    )
    out_specs = (
        P(None, "wide", "narrow", None),
        P(None, "wide", "narrow", None),
        P(),
        P("wide", "narrow"),
        P("wide", "narrow"),
        P("wide", "narrow"),
        P("narrow", "wide"),
        P(),
        P("wide", "narrow"),
        P("wide", "narrow"),
        P("narrow", "wide"),
    )
    return jax.shard_map(
        on_device, mesh=mesh, in_specs=in_specs, out_specs=out_specs, check_vma=False
    )
```

```python
import functools

import jax
import jax.numpy as jnp
from jax import lax
from jax.experimental import pallas as pl
from jax.experimental.pallas import tpu as pltpu
from jax.sharding import PartitionSpec as P

HD = 64
EPSILON = 1e-06
MASKED = -1e30
TILE = 256
FEED_ROWS = 1024
QUERY_ROWS = 1024
MIDDLE_LIMIT = 40 * 1024 * 1024
ATTEND_LIMIT = 40 * 1024 * 1024
FEED_LIMIT = 40 * 1024 * 1024
COST = pl.CostEstimate(flops=10**6, bytes_accessed=10**5, transcendentals=0)
BF = jnp.bfloat16
F32 = jnp.float32


def mm(left, right):
    return jnp.dot(left, right, preferred_element_type=F32)


def mm_nt(left, right):
    return lax.dot_general(left, right, (((1,), (1,)), ((), ())), preferred_element_type=F32)


def mm_tn(left, right):
    return lax.dot_general(left, right, (((0,), (0,)), ((), ())), preferred_element_type=F32)


def inverse_rms(features):
    return lax.rsqrt(jnp.mean(features * features, axis=-1, keepdims=True) + EPSILON)


def place(meta, base, pieces, dest, rows):
    index = base
    for piece in pieces:
        for start in range(0, piece.shape[0], rows):
            at = 0 if rows == dest.shape[0] else pl.multiple_of(meta[index], 16)
            dest[pl.ds(at, rows), :] = piece[start : start + rows, :]
            index += 1


def disperse(meta, base, source, groups, orders, rows):
    for group, order in zip(groups, orders):
        for place, index in enumerate(order):
            at = 0 if rows == source.shape[0] else pl.multiple_of(meta[base + index], 16)
            group[place * rows : (place + 1) * rows, :] = source[pl.ds(at, rows), :]


def row_block(refs, block):
    start = block * TILE
    for ref in refs:
        if start < ref.shape[0]:
            return ref[start : start + TILE, :]
        start -= ref.shape[0]


def forward_kernel(heads, n_rows, n_pieces, block_rows, meta, *refs):
    first = n_rows > 0
    refs = list(refs)
    take = lambda count: [refs.pop(0) for _ in range(count)]
    width = heads * HD
    if first:
        rows_in = take(n_rows)
        (gain,) = take(1)
    else:
        normed, context_first, weight_first = take(3)
    pieces = take(n_pieces)
    if first:
        (normed,) = take(1)
    weight, proj, inverse, context, expo = take(5)
    if not first:
        (partial,) = take(1)
    q_ext, k_ext, v_flip = take(3)
    total = 4 * TILE
    place(meta, 0, pieces, weight, block_rows)
    if first:
        for block in range(4):
            features = row_block(rows_in, block).astype(F32)
            normed[block * TILE : (block + 1) * TILE, :] = (
                features * inverse_rms(features) * gain[...]
            ).astype(BF)
    proj[...] = mm(normed[...], weight[...]).astype(BF)
    lanes = lax.broadcasted_iota(jnp.int32, (TILE, HD), 1)
    index = lax.broadcasted_iota(jnp.int32, (TILE, HD), 0)
    ones = jnp.where(lanes == 0, 1.0, 0.0).astype(BF)
    below = jnp.where(lax.broadcasted_iota(jnp.int32, (16, total), 0) == 0, 1.0, 0.0).astype(BF)
    for block in range(4):
        rows = slice(block * TILE, (block + 1) * TILE)
        usable = meta[8 + block] + index < meta[12]
        bias = jnp.where((lanes == 0) & ~usable, MASKED, 0.0).astype(BF)
        for head in range(heads):
            at = width + head * HD
            q_ext[head, rows, 0:HD] = proj[rows, at : at + HD]
            q_ext[head, rows, HD : 2 * HD] = ones
            at = 2 * width + head * HD
            k_ext[head, rows, 0:HD] = proj[rows, at : at + HD]
            k_ext[head, rows, HD : 2 * HD] = bias
    for head in range(heads):
        at = 3 * width + head * HD
        v_flip[head, 0:HD, :] = proj[:, at : at + HD].T
        v_flip[head, HD : HD + 16, :] = below
    inverse[...] = jnp.ones_like(inverse)
    for head in range(heads):
        for start in range(0, total, QUERY_ROWS):
            rows = slice(start, start + QUERY_ROWS)
            scores = mm_nt(k_ext[head], q_ext[head, rows, :])
            top = jnp.max(scores, axis=0, keepdims=True)
            raised = jnp.exp(scores - top).astype(BF)
            expo[head, :, rows] = raised
            mixed = mm(v_flip[head], raised)
            inv = 1.0 / mixed[HD : HD + 1, :]
            inverse[head : head + 1, rows] = inv
            context[rows, head * HD : (head + 1) * HD] = (mixed[0:HD, :] * inv).astype(BF).T
    if not first:
        partial[...] = (
            mm_nt(context_first[...], weight_first[:, 0:width])
            + mm_nt(context[...], weight[:, 0:width])
        ).astype(BF)


SMEM = pl.BlockSpec(memory_space=pltpu.SMEM)
VMEM = pl.BlockSpec(memory_space=pltpu.VMEM)


def attention_forward(meta, heads, block_rows, pieces, rows_in=(), gain=None, before=None):
    width = pieces[0].shape[1]
    model = width if before is None else before[0].shape[1]
    model = rows_in[0].shape[1] if rows_in else model
    total = 4 * TILE
    head_width = heads * HD
    out_shape = [
        jax.ShapeDtypeStruct((model, width), BF),
        jax.ShapeDtypeStruct((total, width), BF),
        jax.ShapeDtypeStruct((8, total), F32),
        jax.ShapeDtypeStruct((total, head_width), BF),
        jax.ShapeDtypeStruct((heads, total, total), BF),
    ]
    rows = jax.ShapeDtypeStruct((total, model), BF)
    if rows_in:
        operands = [meta, *rows_in, gain, *pieces]
        out_shape = [rows] + out_shape
    else:
        operands = [meta, *before, *pieces]
        out_shape = out_shape + [rows]
    return pl.pallas_call(
        functools.partial(forward_kernel, heads, len(rows_in), len(pieces), block_rows),
        in_specs=[SMEM] + [VMEM] * (len(operands) - 1),
        out_specs=[VMEM] * len(out_shape),
        out_shape=out_shape,
        scratch_shapes=[
            pltpu.VMEM((heads, total, 2 * HD), BF),
            pltpu.VMEM((heads, total, 2 * HD), BF),
            pltpu.VMEM((heads, HD + 16, total), BF),
        ],
        compiler_params=pltpu.CompilerParams(vmem_limit_bytes=ATTEND_LIMIT),
        cost_estimate=COST,
        name="attention_forward",
    )(*operands)


def gelu_terms(gate):
    scale = 0.7978845608028654
    cube = 0.044715
    square = gate * gate
    bent = jnp.tanh(scale * gate * (1.0 + cube * square))
    half = 0.5 * (1.0 + bent)
    slope = half + 0.5 * gate * (1.0 - bent * bent) * (scale * (1.0 + 3.0 * cube * square))
    return gate * half, slope


def feed_kernel(n_rows, n_cots, n_pieces, orders, block_rows, meta, *refs):
    first = n_rows > 0
    refs = list(refs)
    take = lambda count: [refs.pop(0) for _ in range(count)]
    if first:
        rows_in = take(n_rows)
        part_mine, part_other, gain = take(3)
    else:
        normed, result_before, back_before = take(3)
    cots = take(n_cots)
    pieces = take(n_pieces)
    if first:
        normed, result, back = take(3)
    else:
        mine, other, back = take(3)
    groups = take(len(orders))
    weight, hidden, d_gate, d_up, cot, grad = take(6)
    units = weight.shape[1] // 3
    place(meta, 16, pieces, weight, block_rows)
    for block in range(4):
        rows = slice(block * TILE, (block + 1) * TILE)
        cot[rows, :] = row_block(cots, block)
        if first:
            swapped = slice(((block + 2) % 4) * TILE, ((block + 2) % 4 + 1) * TILE)
            features = (
                row_block(rows_in, block).astype(F32)
                + part_mine[rows, :].astype(F32)
                + part_other[swapped, :].astype(F32)
            )
            features = features.astype(BF).astype(F32)
            normed[rows, :] = (features * inverse_rms(features) * gain[...]).astype(BF)
    for start in range(0, 4 * TILE, FEED_ROWS):
        rows = slice(start, start + FEED_ROWS)
        pre = mm(normed[rows, :], weight[:, 0 : 2 * units])
        act, slope = gelu_terms(pre[:, :units])
        up = pre[:, units:]
        low = (act * up).astype(BF)
        hidden[rows, :] = low
        d_hidden = mm(cot[rows, :], weight[:, 2 * units :])
        gate_low = (d_hidden * up * slope).astype(BF)
        up_low = (d_hidden * act).astype(BF)
        d_gate[rows, :] = gate_low
        d_up[rows, :] = up_low
        down = mm_nt(low, weight[:, 2 * units :])
        through = mm_nt(gate_low, weight[:, 0:units]) + mm_nt(up_low, weight[:, units : 2 * units])
        if first:
            result[rows, :] = down.astype(BF)
            back[rows, :] = through.astype(BF)
        else:
            down = (down + result_before[rows, :].astype(F32)).astype(BF)
            if start < 2 * TILE:
                mine[rows, :] = down[: 2 * TILE - start]
            if start + FEED_ROWS > 2 * TILE:
                begin = max(start - 2 * TILE, 0)
                other[begin : start + FEED_ROWS - 2 * TILE, :] = down[begin + 2 * TILE - start :]
            back[rows, :] = (through + back_before[rows, :].astype(F32)).astype(BF)
    grad[:, 2 * units :] = mm_tn(cot[...], hidden[...]).astype(BF)
    grad[:, 0:units] = mm_tn(normed[...], d_gate[...]).astype(BF)
    grad[:, units : 2 * units] = mm_tn(normed[...], d_up[...]).astype(BF)
    disperse(meta, 16, grad, groups, orders, block_rows)


def feed_forward(meta, block_rows, cots, pieces, orders, rows_in=(), before=()):
    width = pieces[0].shape[1]
    model = cots[0].shape[1]
    total = 4 * TILE
    units = width // 3
    full = jax.ShapeDtypeStruct((total, model), BF)
    half = jax.ShapeDtypeStruct((2 * TILE, model), BF)
    operands = [*rows_in, *before, *cots, *pieces]
    out_shape = [full, full, full] if rows_in else [half, half, full]
    out_shape += [
        jax.ShapeDtypeStruct((len(order) * block_rows, width), BF) for order in orders
    ]
    return pl.pallas_call(
        functools.partial(
            feed_kernel, len(rows_in), len(cots), len(pieces), orders, block_rows
        ),
        in_specs=[SMEM] + [VMEM] * len(operands),
        out_specs=[VMEM] * len(out_shape),
        out_shape=out_shape,
        scratch_shapes=[
            pltpu.VMEM((model, width), BF),
            pltpu.VMEM((total, units), BF),
            pltpu.VMEM((total, units), BF),
            pltpu.VMEM((total, units), BF),
            pltpu.VMEM((total, model), BF),
            pltpu.VMEM((model, width), BF),
        ],
        compiler_params=pltpu.CompilerParams(vmem_limit_bytes=FEED_LIMIT),
        cost_estimate=COST,
        name="feed_forward",
    )(meta, *operands)


def middle_kernel(heads, n_rows, n_cots, *refs):
    refs = list(refs)
    take = lambda count: [refs.pop(0) for _ in range(count)]
    rows_in = take(n_rows)
    part_mine, part_other, gain = take(3)
    cots = take(n_cots)
    d_mine, d_other, context_near, context_far, weight_near, weight_far = take(6)
    d_middle, d_context_near, d_context_far, grad_near, grad_far, d_gain = take(6)
    (d_all,) = take(1)
    width = heads * HD
    gains = 0.0
    for block in range(4):
        rows = slice(block * TILE, (block + 1) * TILE)
        swapped = slice(((block + 2) % 4) * TILE, ((block + 2) % 4 + 1) * TILE)
        features = (
            row_block(rows_in, block).astype(F32)
            + part_mine[rows, :].astype(F32)
            + part_other[swapped, :].astype(F32)
        )
        features = features.astype(BF).astype(F32)
        inverse = inverse_rms(features)
        back = d_mine[rows, :].astype(F32) + d_other[swapped, :].astype(F32)
        scaled = back * gain[...]
        inner = jnp.mean(scaled * features, axis=-1, keepdims=True)
        result = (
            row_block(cots, block).astype(F32)
            + inverse * scaled
            - features * (inverse * inverse * inverse * inner)
        )
        d_all[rows, :] = result.astype(BF)
        if block < 2:
            d_middle[rows, :] = result
            gains += jnp.sum(back * features * inverse, axis=0, keepdims=True)
    d_gain[...] = jnp.broadcast_to(gains, d_gain.shape)
    d_context_near[...] = mm(d_all[...], weight_near[:, 0:width]).astype(BF)
    d_context_far[...] = mm(d_all[...], weight_far[:, 0:width]).astype(BF)
    grad_near[...] = mm_tn(d_all[...], context_near[...]).astype(BF)
    grad_far[...] = mm_tn(d_all[...], context_far[...]).astype(BF)


def middle_backward(heads, rows_in, parts, gain, cots, d_normed, contexts, weights):
    model = gain.shape[1]
    total = 4 * TILE
    width = heads * HD
    operands = [*rows_in, *parts, gain, *cots, *d_normed, *contexts, *weights]
    return pl.pallas_call(
        functools.partial(middle_kernel, heads, len(rows_in), len(cots)),
        in_specs=[VMEM] * len(operands),
        out_specs=[VMEM] * 6,
        out_shape=[
            jax.ShapeDtypeStruct((2 * TILE, model), F32),
            jax.ShapeDtypeStruct((total, width), BF),
            jax.ShapeDtypeStruct((total, width), BF),
            jax.ShapeDtypeStruct((model, width), BF),
            jax.ShapeDtypeStruct((model, width), BF),
            jax.ShapeDtypeStruct((8, model), F32),
        ],
        scratch_shapes=[pltpu.VMEM((total, model), BF)],
        compiler_params=pltpu.CompilerParams(vmem_limit_bytes=MIDDLE_LIMIT),
        cost_estimate=COST,
        name="middle_backward",
    )(*operands)


def backward_kernel(heads, orders, block_rows, last, meta, *refs):
    refs = list(refs)
    take = lambda count: [refs.pop(0) for _ in range(count)]
    normed, weight, proj, inverse, context, expo, d_context, grad_out = take(8)
    if last:
        (before,) = take(1)
        mine, other = take(2)
    else:
        (result,) = take(1)
    groups = take(len(orders))
    do_ext, v_ext, d_proj, grad = take(4)
    width = heads * HD
    total = 4 * TILE
    lanes = lax.broadcasted_iota(jnp.int32, (total, HD), 1)
    columns = inverse[...].T
    d_proj[:, 0:width] = jnp.zeros((total, width), BF)
    for head in range(heads):
        at = head * HD
        scaled = (d_context[:, at : at + HD].astype(F32) * columns[:, head : head + 1]).astype(BF)
        inner = -jnp.sum(
            scaled.astype(F32) * context[:, at : at + HD].astype(F32), axis=-1, keepdims=True
        )
        high = inner.astype(BF).astype(F32)
        do_ext[head, :, 0:HD] = scaled
        do_ext[head, :, HD : 2 * HD] = jnp.where(
            lanes == 0, high, jnp.where(lanes == 1, inner - high, 0.0)
        ).astype(BF)
        v_ext[head, :, 0:HD] = proj[:, 3 * width + at : 3 * width + at + HD]
        v_ext[head, :, HD : 2 * HD] = jnp.where(lanes < 2, 1.0, 0.0).astype(BF)
    for head in range(heads):
        q_at, k_at, v_at = (part * width + head * HD for part in (1, 2, 3))
        raised = expo[head]
        d_probs = mm_nt(v_ext[head], do_ext[head])
        d_scores = (raised.astype(F32) * d_probs).astype(BF)
        d_queries = mm(proj[:, k_at : k_at + HD].T, d_scores)
        d_keys = mm_nt(proj[:, q_at : q_at + HD].T, d_scores)
        d_values = mm_nt(do_ext[head, :, 0:HD].T, raised)
        d_proj[:, q_at : q_at + HD] = d_queries.astype(BF).T
        d_proj[:, k_at : k_at + HD] = d_keys.astype(BF).T
        d_proj[:, v_at : v_at + HD] = d_values.astype(BF).T
    grad[...] = mm_tn(normed[...], d_proj[...]).astype(BF)
    grad[:, 0:width] = grad_out[...]
    disperse(meta, 0, grad, groups, orders, block_rows)
    through = mm_nt(d_proj[...], weight[...])
    if last:
        through = through + before[...].astype(F32)
        mine[...] = through[0 : 2 * TILE].astype(BF)
        other[...] = through[2 * TILE :].astype(BF)
    else:
        result[...] = through.astype(BF)


def attention_backward(meta, heads, block_rows, normed, saved, d_context, grad_out, orders, before=None):
    last = before is not None
    model = normed.shape[1]
    width = saved[1].shape[1]
    total = 4 * TILE
    operands = [normed, *saved, d_context, grad_out]
    if last:
        operands += [before]
        out_shape = [jax.ShapeDtypeStruct((2 * TILE, model), BF)] * 2
    else:
        out_shape = [jax.ShapeDtypeStruct((total, model), BF)]
    out_shape += [
        jax.ShapeDtypeStruct((len(order) * block_rows, width), BF) for order in orders
    ]
    return pl.pallas_call(
        functools.partial(backward_kernel, heads, orders, block_rows, last),
        in_specs=[SMEM] + [VMEM] * len(operands),
        out_specs=[VMEM] * len(out_shape),
        out_shape=out_shape,
        scratch_shapes=[
            pltpu.VMEM((heads, total, 2 * HD), BF),
            pltpu.VMEM((heads, total, 2 * HD), BF),
            pltpu.VMEM((total, width), BF),
            pltpu.VMEM((model, width), BF),
        ],
        compiler_params=pltpu.CompilerParams(vmem_limit_bytes=ATTEND_LIMIT),
        cost_estimate=COST,
        name="attention_backward",
    )(meta, *operands)


def add(*terms):
    return sum(term.astype(F32) for term in terms)


def hold(values, *others):
    values, others = lax.optimization_barrier((values, others))
    return values, *others


class Links:
    def __init__(self, wide, narrow):
        self.wide, self.narrow = wide, narrow
        self.planes = wide // 2
        self.staged = wide == 8

    def y(self, values):
        return lax.ppermute(values, "narrow", [(i, (i + 2) % 4) for i in range(4)])

    def core(self, values):
        return lax.ppermute(values, "narrow", [(i, i ^ 1) for i in range(4)])

    def x(self, values):
        return lax.ppermute(values, "wide", [(i, i ^ 1) for i in range(self.wide)])

    def z(self, values, ahead):
        turn = lambda i: ((i // 2 + ahead) % self.planes) * 2 + i % 2
        return lax.ppermute(values, "wide", [(i, turn(i)) for i in range(self.wide)])

    def columns(self):
        return [[z * 2 + x for z in range(self.planes)] for x in range(2)]

    def whole_gather(self, piece):
        near = lax.all_gather(piece, "wide", axis=0, tiled=True)
        return [near], [self.y(near)]

    def whole_reduce(self, near, far):
        return lax.psum_scatter(near, "wide", scatter_dimension=0, tiled=True).astype(
            F32
        ) + lax.psum_scatter(self.y(far), "wide", scatter_dimension=0, tiled=True).astype(F32)

    def everywhere(self, values):
        values = values + self.core(values)
        if not self.staged:
            return lax.psum(values + self.y(values), "wide")
        over_x, over_y = self.x(values), self.y(values)
        values = values + over_x + (over_y + self.x(over_y))
        return values + sum(self.z(values, k) for k in range(1, self.planes))


def on_device(
    tokens,
    lengths,
    norm_one,
    w_query,
    w_key,
    w_value,
    w_out,
    norm_two,
    w_gate,
    w_up,
    w_down,
    cotangent,
):
    model = tokens.shape[-1]
    wide, narrow = lax.axis_size("wide"), lax.axis_size("narrow")
    links = Links(wide, narrow)
    heads = w_query.shape[1] // HD
    head_width = heads * HD
    units = w_gate.shape[1]
    at_wide, at_narrow = lax.axis_index("wide"), lax.axis_index("narrow")
    y, c = at_narrow // 2, at_narrow % 2
    x, z = at_wide % 2, at_wide // 2

    staged = links.staged
    planes = links.planes
    rows = model // wide
    turned = [((z + k) % planes) * 2 + (x ^ side) for side in range(2) for k in range(4)]
    straight = [k * 2 + (x ^ side) for side in range(2) for k in range(4)]
    blocks = [((y ^ far) * 2 + (c ^ side)) * TILE for side in range(2) for far in range(2)]
    length = lax.dynamic_index_in_dim(lengths, y, 0, keepdims=False)[0]
    numbers = [
        *(place * rows for place in turned),
        *blocks,
        *[length] * 4,
        *(place * rows for place in straight),
    ]
    meta = jnp.stack([jnp.asarray(number, jnp.int32) for number in numbers])

    gain_one = norm_one.reshape(1, model)
    gain_two = norm_two.reshape(1, model)

    def keep_give(rows):
        flat = rows.reshape(2, TILE, model)
        return (
            lax.dynamic_index_in_dim(flat, y, 0, keepdims=False),
            lax.dynamic_index_in_dim(flat, 1 - y, 0, keepdims=False),
        )

    def bring_back(rows):
        mine, theirs = rows[:TILE], rows[TILE:]
        got = links.y(theirs)
        stacked = jnp.where(y == 0, jnp.stack([mine, got]), jnp.stack([got, mine]))
        return stacked.reshape(tokens.shape)

    attn_piece = jnp.concatenate([w_out.T, w_query, w_key, w_value], axis=1)
    feed_piece = jnp.concatenate([w_gate, w_up, w_down.T], axis=1)
    keep, give = keep_give(tokens)
    keep_cot, give_cot = keep_give(cotangent)
    half = planes // 2 * rows
    if staged:
        block_rows = rows
        halves = ((0, 1), (2, 3), (4, 5), (6, 7))
        feed_near_orders = ((0, 1, 2, 3), (4, 5), (6, 7))
        attn_far_orders = ((0, 1, 4, 5), (2, 3), (6, 7))
    else:
        block_rows = model
        halves = feed_near_orders = attn_far_orders = ((0,),)

    got = links.y(give)
    if staged:
        column = [attn_piece] + [links.z(attn_piece, planes - k) for k in range(1, planes)]
        over_x = [links.x(block) for block in column]
        attn_near = column + over_x
        over_y = links.y(jnp.concatenate(column, axis=0))
        feed_column = lax.all_gather(
            feed_piece, "wide", axis=0, tiled=True, axis_index_groups=links.columns()
        )
    else:
        attn_near, attn_far = links.whole_gather(attn_piece)
        feed_near, feed_far = links.whole_gather(feed_piece)
    rows_in = [keep, got, links.core(keep), links.core(got)]
    if staged:
        rows_in, over_y = hold(rows_in, over_y)
        attn_far = [
            over_y,
            links.y(jnp.concatenate(over_x[: planes // 2], axis=0)),
            links.x(over_y[half:]),
        ]
    got_cot = links.y(give_cot)

    normed, *saved_near = attention_forward(
        meta, heads, block_rows, attn_near, rows_in=rows_in, gain=gain_one
    )
    if staged:
        normed, feed_column, got_cot = hold(normed, feed_column, got_cot)
        feed_x_low = links.x(feed_column[:half])
        feed_y_high = links.y(feed_column[half:])
    own_cot = jnp.concatenate([keep_cot, got_cot], axis=0)
    cots = [own_cot, links.core(own_cot)]
    *saved_far, part_mine = attention_forward(
        meta, heads, block_rows, attn_far, before=(normed, saved_near[3], saved_near[0])
    )
    if staged:
        part_mine, feed_x_low, feed_y_high = hold(part_mine, feed_x_low, feed_y_high)
        feed_x_high = links.x(feed_column[half:])
        feed_y_low = links.y(feed_column[:half])
    part_other = links.core(part_mine)
    if staged:
        part_other, feed_x_high, feed_y_low = hold(part_other, feed_x_high, feed_y_low)
        feed_near = [feed_column, feed_x_low, feed_x_high]
        feed_far = [feed_y_low, feed_y_high, links.y(feed_x_low), links.x(feed_y_high)]
    parts = (part_mine, part_other)

    normed_two, down_near, back_near, *near = feed_forward(
        meta, block_rows, cots, feed_near, feed_near_orders, rows_in=rows_in, before=(*parts, gain_two)
    )
    if staged:
        own, x_low, x_high = near
        from_x_high = links.x(x_high)
    mlp_mine, mlp_other, d_mine, *far = feed_forward(
        meta, block_rows, cots, feed_far, halves, before=(normed_two, down_near, back_near)
    )
    d_other = links.core(d_mine)
    if staged:
        y_low, y_high, xy_low, xy_high = far
        from_xy_high = links.x(xy_high)
        from_xy_low = links.y(xy_low)
        from_y_low = links.y(y_low)
    else:
        feed_grad = links.whole_reduce(*near, *far)
    d_middle, d_context_near, d_context_far, out_near, out_far, gain_rows = middle_backward(
        heads,
        rows_in,
        parts,
        gain_two,
        cots,
        (d_mine, d_other),
        (saved_near[3], saved_far[3]),
        (saved_near[0], saved_far[0]),
    )
    d_first, *far = attention_backward(
        meta, heads, block_rows, normed, saved_far, d_context_far, out_far, attn_far_orders
    )
    if staged:
        d_first, from_x_high, from_xy_high, from_xy_low, from_y_low = hold(
            d_first, from_x_high, from_xy_high, from_xy_low, from_y_low
        )
        from_y_high = links.y(add(y_high, from_xy_high).astype(BF))
        from_x_low = links.x(add(x_low, from_xy_low).astype(BF))
        both_low, y_high, xy_high = far
        from_both_low = links.y(both_low)
        from_xy_high = links.x(xy_high)
    last_mine, last_other, *near = attention_backward(
        meta, heads, block_rows, normed, saved_near, d_context_near, out_near, halves,
        before=d_first,
    )
    if staged:
        last_mine, from_y_high, from_x_low, from_both_low, from_xy_high = hold(
            last_mine, from_y_high, from_x_low, from_both_low, from_xy_high
        )
        own_low, own_high, x_low, x_high = near
        from_x_high_last = links.x(x_high)
        from_x_low_last = links.x(add(x_low, from_both_low[half:]).astype(BF))
        from_y_high_last = links.y(add(y_high, from_xy_high).astype(BF))
        total = add(own, jnp.concatenate([from_x_low, from_x_high], axis=0)) + jnp.concatenate(
            [from_y_low, from_y_high], axis=0
        ).astype(F32)
        feed_grad = lax.psum_scatter(
            total.astype(BF),
            "wide",
            scatter_dimension=0,
            tiled=True,
            axis_index_groups=links.columns(),
        ).astype(F32)
        low = add(own_low, from_x_low_last, from_both_low[:half])
        high = add(own_high, from_x_high_last, from_y_high_last)
        blocks = [piece[k * rows : (k + 1) * rows] for piece in (low, high) for k in range(2)]
        attn_grad = add(
            blocks[0], *(links.z(blocks[k].astype(BF), k) for k in range(1, planes))
        )
    else:
        attn_grad = links.whole_reduce(*near, *far)

    half_rows = 2 * TILE
    own_rows = jnp.concatenate(rows_in[:2], axis=0).astype(F32)
    d_normed = last_mine.astype(F32) + links.core(last_other).astype(F32)
    inverse = inverse_rms(own_rows)
    scaled = d_normed * gain_one
    inner = jnp.mean(scaled * own_rows, axis=-1, keepdims=True)
    d_tokens = (
        d_middle + inverse * scaled - own_rows * (inverse * inverse * inverse * inner)
    ).astype(BF)
    input_grad = bring_back(d_tokens)
    output = bring_back(
        (
            own_rows
            + part_mine[:half_rows].astype(F32)
            + part_other[half_rows:].astype(F32)
            + mlp_mine.astype(F32)
            + links.core(mlp_other).astype(F32)
        ).astype(BF)
    )
    gain_first = jnp.sum(d_normed * own_rows * inverse, axis=0)
    gains = links.everywhere(jnp.stack([gain_first, gain_rows[0]]))
    return (
        output,
        input_grad,
        gains[0],
        attn_grad[:, head_width : 2 * head_width],
        attn_grad[:, 2 * head_width : 3 * head_width],
        attn_grad[:, 3 * head_width :],
        attn_grad[:, :head_width].T,
        gains[1],
        feed_grad[:, :units],
        feed_grad[:, units : 2 * units],
        feed_grad[:, 2 * units :].T,
    )


def solution(mesh):
    in_specs = (
        P(None, "wide", "narrow", None),
        P(None, "wide"),
        P(),
        P("wide", "narrow"),
        P("wide", "narrow"),
        P("wide", "narrow"),
        P("narrow", "wide"),
        P(),
        P("wide", "narrow"),
        P("wide", "narrow"),
        P("narrow", "wide"),
        P(None, "wide", "narrow", None),
    )
    out_specs = (
        P(None, "wide", "narrow", None),
        P(None, "wide", "narrow", None),
        P(),
        P("wide", "narrow"),
        P("wide", "narrow"),
        P("wide", "narrow"),
        P("narrow", "wide"),
        P(),
        P("wide", "narrow"),
        P("wide", "narrow"),
        P("narrow", "wide"),
    )
    return jax.shard_map(
        on_device, mesh=mesh, in_specs=in_specs, out_specs=out_specs, check_vma=False
    )
```

```python
import functools

import jax
import jax.numpy as jnp
from jax import lax
from jax.experimental import pallas as pl
from jax.experimental.pallas import tpu as pltpu
from jax.sharding import PartitionSpec as P

HD = 64
EPSILON = 1e-06
MASKED = -1e30
TILE = 256
FEED_ROWS = 1024
QUERY_ROWS = 1024
MIDDLE_LIMIT = 8 * 1024 * 1024
ATTEND_LIMIT = 11 * 1024 * 1024
FEED_LIMIT = 22 * 1024 * 1024
COST = pl.CostEstimate(flops=10**6, bytes_accessed=10**5, transcendentals=0)
BF = jnp.bfloat16
F32 = jnp.float32


def mm(left, right):
    return jnp.dot(left, right, preferred_element_type=F32)


def mm_nt(left, right):
    return lax.dot_general(left, right, (((1,), (1,)), ((), ())), preferred_element_type=F32)


def mm_tn(left, right):
    return lax.dot_general(left, right, (((0,), (0,)), ((), ())), preferred_element_type=F32)


def inverse_rms(features):
    return lax.rsqrt(jnp.mean(features * features, axis=-1, keepdims=True) + EPSILON)


def place(meta, pieces, orders, dest, rows):
    for piece, order in zip(pieces, orders):
        for number, index in enumerate(order):
            at = 0 if rows == dest.shape[0] else pl.multiple_of(meta[index], 16)
            dest[pl.ds(at, rows), :] = piece[number * rows : (number + 1) * rows, :]


def disperse(meta, source, groups, orders, rows):
    for group, order in zip(groups, orders):
        for place, index in enumerate(order):
            at = 0 if rows == source.shape[0] else pl.multiple_of(meta[index], 16)
            group[place * rows : (place + 1) * rows, :] = source[pl.ds(at, rows), :]


def row_block(refs, block):
    start = block * TILE
    for ref in refs:
        if start < ref.shape[0]:
            return ref[start : start + TILE, :]
        start -= ref.shape[0]


def forward_kernel(heads, n_rows, orders, block_rows, meta, *refs):
    first = n_rows > 0
    refs = list(refs)
    take = lambda count: [refs.pop(0) for _ in range(count)]
    width = heads * HD
    if first:
        rows_in = take(n_rows)
        (gain,) = take(1)
    else:
        normed, context_first, weight_first = take(3)
    pieces = take(len(orders))
    if first:
        (normed,) = take(1)
    weight, proj, inverse, context, expo = take(5)
    if not first:
        (partial,) = take(1)
    q_ext, k_ext, v_flip = take(3)
    total = 4 * TILE
    place(meta, pieces, orders, weight, block_rows)
    if first:
        for block in range(4):
            features = row_block(rows_in, block).astype(F32)
            normed[block * TILE : (block + 1) * TILE, :] = (
                features * inverse_rms(features) * gain[...]
            ).astype(BF)
    proj[...] = mm(normed[...], weight[...]).astype(BF)
    lanes = lax.broadcasted_iota(jnp.int32, (TILE, HD), 1)
    index = lax.broadcasted_iota(jnp.int32, (TILE, HD), 0)
    ones = jnp.where(lanes == 0, 1.0, 0.0).astype(BF)
    below = jnp.where(lax.broadcasted_iota(jnp.int32, (16, total), 0) == 0, 1.0, 0.0).astype(BF)
    for block in range(4):
        rows = slice(block * TILE, (block + 1) * TILE)
        usable = meta[8 + block] + index < meta[12]
        bias = jnp.where((lanes == 0) & ~usable, MASKED, 0.0).astype(BF)
        for head in range(heads):
            at = width + head * HD
            q_ext[head, rows, 0:HD] = proj[rows, at : at + HD]
            q_ext[head, rows, HD : 2 * HD] = ones
            at = 2 * width + head * HD
            k_ext[head, rows, 0:HD] = proj[rows, at : at + HD]
            k_ext[head, rows, HD : 2 * HD] = bias
    for head in range(heads):
        at = 3 * width + head * HD
        v_flip[head, 0:HD, :] = proj[:, at : at + HD].T
        v_flip[head, HD : HD + 16, :] = below
    inverse[...] = jnp.ones_like(inverse)
    for head in range(heads):
        for start in range(0, total, QUERY_ROWS):
            rows = slice(start, start + QUERY_ROWS)
            scores = mm_nt(k_ext[head], q_ext[head, rows, :])
            top = jnp.max(scores, axis=0, keepdims=True)
            raised = jnp.exp(scores - top).astype(BF)
            expo[head, :, rows] = raised
            mixed = mm(v_flip[head], raised)
            inv = 1.0 / mixed[HD : HD + 1, :]
            inverse[head : head + 1, rows] = inv
            context[rows, head * HD : (head + 1) * HD] = (mixed[0:HD, :] * inv).astype(BF).T
    if not first:
        partial[...] = (
            mm_nt(context_first[...], weight_first[:, 0:width])
            + mm_nt(context[...], weight[:, 0:width])
        ).astype(BF)


SMEM = pl.BlockSpec(memory_space=pltpu.SMEM)
VMEM = pl.BlockSpec(memory_space=pltpu.VMEM)


def attention_forward(meta, heads, block_rows, pieces, orders, rows_in=(), gain=None, before=None):
    width = pieces[0].shape[1]
    model = width if before is None else before[0].shape[1]
    model = rows_in[0].shape[1] if rows_in else model
    total = 4 * TILE
    head_width = heads * HD
    out_shape = [
        jax.ShapeDtypeStruct((model, width), BF),
        jax.ShapeDtypeStruct((total, width), BF),
        jax.ShapeDtypeStruct((8, total), F32),
        jax.ShapeDtypeStruct((total, head_width), BF),
        jax.ShapeDtypeStruct((heads, total, total), BF),
    ]
    rows = jax.ShapeDtypeStruct((total, model), BF)
    if rows_in:
        operands = [meta, *rows_in, gain, *pieces]
        out_shape = [rows] + out_shape
    else:
        operands = [meta, *before, *pieces]
        out_shape = out_shape + [rows]
    return pl.pallas_call(
        functools.partial(forward_kernel, heads, len(rows_in), orders, block_rows),
        in_specs=[SMEM] + [VMEM] * (len(operands) - 1),
        out_specs=[VMEM] * len(out_shape),
        out_shape=out_shape,
        scratch_shapes=[
            pltpu.VMEM((heads, total, 2 * HD), BF),
            pltpu.VMEM((heads, total, 2 * HD), BF),
            pltpu.VMEM((heads, HD + 16, total), BF),
        ],
        compiler_params=pltpu.CompilerParams(vmem_limit_bytes=ATTEND_LIMIT),
        cost_estimate=COST,
        name="attention_forward",
    )(*operands)


def gelu_terms(gate):
    scale = 0.7978845608028654
    cube = 0.044715
    square = gate * gate
    bent = jnp.tanh(scale * gate * (1.0 + cube * square))
    half = 0.5 * (1.0 + bent)
    slope = half + 0.5 * gate * (1.0 - bent * bent) * (scale * (1.0 + 3.0 * cube * square))
    return gate * half, slope


def feed_kernel(n_rows, n_cots, in_orders, orders, block_rows, meta, *refs):
    first = n_rows > 0
    refs = list(refs)
    take = lambda count: [refs.pop(0) for _ in range(count)]
    if first:
        rows_in = take(n_rows)
        part_mine, part_other, gain = take(3)
    else:
        normed, result_before, back_before = take(3)
    cots = take(n_cots)
    pieces = take(len(in_orders))
    if first:
        normed, result, back = take(3)
    else:
        mine, other, back = take(3)
    groups = take(len(orders))
    weight, hidden, d_gate, d_up, cot, grad = take(6)
    units = weight.shape[1] // 3
    place(meta, pieces, in_orders, weight, block_rows)
    for block in range(4):
        rows = slice(block * TILE, (block + 1) * TILE)
        cot[rows, :] = row_block(cots, block)
        if first:
            swapped = slice(((block + 2) % 4) * TILE, ((block + 2) % 4 + 1) * TILE)
            features = (
                row_block(rows_in, block).astype(F32)
                + part_mine[rows, :].astype(F32)
                + part_other[swapped, :].astype(F32)
            )
            features = features.astype(BF).astype(F32)
            normed[rows, :] = (features * inverse_rms(features) * gain[...]).astype(BF)
    for start in range(0, 4 * TILE, FEED_ROWS):
        rows = slice(start, start + FEED_ROWS)
        pre = mm(normed[rows, :], weight[:, 0 : 2 * units])
        act, slope = gelu_terms(pre[:, :units])
        up = pre[:, units:]
        low = (act * up).astype(BF)
        hidden[rows, :] = low
        d_hidden = mm(cot[rows, :], weight[:, 2 * units :])
        gate_low = (d_hidden * up * slope).astype(BF)
        up_low = (d_hidden * act).astype(BF)
        d_gate[rows, :] = gate_low
        d_up[rows, :] = up_low
        down = mm_nt(low, weight[:, 2 * units :])
        through = mm_nt(gate_low, weight[:, 0:units]) + mm_nt(up_low, weight[:, units : 2 * units])
        if first:
            result[rows, :] = down.astype(BF)
            back[rows, :] = through.astype(BF)
        else:
            down = (down + result_before[rows, :].astype(F32)).astype(BF)
            if start < 2 * TILE:
                mine[rows, :] = down[: 2 * TILE - start]
            if start + FEED_ROWS > 2 * TILE:
                begin = max(start - 2 * TILE, 0)
                other[begin : start + FEED_ROWS - 2 * TILE, :] = down[begin + 2 * TILE - start :]
            back[rows, :] = (through + back_before[rows, :].astype(F32)).astype(BF)
    grad[:, 2 * units :] = mm_tn(cot[...], hidden[...]).astype(BF)
    grad[:, 0:units] = mm_tn(normed[...], d_gate[...]).astype(BF)
    grad[:, units : 2 * units] = mm_tn(normed[...], d_up[...]).astype(BF)
    disperse(meta, grad, groups, orders, block_rows)


def feed_forward(meta, block_rows, cots, pieces, in_orders, orders, rows_in=(), before=()):
    width = pieces[0].shape[1]
    model = cots[0].shape[1]
    total = 4 * TILE
    units = width // 3
    full = jax.ShapeDtypeStruct((total, model), BF)
    half = jax.ShapeDtypeStruct((2 * TILE, model), BF)
    operands = [*rows_in, *before, *cots, *pieces]
    out_shape = [full, full, full] if rows_in else [half, half, full]
    out_shape += [
        jax.ShapeDtypeStruct((len(order) * block_rows, width), BF) for order in orders
    ]
    return pl.pallas_call(
        functools.partial(
            feed_kernel, len(rows_in), len(cots), in_orders, orders, block_rows
        ),
        in_specs=[SMEM] + [VMEM] * len(operands),
        out_specs=[VMEM] * len(out_shape),
        out_shape=out_shape,
        scratch_shapes=[
            pltpu.VMEM((model, width), BF),
            pltpu.VMEM((total, units), BF),
            pltpu.VMEM((total, units), BF),
            pltpu.VMEM((total, units), BF),
            pltpu.VMEM((total, model), BF),
            pltpu.VMEM((model, width), BF),
        ],
        compiler_params=pltpu.CompilerParams(vmem_limit_bytes=FEED_LIMIT),
        cost_estimate=COST,
        name="feed_forward",
    )(meta, *operands)


def middle_kernel(heads, n_rows, n_cots, *refs):
    refs = list(refs)
    take = lambda count: [refs.pop(0) for _ in range(count)]
    rows_in = take(n_rows)
    part_mine, part_other, gain = take(3)
    cots = take(n_cots)
    d_mine, d_other, context_near, context_far, weight_near, weight_far = take(6)
    d_middle, d_context_near, d_context_far, grad_near, grad_far, d_gain = take(6)
    (d_all,) = take(1)
    width = heads * HD
    gains = 0.0
    for block in range(4):
        rows = slice(block * TILE, (block + 1) * TILE)
        swapped = slice(((block + 2) % 4) * TILE, ((block + 2) % 4 + 1) * TILE)
        features = (
            row_block(rows_in, block).astype(F32)
            + part_mine[rows, :].astype(F32)
            + part_other[swapped, :].astype(F32)
        )
        features = features.astype(BF).astype(F32)
        inverse = inverse_rms(features)
        back = d_mine[rows, :].astype(F32) + d_other[swapped, :].astype(F32)
        scaled = back * gain[...]
        inner = jnp.mean(scaled * features, axis=-1, keepdims=True)
        result = (
            row_block(cots, block).astype(F32)
            + inverse * scaled
            - features * (inverse * inverse * inverse * inner)
        )
        d_all[rows, :] = result.astype(BF)
        if block < 2:
            d_middle[rows, :] = result
            gains += jnp.sum(back * features * inverse, axis=0, keepdims=True)
    d_gain[...] = jnp.broadcast_to(gains, d_gain.shape)
    d_context_near[...] = mm(d_all[...], weight_near[:, 0:width]).astype(BF)
    d_context_far[...] = mm(d_all[...], weight_far[:, 0:width]).astype(BF)
    grad_near[...] = mm_tn(d_all[...], context_near[...]).astype(BF)
    grad_far[...] = mm_tn(d_all[...], context_far[...]).astype(BF)


def middle_backward(heads, rows_in, parts, gain, cots, d_normed, contexts, weights):
    model = gain.shape[1]
    total = 4 * TILE
    width = heads * HD
    operands = [*rows_in, *parts, gain, *cots, *d_normed, *contexts, *weights]
    return pl.pallas_call(
        functools.partial(middle_kernel, heads, len(rows_in), len(cots)),
        in_specs=[VMEM] * len(operands),
        out_specs=[VMEM] * 6,
        out_shape=[
            jax.ShapeDtypeStruct((2 * TILE, model), F32),
            jax.ShapeDtypeStruct((total, width), BF),
            jax.ShapeDtypeStruct((total, width), BF),
            jax.ShapeDtypeStruct((model, width), BF),
            jax.ShapeDtypeStruct((model, width), BF),
            jax.ShapeDtypeStruct((8, model), F32),
        ],
        scratch_shapes=[pltpu.VMEM((total, model), BF)],
        compiler_params=pltpu.CompilerParams(vmem_limit_bytes=MIDDLE_LIMIT),
        cost_estimate=COST,
        name="middle_backward",
    )(*operands)


def backward_kernel(heads, orders, block_rows, last, meta, *refs):
    refs = list(refs)
    take = lambda count: [refs.pop(0) for _ in range(count)]
    normed, weight, proj, inverse, context, expo, d_context, grad_out = take(8)
    if last:
        (before,) = take(1)
        mine, other = take(2)
    else:
        (result,) = take(1)
    groups = take(len(orders))
    do_ext, v_ext, d_proj, grad = take(4)
    width = heads * HD
    total = 4 * TILE
    lanes = lax.broadcasted_iota(jnp.int32, (total, HD), 1)
    columns = inverse[...].T
    d_proj[:, 0:width] = jnp.zeros((total, width), BF)
    for head in range(heads):
        at = head * HD
        scaled = (d_context[:, at : at + HD].astype(F32) * columns[:, head : head + 1]).astype(BF)
        inner = -jnp.sum(
            scaled.astype(F32) * context[:, at : at + HD].astype(F32), axis=-1, keepdims=True
        )
        high = inner.astype(BF).astype(F32)
        do_ext[head, :, 0:HD] = scaled
        do_ext[head, :, HD : 2 * HD] = jnp.where(
            lanes == 0, high, jnp.where(lanes == 1, inner - high, 0.0)
        ).astype(BF)
        v_ext[head, :, 0:HD] = proj[:, 3 * width + at : 3 * width + at + HD]
        v_ext[head, :, HD : 2 * HD] = jnp.where(lanes < 2, 1.0, 0.0).astype(BF)
    for head in range(heads):
        q_at, k_at, v_at = (part * width + head * HD for part in (1, 2, 3))
        raised = expo[head]
        d_probs = mm_nt(v_ext[head], do_ext[head])
        d_scores = (raised.astype(F32) * d_probs).astype(BF)
        d_queries = mm(proj[:, k_at : k_at + HD].T, d_scores)
        d_keys = mm_nt(proj[:, q_at : q_at + HD].T, d_scores)
        d_values = mm_nt(do_ext[head, :, 0:HD].T, raised)
        d_proj[:, q_at : q_at + HD] = d_queries.astype(BF).T
        d_proj[:, k_at : k_at + HD] = d_keys.astype(BF).T
        d_proj[:, v_at : v_at + HD] = d_values.astype(BF).T
    grad[...] = mm_tn(normed[...], d_proj[...]).astype(BF)
    grad[:, 0:width] = grad_out[...]
    disperse(meta, grad, groups, orders, block_rows)
    through = mm_nt(d_proj[...], weight[...])
    if last:
        through = through + before[...].astype(F32)
        mine[...] = through[0 : 2 * TILE].astype(BF)
        other[...] = through[2 * TILE :].astype(BF)
    else:
        result[...] = through.astype(BF)


def attention_backward(meta, heads, block_rows, normed, saved, d_context, grad_out, orders, before=None):
    last = before is not None
    model = normed.shape[1]
    width = saved[1].shape[1]
    total = 4 * TILE
    operands = [normed, *saved, d_context, grad_out]
    if last:
        operands += [before]
        out_shape = [jax.ShapeDtypeStruct((2 * TILE, model), BF)] * 2
    else:
        out_shape = [jax.ShapeDtypeStruct((total, model), BF)]
    out_shape += [
        jax.ShapeDtypeStruct((len(order) * block_rows, width), BF) for order in orders
    ]
    return pl.pallas_call(
        functools.partial(backward_kernel, heads, orders, block_rows, last),
        in_specs=[SMEM] + [VMEM] * len(operands),
        out_specs=[VMEM] * len(out_shape),
        out_shape=out_shape,
        scratch_shapes=[
            pltpu.VMEM((heads, total, 2 * HD), BF),
            pltpu.VMEM((heads, total, 2 * HD), BF),
            pltpu.VMEM((total, width), BF),
            pltpu.VMEM((model, width), BF),
        ],
        compiler_params=pltpu.CompilerParams(vmem_limit_bytes=ATTEND_LIMIT),
        cost_estimate=COST,
        name="attention_backward",
    )(meta, *operands)


def add(*terms):
    return sum(term.astype(F32) for term in terms)


def hold(values, *others):
    values, others = lax.optimization_barrier((values, others))
    return values, *others


class Links:
    def __init__(self, wide, narrow):
        self.wide, self.narrow = wide, narrow
        self.planes = wide // 2
        self.staged = wide == 8

    def y(self, values):
        return lax.ppermute(values, "narrow", [(i, (i + 2) % 4) for i in range(4)])

    def core(self, values):
        return lax.ppermute(values, "narrow", [(i, i ^ 1) for i in range(4)])

    def x(self, values):
        return lax.ppermute(values, "wide", [(i, i ^ 1) for i in range(self.wide)])

    def z(self, values, ahead):
        turn = lambda i: ((i // 2 + ahead) % self.planes) * 2 + i % 2
        return lax.ppermute(values, "wide", [(i, turn(i)) for i in range(self.wide)])

    def whole_gather(self, piece):
        near = lax.all_gather(piece, "wide", axis=0, tiled=True)
        return [near], [self.y(near)]

    def whole_reduce(self, near, far):
        return lax.psum_scatter(near, "wide", scatter_dimension=0, tiled=True).astype(
            F32
        ) + lax.psum_scatter(self.y(far), "wide", scatter_dimension=0, tiled=True).astype(F32)

    def everywhere(self, values):
        values = values + self.core(values)
        if not self.staged:
            return lax.psum(values + self.y(values), "wide")
        values = values + self.x(values)
        values = values + self.y(values)
        return values + sum(self.z(values, k) for k in range(1, self.planes))


def on_device(
    tokens,
    lengths,
    norm_one,
    w_query,
    w_key,
    w_value,
    w_out,
    norm_two,
    w_gate,
    w_up,
    w_down,
    cotangent,
):
    model = tokens.shape[-1]
    wide, narrow = lax.axis_size("wide"), lax.axis_size("narrow")
    links = Links(wide, narrow)
    heads = w_query.shape[1] // HD
    head_width = heads * HD
    units = w_gate.shape[1]
    at_wide, at_narrow = lax.axis_index("wide"), lax.axis_index("narrow")
    y, c = at_narrow // 2, at_narrow % 2
    x, z = at_wide % 2, at_wide // 2

    staged = links.staged
    planes = links.planes
    rows = model // wide
    turned = [((z + k) % planes) * 2 + (x ^ side) for side in range(2) for k in range(4)]
    blocks = [((y ^ far) * 2 + (c ^ side)) * TILE for side in range(2) for far in range(2)]
    length = lax.dynamic_index_in_dim(lengths, y, 0, keepdims=False)[0]
    numbers = [
        *(spot * rows for spot in turned),
        *blocks,
        length,
    ]
    meta = jnp.stack([jnp.asarray(number, jnp.int32) for number in numbers])

    gain_one = norm_one.reshape(1, model)
    gain_two = norm_two.reshape(1, model)

    def keep_give(rows):
        flat = rows.reshape(2, TILE, model)
        return (
            lax.dynamic_index_in_dim(flat, y, 0, keepdims=False),
            lax.dynamic_index_in_dim(flat, 1 - y, 0, keepdims=False),
        )

    def bring_back(rows):
        mine, theirs = rows[:TILE], rows[TILE:]
        got = links.y(theirs)
        stacked = jnp.where(y == 0, jnp.stack([mine, got]), jnp.stack([got, mine]))
        return stacked.reshape(tokens.shape)

    attn_piece = jnp.concatenate([w_out.T, w_query, w_key, w_value], axis=1)
    feed_piece = jnp.concatenate([w_gate, w_up, w_down.T], axis=1)
    keep, give = keep_give(tokens)
    keep_cot, give_cot = keep_give(cotangent)
    half = planes // 2 * rows
    if staged:
        block_rows = rows
        quarters = ((0, 1), (2, 3), (4, 5), (6, 7))
        attn_near_in = tuple((k,) for k in range(8))
        attn_far_in = ((0, 1, 2, 3), (4, 5, 6, 7))
        feed_near_in = ((0,), (1,), (3,), (2,), (4, 5, 7), (6,))
        feed_far_in = ((0, 1, 3), (2,), (4, 5), (7, 6))
        attn_far_out = ((0, 1, 4, 5), (2, 3), (6, 7))
    else:
        block_rows = model
        quarters = attn_far_out = ((0,),)
        attn_near_in = attn_far_in = feed_near_in = feed_far_in = ((0,),)

    got = links.y(give)
    if staged:
        column = [attn_piece] + [links.z(attn_piece, planes - k) for k in range(1, planes)]
        over_x = [links.x(block) for block in column]
        attn_near = column + over_x
        over_y = links.y(jnp.concatenate(column, axis=0))
        feed_piece, column = hold(feed_piece, column)
        feed_one = links.z(feed_piece, planes - 1)
        feed_three = links.z(feed_piece, planes - 3)
    else:
        attn_near, attn_far = links.whole_gather(attn_piece)
        feed_near, feed_far = links.whole_gather(feed_piece)
    rows_in = [keep, got, links.core(keep), links.core(got)]
    if staged:
        rows_in, over_y = hold(rows_in, over_y)
        attn_far = [over_y, links.x(over_y)]
    got_cot = links.y(give_cot)

    normed, *saved_near = attention_forward(
        meta, heads, block_rows, attn_near, attn_near_in, rows_in=rows_in, gain=gain_one
    )
    if staged:
        normed, feed_one, feed_three, got_cot = hold(normed, feed_one, feed_three, got_cot)
        three = jnp.concatenate([feed_piece, feed_one, feed_three], axis=0)
        feed_x = links.x(three)
        feed_y = links.y(three)
        feed_piece, feed_one = hold(feed_piece, feed_one)
        feed_two = links.z(feed_piece, planes - 2)
    own_cot = jnp.concatenate([keep_cot, got_cot], axis=0)
    cots = [own_cot, links.core(own_cot)]
    *saved_far, part_mine = attention_forward(
        meta, heads, block_rows, attn_far, attn_far_in, before=(normed, saved_near[3], saved_near[0])
    )
    if staged:
        part_mine, feed_two, feed_x, feed_y = hold(part_mine, feed_two, feed_x, feed_y)
        feed_x_two = links.x(feed_two)
        feed_y_two = links.y(feed_two)
    part_other = links.core(part_mine)
    if staged:
        part_other, feed_x_two, feed_y_two = hold(part_other, feed_x_two, feed_y_two)
        feed_near = [feed_piece, feed_one, feed_three, feed_two, feed_x, feed_x_two]
        feed_far = [
            feed_y,
            feed_y_two,
            links.y(feed_x[: 2 * rows]),
            links.x(jnp.concatenate([feed_y[2 * rows :], feed_y_two], axis=0)),
        ]
    parts = (part_mine, part_other)

    normed_two, down_near, back_near, *near = feed_forward(
        meta, block_rows, cots, feed_near, feed_near_in, quarters, rows_in=rows_in,
        before=(*parts, gain_two),
    )
    if staged:
        own_low, own_high, x_low, x_high = near
    mlp_mine, mlp_other, d_mine, *far = feed_forward(
        meta, block_rows, cots, feed_far, feed_far_in, quarters,
        before=(normed_two, down_near, back_near),
    )
    d_other = links.core(d_mine)
    if staged:
        y_low, y_high, xy_low, xy_high = far
        from_xy_high = links.x(xy_high)
        from_xy_low = links.y(xy_low)
    else:
        feed_grad = links.whole_reduce(*near, *far)
    d_middle, d_context_near, d_context_far, out_near, out_far, gain_rows = middle_backward(
        heads,
        rows_in,
        parts,
        gain_two,
        cots,
        (d_mine, d_other),
        (saved_near[3], saved_far[3]),
        (saved_near[0], saved_far[0]),
    )
    if staged:
        d_context_far, from_xy_high = hold(d_context_far, from_xy_high)
        from_y_high = links.y(add(y_high, from_xy_high).astype(BF))
        from_x_high = links.x(x_high)
    d_first, *far = attention_backward(
        meta, heads, block_rows, normed, saved_far, d_context_far, out_far, attn_far_out
    )
    if staged:
        d_first, from_x_high, from_y_high, from_xy_low = hold(
            d_first, from_x_high, from_y_high, from_xy_low
        )
        high = add(own_high, from_x_high, from_y_high).astype(BF)
        feed_parts = [links.z(high[:rows], 2), links.z(high[rows:], 3)]
        from_x_low = links.x(add(x_low, from_xy_low).astype(BF))
        from_y_low = links.y(y_low)
        both_low, y_high, xy_high = far
        from_xy_high = links.x(xy_high)
    last_mine, last_other, *near = attention_backward(
        meta, heads, block_rows, normed, saved_near, d_context_near, out_near, quarters,
        before=d_first,
    )
    if staged:
        last_mine, from_x_low, from_y_low, from_xy_high, feed_parts = hold(
            last_mine, from_x_low, from_y_low, from_xy_high, feed_parts
        )
        low = add(own_low, from_x_low, from_y_low)
        own_low, own_high, x_low, x_high = near
        from_both_low = links.y(both_low)
        from_x_high = links.x(x_high)
        feed_parts.append(links.z(low[rows:].astype(BF), 1))
        feed_grad = add(low[:rows], *feed_parts)
        from_y_high = links.y(add(y_high, from_xy_high).astype(BF))
        from_x_low = links.x(add(x_low, from_both_low[half:]).astype(BF))
        low = add(own_low, from_x_low, from_both_low[:half])
        high = add(own_high, from_x_high, from_y_high)
        blocks = [piece[k * rows : (k + 1) * rows] for piece in (low, high) for k in range(2)]
        attn_grad = add(
            blocks[0], *(links.z(blocks[k].astype(BF), k) for k in range(1, planes))
        )
    else:
        attn_grad = links.whole_reduce(*near, *far)

    half_rows = 2 * TILE
    own_rows = jnp.concatenate(rows_in[:2], axis=0).astype(F32)
    d_normed = last_mine.astype(F32) + links.core(last_other).astype(F32)
    inverse = inverse_rms(own_rows)
    scaled = d_normed * gain_one
    inner = jnp.mean(scaled * own_rows, axis=-1, keepdims=True)
    d_tokens = (
        d_middle + inverse * scaled - own_rows * (inverse * inverse * inverse * inner)
    ).astype(BF)
    input_grad = bring_back(d_tokens)
    output = bring_back(
        (
            own_rows
            + part_mine[:half_rows].astype(F32)
            + part_other[half_rows:].astype(F32)
            + mlp_mine.astype(F32)
            + links.core(mlp_other).astype(F32)
        ).astype(BF)
    )
    gain_first = jnp.sum(d_normed * own_rows * inverse, axis=0)
    gains = links.everywhere(jnp.stack([gain_first, gain_rows[0]]))
    return (
        output,
        input_grad,
        gains[0],
        attn_grad[:, head_width : 2 * head_width],
        attn_grad[:, 2 * head_width : 3 * head_width],
        attn_grad[:, 3 * head_width :],
        attn_grad[:, :head_width].T,
        gains[1],
        feed_grad[:, :units],
        feed_grad[:, units : 2 * units],
        feed_grad[:, 2 * units :].T,
    )


def solution(mesh):
    in_specs = (
        P(None, "wide", "narrow", None),
        P(None, "wide"),
        P(),
        P("wide", "narrow"),
        P("wide", "narrow"),
        P("wide", "narrow"),
        P("narrow", "wide"),
        P(),
        P("wide", "narrow"),
        P("wide", "narrow"),
        P("narrow", "wide"),
        P(None, "wide", "narrow", None),
    )
    out_specs = (
        P(None, "wide", "narrow", None),
        P(None, "wide", "narrow", None),
        P(),
        P("wide", "narrow"),
        P("wide", "narrow"),
        P("wide", "narrow"),
        P("narrow", "wide"),
        P(),
        P("wide", "narrow"),
        P("wide", "narrow"),
        P("narrow", "wide"),
    )
    return jax.shard_map(
        on_device, mesh=mesh, in_specs=in_specs, out_specs=out_specs, check_vma=False
    )
```

```python
import functools

import jax
import jax.numpy as jnp
from jax import lax
from jax.experimental import pallas as pl
from jax.experimental.pallas import tpu as pltpu
from jax.sharding import PartitionSpec as P

HD = 64
EPSILON = 1e-06
MASKED = -1e30
TILE = 256
FEED_ROWS = 1024
QUERY_ROWS = 1024
MIDDLE_LIMIT = 8 * 1024 * 1024
ATTEND_LIMIT = 18 * 1024 * 1024
FEED_LIMIT = 22 * 1024 * 1024
COST = pl.CostEstimate(flops=10**6, bytes_accessed=10**5, transcendentals=0)
BF = jnp.bfloat16
F32 = jnp.float32


def mm(left, right):
    return jnp.dot(left, right, preferred_element_type=F32)


def mm_nt(left, right):
    return lax.dot_general(left, right, (((1,), (1,)), ((), ())), preferred_element_type=F32)


def mm_tn(left, right):
    return lax.dot_general(left, right, (((0,), (0,)), ((), ())), preferred_element_type=F32)


def inverse_rms(features):
    return lax.rsqrt(jnp.mean(features * features, axis=-1, keepdims=True) + EPSILON)


def place(meta, pieces, orders, dest, rows, sems):
    copies = []
    for piece, order in zip(pieces, orders):
        for number, index in enumerate(order):
            at = 0 if rows == dest.shape[0] else pl.multiple_of(meta[index], 16)
            copy = pltpu.make_async_copy(
                piece.at[pl.ds(number * rows, rows), :],
                dest.at[pl.ds(at, rows), :],
                sems.at[len(copies)],
            )
            copy.start()
            copies.append(copy)
    return copies


def wait_all(copies):
    for copy in copies:
        copy.wait()


def blocks_of(orders):
    return sum(len(order) for order in orders)


def disperse(meta, source, groups, orders, rows):
    for group, order in zip(groups, orders):
        for place, index in enumerate(order):
            at = 0 if rows == source.shape[0] else pl.multiple_of(meta[index], 16)
            group[place * rows : (place + 1) * rows, :] = source[pl.ds(at, rows), :]


def row_block(refs, block):
    start = block * TILE
    for ref in refs:
        if start < ref.shape[0]:
            return ref[start : start + TILE, :]
        start -= ref.shape[0]


def forward_kernel(heads, n_rows, orders, block_rows, meta, *refs):
    first = n_rows > 0
    refs = list(refs)
    take = lambda count: [refs.pop(0) for _ in range(count)]
    width = heads * HD
    if first:
        rows_in = take(n_rows)
        (gain,) = take(1)
    else:
        normed, context_first, weight_first = take(3)
    pieces = take(len(orders))
    if first:
        (normed,) = take(1)
    weight, proj, inverse, context, expo = take(5)
    if not first:
        (partial,) = take(1)
    q_ext, k_ext, v_flip, raised_all, sems, sems_out = take(6)
    total = 4 * TILE
    copies = place(meta, pieces, orders, weight, block_rows, sems)
    if first:
        for block in range(4):
            features = row_block(rows_in, block).astype(F32)
            normed[block * TILE : (block + 1) * TILE, :] = (
                features * inverse_rms(features) * gain[...]
            ).astype(BF)
    wait_all(copies)
    copies = []
    proj[...] = mm(normed[...], weight[...]).astype(BF)
    lanes = lax.broadcasted_iota(jnp.int32, (TILE, HD), 1)
    index = lax.broadcasted_iota(jnp.int32, (TILE, HD), 0)
    ones = jnp.where(lanes == 0, 1.0, 0.0).astype(BF)
    below = jnp.where(lax.broadcasted_iota(jnp.int32, (16, total), 0) == 0, 1.0, 0.0).astype(BF)
    for block in range(4):
        rows = slice(block * TILE, (block + 1) * TILE)
        usable = meta[8 + block] + index < meta[12]
        bias = jnp.where((lanes == 0) & ~usable, MASKED, 0.0).astype(BF)
        for head in range(heads):
            at = width + head * HD
            q_ext[head, rows, 0:HD] = proj[rows, at : at + HD]
            q_ext[head, rows, HD : 2 * HD] = ones
            at = 2 * width + head * HD
            k_ext[head, rows, 0:HD] = proj[rows, at : at + HD]
            k_ext[head, rows, HD : 2 * HD] = bias
    for head in range(heads):
        at = 3 * width + head * HD
        v_flip[head, 0:HD, :] = proj[:, at : at + HD].T
        v_flip[head, HD : HD + 16, :] = below
    inverse[...] = jnp.ones_like(inverse)
    for head in range(heads):
        for start in range(0, total, QUERY_ROWS):
            rows = slice(start, start + QUERY_ROWS)
            scores = mm_nt(k_ext[head], q_ext[head, rows, :])
            top = jnp.max(scores, axis=0, keepdims=True)
            raised = jnp.exp(scores - top).astype(BF)
            raised_all[head, :, rows] = raised
            mixed = mm(v_flip[head], raised)
            inv = 1.0 / mixed[HD : HD + 1, :]
            inverse[head : head + 1, rows] = inv
            context[rows, head * HD : (head + 1) * HD] = (mixed[0:HD, :] * inv).astype(BF).T
        for part in range(4):
            share = pl.ds(part * TILE, TILE)
            copy = pltpu.make_async_copy(
                raised_all.at[head, share], expo.at[head, share], sems_out.at[head, part]
            )
            copy.start()
            copies.append(copy)
    if not first:
        partial[...] = (
            mm_nt(context_first[...], weight_first[:, 0:width])
            + mm_nt(context[...], weight[:, 0:width])
        ).astype(BF)
    wait_all(copies)


SMEM = pl.BlockSpec(memory_space=pltpu.SMEM)
VMEM = pl.BlockSpec(memory_space=pltpu.VMEM)
ANY = pl.BlockSpec(memory_space=pl.ANY)


def attention_forward(meta, heads, block_rows, pieces, orders, rows_in=(), gain=None, before=None):
    width = pieces[0].shape[1]
    model = width if before is None else before[0].shape[1]
    model = rows_in[0].shape[1] if rows_in else model
    total = 4 * TILE
    head_width = heads * HD
    out_shape = [
        jax.ShapeDtypeStruct((model, width), BF),
        jax.ShapeDtypeStruct((total, width), BF),
        jax.ShapeDtypeStruct((8, total), F32),
        jax.ShapeDtypeStruct((total, head_width), BF),
        jax.ShapeDtypeStruct((heads, total, total), BF),
    ]
    rows = jax.ShapeDtypeStruct((total, model), BF)
    if rows_in:
        operands = [meta, *rows_in, gain, *pieces]
        out_shape = [rows] + out_shape
    else:
        operands = [meta, *before, *pieces]
        out_shape = out_shape + [rows]
    return pl.pallas_call(
        functools.partial(forward_kernel, heads, len(rows_in), orders, block_rows),
        in_specs=[SMEM] + [VMEM] * (len(operands) - 1 - len(pieces)) + [ANY] * len(pieces),
        out_specs=[ANY if shape.ndim == 3 else VMEM for shape in out_shape],
        out_shape=out_shape,
        scratch_shapes=[
            pltpu.VMEM((heads, total, 2 * HD), BF),
            pltpu.VMEM((heads, total, 2 * HD), BF),
            pltpu.VMEM((heads, HD + 16, total), BF),
            pltpu.VMEM((heads, total, total), BF),
            pltpu.SemaphoreType.DMA((blocks_of(orders),)),
            pltpu.SemaphoreType.DMA((heads, 4)),
        ],
        compiler_params=pltpu.CompilerParams(vmem_limit_bytes=ATTEND_LIMIT),
        cost_estimate=COST,
        name="attention_forward",
    )(*operands)


def gelu_terms(gate):
    scale = 0.7978845608028654
    cube = 0.044715
    square = gate * gate
    bent = jnp.tanh(scale * gate * (1.0 + cube * square))
    half = 0.5 * (1.0 + bent)
    slope = half + 0.5 * gate * (1.0 - bent * bent) * (scale * (1.0 + 3.0 * cube * square))
    return gate * half, slope


def feed_kernel(n_rows, n_cots, in_orders, orders, block_rows, meta, *refs):
    first = n_rows > 0
    refs = list(refs)
    take = lambda count: [refs.pop(0) for _ in range(count)]
    if first:
        rows_in = take(n_rows)
        part_mine, part_other, gain = take(3)
    else:
        normed, result_before, back_before = take(3)
    cots = take(n_cots)
    pieces = take(len(in_orders))
    if first:
        normed, result, back = take(3)
    else:
        mine, other, back = take(3)
    groups = take(len(orders))
    weight, hidden, d_gate, d_up, cot, grad, sems = take(7)
    units = weight.shape[1] // 3
    copies = place(meta, pieces, in_orders, weight, block_rows, sems)
    for block in range(4):
        rows = slice(block * TILE, (block + 1) * TILE)
        cot[rows, :] = row_block(cots, block)
        if first:
            swapped = slice(((block + 2) % 4) * TILE, ((block + 2) % 4 + 1) * TILE)
            features = (
                row_block(rows_in, block).astype(F32)
                + part_mine[rows, :].astype(F32)
                + part_other[swapped, :].astype(F32)
            )
            features = features.astype(BF).astype(F32)
            normed[rows, :] = (features * inverse_rms(features) * gain[...]).astype(BF)
    wait_all(copies)
    for start in range(0, 4 * TILE, FEED_ROWS):
        rows = slice(start, start + FEED_ROWS)
        pre = mm(normed[rows, :], weight[:, 0 : 2 * units])
        act, slope = gelu_terms(pre[:, :units])
        up = pre[:, units:]
        low = (act * up).astype(BF)
        hidden[rows, :] = low
        d_hidden = mm(cot[rows, :], weight[:, 2 * units :])
        gate_low = (d_hidden * up * slope).astype(BF)
        up_low = (d_hidden * act).astype(BF)
        d_gate[rows, :] = gate_low
        d_up[rows, :] = up_low
        down = mm_nt(low, weight[:, 2 * units :])
        through = mm_nt(gate_low, weight[:, 0:units]) + mm_nt(up_low, weight[:, units : 2 * units])
        if first:
            result[rows, :] = down.astype(BF)
            back[rows, :] = through.astype(BF)
        else:
            down = (down + result_before[rows, :].astype(F32)).astype(BF)
            if start < 2 * TILE:
                mine[rows, :] = down[: 2 * TILE - start]
            if start + FEED_ROWS > 2 * TILE:
                begin = max(start - 2 * TILE, 0)
                other[begin : start + FEED_ROWS - 2 * TILE, :] = down[begin + 2 * TILE - start :]
            back[rows, :] = (through + back_before[rows, :].astype(F32)).astype(BF)
    grad[:, 2 * units :] = mm_tn(cot[...], hidden[...]).astype(BF)
    grad[:, 0:units] = mm_tn(normed[...], d_gate[...]).astype(BF)
    grad[:, units : 2 * units] = mm_tn(normed[...], d_up[...]).astype(BF)
    disperse(meta, grad, groups, orders, block_rows)


def feed_forward(meta, block_rows, cots, pieces, in_orders, orders, rows_in=(), before=()):
    width = pieces[0].shape[1]
    model = cots[0].shape[1]
    total = 4 * TILE
    units = width // 3
    full = jax.ShapeDtypeStruct((total, model), BF)
    half = jax.ShapeDtypeStruct((2 * TILE, model), BF)
    operands = [*rows_in, *before, *cots, *pieces]
    out_shape = [full, full, full] if rows_in else [half, half, full]
    out_shape += [
        jax.ShapeDtypeStruct((len(order) * block_rows, width), BF) for order in orders
    ]
    return pl.pallas_call(
        functools.partial(
            feed_kernel, len(rows_in), len(cots), in_orders, orders, block_rows
        ),
        in_specs=[SMEM] + [VMEM] * (len(operands) - len(pieces)) + [ANY] * len(pieces),
        out_specs=[VMEM] * len(out_shape),
        out_shape=out_shape,
        scratch_shapes=[
            pltpu.VMEM((model, width), BF),
            pltpu.VMEM((total, units), BF),
            pltpu.VMEM((total, units), BF),
            pltpu.VMEM((total, units), BF),
            pltpu.VMEM((total, model), BF),
            pltpu.VMEM((model, width), BF),
            pltpu.SemaphoreType.DMA((blocks_of(in_orders),)),
        ],
        compiler_params=pltpu.CompilerParams(vmem_limit_bytes=FEED_LIMIT),
        cost_estimate=COST,
        name="feed_forward",
    )(meta, *operands)


def middle_kernel(heads, n_rows, n_cots, *refs):
    refs = list(refs)
    take = lambda count: [refs.pop(0) for _ in range(count)]
    rows_in = take(n_rows)
    part_mine, part_other, gain = take(3)
    cots = take(n_cots)
    d_mine, d_other, context_near, context_far, weight_near, weight_far = take(6)
    d_middle, d_context_near, d_context_far, grad_near, grad_far, d_gain = take(6)
    (d_all,) = take(1)
    width = heads * HD
    gains = 0.0
    for block in range(4):
        rows = slice(block * TILE, (block + 1) * TILE)
        swapped = slice(((block + 2) % 4) * TILE, ((block + 2) % 4 + 1) * TILE)
        features = (
            row_block(rows_in, block).astype(F32)
            + part_mine[rows, :].astype(F32)
            + part_other[swapped, :].astype(F32)
        )
        features = features.astype(BF).astype(F32)
        inverse = inverse_rms(features)
        back = d_mine[rows, :].astype(F32) + d_other[swapped, :].astype(F32)
        scaled = back * gain[...]
        inner = jnp.mean(scaled * features, axis=-1, keepdims=True)
        result = (
            row_block(cots, block).astype(F32)
            + inverse * scaled
            - features * (inverse * inverse * inverse * inner)
        )
        d_all[rows, :] = result.astype(BF)
        if block < 2:
            d_middle[rows, :] = result
            gains += jnp.sum(back * features * inverse, axis=0, keepdims=True)
    d_gain[...] = jnp.broadcast_to(gains, d_gain.shape)
    d_context_near[...] = mm(d_all[...], weight_near[:, 0:width]).astype(BF)
    d_context_far[...] = mm(d_all[...], weight_far[:, 0:width]).astype(BF)
    grad_near[...] = mm_tn(d_all[...], context_near[...]).astype(BF)
    grad_far[...] = mm_tn(d_all[...], context_far[...]).astype(BF)


def middle_backward(heads, rows_in, parts, gain, cots, d_normed, contexts, weights):
    model = gain.shape[1]
    total = 4 * TILE
    width = heads * HD
    operands = [*rows_in, *parts, gain, *cots, *d_normed, *contexts, *weights]
    return pl.pallas_call(
        functools.partial(middle_kernel, heads, len(rows_in), len(cots)),
        in_specs=[VMEM] * len(operands),
        out_specs=[VMEM] * 6,
        out_shape=[
            jax.ShapeDtypeStruct((2 * TILE, model), F32),
            jax.ShapeDtypeStruct((total, width), BF),
            jax.ShapeDtypeStruct((total, width), BF),
            jax.ShapeDtypeStruct((model, width), BF),
            jax.ShapeDtypeStruct((model, width), BF),
            jax.ShapeDtypeStruct((8, model), F32),
        ],
        scratch_shapes=[pltpu.VMEM((total, model), BF)],
        compiler_params=pltpu.CompilerParams(vmem_limit_bytes=MIDDLE_LIMIT),
        cost_estimate=COST,
        name="middle_backward",
    )(*operands)


def in_two(*rows):
    high = [row.astype(BF).astype(F32) for row in rows]
    index = lax.broadcasted_iota(jnp.int32, (16, rows[0].shape[1]), 0)
    result = jnp.zeros((16, rows[0].shape[1]), F32)
    for number, row in enumerate(rows):
        result = jnp.where(index == 2 * number, high[number], result)
        result = jnp.where(index == 2 * number + 1, row - high[number], result)
    return result.astype(BF)


def from_two(rows):
    return [
        rows[2 * k : 2 * k + 1].astype(F32) + rows[2 * k + 1 : 2 * k + 2].astype(F32)
        for k in range(2)
    ]


def finish_kernel(d_mine, d_other, keep, got, d_middle, gain, sums, sums_x, mine, theirs):
    for block, rows_in in enumerate((keep, got)):
        rows = slice(block * TILE, (block + 1) * TILE)
        features = rows_in[...].astype(F32)
        inverse = inverse_rms(features)
        scaled = (d_mine[rows, :].astype(F32) + d_other[rows, :].astype(F32)) * gain[...]
        inner = jnp.mean(scaled * features, axis=-1, keepdims=True)
        result = (
            d_middle[rows, :] + inverse * scaled - features * (inverse * inverse * inverse * inner)
        ).astype(BF)
        if block == 0:
            mine[...] = result
        else:
            theirs[0:TILE, :] = result
    own, other = sums[...], sums_x[...]
    theirs[TILE : TILE + 16, :] = in_two(*(a + b for a, b in zip(from_two(own), from_two(other))))


def finish(d_mine, d_other, keep, got, d_middle, gain, sums, sums_x):
    model = keep.shape[1]
    return pl.pallas_call(
        finish_kernel,
        in_specs=[VMEM] * 8,
        out_specs=[VMEM] * 2,
        out_shape=[
            jax.ShapeDtypeStruct((TILE, model), BF),
            jax.ShapeDtypeStruct((TILE + 16, model), BF),
        ],
        compiler_params=pltpu.CompilerParams(vmem_limit_bytes=MIDDLE_LIMIT),
        cost_estimate=COST,
        name="finish_backward",
    )(d_mine, d_other, keep, got, d_middle, gain, sums, sums_x)


def backward_kernel(heads, orders, block_rows, last, meta, *refs):
    refs = list(refs)
    take = lambda count: [refs.pop(0) for _ in range(count)]
    normed, weight, proj, inverse, context, d_context, grad_out = take(7)
    if last:
        before, gain, gain_rows = take(3)
    (expo,) = take(1)
    if last:
        mine, other = take(2)
    else:
        (result,) = take(1)
    groups = take(len(orders))
    do_ext, v_ext, d_proj, grad, raised_all, sems = take(6)
    width = heads * HD
    total = 4 * TILE
    copies = []
    for head in range(heads):
        for part in range(4):
            share = pl.ds(part * TILE, TILE)
            copy = pltpu.make_async_copy(
                expo.at[head, share], raised_all.at[head, share], sems.at[head, part]
            )
            copy.start()
            copies.append(copy)
    lanes = lax.broadcasted_iota(jnp.int32, (total, HD), 1)
    columns = inverse[...].T
    d_proj[:, 0:width] = jnp.zeros((total, width), BF)
    for head in range(heads):
        at = head * HD
        scaled = (d_context[:, at : at + HD].astype(F32) * columns[:, head : head + 1]).astype(BF)
        inner = -jnp.sum(
            scaled.astype(F32) * context[:, at : at + HD].astype(F32), axis=-1, keepdims=True
        )
        high = inner.astype(BF).astype(F32)
        do_ext[head, :, 0:HD] = scaled
        do_ext[head, :, HD : 2 * HD] = jnp.where(
            lanes == 0, high, jnp.where(lanes == 1, inner - high, 0.0)
        ).astype(BF)
        v_ext[head, :, 0:HD] = proj[:, 3 * width + at : 3 * width + at + HD]
        v_ext[head, :, HD : 2 * HD] = jnp.where(lanes < 2, 1.0, 0.0).astype(BF)
    for head in range(heads):
        q_at, k_at, v_at = (part * width + head * HD for part in (1, 2, 3))
        wait_all(copies[4 * head : 4 * head + 4])
        raised = raised_all[head]
        d_probs = mm_nt(v_ext[head], do_ext[head])
        d_scores = (raised.astype(F32) * d_probs).astype(BF)
        d_queries = mm(proj[:, k_at : k_at + HD].T, d_scores)
        d_keys = mm_nt(proj[:, q_at : q_at + HD].T, d_scores)
        d_values = mm_nt(do_ext[head, :, 0:HD].T, raised)
        d_proj[:, q_at : q_at + HD] = d_queries.astype(BF).T
        d_proj[:, k_at : k_at + HD] = d_keys.astype(BF).T
        d_proj[:, v_at : v_at + HD] = d_values.astype(BF).T
    grad[...] = mm_tn(normed[...], d_proj[...]).astype(BF)
    grad[:, 0:width] = grad_out[...]
    disperse(meta, grad, groups, orders, block_rows)
    through = mm_nt(d_proj[...], weight[...])
    if last:
        through = through + before[...].astype(F32)
        mine[...] = through[0 : 2 * TILE].astype(BF)
        other[...] = through[2 * TILE :].astype(BF)
        first = jnp.sum(through * normed[...].astype(F32), axis=0, keepdims=True) / gain[...]
        end = len(orders[-1]) * block_rows
        groups[-1][end : end + 16, :] = in_two(first, gain_rows[0:1, :])
    else:
        result[...] = through.astype(BF)


def attention_backward(meta, heads, block_rows, normed, saved, d_context, grad_out, orders, before=None):
    last = before is not None
    model = normed.shape[1]
    width = saved[1].shape[1]
    total = 4 * TILE
    weight, proj, inverse, context, expo = saved
    operands = [normed, weight, proj, inverse, context, d_context, grad_out]
    if last:
        operands += [*before]
        out_shape = [jax.ShapeDtypeStruct((2 * TILE, model), BF)] * 2
    else:
        out_shape = [jax.ShapeDtypeStruct((total, model), BF)]
    sizes = [len(order) * block_rows for order in orders]
    if last:
        sizes[-1] += 16
    out_shape += [jax.ShapeDtypeStruct((size, width), BF) for size in sizes]
    return pl.pallas_call(
        functools.partial(backward_kernel, heads, orders, block_rows, last),
        in_specs=[SMEM] + [VMEM] * len(operands) + [ANY],
        out_specs=[VMEM] * len(out_shape),
        out_shape=out_shape,
        scratch_shapes=[
            pltpu.VMEM((heads, total, 2 * HD), BF),
            pltpu.VMEM((heads, total, 2 * HD), BF),
            pltpu.VMEM((total, width), BF),
            pltpu.VMEM((model, width), BF),
            pltpu.VMEM((heads, total, total), BF),
            pltpu.SemaphoreType.DMA((heads, 4)),
        ],
        compiler_params=pltpu.CompilerParams(vmem_limit_bytes=ATTEND_LIMIT),
        cost_estimate=COST,
        name="attention_backward",
    )(meta, *operands, expo)


def add(*terms):
    return sum(term.astype(F32) for term in terms)


def hold(values, *others):
    values, others = lax.optimization_barrier((values, others))
    return values, *others


class Links:
    def __init__(self, wide, narrow):
        self.wide, self.narrow = wide, narrow
        self.planes = wide // 2
        self.staged = wide == 8

    def y(self, values):
        return lax.ppermute(values, "narrow", [(i, (i + 2) % 4) for i in range(4)])

    def core(self, values):
        return lax.ppermute(values, "narrow", [(i, i ^ 1) for i in range(4)])

    def x(self, values):
        return lax.ppermute(values, "wide", [(i, i ^ 1) for i in range(self.wide)])

    def z(self, values, ahead):
        turn = lambda i: ((i // 2 + ahead) % self.planes) * 2 + i % 2
        return lax.ppermute(values, "wide", [(i, turn(i)) for i in range(self.wide)])

    def whole_gather(self, piece):
        near = lax.all_gather(piece, "wide", axis=0, tiled=True)
        return [near], [self.y(near)]

    def whole_reduce(self, near, far):
        return lax.psum_scatter(near, "wide", scatter_dimension=0, tiled=True).astype(
            F32
        ) + lax.psum_scatter(self.y(far), "wide", scatter_dimension=0, tiled=True).astype(F32)


def on_device(
    tokens,
    lengths,
    norm_one,
    w_query,
    w_key,
    w_value,
    w_out,
    norm_two,
    w_gate,
    w_up,
    w_down,
    cotangent,
):
    model = tokens.shape[-1]
    wide, narrow = lax.axis_size("wide"), lax.axis_size("narrow")
    links = Links(wide, narrow)
    heads = w_query.shape[1] // HD
    head_width = heads * HD
    units = w_gate.shape[1]
    at_wide, at_narrow = lax.axis_index("wide"), lax.axis_index("narrow")
    y, c = at_narrow // 2, at_narrow % 2
    x, z = at_wide % 2, at_wide // 2

    staged = links.staged
    planes = links.planes
    rows = model // wide
    turned = [((z + k) % planes) * 2 + (x ^ side) for side in range(2) for k in range(4)]
    blocks = [((y ^ far) * 2 + (c ^ side)) * TILE for side in range(2) for far in range(2)]
    length = lax.dynamic_index_in_dim(lengths, y, 0, keepdims=False)[0]
    numbers = [
        *(spot * rows for spot in turned),
        *blocks,
        length,
    ]
    meta = jnp.stack([jnp.asarray(number, jnp.int32) for number in numbers])

    gain_one = norm_one.reshape(1, model)
    gain_two = norm_two.reshape(1, model)

    def keep_give(rows):
        flat = rows.reshape(2, TILE, model)
        return (
            lax.dynamic_index_in_dim(flat, y, 0, keepdims=False),
            lax.dynamic_index_in_dim(flat, 1 - y, 0, keepdims=False),
        )

    attn_piece = jnp.concatenate([w_out.T, w_query, w_key, w_value], axis=1)
    feed_piece = jnp.concatenate([w_gate, w_up, w_down.T], axis=1)
    keep, give = keep_give(tokens)
    keep_cot, give_cot = keep_give(cotangent)
    half = planes // 2 * rows
    if staged:
        block_rows = rows
        quarters = ((0, 1), (2, 3), (4, 5), (6, 7))
        attn_near_in = tuple((k,) for k in range(8))
        attn_far_in = ((0, 1, 2, 3), (4, 5, 6, 7))
        feed_near_in = ((0,), (1,), (3,), (2,), (4, 5, 7), (6,))
        feed_far_in = ((0, 1, 3), (2,), (4, 5), (7, 6))
        attn_far_out = ((0, 1, 4, 5), (2, 3), (6, 7))
    else:
        block_rows = model
        quarters = attn_far_out = ((0,),)
        attn_near_in = attn_far_in = feed_near_in = feed_far_in = ((0,),)

    got = links.y(give)
    if staged:
        column = [attn_piece] + [links.z(attn_piece, planes - k) for k in range(1, planes)]
        over_x = [links.x(block) for block in column]
        over_y = links.y(jnp.concatenate(column, axis=0))
        feed_piece, over_x = hold(feed_piece, over_x)
        feed_one = links.z(feed_piece, planes - 1)
        feed_three = links.z(feed_piece, planes - 3)
    else:
        attn_near, attn_far = links.whole_gather(attn_piece)
        feed_near, feed_far = links.whole_gather(feed_piece)
    rows_in = [keep, got, links.core(keep), links.core(got)]
    if staged:
        over_y, rows_in, over_x = hold(over_y, rows_in, over_x)
        give_cot, over_y = hold(give_cot, over_y)
        attn_near = column + over_x
        attn_far = [over_y, links.x(over_y)]
    got_cot = links.y(give_cot)

    normed, *saved_near = attention_forward(
        meta, heads, block_rows, attn_near, attn_near_in, rows_in=rows_in, gain=gain_one
    )
    if staged:
        normed, feed_one, feed_three, got_cot, attn_far = hold(
            normed, feed_one, feed_three, got_cot, attn_far
        )
        three = jnp.concatenate([feed_piece, feed_one, feed_three], axis=0)
        feed_x = links.x(three)
        feed_y = links.y(three)
        feed_piece, feed_one = hold(feed_piece, feed_one)
        feed_two = links.z(feed_piece, planes - 2)
    own_cot = jnp.concatenate([keep_cot, got_cot], axis=0)
    cots = [own_cot, links.core(own_cot)]
    *saved_far, part_mine = attention_forward(
        meta, heads, block_rows, attn_far, attn_far_in, before=(normed, saved_near[3], saved_near[0])
    )
    if staged:
        part_mine, feed_two, feed_x, feed_y = hold(part_mine, feed_two, feed_x, feed_y)
        feed_x_two = links.x(feed_two)
        feed_y_two = links.y(feed_two)
    part_other = links.core(part_mine)
    if staged:
        part_other, feed_x_two, feed_y_two = hold(part_other, feed_x_two, feed_y_two)
        feed_near = [feed_piece, feed_one, feed_three, feed_two, feed_x, feed_x_two]
        feed_far = [
            feed_y,
            feed_y_two,
            links.y(feed_x[: 2 * rows]),
            links.x(jnp.concatenate([feed_y[2 * rows :], feed_y_two], axis=0)),
        ]
    parts = (part_mine, part_other)

    normed_two, down_near, back_near, *near = feed_forward(
        meta, block_rows, cots, feed_near, feed_near_in, quarters, rows_in=rows_in,
        before=(*parts, gain_two),
    )
    if staged:
        own_low, own_high, x_low, x_high = near
        from_x_high = links.x(x_high)
    mlp_mine, mlp_other, d_mine, *far = feed_forward(
        meta, block_rows, cots, feed_far, feed_far_in, quarters,
        before=(normed_two, down_near, back_near),
    )
    if staged:
        d_mine, from_x_high = hold(d_mine, from_x_high)
        y_low, y_high, xy_low, xy_high = far
        from_xy_high = links.x(xy_high)
    else:
        feed_grad = links.whole_reduce(*near, *far)
    d_other = links.core(d_mine)
    half_rows = 2 * TILE
    output = (
        jnp.concatenate(rows_in[:2], axis=0).astype(F32)
        + part_mine[:half_rows].astype(F32)
        + part_other[half_rows:].astype(F32)
        + mlp_mine.astype(F32)
        + links.core(mlp_other).astype(F32)
    ).astype(BF)
    output_back = links.y(output[TILE:])
    d_middle, d_context_near, d_context_far, out_near, out_far, gain_rows = middle_backward(
        heads,
        rows_in,
        parts,
        gain_two,
        cots,
        (d_mine, d_other),
        (saved_near[3], saved_far[3]),
        (saved_near[0], saved_far[0]),
    )
    if staged:
        d_context_far, from_xy_high = hold(d_context_far, from_xy_high)
        xy_low, from_xy_high = hold(xy_low, from_xy_high)
        from_y_high = links.y(add(y_high, from_xy_high).astype(BF))
        from_xy_low = links.x(xy_low)
    d_first, *far = attention_backward(
        meta, heads, block_rows, normed, saved_far, d_context_far, out_far, attn_far_out
    )
    if staged:
        d_first, from_y_high, from_xy_low, output_back = hold(
            d_first, from_y_high, from_xy_low, output_back
        )
        high = add(own_high, from_x_high, from_y_high).astype(BF)
        feed_parts = [links.z(high[:rows], 2), links.z(high[rows:], 3)]
        feed_low, feed_y_low = own_low, add(y_low, from_xy_low).astype(BF)
        both_low, y_high, xy_high = far
        from_both_low = links.y(both_low)
        from_xy_high = links.x(xy_high)
        from_feed_x = links.x(x_low)
    last_mine, last_other, *near = attention_backward(
        meta, heads, block_rows, normed, saved_near, d_context_near, out_near, quarters,
        before=(d_first, gain_one, gain_rows),
    )
    if staged:
        last_other, near, from_both_low, from_xy_high, feed_parts[0] = hold(
            last_other, near, from_both_low, from_xy_high, feed_parts[0]
        )
        own_low, own_high, x_low, x_high = near
        from_x_high = links.x(x_high)
        from_y_high = links.y(add(y_high, from_xy_high).astype(BF))
        from_x_low = links.x(add(x_low, from_both_low[half:]).astype(BF))
        from_feed_y = links.y(feed_y_low)
        sums, sums_x = x_high[half:], from_x_high[half:]
    else:
        attn_grad = links.whole_reduce(near[0][:model], *far)
        sums = near[0][model:]
        sums_x = jnp.zeros_like(sums)
    mine, theirs = finish(
        last_mine, links.core(last_other), *rows_in[:2], d_middle, gain_one, sums, sums_x
    )
    back = links.y(theirs)
    gains = jnp.concatenate(
        [a + b for a, b in zip(from_two(theirs[TILE:]), from_two(back[TILE:]))], axis=0
    )
    if staged:
        low = add(own_low, from_x_low, from_both_low[:half])
        high = add(own_high, from_x_high[:half], from_y_high)
        coarse = lax.reduce_precision(gains, 8, 7)
        pairs = jnp.stack([coarse[0], gains[0] - coarse[0], coarse[1], gains[1] - coarse[1]])
        tail = jnp.concatenate([pairs, jnp.zeros((12, model), F32)], axis=0).astype(BF)
        blocks = [piece[k * rows : (k + 1) * rows] for piece in (low, high) for k in range(2)]
        parts = [
            links.z(jnp.concatenate([blocks[k].astype(BF), tail], axis=0), k)
            for k in range(1, planes)
        ]
        attn_grad = add(blocks[0], *(part[:rows] for part in parts))
        gains = gains + sum(
            jnp.concatenate(from_two(part[rows:]), axis=0) for part in parts
        )
        feed_low = add(feed_low, from_feed_x, from_feed_y)
        feed_parts.append(links.z(feed_low[rows:].astype(BF), 1))
        feed_grad = add(feed_low[:rows], *feed_parts)
    else:
        gains = lax.psum(gains, "wide")
    gains = gains + links.core(gains)

    def bring_back(own, other):
        stacked = jnp.where(y == 0, jnp.stack([own, other]), jnp.stack([other, own]))
        return stacked.reshape(tokens.shape)

    return (
        bring_back(output[:TILE], output_back),
        bring_back(mine, back[:TILE]),
        gains[0],
        attn_grad[:, head_width : 2 * head_width],
        attn_grad[:, 2 * head_width : 3 * head_width],
        attn_grad[:, 3 * head_width :],
        attn_grad[:, :head_width].T,
        gains[1],
        feed_grad[:, :units],
        feed_grad[:, units : 2 * units],
        feed_grad[:, 2 * units :].T,
    )


def solution(mesh):
    in_specs = (
        P(None, "wide", "narrow", None),
        P(None, "wide"),
        P(),
        P("wide", "narrow"),
        P("wide", "narrow"),
        P("wide", "narrow"),
        P("narrow", "wide"),
        P(),
        P("wide", "narrow"),
        P("wide", "narrow"),
        P("narrow", "wide"),
        P(None, "wide", "narrow", None),
    )
    out_specs = (
        P(None, "wide", "narrow", None),
        P(None, "wide", "narrow", None),
        P(),
        P("wide", "narrow"),
        P("wide", "narrow"),
        P("wide", "narrow"),
        P("narrow", "wide"),
        P(),
        P("wide", "narrow"),
        P("wide", "narrow"),
        P("narrow", "wide"),
    )
    return jax.shard_map(
        on_device, mesh=mesh, in_specs=in_specs, out_specs=out_specs, check_vma=False
    )
```

```python
import functools

import jax
import jax.numpy as jnp
from jax import lax
from jax.experimental import pallas as pl
from jax.experimental.pallas import tpu as pltpu
from jax.sharding import PartitionSpec as P

HD = 64
EPSILON = 1e-06
MASKED = -1e30
TILE = 256
FEED_ROWS = 1024
QUERY_ROWS = 1024
MIDDLE_LIMIT = 8 * 1024 * 1024
BACK_LIMIT = 14 * 1024 * 1024
ATTEND_LIMIT = 11 * 1024 * 1024
FEED_LIMIT = 22 * 1024 * 1024
COST = pl.CostEstimate(flops=10**6, bytes_accessed=10**5, transcendentals=0)
BF = jnp.bfloat16
F32 = jnp.float32


def mm(left, right):
    return jnp.dot(left, right, preferred_element_type=F32)


def mm_nt(left, right):
    return lax.dot_general(left, right, (((1,), (1,)), ((), ())), preferred_element_type=F32)


def mm_tn(left, right):
    return lax.dot_general(left, right, (((0,), (0,)), ((), ())), preferred_element_type=F32)


def inverse_rms(features):
    return lax.rsqrt(jnp.mean(features * features, axis=-1, keepdims=True) + EPSILON)


def place(meta, pieces, orders, dest, rows, sems):
    copies = []
    for piece, order in zip(pieces, orders):
        for number, index in enumerate(order):
            at = 0 if rows == dest.shape[0] else pl.multiple_of(meta[index], 16)
            copy = pltpu.make_async_copy(
                piece.at[pl.ds(number * rows, rows), :],
                dest.at[pl.ds(at, rows), :],
                sems.at[len(copies)],
            )
            copy.start()
            copies.append(copy)
    return copies


def wait_all(copies):
    for copy in copies:
        copy.wait()


def blocks_of(orders):
    return sum(len(order) for order in orders)


def disperse(meta, source, groups, orders, rows):
    for group, order in zip(groups, orders):
        for place, index in enumerate(order):
            at = 0 if rows == source.shape[0] else pl.multiple_of(meta[index], 16)
            group[place * rows : (place + 1) * rows, :] = source[pl.ds(at, rows), :]


def row_block(refs, block):
    start = block * TILE
    for ref in refs:
        if start < ref.shape[0]:
            return ref[start : start + TILE, :]
        start -= ref.shape[0]


def forward_kernel(heads, n_rows, orders, block_rows, meta, *refs):
    first = n_rows > 0
    refs = list(refs)
    take = lambda count: [refs.pop(0) for _ in range(count)]
    width = heads * HD
    total = 4 * TILE
    if first:
        (gain,) = take(1)
        sources = take(n_rows)
    else:
        normed, context_first, weight_first, expo_first = take(4)
    pieces = take(len(orders))
    inverse, context, expo, weight, proj = take(5)
    if first:
        (normed,) = take(1)
    else:
        partial, expo_out = take(2)
    q_ext, k_ext, v_flip, sems, sems_more = take(5)
    copies = place(meta, pieces, orders, weight, block_rows, sems)
    outs = []

    def carry(source, dest):
        copy = pltpu.make_async_copy(source, dest, sems_more.at[len(outs)])
        copy.start()
        outs.append(copy)

    if first:
        (extra,) = take(1)
        starts = [sum(ref.shape[0] for ref in sources[:k]) for k in range(n_rows)]
        for start, source in zip(starts, sources):
            carry(source, extra.at[pl.ds(start, source.shape[0]), :])
        wait_all(outs)
        for block in range(4):
            rows = slice(block * TILE, (block + 1) * TILE)
            features = extra[rows, :].astype(F32)
            normed[rows, :] = (features * inverse_rms(features) * gain[...]).astype(BF)
    else:
        for head in range(heads):
            carry(expo_first.at[head], expo_out.at[head])
    wait_all(copies)
    proj[...] = mm(normed[...], weight[...]).astype(BF)
    lanes = lax.broadcasted_iota(jnp.int32, (TILE, HD), 1)
    index = lax.broadcasted_iota(jnp.int32, (TILE, HD), 0)
    ones = jnp.where(lanes == 0, 1.0, 0.0).astype(BF)
    below = jnp.where(lax.broadcasted_iota(jnp.int32, (16, total), 0) == 0, 1.0, 0.0).astype(BF)
    for block in range(4):
        rows = slice(block * TILE, (block + 1) * TILE)
        usable = meta[8 + block] + index < meta[12]
        bias = jnp.where((lanes == 0) & ~usable, MASKED, 0.0).astype(BF)
        for head in range(heads):
            at = width + head * HD
            q_ext[head, rows, 0:HD] = proj[rows, at : at + HD]
            q_ext[head, rows, HD : 2 * HD] = ones
            at = 2 * width + head * HD
            k_ext[head, rows, 0:HD] = proj[rows, at : at + HD]
            k_ext[head, rows, HD : 2 * HD] = bias
    for head in range(heads):
        at = 3 * width + head * HD
        v_flip[head, 0:HD, :] = proj[:, at : at + HD].T
        v_flip[head, HD : HD + 16, :] = below
    inverse[...] = jnp.ones_like(inverse)
    for head in range(heads):
        for start in range(0, total, QUERY_ROWS):
            rows = slice(start, start + QUERY_ROWS)
            scores = mm_nt(k_ext[head], q_ext[head, rows, :])
            top = jnp.max(scores, axis=0, keepdims=True)
            raised = jnp.exp(scores - top).astype(BF)
            expo[head, :, rows] = raised
            mixed = mm(v_flip[head], raised)
            inv = 1.0 / mixed[HD : HD + 1, :]
            inverse[head : head + 1, rows] = inv
            context[rows, head * HD : (head + 1) * HD] = (mixed[0:HD, :] * inv).astype(BF).T
    if not first:
        partial[...] = (
            mm_nt(context_first[...], weight_first[:, 0:width])
            + mm_nt(context[...], weight[:, 0:width])
        ).astype(BF)
        wait_all(outs)


SMEM = pl.BlockSpec(memory_space=pltpu.SMEM)
VMEM = pl.BlockSpec(memory_space=pltpu.VMEM)
HBM = pl.BlockSpec(memory_space=pltpu.HBM)


def attention_forward(meta, heads, block_rows, pieces, orders, rows_in=(), gain=None, before=None):
    width = pieces[0].shape[1]
    model = rows_in[0].shape[1] if rows_in else before[0].shape[1]
    total = 4 * TILE
    rows = jax.ShapeDtypeStruct((total, model), BF)
    numerators = jax.ShapeDtypeStruct((heads, total, total), BF)
    if rows_in:
        in_fast, in_slow = [gain], [*rows_in, *pieces]
        more, extra = [rows], [pltpu.VMEM((total, model), BF)]
    else:
        in_fast, in_slow = [*before], [*pieces]
        more, extra = [rows, numerators], []
    return pl.pallas_call(
        functools.partial(forward_kernel, heads, len(rows_in), orders, block_rows),
        in_specs=[SMEM] + [VMEM] * len(in_fast) + [HBM] * len(in_slow),
        out_specs=[VMEM] * 6 + [HBM] * (len(more) - 1),
        out_shape=[
            jax.ShapeDtypeStruct((8, total), F32),
            jax.ShapeDtypeStruct((total, heads * HD), BF),
            numerators,
            jax.ShapeDtypeStruct((model, width), BF),
            jax.ShapeDtypeStruct((total, width), BF),
            *more,
        ],
        scratch_shapes=[
            pltpu.VMEM((heads, total, 2 * HD), BF),
            pltpu.VMEM((heads, total, 2 * HD), BF),
            pltpu.VMEM((heads, HD + 16, total), BF),
            pltpu.SemaphoreType.DMA((blocks_of(orders),)),
            pltpu.SemaphoreType.DMA((4,)),
            *extra,
        ],
        compiler_params=pltpu.CompilerParams(vmem_limit_bytes=ATTEND_LIMIT),
        cost_estimate=COST,
        name="attention_forward",
    )(meta, *in_fast, *in_slow)


def gelu_terms(gate):
    scale = 0.7978845608028654
    cube = 0.044715
    square = gate * gate
    bent = jnp.tanh(scale * gate * (1.0 + cube * square))
    half = 0.5 * (1.0 + bent)
    slope = half + 0.5 * gate * (1.0 - bent * bent) * (scale * (1.0 + 3.0 * cube * square))
    return gate * half, slope


def feed_kernel(n_rows, n_cots, in_orders, orders, block_rows, meta, *refs):
    first = n_rows > 0
    refs = list(refs)
    take = lambda count: [refs.pop(0) for _ in range(count)]
    if first:
        rows_in = take(n_rows)
        part_mine, part_other, gain = take(3)
    else:
        normed, result_before, back_before = take(3)
    cots = take(n_cots)
    pieces = take(len(in_orders))
    if first:
        normed, result, back = take(3)
    else:
        mine, other, back = take(3)
    groups = take(len(orders))
    weight, hidden, d_gate, d_up, cot, grad, sems = take(7)
    units = weight.shape[1] // 3
    copies = place(meta, pieces, in_orders, weight, block_rows, sems)
    for block in range(4):
        rows = slice(block * TILE, (block + 1) * TILE)
        cot[rows, :] = row_block(cots, block)
        if first:
            swapped = slice(((block + 2) % 4) * TILE, ((block + 2) % 4 + 1) * TILE)
            features = (
                row_block(rows_in, block).astype(F32)
                + part_mine[rows, :].astype(F32)
                + part_other[swapped, :].astype(F32)
            )
            features = features.astype(BF).astype(F32)
            normed[rows, :] = (features * inverse_rms(features) * gain[...]).astype(BF)
    wait_all(copies)
    for start in range(0, 4 * TILE, FEED_ROWS):
        rows = slice(start, start + FEED_ROWS)
        pre = mm(normed[rows, :], weight[:, 0 : 2 * units])
        act, slope = gelu_terms(pre[:, :units])
        up = pre[:, units:]
        low = (act * up).astype(BF)
        hidden[rows, :] = low
        d_hidden = mm(cot[rows, :], weight[:, 2 * units :])
        gate_low = (d_hidden * up * slope).astype(BF)
        up_low = (d_hidden * act).astype(BF)
        d_gate[rows, :] = gate_low
        d_up[rows, :] = up_low
        down = mm_nt(low, weight[:, 2 * units :])
        through = mm_nt(gate_low, weight[:, 0:units]) + mm_nt(up_low, weight[:, units : 2 * units])
        if first:
            result[rows, :] = down.astype(BF)
            back[rows, :] = through.astype(BF)
        else:
            down = (down + result_before[rows, :].astype(F32)).astype(BF)
            if start < 2 * TILE:
                mine[rows, :] = down[: 2 * TILE - start]
            if start + FEED_ROWS > 2 * TILE:
                begin = max(start - 2 * TILE, 0)
                other[begin : start + FEED_ROWS - 2 * TILE, :] = down[begin + 2 * TILE - start :]
            back[rows, :] = (through + back_before[rows, :].astype(F32)).astype(BF)
    grad[:, 2 * units :] = mm_tn(cot[...], hidden[...]).astype(BF)
    grad[:, 0:units] = mm_tn(normed[...], d_gate[...]).astype(BF)
    grad[:, units : 2 * units] = mm_tn(normed[...], d_up[...]).astype(BF)
    disperse(meta, grad, groups, orders, block_rows)


def feed_forward(meta, block_rows, cots, pieces, in_orders, orders, rows_in=(), before=()):
    width = pieces[0].shape[1]
    model = cots[0].shape[1]
    total = 4 * TILE
    units = width // 3
    full = jax.ShapeDtypeStruct((total, model), BF)
    half = jax.ShapeDtypeStruct((2 * TILE, model), BF)
    operands = [*rows_in, *before, *cots, *pieces]
    out_shape = [full, full, full] if rows_in else [half, half, full]
    out_shape += [
        jax.ShapeDtypeStruct((len(order) * block_rows, width), BF) for order in orders
    ]
    return pl.pallas_call(
        functools.partial(
            feed_kernel, len(rows_in), len(cots), in_orders, orders, block_rows
        ),
        in_specs=[SMEM] + [VMEM] * (len(operands) - len(pieces)) + [HBM] * len(pieces),
        out_specs=[VMEM] * len(out_shape),
        out_shape=out_shape,
        scratch_shapes=[
            pltpu.VMEM((model, width), BF),
            pltpu.VMEM((total, units), BF),
            pltpu.VMEM((total, units), BF),
            pltpu.VMEM((total, units), BF),
            pltpu.VMEM((total, model), BF),
            pltpu.VMEM((model, width), BF),
            pltpu.SemaphoreType.DMA((blocks_of(in_orders),)),
        ],
        compiler_params=pltpu.CompilerParams(vmem_limit_bytes=FEED_LIMIT),
        cost_estimate=COST,
        name="feed_forward",
    )(meta, *operands)


def middle_kernel(heads, n_rows, n_cots, *refs):
    refs = list(refs)
    take = lambda count: [refs.pop(0) for _ in range(count)]
    rows_in = take(n_rows)
    part_mine, part_other, gain = take(3)
    cots = take(n_cots)
    d_mine, d_other, context_near, context_far = take(4)
    weight_near, weight_far = take(2)
    d_middle, d_context_near, d_context_far, grad_near, grad_far, d_gain = take(6)
    (d_all,) = take(1)
    width = heads * HD
    gains = 0.0
    for block in range(4):
        rows = slice(block * TILE, (block + 1) * TILE)
        swapped = slice(((block + 2) % 4) * TILE, ((block + 2) % 4 + 1) * TILE)
        features = (
            row_block(rows_in, block).astype(F32)
            + part_mine[rows, :].astype(F32)
            + part_other[swapped, :].astype(F32)
        )
        features = features.astype(BF).astype(F32)
        inverse = inverse_rms(features)
        back = d_mine[rows, :].astype(F32) + d_other[swapped, :].astype(F32)
        scaled = back * gain[...]
        inner = jnp.mean(scaled * features, axis=-1, keepdims=True)
        result = (
            row_block(cots, block).astype(F32)
            + inverse * scaled
            - features * (inverse * inverse * inverse * inner)
        )
        d_all[rows, :] = result.astype(BF)
        if block < 2:
            d_middle[rows, :] = result
            gains += jnp.sum(back * features * inverse, axis=0, keepdims=True)
    d_gain[...] = jnp.broadcast_to(gains, d_gain.shape)
    d_context_near[...] = mm(d_all[...], weight_near[:, 0:width]).astype(BF)
    d_context_far[...] = mm(d_all[...], weight_far[:, 0:width]).astype(BF)
    grad_near[...] = mm_tn(d_all[...], context_near[...]).astype(BF)
    grad_far[...] = mm_tn(d_all[...], context_far[...]).astype(BF)


def middle_backward(heads, rows_in, parts, gain, cots, d_normed, contexts, weights):
    model = gain.shape[1]
    total = 4 * TILE
    width = heads * HD
    operands = [*rows_in, *parts, gain, *cots, *d_normed, *contexts, *weights]
    return pl.pallas_call(
        functools.partial(middle_kernel, heads, len(rows_in), len(cots)),
        in_specs=[VMEM] * len(operands),
        out_specs=[VMEM] * 6,
        out_shape=[
            jax.ShapeDtypeStruct((2 * TILE, model), F32),
            jax.ShapeDtypeStruct((total, width), BF),
            jax.ShapeDtypeStruct((total, width), BF),
            jax.ShapeDtypeStruct((model, width), BF),
            jax.ShapeDtypeStruct((model, width), BF),
            jax.ShapeDtypeStruct((8, model), F32),
        ],
        scratch_shapes=[
            pltpu.VMEM((total, model), BF),
        ],
        compiler_params=pltpu.CompilerParams(vmem_limit_bytes=MIDDLE_LIMIT),
        cost_estimate=COST,
        name="middle_backward",
    )(*operands)


def in_two(*rows):
    high = [row.astype(BF).astype(F32) for row in rows]
    index = lax.broadcasted_iota(jnp.int32, (16, rows[0].shape[1]), 0)
    result = jnp.zeros((16, rows[0].shape[1]), F32)
    for number, row in enumerate(rows):
        result = jnp.where(index == 2 * number, high[number], result)
        result = jnp.where(index == 2 * number + 1, row - high[number], result)
    return result.astype(BF)


def from_two(rows):
    return [
        rows[2 * k : 2 * k + 1].astype(F32) + rows[2 * k + 1 : 2 * k + 2].astype(F32)
        for k in range(2)
    ]


def finish_kernel(d_mine, d_other, keep, got, d_middle, gain, mine, theirs):
    for block, rows_in in enumerate((keep, got)):
        rows = slice(block * TILE, (block + 1) * TILE)
        features = rows_in[...].astype(F32)
        inverse = inverse_rms(features)
        scaled = (d_mine[rows, :].astype(F32) + d_other[rows, :].astype(F32)) * gain[...]
        inner = jnp.mean(scaled * features, axis=-1, keepdims=True)
        result = (
            d_middle[rows, :] + inverse * scaled - features * (inverse * inverse * inverse * inner)
        ).astype(BF)
        if block == 0:
            mine[...] = result
        else:
            theirs[...] = result


def finish(d_mine, d_other, keep, got, d_middle, gain):
    model = keep.shape[1]
    return pl.pallas_call(
        finish_kernel,
        in_specs=[VMEM] * 6,
        out_specs=[VMEM] * 2,
        out_shape=[jax.ShapeDtypeStruct((TILE, model), BF)] * 2,
        compiler_params=pltpu.CompilerParams(vmem_limit_bytes=MIDDLE_LIMIT),
        cost_estimate=COST,
        name="finish_backward",
    )(d_mine, d_other, keep, got, d_middle, gain)


def backward_kernel(heads, orders, block_rows, last, meta, *refs):
    refs = list(refs)
    take = lambda count: [refs.pop(0) for _ in range(count)]
    inverse, context, expo, weight, proj, normed, d_context, grad_out = take(8)
    if last:
        gain, gain_rows = take(2)
    late = take(1)
    if last:
        mine, other = take(2)
    else:
        result, expo_next = take(2)
    groups = take(len(orders))
    do_ext, v_ext, d_proj, grad, sems = take(5)
    if last:
        (before,) = take(1)
    held = [before if last else expo_next]
    width = heads * HD
    total = 4 * TILE
    late = [
        pltpu.make_async_copy(source, dest, sems.at[k])
        for k, (source, dest) in enumerate(zip(late, held))
    ]
    for copy in late:
        copy.start()
    lanes = lax.broadcasted_iota(jnp.int32, (total, HD), 1)
    columns = inverse[...].T
    d_proj[:, 0:width] = jnp.zeros((total, width), BF)
    for head in range(heads):
        at = head * HD
        scaled = (d_context[:, at : at + HD].astype(F32) * columns[:, head : head + 1]).astype(BF)
        inner = -jnp.sum(
            scaled.astype(F32) * context[:, at : at + HD].astype(F32), axis=-1, keepdims=True
        )
        high = inner.astype(BF).astype(F32)
        do_ext[head, :, 0:HD] = scaled
        do_ext[head, :, HD : 2 * HD] = jnp.where(
            lanes == 0, high, jnp.where(lanes == 1, inner - high, 0.0)
        ).astype(BF)
    for head in range(heads):
        at = 3 * width + head * HD
        v_ext[head, :, 0:HD] = proj[:, at : at + HD]
        v_ext[head, :, HD : 2 * HD] = jnp.where(lanes < 2, 1.0, 0.0).astype(BF)
    for head in range(heads):
        q_at, k_at, v_at = (part * width + head * HD for part in (1, 2, 3))
        raised = expo[head]
        d_probs = mm_nt(v_ext[head], do_ext[head])
        d_scores = (raised.astype(F32) * d_probs).astype(BF)
        d_queries = mm(proj[:, k_at : k_at + HD].T, d_scores)
        d_keys = mm_nt(proj[:, q_at : q_at + HD].T, d_scores)
        d_values = mm_nt(do_ext[head, :, 0:HD].T, raised)
        d_proj[:, q_at : q_at + HD] = d_queries.astype(BF).T
        d_proj[:, k_at : k_at + HD] = d_keys.astype(BF).T
        d_proj[:, v_at : v_at + HD] = d_values.astype(BF).T
    grad[...] = mm_tn(normed[...], d_proj[...]).astype(BF)
    grad[:, 0:width] = grad_out[...]
    disperse(meta, grad, groups, orders, block_rows)
    through = mm_nt(d_proj[...], weight[...])
    wait_all(late)
    if last:
        through = through + before[...].astype(F32)
        mine[...] = through[0 : 2 * TILE].astype(BF)
        other[...] = through[2 * TILE :].astype(BF)
        first = jnp.sum(through * normed[...].astype(F32), axis=0, keepdims=True) / gain[...]
        end = len(orders[-1]) * block_rows
        groups[-1][end : end + 16, :] = in_two(first, gain_rows[0:1, :])
    else:
        result[...] = through.astype(BF)


def attention_backward(
    meta, heads, block_rows, normed, saved, d_context, grad_out, orders, expo_kept=None, before=None
):
    last = before is not None
    weight, proj = saved[3:]
    model, width = weight.shape
    total = proj.shape[0]
    rows = jax.ShapeDtypeStruct((total, model), BF)
    in_fast = [*saved, normed, d_context, grad_out]
    scratch = [
        pltpu.VMEM((heads, total, 2 * HD), BF),
        pltpu.VMEM((heads, total, 2 * HD), BF),
        pltpu.VMEM((total, width), BF),
        pltpu.VMEM((model, width), BF),
        pltpu.SemaphoreType.DMA((1,)),
    ]
    sizes = [len(order) * block_rows for order in orders]
    if last:
        in_fast += [*before[1:]]
        in_slow = [before[0]]
        out_shape = [jax.ShapeDtypeStruct((2 * TILE, model), BF)] * 2
        sizes[-1] += 16
        scratch.append(pltpu.VMEM((total, model), BF))
    else:
        in_slow = [expo_kept]
        out_shape = [rows, jax.ShapeDtypeStruct(expo_kept.shape, BF)]
    out_shape += [jax.ShapeDtypeStruct((size, width), BF) for size in sizes]
    return pl.pallas_call(
        functools.partial(backward_kernel, heads, orders, block_rows, last),
        in_specs=[SMEM] + [VMEM] * len(in_fast) + [HBM] * len(in_slow),
        out_specs=[VMEM] * len(out_shape),
        out_shape=out_shape,
        scratch_shapes=scratch,
        compiler_params=pltpu.CompilerParams(vmem_limit_bytes=BACK_LIMIT),
        cost_estimate=COST,
        name="attention_backward",
    )(meta, *in_fast, *in_slow)


def add(*terms):
    return sum(term.astype(F32) for term in terms)


def hold(values, *others):
    values, others = lax.optimization_barrier((values, others))
    return values, *others


class Links:
    def __init__(self, wide, narrow):
        self.wide, self.narrow = wide, narrow
        self.planes = wide // 2
        self.staged = wide == 8

    def y(self, values):
        return lax.ppermute(values, "narrow", [(i, (i + 2) % 4) for i in range(4)])

    def core(self, values):
        return lax.ppermute(values, "narrow", [(i, i ^ 1) for i in range(4)])

    def across(self, values):
        return lax.ppermute(values, "narrow", [(i, (i + 2) % 4 ^ 1) for i in range(4)])

    def x(self, values):
        return lax.ppermute(values, "wide", [(i, i ^ 1) for i in range(self.wide)])

    def z(self, values, ahead):
        turn = lambda i: ((i // 2 + ahead) % self.planes) * 2 + i % 2
        return lax.ppermute(values, "wide", [(i, turn(i)) for i in range(self.wide)])

    def whole_gather(self, piece):
        near = lax.all_gather(piece, "wide", axis=0, tiled=True)
        return [near], [self.y(near)]

    def whole_reduce(self, near, far):
        return lax.psum_scatter(near, "wide", scatter_dimension=0, tiled=True).astype(
            F32
        ) + lax.psum_scatter(self.y(far), "wide", scatter_dimension=0, tiled=True).astype(F32)


def on_device(
    tokens,
    lengths,
    norm_one,
    w_query,
    w_key,
    w_value,
    w_out,
    norm_two,
    w_gate,
    w_up,
    w_down,
    cotangent,
):
    model = tokens.shape[-1]
    wide, narrow = lax.axis_size("wide"), lax.axis_size("narrow")
    links = Links(wide, narrow)
    heads = w_query.shape[1] // HD
    head_width = heads * HD
    units = w_gate.shape[1]
    at_wide, at_narrow = lax.axis_index("wide"), lax.axis_index("narrow")
    y, c = at_narrow // 2, at_narrow % 2
    x, z = at_wide % 2, at_wide // 2

    staged = links.staged
    planes = links.planes
    rows = model // wide
    turned = [((z + k) % planes) * 2 + (x ^ side) for side in range(2) for k in range(4)]
    blocks = [((y ^ far) * 2 + (c ^ side)) * TILE for side in range(2) for far in range(2)]
    length = lax.dynamic_index_in_dim(lengths, y, 0, keepdims=False)[0]
    numbers = [
        *(spot * rows for spot in turned),
        *blocks,
        length,
    ]
    meta = jnp.stack([jnp.asarray(number, jnp.int32) for number in numbers])

    gain_one = norm_one.reshape(1, model)
    gain_two = norm_two.reshape(1, model)

    def keep_give(rows):
        flat = rows.reshape(2, TILE, model)
        return (
            lax.dynamic_index_in_dim(flat, y, 0, keepdims=False),
            lax.dynamic_index_in_dim(flat, 1 - y, 0, keepdims=False),
        )

    attn_piece = jnp.concatenate([w_out.T, w_query, w_key, w_value], axis=1)
    feed_piece = jnp.concatenate([w_gate, w_up, w_down.T], axis=1)
    keep, give = keep_give(tokens)
    keep_cot, give_cot = keep_give(cotangent)
    half = planes // 2 * rows
    if staged:
        block_rows = rows
        quarters = ((0, 1), (2, 3), (4, 5), (6, 7))
        attn_near_in = attn_far_in = ((0, 1, 2, 3), (4, 5, 6, 7))
        feed_near_in = ((0,), (1,), (3,), (2,), (4, 5, 7), (6,))
        feed_far_in = ((0, 1, 3), (2,), (4, 5), (7, 6))
        attn_far_out = ((0, 1, 4, 5), (2, 3), (6, 7))
    else:
        block_rows = model
        quarters = attn_far_out = ((0,),)
        attn_near_in = attn_far_in = feed_near_in = feed_far_in = ((0,),)

    got = links.y(give)
    if staged:
        column = [attn_piece] + [links.z(attn_piece, planes - k) for k in range(1, planes)]
        column = jnp.concatenate(column, axis=0)
        over_x, over_y = links.x(column), links.y(column)
        feed_piece, column = hold(feed_piece, column)
        feed_one = links.z(feed_piece, planes - 1)
        feed_three = links.z(feed_piece, planes - 3)
    else:
        attn_near, attn_far = links.whole_gather(attn_piece)
        feed_near, feed_far = links.whole_gather(feed_piece)
    rows_in = [keep, got, links.core(keep), links.core(got)]
    if staged:
        over_y, rows_in, over_x = hold(over_y, rows_in, over_x)
        give_cot, over_y = hold(give_cot, over_y)
        attn_near = [column, over_x]
        attn_far = [over_y, links.x(over_y)]
    got_cot = links.y(give_cot)

    inv_near, context_near, expo_near, *kept_near, normed = attention_forward(
        meta, heads, block_rows, attn_near, attn_near_in, rows_in=rows_in, gain=gain_one
    )
    if staged:
        normed, got_cot, attn_far, feed_one, feed_three = hold(
            normed, got_cot, attn_far, feed_one, feed_three
        )
        feed_piece, feed_one = hold(feed_piece, feed_one)
        feed_two = links.z(feed_piece, planes - 2)
        three = jnp.concatenate([feed_piece, feed_one, feed_three], axis=0)
        feed_y = links.y(three)
        feed_x = links.x(three)
    own_cot = jnp.concatenate([keep_cot, got_cot], axis=0)
    cots = [own_cot, links.core(own_cot)]
    inv_far, context_far, expo_far, *kept_far, part_mine, expo_kept = attention_forward(
        meta, heads, block_rows, attn_far, attn_far_in,
        before=(normed, context_near, kept_near[0], expo_near),
    )
    if staged:
        part_mine, feed_two, feed_x, feed_y = hold(part_mine, feed_two, feed_x, feed_y)
        feed_x_two = links.x(feed_two)
        feed_y_two = links.y(feed_two)
    part_other = links.core(part_mine)
    if staged:
        part_other, feed_x_two, feed_y_two = hold(part_other, feed_x_two, feed_y_two)
        feed_near = [feed_piece, feed_one, feed_three, feed_two, feed_x, feed_x_two]
        feed_far = [
            feed_y,
            feed_y_two,
            links.y(feed_x[: 2 * rows]),
            links.x(jnp.concatenate([feed_y[2 * rows :], feed_y_two], axis=0)),
        ]
    parts = (part_mine, part_other)

    normed_two, down_near, back_near, *near = feed_forward(
        meta, block_rows, cots, feed_near, feed_near_in, quarters, rows_in=rows_in,
        before=(*parts, gain_two),
    )
    if staged:
        own_low, own_high, x_low, x_high = near
        from_x_high = links.x(x_high)
    mlp_mine, mlp_other, d_mine, *far = feed_forward(
        meta, block_rows, cots, feed_far, feed_far_in, quarters,
        before=(normed_two, down_near, back_near),
    )
    if staged:
        d_mine, from_x_high = hold(d_mine, from_x_high)
        y_low, y_high, xy_low, xy_high = far
        from_xy_high = links.x(xy_high)
    else:
        feed_grad = links.whole_reduce(*near, *far)
    d_other = links.core(d_mine)
    half_rows = 2 * TILE
    output = (
        jnp.concatenate(rows_in[:2], axis=0).astype(F32)
        + part_mine[:half_rows].astype(F32)
        + part_other[half_rows:].astype(F32)
        + mlp_mine.astype(F32)
        + links.core(mlp_other).astype(F32)
    ).astype(BF)
    output_back = links.y(output[TILE:])
    d_middle, d_context_near, d_context_far, out_near, out_far, gain_rows = middle_backward(
        heads,
        rows_in,
        parts,
        gain_two,
        cots,
        (d_mine, d_other),
        (context_near, context_far),
        (kept_near[0], kept_far[0]),
    )
    if staged:
        d_context_far, from_xy_high, output_back = hold(d_context_far, from_xy_high, output_back)
        xy_low, from_xy_high = hold(xy_low, from_xy_high)
        from_y_high = links.y(add(y_high, from_xy_high).astype(BF))
        from_xy_low = links.x(xy_low)
    d_first, expo_near, *far = attention_backward(
        meta, heads, block_rows, normed, (inv_far, context_far, expo_far, *kept_far),
        d_context_far, out_far, attn_far_out, expo_kept=expo_kept,
    )
    if staged:
        d_first, from_y_high, from_xy_low = hold(d_first, from_y_high, from_xy_low)
        x_low, from_xy_low = hold(x_low, from_xy_low)
        high = add(own_high, from_x_high, from_y_high).astype(BF)
        feed_parts = [links.z(high[:rows], 2), links.z(high[rows:], 3)]
        feed_low, feed_y_low = own_low, add(y_low, from_xy_low).astype(BF)
        both_low, y_high, xy_high = far
        from_both_low = links.y(both_low)
        from_xy_high = links.x(xy_high)
        from_feed_x, from_feed_y = links.x(x_low), links.y(feed_y_low)
    last_mine, last_other, *near = attention_backward(
        meta, heads, block_rows, normed, (inv_near, context_near, expo_near, *kept_near),
        d_context_near, out_near, quarters, before=(d_first, gain_one, gain_rows),
    )
    if staged:
        last_other, near, from_both_low, from_xy_high, from_feed_x, from_feed_y, feed_two = hold(
            last_other, near, from_both_low, from_xy_high, from_feed_x, from_feed_y, feed_parts[0]
        )
        feed_low = add(feed_low, from_feed_x, from_feed_y)
        feed_parts = [feed_two, feed_parts[1], links.z(feed_low[rows:].astype(BF), 1)]
        own_low, own_high, x_low, x_high = near
        from_x_high = links.x(x_high)
        from_y_high = links.y(add(y_high, from_xy_high).astype(BF))
        from_x_low = links.x(add(x_low, from_both_low[half:]).astype(BF))
        sums = [a + b for a, b in zip(from_two(x_high[half:]), from_two(from_x_high[half:]))]
    else:
        attn_grad = links.whole_reduce(near[0][:model], *far)
        gains = lax.psum(jnp.concatenate(from_two(near[0][model:]), axis=0), "wide")
    mine, theirs = finish(last_mine, links.core(last_other), *rows_in[:2], d_middle, gain_one)
    if staged:
        sums, theirs = hold(sums, theirs)
    back = links.y(theirs)
    if staged:
        low = add(own_low, from_x_low, from_both_low[:half])
        high = add(own_high, from_x_high[:half], from_y_high)
        coarse = [lax.reduce_precision(value, 8, 7) for value in sums]
        pairs = [coarse[0], sums[0] - coarse[0], coarse[1], sums[1] - coarse[1]]
        tail = jnp.concatenate([*pairs, jnp.zeros((12, model), F32)], axis=0).astype(BF)
        blocks = [piece[k * rows : (k + 1) * rows] for piece in (low, high) for k in range(2)]
        arrived = [
            links.z(jnp.concatenate([blocks[k].astype(BF), tail], axis=0), k)
            for k in range(1, planes)
        ]
        attn_grad = add(blocks[0], *(part[:rows] for part in arrived))
        gains = jnp.concatenate(sums, axis=0) + sum(
            jnp.concatenate(from_two(part[rows:]), axis=0) for part in arrived
        )
        feed_grad = add(feed_low[:rows], *feed_parts)
    gains = (gains + links.core(gains)) + (links.y(gains) + links.across(gains))

    def in_order(own, other):
        stacked = jnp.where(y == 0, jnp.stack([own, other]), jnp.stack([other, own]))
        return stacked.reshape(tokens.shape)

    return (
        in_order(output[:TILE], output_back),
        in_order(mine, back),
        gains[0],
        attn_grad[:, head_width : 2 * head_width],
        attn_grad[:, 2 * head_width : 3 * head_width],
        attn_grad[:, 3 * head_width :],
        attn_grad[:, :head_width].T,
        gains[1],
        feed_grad[:, :units],
        feed_grad[:, units : 2 * units],
        feed_grad[:, 2 * units :].T,
    )


def solution(mesh):
    in_specs = (
        P(None, "wide", "narrow", None),
        P(None, "wide"),
        P(),
        P("wide", "narrow"),
        P("wide", "narrow"),
        P("wide", "narrow"),
        P("narrow", "wide"),
        P(),
        P("wide", "narrow"),
        P("wide", "narrow"),
        P("narrow", "wide"),
        P(None, "wide", "narrow", None),
    )
    out_specs = (
        P(None, "wide", "narrow", None),
        P(None, "wide", "narrow", None),
        P(),
        P("wide", "narrow"),
        P("wide", "narrow"),
        P("wide", "narrow"),
        P("narrow", "wide"),
        P(),
        P("wide", "narrow"),
        P("wide", "narrow"),
        P("narrow", "wide"),
    )
    return jax.shard_map(
        on_device, mesh=mesh, in_specs=in_specs, out_specs=out_specs, check_vma=False
    )
```

```python
import functools

import jax
import jax.numpy as jnp
from jax import lax
from jax.experimental import pallas as pl
from jax.experimental.pallas import tpu as pltpu
from jax.sharding import PartitionSpec as P

HD = 64
EPSILON = 1e-06
MASKED = -1e30
TILE = 256
FEED_ROWS = 1024
QUERY_ROWS = 1024
MIDDLE_LIMIT = 8 * 1024 * 1024
BACK_LIMIT = 14 * 1024 * 1024
ATTEND_LIMIT = 11 * 1024 * 1024
FEED_LIMIT = 22 * 1024 * 1024
COST = pl.CostEstimate(flops=10**6, bytes_accessed=10**5, transcendentals=0)
BF = jnp.bfloat16
F32 = jnp.float32


def mm(left, right):
    return jnp.dot(left, right, preferred_element_type=F32)


def mm_nt(left, right):
    return lax.dot_general(left, right, (((1,), (1,)), ((), ())), preferred_element_type=F32)


def mm_tn(left, right):
    return lax.dot_general(left, right, (((0,), (0,)), ((), ())), preferred_element_type=F32)


def inverse_rms(features):
    return lax.rsqrt(jnp.mean(features * features, axis=-1, keepdims=True) + EPSILON)


def place(meta, pieces, orders, dest, rows, sems):
    copies = []
    for piece, order in zip(pieces, orders):
        for number, index in enumerate(order):
            at = 0 if rows == dest.shape[0] else pl.multiple_of(meta[index], 16)
            copy = pltpu.make_async_copy(
                piece.at[pl.ds(number * rows, rows), :],
                dest.at[pl.ds(at, rows), :],
                sems.at[len(copies)],
            )
            copy.start()
            copies.append(copy)
    return copies


def wait_all(copies):
    for copy in copies:
        copy.wait()


def blocks_of(orders):
    return sum(len(order) for order in orders)


def disperse(meta, source, groups, orders, rows):
    for group, order in zip(groups, orders):
        for place, index in enumerate(order):
            at = 0 if rows == source.shape[0] else pl.multiple_of(meta[index], 16)
            group[place * rows : (place + 1) * rows, :] = source[pl.ds(at, rows), :]


def row_block(refs, block):
    start = block * TILE
    for ref in refs:
        if start < ref.shape[0]:
            return ref[start : start + TILE, :]
        start -= ref.shape[0]


def forward_kernel(heads, n_rows, orders, block_rows, meta, *refs):
    first = n_rows > 0
    refs = list(refs)
    take = lambda count: [refs.pop(0) for _ in range(count)]
    width = heads * HD
    total = 4 * TILE
    if first:
        (gain,) = take(1)
        sources = take(n_rows)
    else:
        normed, context_first, weight_first = take(3)
    pieces = take(len(orders))
    inverse, context, expo, weight, proj = take(5)
    if first:
        (normed,) = take(1)
    else:
        (partial,) = take(1)
    q_ext, k_ext, v_flip, sems, sems_more = take(5)
    copies = place(meta, pieces, orders, weight, block_rows, sems)
    outs = []

    def carry(source, dest):
        copy = pltpu.make_async_copy(source, dest, sems_more.at[len(outs)])
        copy.start()
        outs.append(copy)

    if first:
        (extra,) = take(1)
        starts = [sum(ref.shape[0] for ref in sources[:k]) for k in range(n_rows)]
        for start, source in zip(starts, sources):
            carry(source, extra.at[pl.ds(start, source.shape[0]), :])
        wait_all(outs)
        for block in range(4):
            rows = slice(block * TILE, (block + 1) * TILE)
            features = extra[rows, :].astype(F32)
            normed[rows, :] = (features * inverse_rms(features) * gain[...]).astype(BF)
    wait_all(copies)
    proj[...] = mm(normed[...], weight[...]).astype(BF)
    lanes = lax.broadcasted_iota(jnp.int32, (TILE, HD), 1)
    index = lax.broadcasted_iota(jnp.int32, (TILE, HD), 0)
    ones = jnp.where(lanes == 0, 1.0, 0.0).astype(BF)
    below = jnp.where(lax.broadcasted_iota(jnp.int32, (16, total), 0) == 0, 1.0, 0.0).astype(BF)
    for block in range(4):
        rows = slice(block * TILE, (block + 1) * TILE)
        usable = meta[8 + block] + index < meta[12]
        bias = jnp.where((lanes == 0) & ~usable, MASKED, 0.0).astype(BF)
        for head in range(heads):
            at = width + head * HD
            q_ext[head, rows, 0:HD] = proj[rows, at : at + HD]
            q_ext[head, rows, HD : 2 * HD] = ones
            at = 2 * width + head * HD
            k_ext[head, rows, 0:HD] = proj[rows, at : at + HD]
            k_ext[head, rows, HD : 2 * HD] = bias
    for head in range(heads):
        at = 3 * width + head * HD
        v_flip[head, 0:HD, :] = proj[:, at : at + HD].T
        v_flip[head, HD : HD + 16, :] = below
    inverse[...] = jnp.ones_like(inverse)
    for head in range(heads):
        for start in range(0, total, QUERY_ROWS):
            rows = slice(start, start + QUERY_ROWS)
            scores = mm_nt(k_ext[head], q_ext[head, rows, :])
            top = jnp.max(scores, axis=0, keepdims=True)
            raised = jnp.exp(scores - top).astype(BF)
            expo[head, :, rows] = raised
            mixed = mm(v_flip[head], raised)
            inv = 1.0 / mixed[HD : HD + 1, :]
            inverse[head : head + 1, rows] = inv
            context[rows, head * HD : (head + 1) * HD] = (mixed[0:HD, :] * inv).astype(BF).T
    if not first:
        partial[...] = (
            mm_nt(context_first[...], weight_first[:, 0:width])
            + mm_nt(context[...], weight[:, 0:width])
        ).astype(BF)


SMEM = pl.BlockSpec(memory_space=pltpu.SMEM)
VMEM = pl.BlockSpec(memory_space=pltpu.VMEM)
HBM = pl.BlockSpec(memory_space=pltpu.HBM)


def attention_forward(meta, heads, block_rows, pieces, orders, rows_in=(), gain=None, before=None):
    width = pieces[0].shape[1]
    model = rows_in[0].shape[1] if rows_in else before[0].shape[1]
    total = 4 * TILE
    rows = jax.ShapeDtypeStruct((total, model), BF)
    numerators = jax.ShapeDtypeStruct((heads, total, total), BF)
    if rows_in:
        in_fast, in_slow = [gain], [*rows_in, *pieces]
        more, extra = [rows], [pltpu.VMEM((total, model), BF)]
    else:
        in_fast, in_slow = [*before], [*pieces]
        more, extra = [rows], []
    return pl.pallas_call(
        functools.partial(forward_kernel, heads, len(rows_in), orders, block_rows),
        in_specs=[SMEM] + [VMEM] * len(in_fast) + [HBM] * len(in_slow),
        out_specs=[VMEM] * 6,
        out_shape=[
            jax.ShapeDtypeStruct((8, total), F32),
            jax.ShapeDtypeStruct((total, heads * HD), BF),
            numerators,
            jax.ShapeDtypeStruct((model, width), BF),
            jax.ShapeDtypeStruct((total, width), BF),
            *more,
        ],
        scratch_shapes=[
            pltpu.VMEM((heads, total, 2 * HD), BF),
            pltpu.VMEM((heads, total, 2 * HD), BF),
            pltpu.VMEM((heads, HD + 16, total), BF),
            pltpu.SemaphoreType.DMA((blocks_of(orders),)),
            pltpu.SemaphoreType.DMA((4,)),
            *extra,
        ],
        compiler_params=pltpu.CompilerParams(vmem_limit_bytes=ATTEND_LIMIT),
        cost_estimate=COST,
        name="attention_forward",
    )(meta, *in_fast, *in_slow)


def gelu_terms(gate):
    scale = 0.7978845608028654
    cube = 0.044715
    square = gate * gate
    bent = jnp.tanh(scale * gate * (1.0 + cube * square))
    half = 0.5 * (1.0 + bent)
    slope = half + 0.5 * gate * (1.0 - bent * bent) * (scale * (1.0 + 3.0 * cube * square))
    return gate * half, slope


def feed_kernel(n_rows, n_cots, in_orders, orders, block_rows, meta, *refs):
    first = n_rows > 0
    refs = list(refs)
    take = lambda count: [refs.pop(0) for _ in range(count)]
    if first:
        rows_in = take(n_rows)
        part_mine, part_other, gain = take(3)
    else:
        normed, result_before, back_before = take(3)
    cots = take(n_cots)
    pieces = take(len(in_orders))
    if first:
        normed, result, back = take(3)
    else:
        mine, other, back = take(3)
    groups = take(len(orders))
    weight, hidden, d_gate, d_up, cot, grad, sems = take(7)
    units = weight.shape[1] // 3
    copies = place(meta, pieces, in_orders, weight, block_rows, sems)
    for block in range(4):
        rows = slice(block * TILE, (block + 1) * TILE)
        cot[rows, :] = row_block(cots, block)
        if first:
            swapped = slice(((block + 2) % 4) * TILE, ((block + 2) % 4 + 1) * TILE)
            features = (
                row_block(rows_in, block).astype(F32)
                + part_mine[rows, :].astype(F32)
                + part_other[swapped, :].astype(F32)
            )
            features = features.astype(BF).astype(F32)
            normed[rows, :] = (features * inverse_rms(features) * gain[...]).astype(BF)
    wait_all(copies)
    for start in range(0, 4 * TILE, FEED_ROWS):
        rows = slice(start, start + FEED_ROWS)
        pre = mm(normed[rows, :], weight[:, 0 : 2 * units])
        act, slope = gelu_terms(pre[:, :units])
        up = pre[:, units:]
        low = (act * up).astype(BF)
        hidden[rows, :] = low
        d_hidden = mm(cot[rows, :], weight[:, 2 * units :])
        gate_low = (d_hidden * up * slope).astype(BF)
        up_low = (d_hidden * act).astype(BF)
        d_gate[rows, :] = gate_low
        d_up[rows, :] = up_low
        down = mm_nt(low, weight[:, 2 * units :])
        through = mm_nt(gate_low, weight[:, 0:units]) + mm_nt(up_low, weight[:, units : 2 * units])
        if first:
            result[rows, :] = down.astype(BF)
            back[rows, :] = through.astype(BF)
        else:
            down = (down + result_before[rows, :].astype(F32)).astype(BF)
            if start < 2 * TILE:
                mine[rows, :] = down[: 2 * TILE - start]
            if start + FEED_ROWS > 2 * TILE:
                begin = max(start - 2 * TILE, 0)
                other[begin : start + FEED_ROWS - 2 * TILE, :] = down[begin + 2 * TILE - start :]
            back[rows, :] = (through + back_before[rows, :].astype(F32)).astype(BF)
    grad[:, 2 * units :] = mm_tn(cot[...], hidden[...]).astype(BF)
    grad[:, 0:units] = mm_tn(normed[...], d_gate[...]).astype(BF)
    grad[:, units : 2 * units] = mm_tn(normed[...], d_up[...]).astype(BF)
    disperse(meta, grad, groups, orders, block_rows)


def feed_forward(meta, block_rows, cots, pieces, in_orders, orders, rows_in=(), before=()):
    width = pieces[0].shape[1]
    model = cots[0].shape[1]
    total = 4 * TILE
    units = width // 3
    full = jax.ShapeDtypeStruct((total, model), BF)
    half = jax.ShapeDtypeStruct((2 * TILE, model), BF)
    operands = [*rows_in, *before, *cots, *pieces]
    out_shape = [full, full, full] if rows_in else [half, half, full]
    out_shape += [
        jax.ShapeDtypeStruct((len(order) * block_rows, width), BF) for order in orders
    ]
    return pl.pallas_call(
        functools.partial(
            feed_kernel, len(rows_in), len(cots), in_orders, orders, block_rows
        ),
        in_specs=[SMEM] + [VMEM] * (len(operands) - len(pieces)) + [HBM] * len(pieces),
        out_specs=[VMEM] * len(out_shape),
        out_shape=out_shape,
        scratch_shapes=[
            pltpu.VMEM((model, width), BF),
            pltpu.VMEM((total, units), BF),
            pltpu.VMEM((total, units), BF),
            pltpu.VMEM((total, units), BF),
            pltpu.VMEM((total, model), BF),
            pltpu.VMEM((model, width), BF),
            pltpu.SemaphoreType.DMA((blocks_of(in_orders),)),
        ],
        compiler_params=pltpu.CompilerParams(vmem_limit_bytes=FEED_LIMIT),
        cost_estimate=COST,
        name="feed_forward",
    )(meta, *operands)


def middle_kernel(heads, n_rows, n_cots, *refs):
    refs = list(refs)
    take = lambda count: [refs.pop(0) for _ in range(count)]
    rows_in = take(n_rows)
    part_mine, part_other, gain = take(3)
    cots = take(n_cots)
    d_mine, d_other, context_near, context_far = take(4)
    weight_near, weight_far = take(2)
    d_middle, d_context_near, d_context_far, grad_near, grad_far, d_gain = take(6)
    (d_all,) = take(1)
    width = heads * HD
    gains = 0.0
    for block in range(4):
        rows = slice(block * TILE, (block + 1) * TILE)
        swapped = slice(((block + 2) % 4) * TILE, ((block + 2) % 4 + 1) * TILE)
        features = (
            row_block(rows_in, block).astype(F32)
            + part_mine[rows, :].astype(F32)
            + part_other[swapped, :].astype(F32)
        )
        features = features.astype(BF).astype(F32)
        inverse = inverse_rms(features)
        back = d_mine[rows, :].astype(F32) + d_other[swapped, :].astype(F32)
        scaled = back * gain[...]
        inner = jnp.mean(scaled * features, axis=-1, keepdims=True)
        result = (
            row_block(cots, block).astype(F32)
            + inverse * scaled
            - features * (inverse * inverse * inverse * inner)
        )
        d_all[rows, :] = result.astype(BF)
        if block < 2:
            d_middle[rows, :] = result
            gains += jnp.sum(back * features * inverse, axis=0, keepdims=True)
    d_gain[...] = jnp.broadcast_to(gains, d_gain.shape)
    d_context_near[...] = mm(d_all[...], weight_near[:, 0:width]).astype(BF)
    d_context_far[...] = mm(d_all[...], weight_far[:, 0:width]).astype(BF)
    grad_near[...] = mm_tn(d_all[...], context_near[...]).astype(BF)
    grad_far[...] = mm_tn(d_all[...], context_far[...]).astype(BF)


def middle_backward(heads, rows_in, parts, gain, cots, d_normed, contexts, weights):
    model = gain.shape[1]
    total = 4 * TILE
    width = heads * HD
    operands = [*rows_in, *parts, gain, *cots, *d_normed, *contexts, *weights]
    return pl.pallas_call(
        functools.partial(middle_kernel, heads, len(rows_in), len(cots)),
        in_specs=[VMEM] * len(operands),
        out_specs=[VMEM] * 6,
        out_shape=[
            jax.ShapeDtypeStruct((2 * TILE, model), F32),
            jax.ShapeDtypeStruct((total, width), BF),
            jax.ShapeDtypeStruct((total, width), BF),
            jax.ShapeDtypeStruct((model, width), BF),
            jax.ShapeDtypeStruct((model, width), BF),
            jax.ShapeDtypeStruct((8, model), F32),
        ],
        scratch_shapes=[
            pltpu.VMEM((total, model), BF),
        ],
        compiler_params=pltpu.CompilerParams(vmem_limit_bytes=MIDDLE_LIMIT),
        cost_estimate=COST,
        name="middle_backward",
    )(*operands)


def in_two(*rows):
    high = [row.astype(BF).astype(F32) for row in rows]
    index = lax.broadcasted_iota(jnp.int32, (16, rows[0].shape[1]), 0)
    result = jnp.zeros((16, rows[0].shape[1]), F32)
    for number, row in enumerate(rows):
        result = jnp.where(index == 2 * number, high[number], result)
        result = jnp.where(index == 2 * number + 1, row - high[number], result)
    return result.astype(BF)


def from_two(rows):
    return [
        rows[2 * k : 2 * k + 1].astype(F32) + rows[2 * k + 1 : 2 * k + 2].astype(F32)
        for k in range(2)
    ]


def finish_kernel(
    d_mine, d_other, keep, got, d_middle, gain, block, block_x, mine, theirs, pairs, sums
):
    for number, rows_in in enumerate((keep, got)):
        rows = slice(number * TILE, (number + 1) * TILE)
        features = rows_in[...].astype(F32)
        inverse = inverse_rms(features)
        scaled = (d_mine[rows, :].astype(F32) + d_other[rows, :].astype(F32)) * gain[...]
        inner = jnp.mean(scaled * features, axis=-1, keepdims=True)
        result = (
            d_middle[rows, :] + inverse * scaled - features * (inverse * inverse * inverse * inner)
        ).astype(BF)
        if number == 0:
            mine[...] = result
        else:
            theirs[...] = result
    end = block.shape[0] - 16
    ours, others = from_two(block[end:, :]), from_two(block_x[end:, :])
    total = [a + b for a, b in zip(ours, others)]
    pairs[...] = in_two(*total)
    index = lax.broadcasted_iota(jnp.int32, sums.shape, 0)
    sums[...] = jnp.where(index == 0, total[0], jnp.where(index == 1, total[1], 0.0))


def finish(d_mine, d_other, keep, got, d_middle, gain, block, block_x):
    model = keep.shape[1]
    return pl.pallas_call(
        finish_kernel,
        in_specs=[VMEM] * 8,
        out_specs=[VMEM] * 4,
        out_shape=[
            jax.ShapeDtypeStruct((TILE, model), BF),
            jax.ShapeDtypeStruct((TILE, model), BF),
            jax.ShapeDtypeStruct((16, model), BF),
            jax.ShapeDtypeStruct((8, model), F32),
        ],
        compiler_params=pltpu.CompilerParams(vmem_limit_bytes=MIDDLE_LIMIT),
        cost_estimate=COST,
        name="finish_backward",
    )(d_mine, d_other, keep, got, d_middle, gain, block, block_x)


def backward_kernel(heads, orders, block_rows, last, meta, *refs):
    refs = list(refs)
    take = lambda count: [refs.pop(0) for _ in range(count)]
    inverse, context, expo, weight, proj, normed, d_context, grad_out = take(8)
    if last:
        gain, gain_rows = take(2)
    if last:
        (before,) = take(1)
        mine, other = take(2)
    else:
        (result,) = take(1)
    groups = take(len(orders))
    do_ext, v_ext, d_proj, grad = take(4)
    width = heads * HD
    total = 4 * TILE
    lanes = lax.broadcasted_iota(jnp.int32, (total, HD), 1)
    columns = inverse[...].T
    d_proj[:, 0:width] = jnp.zeros((total, width), BF)
    for head in range(heads):
        at = head * HD
        scaled = (d_context[:, at : at + HD].astype(F32) * columns[:, head : head + 1]).astype(BF)
        inner = -jnp.sum(
            scaled.astype(F32) * context[:, at : at + HD].astype(F32), axis=-1, keepdims=True
        )
        high = inner.astype(BF).astype(F32)
        do_ext[head, :, 0:HD] = scaled
        do_ext[head, :, HD : 2 * HD] = jnp.where(
            lanes == 0, high, jnp.where(lanes == 1, inner - high, 0.0)
        ).astype(BF)
    for head in range(heads):
        at = 3 * width + head * HD
        v_ext[head, :, 0:HD] = proj[:, at : at + HD]
        v_ext[head, :, HD : 2 * HD] = jnp.where(lanes < 2, 1.0, 0.0).astype(BF)
    for head in range(heads):
        q_at, k_at, v_at = (part * width + head * HD for part in (1, 2, 3))
        raised = expo[head]
        d_probs = mm_nt(v_ext[head], do_ext[head])
        d_scores = (raised.astype(F32) * d_probs).astype(BF)
        d_queries = mm(proj[:, k_at : k_at + HD].T, d_scores)
        d_keys = mm_nt(proj[:, q_at : q_at + HD].T, d_scores)
        d_values = mm_nt(do_ext[head, :, 0:HD].T, raised)
        d_proj[:, q_at : q_at + HD] = d_queries.astype(BF).T
        d_proj[:, k_at : k_at + HD] = d_keys.astype(BF).T
        d_proj[:, v_at : v_at + HD] = d_values.astype(BF).T
    grad[...] = mm_tn(normed[...], d_proj[...]).astype(BF)
    grad[:, 0:width] = grad_out[...]
    disperse(meta, grad, groups, orders, block_rows)
    through = mm_nt(d_proj[...], weight[...])
    if last:
        through = through + before[...].astype(F32)
        mine[...] = through[0 : 2 * TILE].astype(BF)
        other[...] = through[2 * TILE :].astype(BF)
        first = jnp.sum(through * normed[...].astype(F32), axis=0, keepdims=True) / gain[...]
        end = len(orders[-1]) * block_rows
        groups[-1][end : end + 16, :] = in_two(first, gain_rows[0:1, :])
    else:
        result[...] = through.astype(BF)


def attention_backward(
    meta, heads, block_rows, normed, saved, d_context, grad_out, orders, before=None
):
    last = before is not None
    weight, proj = saved[3:]
    model, width = weight.shape
    total = proj.shape[0]
    rows = jax.ShapeDtypeStruct((total, model), BF)
    in_fast = [*saved, normed, d_context, grad_out]
    scratch = [
        pltpu.VMEM((heads, total, 2 * HD), BF),
        pltpu.VMEM((heads, total, 2 * HD), BF),
        pltpu.VMEM((total, width), BF),
        pltpu.VMEM((model, width), BF),
    ]
    sizes = [len(order) * block_rows for order in orders]
    if last:
        in_fast += [*before[1:], before[0]]
        out_shape = [jax.ShapeDtypeStruct((2 * TILE, model), BF)] * 2
        sizes[-1] += 16
    else:
        out_shape = [rows]
    out_shape += [jax.ShapeDtypeStruct((size, width), BF) for size in sizes]
    return pl.pallas_call(
        functools.partial(backward_kernel, heads, orders, block_rows, last),
        in_specs=[SMEM] + [VMEM] * len(in_fast),
        out_specs=[VMEM] * len(out_shape),
        out_shape=out_shape,
        scratch_shapes=scratch,
        compiler_params=pltpu.CompilerParams(vmem_limit_bytes=BACK_LIMIT),
        cost_estimate=COST,
        name="attention_backward",
    )(meta, *in_fast)


def add(*terms):
    return sum(term.astype(F32) for term in terms)


def hold(values, *others):
    values, others = lax.optimization_barrier((values, others))
    return values, *others


def fold_kernel(own_low, own_high, x_low, x_high, both_low, y_high, sums, total, *messages):
    rows = total.shape[0]
    for index in range(4):
        at = slice((index % 2) * rows, (index % 2 + 1) * rows)
        own, over_x, over_y = (
            (own_low, x_low, both_low) if index < 2 else (own_high, x_high, y_high)
        )
        block = own[at, :].astype(F32) + over_x[at, :].astype(F32) + over_y[at, :].astype(F32)
        if index == 0:
            total[...] = block
        else:
            messages[index - 1][0:rows, :] = block.astype(BF)
            messages[index - 1][rows:, :] = sums[...]


def fold(rows, *operands):
    width = operands[0].shape[1]
    message = jax.ShapeDtypeStruct((rows + 16, width), BF)
    return pl.pallas_call(
        fold_kernel,
        in_specs=[VMEM] * len(operands),
        out_specs=[VMEM] * 4,
        out_shape=[jax.ShapeDtypeStruct((rows, width), F32), message, message, message],
        compiler_params=pltpu.CompilerParams(vmem_limit_bytes=MIDDLE_LIMIT),
        cost_estimate=COST,
        name="fold_backward",
    )(*operands)


class Links:
    def __init__(self, wide, narrow):
        self.wide, self.narrow = wide, narrow
        self.planes = wide // 2
        self.staged = wide == 8

    def y(self, values):
        return lax.ppermute(values, "narrow", [(i, (i + 2) % 4) for i in range(4)])

    def core(self, values):
        return lax.ppermute(values, "narrow", [(i, i ^ 1) for i in range(4)])

    def across(self, values):
        return lax.ppermute(values, "narrow", [(i, (i + 2) % 4 ^ 1) for i in range(4)])

    def x(self, values):
        return lax.ppermute(values, "wide", [(i, i ^ 1) for i in range(self.wide)])

    def z(self, values, ahead):
        turn = lambda i: ((i // 2 + ahead) % self.planes) * 2 + i % 2
        return lax.ppermute(values, "wide", [(i, turn(i)) for i in range(self.wide)])

    def whole_gather(self, piece):
        near = lax.all_gather(piece, "wide", axis=0, tiled=True)
        return [near], [self.y(near)]

    def whole_reduce(self, near, far):
        return lax.psum_scatter(near, "wide", scatter_dimension=0, tiled=True).astype(
            F32
        ) + lax.psum_scatter(self.y(far), "wide", scatter_dimension=0, tiled=True).astype(F32)


def on_device(
    tokens,
    lengths,
    norm_one,
    w_query,
    w_key,
    w_value,
    w_out,
    norm_two,
    w_gate,
    w_up,
    w_down,
    cotangent,
):
    model = tokens.shape[-1]
    wide, narrow = lax.axis_size("wide"), lax.axis_size("narrow")
    links = Links(wide, narrow)
    heads = w_query.shape[1] // HD
    head_width = heads * HD
    units = w_gate.shape[1]
    at_wide, at_narrow = lax.axis_index("wide"), lax.axis_index("narrow")
    y, c = at_narrow >> 1, at_narrow & 1
    x, z = at_wide & 1, at_wide >> 1

    staged = links.staged
    planes = links.planes
    rows = model // wide
    turned = [((z + k) & (planes - 1)) * 2 + (x ^ side) for side in range(2) for k in range(4)]
    blocks = [((y ^ far) * 2 + (c ^ side)) * TILE for side in range(2) for far in range(2)]
    length = lax.dynamic_index_in_dim(lengths, y, 0, keepdims=False)[0]
    numbers = [
        *(spot * rows for spot in turned),
        *blocks,
        length,
    ]
    meta = jnp.stack([jnp.asarray(number, jnp.int32) for number in numbers])
    first_item = (y == 0).astype(jnp.int32)
    w_out, meta, y, first_item = hold(w_out, meta, y, first_item)

    gain_one = norm_one.reshape(1, model)
    gain_two = norm_two.reshape(1, model)

    def keep_give(rows):
        flat = rows.reshape(2, TILE, model)
        return (
            lax.dynamic_index_in_dim(flat, y, 0, keepdims=False),
            lax.dynamic_index_in_dim(flat, 1 - y, 0, keepdims=False),
        )

    attn_piece = jnp.concatenate([w_out.T, w_query, w_key, w_value], axis=1)
    feed_piece = jnp.concatenate([w_gate, w_up, w_down.T], axis=1)
    keep, give = keep_give(tokens)
    keep_cot, give_cot = keep_give(cotangent)
    half = planes // 2 * rows
    if staged:
        block_rows = rows
        quarters = ((0, 1), (2, 3), (4, 5), (6, 7))
        attn_near_in = attn_far_in = ((0, 1, 2, 3), (4, 5, 6, 7))
        feed_near_in = ((0,), (1,), (3,), (2,), (4, 5, 7), (6,))
        feed_far_in = ((0, 1, 3), (2,), (4, 5), (7, 6))
        attn_far_out = ((0, 1, 4, 5), (2, 3), (6, 7))
    else:
        block_rows = model
        quarters = attn_far_out = ((0,),)
        attn_near_in = attn_far_in = feed_near_in = feed_far_in = ((0,),)

    got = links.y(give)
    if staged:
        column = [attn_piece] + [links.z(attn_piece, planes - k) for k in range(1, planes)]
        column = jnp.concatenate(column, axis=0)
        over_x, over_y = links.x(column), links.y(column)
        feed_piece, column = hold(feed_piece, column)
        feed_one = links.z(feed_piece, planes - 1)
        feed_three = links.z(feed_piece, planes - 3)
    else:
        attn_near, attn_far = links.whole_gather(attn_piece)
        feed_near, feed_far = links.whole_gather(feed_piece)
    rows_in = [keep, got, links.core(keep), links.core(got)]
    if staged:
        over_y, rows_in, over_x = hold(over_y, rows_in, over_x)
        give_cot, over_y = hold(give_cot, over_y)
        attn_near = [column, over_x]
        attn_far = [over_y, links.x(over_y)]
    got_cot = links.y(give_cot)

    inv_near, context_near, expo_near, *kept_near, normed = attention_forward(
        meta, heads, block_rows, attn_near, attn_near_in, rows_in=rows_in, gain=gain_one
    )
    if staged:
        normed, got_cot, attn_far, feed_one, feed_three = hold(
            normed, got_cot, attn_far, feed_one, feed_three
        )
        feed_piece, feed_one = hold(feed_piece, feed_one)
        feed_two = links.z(feed_piece, planes - 2)
        three = jnp.concatenate([feed_piece, feed_one, feed_three], axis=0)
        feed_y = links.y(three)
        feed_x = links.x(three)
    own_cot = jnp.concatenate([keep_cot, got_cot], axis=0)
    cots = [own_cot, links.core(own_cot)]
    inv_far, context_far, expo_far, *kept_far, part_mine = attention_forward(
        meta, heads, block_rows, attn_far, attn_far_in,
        before=(normed, context_near, kept_near[0]),
    )
    if staged:
        part_mine, feed_two, feed_x, feed_y = hold(part_mine, feed_two, feed_x, feed_y)
        feed_x_two = links.x(feed_two)
        feed_y_two = links.y(feed_two)
    part_other = links.core(part_mine)
    if staged:
        part_other, feed_x_two, feed_y_two = hold(part_other, feed_x_two, feed_y_two)
        feed_near = [feed_piece, feed_one, feed_three, feed_two, feed_x, feed_x_two]
        feed_far = [
            feed_y,
            feed_y_two,
            links.y(feed_x[: 2 * rows]),
            links.x(jnp.concatenate([feed_y[2 * rows :], feed_y_two], axis=0)),
        ]
    parts = (part_mine, part_other)

    normed_two, down_near, back_near, *near = feed_forward(
        meta, block_rows, cots, feed_near, feed_near_in, quarters, rows_in=rows_in,
        before=(*parts, gain_two),
    )
    if staged:
        own_low, own_high, x_low, x_high = near
        from_x_high = links.x(x_high)
    mlp_mine, mlp_other, d_mine, *far = feed_forward(
        meta, block_rows, cots, feed_far, feed_far_in, quarters,
        before=(normed_two, down_near, back_near),
    )
    if staged:
        d_mine, from_x_high = hold(d_mine, from_x_high)
        y_low, y_high, xy_low, xy_high = far
        from_xy_high = links.x(xy_high)
    else:
        feed_grad = links.whole_reduce(*near, *far)
    d_other = links.core(d_mine)
    half_rows = 2 * TILE
    output = (
        jnp.concatenate(rows_in[:2], axis=0).astype(F32)
        + part_mine[:half_rows].astype(F32)
        + part_other[half_rows:].astype(F32)
        + mlp_mine.astype(F32)
        + links.core(mlp_other).astype(F32)
    ).astype(BF)
    output_back = links.y(output[TILE:])
    d_middle, d_context_near, d_context_far, out_near, out_far, gain_rows = middle_backward(
        heads,
        rows_in,
        parts,
        gain_two,
        cots,
        (d_mine, d_other),
        (context_near, context_far),
        (kept_near[0], kept_far[0]),
    )
    if staged:
        d_context_far, from_xy_high, output_back = hold(d_context_far, from_xy_high, output_back)
        xy_low, from_xy_high = hold(xy_low, from_xy_high)
        from_y_high = links.y(add(y_high, from_xy_high).astype(BF))
        from_xy_low = links.x(xy_low)
    d_first, *far = attention_backward(
        meta, heads, block_rows, normed, (inv_far, context_far, expo_far, *kept_far),
        d_context_far, out_far, attn_far_out,
    )
    if staged:
        d_first, from_y_high, from_xy_low = hold(d_first, from_y_high, from_xy_low)
        x_low, from_xy_low = hold(x_low, from_xy_low)
        high = add(own_high, from_x_high, from_y_high).astype(BF)
        feed_parts = [links.z(high[:rows], 2), links.z(high[rows:], 3)]
        feed_low, feed_y_low = own_low, add(y_low, from_xy_low).astype(BF)
        both_low, y_high, xy_high = far
        from_both_low = links.y(both_low)
        from_xy_high = links.x(xy_high)
        from_feed_x, from_feed_y = links.x(x_low), links.y(feed_y_low)
    last_mine, last_other, *near = attention_backward(
        meta, heads, block_rows, normed, (inv_near, context_near, expo_near, *kept_near),
        d_context_near, out_near, quarters, before=(d_first, gain_one, gain_rows),
    )
    if staged:
        last_other, near, from_both_low, from_xy_high, from_feed_x, from_feed_y, feed_two = hold(
            last_other, near, from_both_low, from_xy_high, from_feed_x, from_feed_y, feed_parts[0]
        )
        feed_low = add(feed_low, from_feed_x, from_feed_y)
        feed_parts = [feed_two, feed_parts[1], links.z(feed_low[rows:].astype(BF), 1)]
        own_low, own_high, x_low, x_high = near
        from_x_high = links.x(x_high)
        from_y_high = links.y(add(y_high, from_xy_high).astype(BF))
        from_x_low = links.x(add(x_low, from_both_low[half:]).astype(BF))
        given = (x_high, from_x_high)
    else:
        attn_grad = links.whole_reduce(near[0][:model], *far)
        given = (near[0], jnp.zeros_like(near[0]))
    mine, theirs, pairs, sums = finish(
        last_mine, links.core(last_other), *rows_in[:2], d_middle, gain_one, *given
    )
    back = links.y(theirs)
    if staged:
        attn_grad, *messages = fold(
            rows, own_low, own_high, from_x_low, from_x_high, from_both_low, from_y_high, pairs
        )
        arrived = [links.z(message, k + 1) for k, message in enumerate(messages)]
        attn_grad = add(attn_grad, *(part[:rows] for part in arrived))
        gains = sums[:2] + sum(
            part[rows : rows + 4].astype(F32).reshape(2, 2, model).sum(axis=1) for part in arrived
        )
        feed_grad = add(feed_low[:rows], *feed_parts)
    else:
        gains = lax.psum(sums[:2], "wide")
    gains = (gains + links.core(gains)) + (links.y(gains) + links.across(gains))

    def in_order(own, other):
        stacked = jnp.where(first_item == 1, jnp.stack([own, other]), jnp.stack([other, own]))
        return stacked.reshape(tokens.shape)

    return (
        in_order(output[:TILE], output_back),
        in_order(mine, back),
        gains[0],
        attn_grad[:, head_width : 2 * head_width],
        attn_grad[:, 2 * head_width : 3 * head_width],
        attn_grad[:, 3 * head_width :],
        attn_grad[:, :head_width].T,
        gains[1],
        feed_grad[:, :units],
        feed_grad[:, units : 2 * units],
        feed_grad[:, 2 * units :].T,
    )


def solution(mesh):
    in_specs = (
        P(None, "wide", "narrow", None),
        P(None, "wide"),
        P(),
        P("wide", "narrow"),
        P("wide", "narrow"),
        P("wide", "narrow"),
        P("narrow", "wide"),
        P(),
        P("wide", "narrow"),
        P("wide", "narrow"),
        P("narrow", "wide"),
        P(None, "wide", "narrow", None),
    )
    out_specs = (
        P(None, "wide", "narrow", None),
        P(None, "wide", "narrow", None),
        P(),
        P("wide", "narrow"),
        P("wide", "narrow"),
        P("wide", "narrow"),
        P("narrow", "wide"),
        P(),
        P("wide", "narrow"),
        P("wide", "narrow"),
        P("narrow", "wide"),
    )
    return jax.shard_map(
        on_device, mesh=mesh, in_specs=in_specs, out_specs=out_specs, check_vma=False
    )
```

```python
import functools

import jax
import jax.numpy as jnp
from jax import lax
from jax.experimental import pallas as pl
from jax.experimental.pallas import tpu as pltpu
from jax.sharding import PartitionSpec as P

HD = 64
EPSILON = 1e-06
MASKED = -1e30
TILE = 256
FEED_ROWS = 1024
QUERY_ROWS = 1024
MIDDLE_LIMIT = 8 * 1024 * 1024
BACK_LIMIT = 14 * 1024 * 1024
ATTEND_LIMIT = 11 * 1024 * 1024
FEED_LIMIT = 22 * 1024 * 1024
COST = pl.CostEstimate(flops=10**6, bytes_accessed=10**5, transcendentals=0)
BF = jnp.bfloat16
F32 = jnp.float32


def mm(left, right):
    return jnp.dot(left, right, preferred_element_type=F32)


def mm_nt(left, right):
    return lax.dot_general(left, right, (((1,), (1,)), ((), ())), preferred_element_type=F32)


def mm_tn(left, right):
    return lax.dot_general(left, right, (((0,), (0,)), ((), ())), preferred_element_type=F32)


def inverse_rms(features):
    return lax.rsqrt(jnp.mean(features * features, axis=-1, keepdims=True) + EPSILON)


def place(meta, pieces, orders, dest, rows, sems):
    copies = []
    for piece, order in zip(pieces, orders):
        for number, index in enumerate(order):
            at = 0 if rows == dest.shape[0] else pl.multiple_of(meta[index], 16)
            copy = pltpu.make_async_copy(
                piece.at[pl.ds(number * rows, rows), :],
                dest.at[pl.ds(at, rows), :],
                sems.at[len(copies)],
            )
            copy.start()
            copies.append(copy)
    return copies


def wait_all(copies):
    for copy in copies:
        copy.wait()


def blocks_of(orders):
    return sum(len(order) for order in orders)


def disperse(meta, source, groups, orders, rows):
    for group, order in zip(groups, orders):
        for place, index in enumerate(order):
            at = 0 if rows == source.shape[0] else pl.multiple_of(meta[index], 16)
            group[place * rows : (place + 1) * rows, :] = source[pl.ds(at, rows), :]


def row_block(refs, block):
    start = block * TILE
    for ref in refs:
        if start < ref.shape[0]:
            return ref[start : start + TILE, :]
        start -= ref.shape[0]


def forward_kernel(heads, n_rows, orders, block_rows, meta, *refs):
    first = n_rows > 0
    refs = list(refs)
    take = lambda count: [refs.pop(0) for _ in range(count)]
    width = heads * HD
    total = 4 * TILE
    if first:
        (gain,) = take(1)
        sources = take(n_rows)
    else:
        normed, context_first, weight_first = take(3)
    pieces = take(len(orders))
    inverse, context, expo, weight, proj = take(5)
    if first:
        (normed,) = take(1)
    else:
        (partial,) = take(1)
    q_ext, k_ext, v_flip, sems, sems_more = take(5)
    copies = place(meta, pieces, orders, weight, block_rows, sems)
    outs = []

    def carry(source, dest):
        copy = pltpu.make_async_copy(source, dest, sems_more.at[len(outs)])
        copy.start()
        outs.append(copy)

    if first:
        (extra,) = take(1)
        starts = [sum(ref.shape[0] for ref in sources[:k]) for k in range(n_rows)]
        for start, source in zip(starts, sources):
            carry(source, extra.at[pl.ds(start, source.shape[0]), :])
        wait_all(outs)
        for block in range(4):
            rows = slice(block * TILE, (block + 1) * TILE)
            features = extra[rows, :].astype(F32)
            normed[rows, :] = (features * inverse_rms(features) * gain[...]).astype(BF)
    wait_all(copies)
    proj[...] = mm(normed[...], weight[...]).astype(BF)
    lanes = lax.broadcasted_iota(jnp.int32, (TILE, HD), 1)
    index = lax.broadcasted_iota(jnp.int32, (TILE, HD), 0)
    ones = jnp.where(lanes == 0, 1.0, 0.0).astype(BF)
    below = jnp.where(lax.broadcasted_iota(jnp.int32, (16, total), 0) == 0, 1.0, 0.0).astype(BF)
    for block in range(4):
        rows = slice(block * TILE, (block + 1) * TILE)
        usable = meta[8 + block] + index < meta[12]
        bias = jnp.where((lanes == 0) & ~usable, MASKED, 0.0).astype(BF)
        for head in range(heads):
            at = width + head * HD
            q_ext[head, rows, 0:HD] = proj[rows, at : at + HD]
            q_ext[head, rows, HD : 2 * HD] = ones
            at = 2 * width + head * HD
            k_ext[head, rows, 0:HD] = proj[rows, at : at + HD]
            k_ext[head, rows, HD : 2 * HD] = bias
    for head in range(heads):
        at = 3 * width + head * HD
        v_flip[head, 0:HD, :] = proj[:, at : at + HD].T
        v_flip[head, HD : HD + 16, :] = below
    inverse[...] = jnp.ones_like(inverse)
    for head in range(heads):
        for start in range(0, total, QUERY_ROWS):
            rows = slice(start, start + QUERY_ROWS)
            scores = mm_nt(k_ext[head], q_ext[head, rows, :])
            top = jnp.max(scores, axis=0, keepdims=True)
            raised = jnp.exp(scores - top).astype(BF)
            expo[head, :, rows] = raised
            mixed = mm(v_flip[head], raised)
            inv = 1.0 / mixed[HD : HD + 1, :]
            inverse[head : head + 1, rows] = inv
            context[rows, head * HD : (head + 1) * HD] = (mixed[0:HD, :] * inv).astype(BF).T
    if not first:
        partial[...] = (
            mm_nt(context_first[...], weight_first[:, 0:width])
            + mm_nt(context[...], weight[:, 0:width])
        ).astype(BF)


SMEM = pl.BlockSpec(memory_space=pltpu.SMEM)
VMEM = pl.BlockSpec(memory_space=pltpu.VMEM)
HBM = pl.BlockSpec(memory_space=pltpu.HBM)


def attention_forward(meta, heads, block_rows, pieces, orders, rows_in=(), gain=None, before=None):
    width = pieces[0].shape[1]
    model = rows_in[0].shape[1] if rows_in else before[0].shape[1]
    total = 4 * TILE
    rows = jax.ShapeDtypeStruct((total, model), BF)
    numerators = jax.ShapeDtypeStruct((heads, total, total), BF)
    if rows_in:
        in_fast, in_slow = [gain], [*rows_in, *pieces]
        more, extra = [rows], [pltpu.VMEM((total, model), BF)]
    else:
        in_fast, in_slow = [*before], [*pieces]
        more, extra = [rows], []
    return pl.pallas_call(
        functools.partial(forward_kernel, heads, len(rows_in), orders, block_rows),
        in_specs=[SMEM] + [VMEM] * len(in_fast) + [HBM] * len(in_slow),
        out_specs=[VMEM] * 6,
        out_shape=[
            jax.ShapeDtypeStruct((8, total), F32),
            jax.ShapeDtypeStruct((total, heads * HD), BF),
            numerators,
            jax.ShapeDtypeStruct((model, width), BF),
            jax.ShapeDtypeStruct((total, width), BF),
            *more,
        ],
        scratch_shapes=[
            pltpu.VMEM((heads, total, 2 * HD), BF),
            pltpu.VMEM((heads, total, 2 * HD), BF),
            pltpu.VMEM((heads, HD + 16, total), BF),
            pltpu.SemaphoreType.DMA((blocks_of(orders),)),
            pltpu.SemaphoreType.DMA((4,)),
            *extra,
        ],
        compiler_params=pltpu.CompilerParams(vmem_limit_bytes=ATTEND_LIMIT),
        cost_estimate=COST,
        name="attention_forward",
    )(meta, *in_fast, *in_slow)


def gelu_terms(gate):
    scale = 0.7978845608028654
    cube = 0.044715
    square = gate * gate
    bent = jnp.tanh(scale * gate * (1.0 + cube * square))
    half = 0.5 * (1.0 + bent)
    slope = half + 0.5 * gate * (1.0 - bent * bent) * (scale * (1.0 + 3.0 * cube * square))
    return gate * half, slope


def feed_kernel(n_rows, n_cots, in_orders, orders, block_rows, meta, *refs):
    first = n_rows > 0
    refs = list(refs)
    take = lambda count: [refs.pop(0) for _ in range(count)]
    if first:
        rows_in = take(n_rows)
        part_mine, part_other, gain = take(3)
    else:
        normed, result_before, back_before = take(3)
    cots = take(n_cots)
    pieces = take(len(in_orders))
    if first:
        normed, result, back = take(3)
    else:
        mine, other, back = take(3)
    groups = take(len(orders))
    weight, hidden, d_gate, d_up, cot, grad, sems = take(7)
    units = weight.shape[1] // 3
    copies = place(meta, pieces, in_orders, weight, block_rows, sems)
    for block in range(4):
        rows = slice(block * TILE, (block + 1) * TILE)
        cot[rows, :] = row_block(cots, block)
        if first:
            swapped = slice(((block + 2) % 4) * TILE, ((block + 2) % 4 + 1) * TILE)
            features = (
                row_block(rows_in, block).astype(F32)
                + part_mine[rows, :].astype(F32)
                + part_other[swapped, :].astype(F32)
            )
            features = features.astype(BF).astype(F32)
            normed[rows, :] = (features * inverse_rms(features) * gain[...]).astype(BF)
    wait_all(copies)
    for start in range(0, 4 * TILE, FEED_ROWS):
        rows = slice(start, start + FEED_ROWS)
        pre = mm(normed[rows, :], weight[:, 0 : 2 * units])
        act, slope = gelu_terms(pre[:, :units])
        up = pre[:, units:]
        low = (act * up).astype(BF)
        hidden[rows, :] = low
        d_hidden = mm(cot[rows, :], weight[:, 2 * units :])
        gate_low = (d_hidden * up * slope).astype(BF)
        up_low = (d_hidden * act).astype(BF)
        d_gate[rows, :] = gate_low
        d_up[rows, :] = up_low
        down = mm_nt(low, weight[:, 2 * units :])
        through = mm_nt(gate_low, weight[:, 0:units]) + mm_nt(up_low, weight[:, units : 2 * units])
        if first:
            result[rows, :] = down.astype(BF)
            back[rows, :] = through.astype(BF)
        else:
            down = (down + result_before[rows, :].astype(F32)).astype(BF)
            if start < 2 * TILE:
                mine[rows, :] = down[: 2 * TILE - start]
            if start + FEED_ROWS > 2 * TILE:
                begin = max(start - 2 * TILE, 0)
                other[begin : start + FEED_ROWS - 2 * TILE, :] = down[begin + 2 * TILE - start :]
            back[rows, :] = (through + back_before[rows, :].astype(F32)).astype(BF)
    grad[:, 2 * units :] = mm_tn(cot[...], hidden[...]).astype(BF)
    grad[:, 0:units] = mm_tn(normed[...], d_gate[...]).astype(BF)
    grad[:, units : 2 * units] = mm_tn(normed[...], d_up[...]).astype(BF)
    disperse(meta, grad, groups, orders, block_rows)


def feed_forward(meta, block_rows, cots, pieces, in_orders, orders, rows_in=(), before=()):
    width = pieces[0].shape[1]
    model = cots[0].shape[1]
    total = 4 * TILE
    units = width // 3
    full = jax.ShapeDtypeStruct((total, model), BF)
    half = jax.ShapeDtypeStruct((2 * TILE, model), BF)
    operands = [*rows_in, *before, *cots, *pieces]
    out_shape = [full, full, full] if rows_in else [half, half, full]
    out_shape += [
        jax.ShapeDtypeStruct((len(order) * block_rows, width), BF) for order in orders
    ]
    return pl.pallas_call(
        functools.partial(
            feed_kernel, len(rows_in), len(cots), in_orders, orders, block_rows
        ),
        in_specs=[SMEM] + [VMEM] * (len(operands) - len(pieces)) + [HBM] * len(pieces),
        out_specs=[VMEM] * len(out_shape),
        out_shape=out_shape,
        scratch_shapes=[
            pltpu.VMEM((model, width), BF),
            pltpu.VMEM((total, units), BF),
            pltpu.VMEM((total, units), BF),
            pltpu.VMEM((total, units), BF),
            pltpu.VMEM((total, model), BF),
            pltpu.VMEM((model, width), BF),
            pltpu.SemaphoreType.DMA((blocks_of(in_orders),)),
        ],
        compiler_params=pltpu.CompilerParams(vmem_limit_bytes=FEED_LIMIT),
        cost_estimate=COST,
        name="feed_forward",
    )(meta, *operands)


def middle_kernel(heads, n_rows, n_cots, *refs):
    refs = list(refs)
    take = lambda count: [refs.pop(0) for _ in range(count)]
    rows_in = take(n_rows)
    part_mine, part_other, gain = take(3)
    cots = take(n_cots)
    d_mine, d_other, context_near, context_far = take(4)
    weight_near, weight_far = take(2)
    d_middle, d_context_near, d_context_far, grad_near, grad_far, d_gain = take(6)
    (d_all,) = take(1)
    width = heads * HD
    gains = 0.0
    for block in range(4):
        rows = slice(block * TILE, (block + 1) * TILE)
        swapped = slice(((block + 2) % 4) * TILE, ((block + 2) % 4 + 1) * TILE)
        features = (
            row_block(rows_in, block).astype(F32)
            + part_mine[rows, :].astype(F32)
            + part_other[swapped, :].astype(F32)
        )
        features = features.astype(BF).astype(F32)
        inverse = inverse_rms(features)
        back = d_mine[rows, :].astype(F32) + d_other[swapped, :].astype(F32)
        scaled = back * gain[...]
        inner = jnp.mean(scaled * features, axis=-1, keepdims=True)
        result = (
            row_block(cots, block).astype(F32)
            + inverse * scaled
            - features * (inverse * inverse * inverse * inner)
        )
        d_all[rows, :] = result.astype(BF)
        if block < 2:
            d_middle[rows, :] = result
            gains += jnp.sum(back * features * inverse, axis=0, keepdims=True)
    d_gain[...] = jnp.broadcast_to(gains, d_gain.shape)
    d_context_near[...] = mm(d_all[...], weight_near[:, 0:width]).astype(BF)
    d_context_far[...] = mm(d_all[...], weight_far[:, 0:width]).astype(BF)
    grad_near[...] = mm_tn(d_all[...], context_near[...]).astype(BF)
    grad_far[...] = mm_tn(d_all[...], context_far[...]).astype(BF)


def middle_backward(heads, rows_in, parts, gain, cots, d_normed, contexts, weights):
    model = gain.shape[1]
    total = 4 * TILE
    width = heads * HD
    operands = [*rows_in, *parts, gain, *cots, *d_normed, *contexts, *weights]
    return pl.pallas_call(
        functools.partial(middle_kernel, heads, len(rows_in), len(cots)),
        in_specs=[VMEM] * len(operands),
        out_specs=[VMEM] * 6,
        out_shape=[
            jax.ShapeDtypeStruct((2 * TILE, model), F32),
            jax.ShapeDtypeStruct((total, width), BF),
            jax.ShapeDtypeStruct((total, width), BF),
            jax.ShapeDtypeStruct((model, width), BF),
            jax.ShapeDtypeStruct((model, width), BF),
            jax.ShapeDtypeStruct((8, model), F32),
        ],
        scratch_shapes=[
            pltpu.VMEM((total, model), BF),
        ],
        compiler_params=pltpu.CompilerParams(vmem_limit_bytes=MIDDLE_LIMIT),
        cost_estimate=COST,
        name="middle_backward",
    )(*operands)


def in_two(*rows):
    high = [row.astype(BF).astype(F32) for row in rows]
    index = lax.broadcasted_iota(jnp.int32, (16, rows[0].shape[1]), 0)
    result = jnp.zeros((16, rows[0].shape[1]), F32)
    for number, row in enumerate(rows):
        result = jnp.where(index == 2 * number, high[number], result)
        result = jnp.where(index == 2 * number + 1, row - high[number], result)
    return result.astype(BF)


def from_two(rows):
    return [
        rows[2 * k : 2 * k + 1].astype(F32) + rows[2 * k + 1 : 2 * k + 2].astype(F32)
        for k in range(2)
    ]


def finish_kernel(d_mine, d_other, keep, got, d_middle, gain, mine, theirs):
    for number, rows_in in enumerate((keep, got)):
        rows = slice(number * TILE, (number + 1) * TILE)
        features = rows_in[...].astype(F32)
        inverse = inverse_rms(features)
        scaled = (d_mine[rows, :].astype(F32) + d_other[rows, :].astype(F32)) * gain[...]
        inner = jnp.mean(scaled * features, axis=-1, keepdims=True)
        result = (
            d_middle[rows, :] + inverse * scaled - features * (inverse * inverse * inverse * inner)
        ).astype(BF)
        if number == 0:
            mine[...] = result
        else:
            theirs[...] = result


def backward_kernel(heads, orders, block_rows, last, meta, *refs):
    refs = list(refs)
    take = lambda count: [refs.pop(0) for _ in range(count)]
    inverse, context, expo, weight, proj, normed, d_context, grad_out = take(8)
    if last:
        gain, gain_rows = take(2)
    if last:
        (before,) = take(1)
        mine, other = take(2)
    else:
        (result,) = take(1)
    groups = take(len(orders))
    do_ext, v_ext, d_proj, grad = take(4)
    width = heads * HD
    total = 4 * TILE
    lanes = lax.broadcasted_iota(jnp.int32, (total, HD), 1)
    columns = inverse[...].T
    d_proj[:, 0:width] = jnp.zeros((total, width), BF)
    for head in range(heads):
        at = head * HD
        scaled = (d_context[:, at : at + HD].astype(F32) * columns[:, head : head + 1]).astype(BF)
        inner = -jnp.sum(
            scaled.astype(F32) * context[:, at : at + HD].astype(F32), axis=-1, keepdims=True
        )
        high = inner.astype(BF).astype(F32)
        do_ext[head, :, 0:HD] = scaled
        do_ext[head, :, HD : 2 * HD] = jnp.where(
            lanes == 0, high, jnp.where(lanes == 1, inner - high, 0.0)
        ).astype(BF)
    for head in range(heads):
        at = 3 * width + head * HD
        v_ext[head, :, 0:HD] = proj[:, at : at + HD]
        v_ext[head, :, HD : 2 * HD] = jnp.where(lanes < 2, 1.0, 0.0).astype(BF)
    for head in range(heads):
        q_at, k_at, v_at = (part * width + head * HD for part in (1, 2, 3))
        raised = expo[head]
        d_probs = mm_nt(v_ext[head], do_ext[head])
        d_scores = (raised.astype(F32) * d_probs).astype(BF)
        d_queries = mm(proj[:, k_at : k_at + HD].T, d_scores)
        d_keys = mm_nt(proj[:, q_at : q_at + HD].T, d_scores)
        d_values = mm_nt(do_ext[head, :, 0:HD].T, raised)
        d_proj[:, q_at : q_at + HD] = d_queries.astype(BF).T
        d_proj[:, k_at : k_at + HD] = d_keys.astype(BF).T
        d_proj[:, v_at : v_at + HD] = d_values.astype(BF).T
    grad[...] = mm_tn(normed[...], d_proj[...]).astype(BF)
    grad[:, 0:width] = grad_out[...]
    disperse(meta, grad, groups, orders, block_rows)
    through = mm_nt(d_proj[...], weight[...])
    if last:
        through = through + before[...].astype(F32)
        mine[...] = through[0 : 2 * TILE].astype(BF)
        other[...] = through[2 * TILE :].astype(BF)
        first = jnp.sum(through * normed[...].astype(F32), axis=0, keepdims=True) / gain[...]
        end = len(orders[-1]) * block_rows
        groups[-1][end : end + 16, :] = in_two(first, gain_rows[0:1, :])
    else:
        result[...] = through.astype(BF)


def attention_backward(
    meta, heads, block_rows, normed, saved, d_context, grad_out, orders, before=None
):
    last = before is not None
    weight, proj = saved[3:]
    model, width = weight.shape
    total = proj.shape[0]
    rows = jax.ShapeDtypeStruct((total, model), BF)
    in_fast = [*saved, normed, d_context, grad_out]
    scratch = [
        pltpu.VMEM((heads, total, 2 * HD), BF),
        pltpu.VMEM((heads, total, 2 * HD), BF),
        pltpu.VMEM((total, width), BF),
        pltpu.VMEM((model, width), BF),
    ]
    sizes = [len(order) * block_rows for order in orders]
    if last:
        in_fast += [*before[1:], before[0]]
        out_shape = [jax.ShapeDtypeStruct((2 * TILE, model), BF)] * 2
        sizes[-1] += 16
    else:
        out_shape = [rows]
    out_shape += [jax.ShapeDtypeStruct((size, width), BF) for size in sizes]
    return pl.pallas_call(
        functools.partial(backward_kernel, heads, orders, block_rows, last),
        in_specs=[SMEM] + [VMEM] * len(in_fast),
        out_specs=[VMEM] * len(out_shape),
        out_shape=out_shape,
        scratch_shapes=scratch,
        compiler_params=pltpu.CompilerParams(vmem_limit_bytes=BACK_LIMIT),
        cost_estimate=COST,
        name="attention_backward",
    )(meta, *in_fast)


def add(*terms):
    return sum(term.astype(F32) for term in terms)


def hold(values, *others):
    values, others = lax.optimization_barrier((values, others))
    return values, *others


def plus(*terms):
    return sum(term.astype(F32) for term in terms)


def call_local(kernel, out_shape, *operands):
    return pl.pallas_call(
        kernel,
        in_specs=[VMEM] * len(operands),
        out_specs=[VMEM] * len(out_shape),
        out_shape=[jax.ShapeDtypeStruct(shape, kind) for shape, kind in out_shape],
        compiler_params=pltpu.CompilerParams(vmem_limit_bytes=MIDDLE_LIMIT),
        cost_estimate=COST,
        name=kernel.__name__.replace("kernel", "backward"),
    )(*operands)


def join_kernel(own_high, x_high, y_high, y_low, xy_low, two, three, y_low_plus):
    rows = two.shape[0]
    for at, dest in ((slice(0, rows), two), (slice(rows, 2 * rows), three)):
        dest[...] = plus(own_high[at, :], x_high[at, :], y_high[at, :]).astype(BF)
    y_low_plus[...] = plus(y_low[...], xy_low[...]).astype(BF)


def meet_kernel(
    x_low, x_high, both_low, y_high, xy_high, own_low, feed_x, feed_y,
    message, y_high_plus, feed_own, feed_one,
):
    half = x_low.shape[0]
    rows = feed_own.shape[0]
    message[0:half, :] = plus(x_low[...], both_low[half:, :]).astype(BF)
    message[half:, :] = x_high[...]
    y_high_plus[...] = plus(y_high[...], xy_high[...]).astype(BF)
    feed_own[...] = plus(own_low[0:rows, :], feed_x[0:rows, :], feed_y[0:rows, :])
    feed_one[...] = plus(own_low[rows:, :], feed_x[rows:, :], feed_y[rows:, :]).astype(BF)


def fold_kernel(own_low, own_high, x_high, over_x, both_low, y_high, total, gains, *messages):
    rows = total.shape[0]
    end = 4 * rows
    mine = from_two(x_high[2 * rows : 2 * rows + 16, :])
    theirs = from_two(over_x[end : end + 16, :])
    pairs = in_two(*(a + b for a, b in zip(mine, theirs)))
    gains[...] = pairs.astype(F32)
    for index in range(4):
        at = slice((index % 2) * rows, (index % 2 + 1) * rows)
        block = plus(
            (own_low if index < 2 else own_high)[at, :],
            over_x[index * rows : (index + 1) * rows, :],
            (both_low if index < 2 else y_high)[at, :],
        )
        if index == 0:
            total[...] = block
        else:
            messages[index - 1][0:rows, :] = block.astype(BF)
            messages[index - 1][rows:, :] = pairs


class Links:
    def __init__(self, wide, narrow):
        self.wide, self.narrow = wide, narrow
        self.planes = wide // 2
        self.staged = wide == 8

    def y(self, values):
        return lax.ppermute(values, "narrow", [(i, (i + 2) % 4) for i in range(4)])

    def core(self, values):
        return lax.ppermute(values, "narrow", [(i, i ^ 1) for i in range(4)])

    def across(self, values):
        return lax.ppermute(values, "narrow", [(i, (i + 2) % 4 ^ 1) for i in range(4)])

    def x(self, values):
        return lax.ppermute(values, "wide", [(i, i ^ 1) for i in range(self.wide)])

    def z(self, values, ahead):
        turn = lambda i: ((i // 2 + ahead) % self.planes) * 2 + i % 2
        return lax.ppermute(values, "wide", [(i, turn(i)) for i in range(self.wide)])

    def whole_gather(self, piece):
        near = lax.all_gather(piece, "wide", axis=0, tiled=True)
        return [near], [self.y(near)]

    def whole_reduce(self, near, far):
        return lax.psum_scatter(near, "wide", scatter_dimension=0, tiled=True).astype(
            F32
        ) + lax.psum_scatter(self.y(far), "wide", scatter_dimension=0, tiled=True).astype(F32)


def on_device(
    tokens,
    lengths,
    norm_one,
    w_query,
    w_key,
    w_value,
    w_out,
    norm_two,
    w_gate,
    w_up,
    w_down,
    cotangent,
):
    model = tokens.shape[-1]
    wide, narrow = lax.axis_size("wide"), lax.axis_size("narrow")
    links = Links(wide, narrow)
    heads = w_query.shape[1] // HD
    head_width = heads * HD
    units = w_gate.shape[1]
    at_wide, at_narrow = lax.axis_index("wide"), lax.axis_index("narrow")
    y, c = at_narrow >> 1, at_narrow & 1
    x, z = at_wide & 1, at_wide >> 1

    staged = links.staged
    planes = links.planes
    rows = model // wide
    turned = [((z + k) & (planes - 1)) * 2 + (x ^ side) for side in range(2) for k in range(4)]
    blocks = [((y ^ far) * 2 + (c ^ side)) * TILE for side in range(2) for far in range(2)]
    length = lax.dynamic_index_in_dim(lengths, y, 0, keepdims=False)[0]
    numbers = [
        *(spot * rows for spot in turned),
        *blocks,
        length,
    ]
    meta = jnp.stack([jnp.asarray(number, jnp.int32) for number in numbers])
    first_item = y == 0

    gain_one = norm_one.reshape(1, model)
    gain_two = norm_two.reshape(1, model)

    def keep_give(rows):
        flat = rows.reshape(2, TILE, model)
        return (
            lax.dynamic_index_in_dim(flat, y, 0, keepdims=False),
            lax.dynamic_index_in_dim(flat, 1 - y, 0, keepdims=False),
        )

    attn_piece = jnp.concatenate([w_out.T, w_query, w_key, w_value], axis=1)
    feed_piece = jnp.concatenate([w_gate, w_up, w_down.T], axis=1)
    keep, give = keep_give(tokens)
    keep_cot, give_cot = keep_give(cotangent)
    half = planes // 2 * rows
    if staged:
        block_rows = rows
        quarters = ((0, 1), (2, 3), (4, 5), (6, 7))
        attn_near_in = attn_far_in = ((0, 1, 2, 3), (4, 5, 6, 7))
        feed_near_in = ((0,), (1,), (3,), (2,), (4, 5, 7), (6,))
        feed_far_in = ((0, 1, 3), (2,), (4, 5), (7, 6))
        attn_far_out = ((0, 1, 4, 5), (2, 3), (6, 7))
    else:
        block_rows = model
        quarters = attn_far_out = ((0,),)
        attn_near_in = attn_far_in = feed_near_in = feed_far_in = ((0,),)

    got = links.y(give)
    if staged:
        column = [attn_piece] + [links.z(attn_piece, planes - k) for k in range(1, planes)]
        column = jnp.concatenate(column, axis=0)
        over_x, over_y = links.x(column), links.y(column)
        feed_piece, column, meta, first_item = hold(feed_piece, column, meta, first_item)
        feed_one = links.z(feed_piece, planes - 1)
        feed_three = links.z(feed_piece, planes - 3)
    else:
        attn_near, attn_far = links.whole_gather(attn_piece)
        feed_near, feed_far = links.whole_gather(feed_piece)
    rows_in = [keep, got, links.core(keep), links.core(got)]
    if staged:
        over_y, rows_in, over_x = hold(over_y, rows_in, over_x)
        give_cot, over_y = hold(give_cot, over_y)
        attn_near = [column, over_x]
        attn_far = [over_y, links.x(over_y)]
    got_cot = links.y(give_cot)

    inv_near, context_near, expo_near, *kept_near, normed = attention_forward(
        meta, heads, block_rows, attn_near, attn_near_in, rows_in=rows_in, gain=gain_one
    )
    if staged:
        normed, got_cot, attn_far, feed_one, feed_three = hold(
            normed, got_cot, attn_far, feed_one, feed_three
        )
        feed_piece, feed_one = hold(feed_piece, feed_one)
        feed_two = links.z(feed_piece, planes - 2)
        three = jnp.concatenate([feed_piece, feed_one, feed_three], axis=0)
        feed_y = links.y(three)
        feed_x = links.x(three)
    own_cot = jnp.concatenate([keep_cot, got_cot], axis=0)
    cots = [own_cot, links.core(own_cot)]
    inv_far, context_far, expo_far, *kept_far, part_mine = attention_forward(
        meta, heads, block_rows, attn_far, attn_far_in,
        before=(normed, context_near, kept_near[0]),
    )
    if staged:
        part_mine, feed_two, feed_x, feed_y = hold(part_mine, feed_two, feed_x, feed_y)
        feed_x_two = links.x(feed_two)
        feed_y_two = links.y(feed_two)
    part_other = links.core(part_mine)
    if staged:
        part_other, feed_x_two, feed_y_two = hold(part_other, feed_x_two, feed_y_two)
        feed_near = [feed_piece, feed_one, feed_three, feed_two, feed_x, feed_x_two]
        feed_far = [
            feed_y,
            feed_y_two,
            links.y(feed_x[: 2 * rows]),
            links.x(jnp.concatenate([feed_y[2 * rows :], feed_y_two], axis=0)),
        ]
    parts = (part_mine, part_other)

    normed_two, down_near, back_near, *near = feed_forward(
        meta, block_rows, cots, feed_near, feed_near_in, quarters, rows_in=rows_in,
        before=(*parts, gain_two),
    )
    if staged:
        own_low, own_high, x_low, x_high = near
        from_x_high = links.x(x_high)
    mlp_mine, mlp_other, d_mine, *far = feed_forward(
        meta, block_rows, cots, feed_far, feed_far_in, quarters,
        before=(normed_two, down_near, back_near),
    )
    if staged:
        mlp_other, from_x_high = hold(mlp_other, from_x_high)
        y_low, y_high, xy_low, xy_high = far
        from_xy_high = links.x(xy_high)
    else:
        feed_grad = links.whole_reduce(*near, *far)
    d_other = links.core(d_mine)
    half_rows = 2 * TILE
    output = (
        jnp.concatenate(rows_in[:2], axis=0).astype(F32)
        + part_mine[:half_rows].astype(F32)
        + part_other[half_rows:].astype(F32)
        + mlp_mine.astype(F32)
        + links.core(mlp_other).astype(F32)
    ).astype(BF)
    output_back = links.y(output[TILE:])
    d_middle, d_context_near, d_context_far, out_near, out_far, gain_rows = middle_backward(
        heads,
        rows_in,
        parts,
        gain_two,
        cots,
        (d_mine, d_other),
        (context_near, context_far),
        (kept_near[0], kept_far[0]),
    )
    if staged:
        d_context_far, from_xy_high, output_back = hold(d_context_far, from_xy_high, output_back)
        xy_low, from_xy_high = hold(xy_low, from_xy_high)
        from_y_high = links.y(add(y_high, from_xy_high).astype(BF))
        from_xy_low = links.x(xy_low)
    d_first, *far = attention_backward(
        meta, heads, block_rows, normed, (inv_far, context_far, expo_far, *kept_far),
        d_context_far, out_far, attn_far_out,
    )
    if staged:
        d_first, from_y_high, from_xy_low = hold(d_first, from_y_high, from_xy_low)
        x_low, from_xy_low = hold(x_low, from_xy_low)
        feed = (rows, feed_piece.shape[1])
        feed_half = (half, feed_piece.shape[1])
        feed_two, feed_three, feed_y_low = call_local(
            join_kernel, [(feed, BF), (feed, BF), (feed_half, BF)],
            own_high, from_x_high, from_y_high, y_low, from_xy_low,
        )
        feed_two = links.z(feed_two, 2)
        feed_low = own_low
        both_low, y_high, xy_high = far
        from_both_low = links.y(both_low)
        from_xy_high = links.x(xy_high)
        from_feed_x, from_feed_y = links.x(x_low), links.y(feed_y_low)
    last_mine, last_other, *near = attention_backward(
        meta, heads, block_rows, normed, (inv_near, context_near, expo_near, *kept_near),
        d_context_near, out_near, quarters, before=(d_first, gain_one, gain_rows),
    )
    if staged:
        last_other, near, from_both_low, from_xy_high, from_feed_x, from_feed_y, feed_two = hold(
            last_other, near, from_both_low, from_xy_high, from_feed_x, from_feed_y, feed_two
        )
        own_low, own_high, x_low, x_high = near
        width = x_low.shape[1]
        message, y_high, feed_own, feed_one = call_local(
            meet_kernel,
            [((2 * half + 16, width), BF), ((half, width), BF), (feed, F32), (feed, BF)],
            x_low, x_high, from_both_low, y_high, from_xy_high, feed_low, from_feed_x, from_feed_y,
        )
        from_x, from_y_high = links.x(message), links.y(y_high)
        feed_parts = [feed_two, links.z(feed_three, 3), links.z(feed_one, 1)]
    else:
        attn_grad = links.whole_reduce(near[0][:model], *far)
        gains = near[0][model:]
    mine, theirs = call_local(
        finish_kernel,
        [((TILE, model), BF)] * 2,
        last_mine, links.core(last_other), *rows_in[:2], d_middle, gain_one,
    )
    if staged:
        from_x, theirs = hold(from_x, theirs)
    back = links.y(theirs)
    if staged:
        attn = (rows, width)
        apart = ((rows + 16, width), BF)
        attn_grad, gains, *messages = call_local(
            fold_kernel, [(attn, F32), ((16, width), F32), apart, apart, apart],
            own_low, own_high, x_high, from_x, from_both_low, from_y_high,
        )
        arrived = [links.z(piece, k + 1) for k, piece in enumerate(messages)]
        attn_grad = add(attn_grad, *(part[:rows] for part in arrived))
        gains = add(gains, *(part[rows:] for part in arrived))
        feed_grad = add(feed_own, *feed_parts)
    else:
        gains = lax.psum(gains.astype(F32), "wide")
    gains = (gains + links.core(gains)) + (links.y(gains) + links.across(gains))

    def in_order(own, other):
        stacked = jnp.where(first_item, jnp.stack([own, other]), jnp.stack([other, own]))
        return stacked.reshape(tokens.shape)

    return (
        in_order(output[:TILE], output_back),
        in_order(mine, back),
        gains[0] + gains[1],
        attn_grad[:, head_width : 2 * head_width],
        attn_grad[:, 2 * head_width : 3 * head_width],
        attn_grad[:, 3 * head_width :],
        attn_grad[:, :head_width].T,
        gains[2] + gains[3],
        feed_grad[:, :units],
        feed_grad[:, units : 2 * units],
        feed_grad[:, 2 * units :].T,
    )


def solution(mesh):
    in_specs = (
        P(None, "wide", "narrow", None),
        P(None, "wide"),
        P(),
        P("wide", "narrow"),
        P("wide", "narrow"),
        P("wide", "narrow"),
        P("narrow", "wide"),
        P(),
        P("wide", "narrow"),
        P("wide", "narrow"),
        P("narrow", "wide"),
        P(None, "wide", "narrow", None),
    )
    out_specs = (
        P(None, "wide", "narrow", None),
        P(None, "wide", "narrow", None),
        P(),
        P("wide", "narrow"),
        P("wide", "narrow"),
        P("wide", "narrow"),
        P("narrow", "wide"),
        P(),
        P("wide", "narrow"),
        P("wide", "narrow"),
        P("narrow", "wide"),
    )
    return jax.shard_map(
        on_device, mesh=mesh, in_specs=in_specs, out_specs=out_specs, check_vma=False
    )
```

```python
import functools

import jax
import jax.numpy as jnp
from jax import lax
from jax.experimental import pallas as pl
from jax.experimental.pallas import tpu as pltpu
from jax.sharding import PartitionSpec as P

HD = 64
EPSILON = 1e-06
MASKED = -1e30
TILE = 256
FEED_ROWS = 1024
QUERY_ROWS = 1024
MIDDLE_LIMIT = 8 * 1024 * 1024
BACK_LIMIT = 14 * 1024 * 1024
ATTEND_LIMIT = 11 * 1024 * 1024
FEED_LIMIT = 22 * 1024 * 1024
COST = pl.CostEstimate(flops=10**6, bytes_accessed=10**5, transcendentals=0)
BF = jnp.bfloat16
F32 = jnp.float32


def mm(left, right):
    return jnp.dot(left, right, preferred_element_type=F32)


def mm_nt(left, right):
    return lax.dot_general(left, right, (((1,), (1,)), ((), ())), preferred_element_type=F32)


def mm_tn(left, right):
    return lax.dot_general(left, right, (((0,), (0,)), ((), ())), preferred_element_type=F32)


def inverse_rms(features):
    return lax.rsqrt(jnp.mean(features * features, axis=-1, keepdims=True) + EPSILON)


def place(meta, pieces, orders, dest, rows, sems):
    copies = []
    for piece, order in zip(pieces, orders):
        for number, index in enumerate(order):
            at = 0 if rows == dest.shape[0] else pl.multiple_of(meta[index], 16)
            copy = pltpu.make_async_copy(
                piece.at[pl.ds(number * rows, rows), :],
                dest.at[pl.ds(at, rows), :],
                sems.at[len(copies)],
            )
            copy.start()
            copies.append(copy)
    return copies


def wait_all(copies):
    for copy in copies:
        copy.wait()


def blocks_of(orders):
    return sum(len(order) for order in orders)


def disperse(meta, source, groups, orders, rows):
    for group, order in zip(groups, orders):
        for place, index in enumerate(order):
            at = 0 if rows == source.shape[0] else pl.multiple_of(meta[index], 16)
            group[place * rows : (place + 1) * rows, :] = source[pl.ds(at, rows), :]


def row_block(refs, block):
    start = block * TILE
    for ref in refs:
        if start < ref.shape[0]:
            return ref[start : start + TILE, :]
        start -= ref.shape[0]


def forward_kernel(heads, n_rows, orders, block_rows, meta, *refs):
    first = n_rows > 0
    refs = list(refs)
    take = lambda count: [refs.pop(0) for _ in range(count)]
    width = heads * HD
    total = 4 * TILE
    if first:
        (gain,) = take(1)
        sources = take(n_rows)
    else:
        normed, context_first, weight_first = take(3)
    pieces = take(len(orders))
    inverse, context, expo, weight, proj = take(5)
    if first:
        (normed,) = take(1)
    else:
        (partial,) = take(1)
    q_ext, k_ext, v_flip, sems, sems_more = take(5)
    copies = place(meta, pieces, orders, weight, block_rows, sems)
    outs = []

    def carry(source, dest):
        copy = pltpu.make_async_copy(source, dest, sems_more.at[len(outs)])
        copy.start()
        outs.append(copy)

    if first:
        (extra,) = take(1)
        starts = [sum(ref.shape[0] for ref in sources[:k]) for k in range(n_rows)]
        for start, source in zip(starts, sources):
            carry(source, extra.at[pl.ds(start, source.shape[0]), :])
        wait_all(outs)
        for block in range(4):
            rows = slice(block * TILE, (block + 1) * TILE)
            features = extra[rows, :].astype(F32)
            normed[rows, :] = (features * inverse_rms(features) * gain[...]).astype(BF)
    wait_all(copies)
    proj[...] = mm(normed[...], weight[...]).astype(BF)
    lanes = lax.broadcasted_iota(jnp.int32, (TILE, HD), 1)
    index = lax.broadcasted_iota(jnp.int32, (TILE, HD), 0)
    ones = jnp.where(lanes == 0, 1.0, 0.0).astype(BF)
    below = jnp.where(lax.broadcasted_iota(jnp.int32, (16, total), 0) == 0, 1.0, 0.0).astype(BF)
    for block in range(4):
        rows = slice(block * TILE, (block + 1) * TILE)
        usable = meta[8 + block] + index < meta[12]
        bias = jnp.where((lanes == 0) & ~usable, MASKED, 0.0).astype(BF)
        for head in range(heads):
            at = width + head * HD
            q_ext[head, rows, 0:HD] = proj[rows, at : at + HD]
            q_ext[head, rows, HD : 2 * HD] = ones
            at = 2 * width + head * HD
            k_ext[head, rows, 0:HD] = proj[rows, at : at + HD]
            k_ext[head, rows, HD : 2 * HD] = bias
    for head in range(heads):
        at = 3 * width + head * HD
        v_flip[head, 0:HD, :] = proj[:, at : at + HD].T
        v_flip[head, HD : HD + 16, :] = below
    inverse[...] = jnp.ones_like(inverse)
    for head in range(heads):
        for start in range(0, total, QUERY_ROWS):
            rows = slice(start, start + QUERY_ROWS)
            scores = mm_nt(k_ext[head], q_ext[head, rows, :])
            top = jnp.max(scores, axis=0, keepdims=True)
            raised = jnp.exp(scores - top).astype(BF)
            expo[head, :, rows] = raised
            mixed = mm(v_flip[head], raised)
            inv = 1.0 / mixed[HD : HD + 1, :]
            inverse[head : head + 1, rows] = inv
            context[rows, head * HD : (head + 1) * HD] = (mixed[0:HD, :] * inv).astype(BF).T
    if not first:
        partial[...] = (
            mm_nt(context_first[...], weight_first[:, 0:width])
            + mm_nt(context[...], weight[:, 0:width])
        ).astype(BF)


SMEM = pl.BlockSpec(memory_space=pltpu.SMEM)
VMEM = pl.BlockSpec(memory_space=pltpu.VMEM)
HBM = pl.BlockSpec(memory_space=pltpu.HBM)


def attention_forward(meta, heads, block_rows, pieces, orders, rows_in=(), gain=None, before=None):
    width = pieces[0].shape[1]
    model = rows_in[0].shape[1] if rows_in else before[0].shape[1]
    total = 4 * TILE
    rows = jax.ShapeDtypeStruct((total, model), BF)
    numerators = jax.ShapeDtypeStruct((heads, total, total), BF)
    if rows_in:
        in_fast, in_slow = [gain], [*rows_in, *pieces]
        more, extra = [rows], [pltpu.VMEM((total, model), BF)]
    else:
        in_fast, in_slow = [*before], [*pieces]
        more, extra = [rows], []
    return pl.pallas_call(
        functools.partial(forward_kernel, heads, len(rows_in), orders, block_rows),
        in_specs=[SMEM] + [VMEM] * len(in_fast) + [HBM] * len(in_slow),
        out_specs=[VMEM] * 6,
        out_shape=[
            jax.ShapeDtypeStruct((8, total), F32),
            jax.ShapeDtypeStruct((total, heads * HD), BF),
            numerators,
            jax.ShapeDtypeStruct((model, width), BF),
            jax.ShapeDtypeStruct((total, width), BF),
            *more,
        ],
        scratch_shapes=[
            pltpu.VMEM((heads, total, 2 * HD), BF),
            pltpu.VMEM((heads, total, 2 * HD), BF),
            pltpu.VMEM((heads, HD + 16, total), BF),
            pltpu.SemaphoreType.DMA((blocks_of(orders),)),
            pltpu.SemaphoreType.DMA((4,)),
            *extra,
        ],
        compiler_params=pltpu.CompilerParams(vmem_limit_bytes=ATTEND_LIMIT),
        cost_estimate=COST,
        name="attention_forward",
    )(meta, *in_fast, *in_slow)


def gelu_terms(gate):
    scale = 0.7978845608028654
    cube = 0.044715
    square = gate * gate
    bent = jnp.tanh(scale * gate * (1.0 + cube * square))
    half = 0.5 * (1.0 + bent)
    slope = half + 0.5 * gate * (1.0 - bent * bent) * (scale * (1.0 + 3.0 * cube * square))
    return gate * half, slope


def feed_kernel(n_rows, n_cots, in_orders, orders, block_rows, meta, *refs):
    first = n_rows > 0
    refs = list(refs)
    take = lambda count: [refs.pop(0) for _ in range(count)]
    if first:
        rows_in = take(n_rows)
        part_mine, part_other, gain = take(3)
    else:
        normed, result_before, back_before = take(3)
    cots = take(n_cots)
    pieces = take(len(in_orders))
    if first:
        normed, result, back = take(3)
    else:
        mine, other, back = take(3)
    groups = take(len(orders))
    weight, hidden, d_gate, d_up, cot, grad, sems = take(7)
    units = weight.shape[1] // 3
    copies = place(meta, pieces, in_orders, weight, block_rows, sems)
    for block in range(4):
        rows = slice(block * TILE, (block + 1) * TILE)
        cot[rows, :] = row_block(cots, block)
        if first:
            swapped = slice(((block + 2) % 4) * TILE, ((block + 2) % 4 + 1) * TILE)
            features = (
                row_block(rows_in, block).astype(F32)
                + part_mine[rows, :].astype(F32)
                + part_other[swapped, :].astype(F32)
            )
            features = features.astype(BF).astype(F32)
            normed[rows, :] = (features * inverse_rms(features) * gain[...]).astype(BF)
    wait_all(copies)
    for start in range(0, 4 * TILE, FEED_ROWS):
        rows = slice(start, start + FEED_ROWS)
        pre = mm(normed[rows, :], weight[:, 0 : 2 * units])
        act, slope = gelu_terms(pre[:, :units])
        up = pre[:, units:]
        low = (act * up).astype(BF)
        hidden[rows, :] = low
        d_hidden = mm(cot[rows, :], weight[:, 2 * units :])
        gate_low = (d_hidden * up * slope).astype(BF)
        up_low = (d_hidden * act).astype(BF)
        d_gate[rows, :] = gate_low
        d_up[rows, :] = up_low
        down = mm_nt(low, weight[:, 2 * units :])
        through = mm_nt(gate_low, weight[:, 0:units]) + mm_nt(up_low, weight[:, units : 2 * units])
        if first:
            result[rows, :] = down.astype(BF)
            back[rows, :] = through.astype(BF)
        else:
            down = (down + result_before[rows, :].astype(F32)).astype(BF)
            if start < 2 * TILE:
                mine[rows, :] = down[: 2 * TILE - start]
            if start + FEED_ROWS > 2 * TILE:
                begin = max(start - 2 * TILE, 0)
                other[begin : start + FEED_ROWS - 2 * TILE, :] = down[begin + 2 * TILE - start :]
            back[rows, :] = (through + back_before[rows, :].astype(F32)).astype(BF)
    grad[:, 2 * units :] = mm_tn(cot[...], hidden[...]).astype(BF)
    grad[:, 0:units] = mm_tn(normed[...], d_gate[...]).astype(BF)
    grad[:, units : 2 * units] = mm_tn(normed[...], d_up[...]).astype(BF)
    disperse(meta, grad, groups, orders, block_rows)


def feed_forward(meta, block_rows, cots, pieces, in_orders, orders, rows_in=(), before=()):
    width = pieces[0].shape[1]
    model = cots[0].shape[1]
    total = 4 * TILE
    units = width // 3
    full = jax.ShapeDtypeStruct((total, model), BF)
    half = jax.ShapeDtypeStruct((2 * TILE, model), BF)
    operands = [*rows_in, *before, *cots, *pieces]
    out_shape = [full, full, full] if rows_in else [half, half, full]
    out_shape += [
        jax.ShapeDtypeStruct((len(order) * block_rows, width), BF) for order in orders
    ]
    return pl.pallas_call(
        functools.partial(
            feed_kernel, len(rows_in), len(cots), in_orders, orders, block_rows
        ),
        in_specs=[SMEM] + [VMEM] * (len(operands) - len(pieces)) + [HBM] * len(pieces),
        out_specs=[VMEM] * len(out_shape),
        out_shape=out_shape,
        scratch_shapes=[
            pltpu.VMEM((model, width), BF),
            pltpu.VMEM((total, units), BF),
            pltpu.VMEM((total, units), BF),
            pltpu.VMEM((total, units), BF),
            pltpu.VMEM((total, model), BF),
            pltpu.VMEM((model, width), BF),
            pltpu.SemaphoreType.DMA((blocks_of(in_orders),)),
        ],
        compiler_params=pltpu.CompilerParams(vmem_limit_bytes=FEED_LIMIT),
        cost_estimate=COST,
        name="feed_forward",
    )(meta, *operands)


def middle_kernel(heads, n_rows, n_cots, *refs):
    refs = list(refs)
    take = lambda count: [refs.pop(0) for _ in range(count)]
    rows_in = take(n_rows)
    part_mine, part_other, gain = take(3)
    cots = take(n_cots)
    d_mine, d_other, context_near, context_far = take(4)
    weight_near, weight_far = take(2)
    d_middle, d_context_near, d_context_far, grad_near, grad_far, d_gain = take(6)
    (d_all,) = take(1)
    width = heads * HD
    gains = 0.0
    for block in range(4):
        rows = slice(block * TILE, (block + 1) * TILE)
        swapped = slice(((block + 2) % 4) * TILE, ((block + 2) % 4 + 1) * TILE)
        features = (
            row_block(rows_in, block).astype(F32)
            + part_mine[rows, :].astype(F32)
            + part_other[swapped, :].astype(F32)
        )
        features = features.astype(BF).astype(F32)
        inverse = inverse_rms(features)
        back = d_mine[rows, :].astype(F32) + d_other[swapped, :].astype(F32)
        scaled = back * gain[...]
        inner = jnp.mean(scaled * features, axis=-1, keepdims=True)
        result = (
            row_block(cots, block).astype(F32)
            + inverse * scaled
            - features * (inverse * inverse * inverse * inner)
        )
        d_all[rows, :] = result.astype(BF)
        if block < 2:
            d_middle[rows, :] = result
            gains += jnp.sum(back * features * inverse, axis=0, keepdims=True)
    d_gain[...] = jnp.broadcast_to(gains, d_gain.shape)
    d_context_near[...] = mm(d_all[...], weight_near[:, 0:width]).astype(BF)
    d_context_far[...] = mm(d_all[...], weight_far[:, 0:width]).astype(BF)
    grad_near[...] = mm_tn(d_all[...], context_near[...]).astype(BF)
    grad_far[...] = mm_tn(d_all[...], context_far[...]).astype(BF)


def middle_backward(heads, rows_in, parts, gain, cots, d_normed, contexts, weights):
    model = gain.shape[1]
    total = 4 * TILE
    width = heads * HD
    operands = [*rows_in, *parts, gain, *cots, *d_normed, *contexts, *weights]
    return pl.pallas_call(
        functools.partial(middle_kernel, heads, len(rows_in), len(cots)),
        in_specs=[VMEM] * len(operands),
        out_specs=[VMEM] * 6,
        out_shape=[
            jax.ShapeDtypeStruct((2 * TILE, model), F32),
            jax.ShapeDtypeStruct((total, width), BF),
            jax.ShapeDtypeStruct((total, width), BF),
            jax.ShapeDtypeStruct((model, width), BF),
            jax.ShapeDtypeStruct((model, width), BF),
            jax.ShapeDtypeStruct((8, model), F32),
        ],
        scratch_shapes=[
            pltpu.VMEM((total, model), BF),
        ],
        compiler_params=pltpu.CompilerParams(vmem_limit_bytes=MIDDLE_LIMIT),
        cost_estimate=COST,
        name="middle_backward",
    )(*operands)


def in_two(*rows):
    high = [row.astype(BF).astype(F32) for row in rows]
    index = lax.broadcasted_iota(jnp.int32, (16, rows[0].shape[1]), 0)
    result = jnp.zeros((16, rows[0].shape[1]), F32)
    for number, row in enumerate(rows):
        result = jnp.where(index == 2 * number, high[number], result)
        result = jnp.where(index == 2 * number + 1, row - high[number], result)
    return result.astype(BF)


def from_two(rows):
    return [
        rows[2 * k : 2 * k + 1].astype(F32) + rows[2 * k + 1 : 2 * k + 2].astype(F32)
        for k in range(2)
    ]


def finish_kernel(d_mine, d_other, keep, got, d_middle, gain, mine, theirs):
    for number, rows_in in enumerate((keep, got)):
        rows = slice(number * TILE, (number + 1) * TILE)
        features = rows_in[...].astype(F32)
        inverse = inverse_rms(features)
        scaled = (d_mine[rows, :].astype(F32) + d_other[rows, :].astype(F32)) * gain[...]
        inner = jnp.mean(scaled * features, axis=-1, keepdims=True)
        result = (
            d_middle[rows, :] + inverse * scaled - features * (inverse * inverse * inverse * inner)
        ).astype(BF)
        if number == 0:
            mine[...] = result
        else:
            theirs[...] = result


def backward_kernel(heads, orders, block_rows, last, meta, *refs):
    refs = list(refs)
    take = lambda count: [refs.pop(0) for _ in range(count)]
    inverse, context, expo, weight, proj, normed, d_context, grad_out = take(8)
    if last:
        gain, gain_rows = take(2)
    if last:
        (before,) = take(1)
        mine, other = take(2)
    else:
        (result,) = take(1)
    groups = take(len(orders))
    do_ext, v_ext, d_proj, grad = take(4)
    width = heads * HD
    total = 4 * TILE
    lanes = lax.broadcasted_iota(jnp.int32, (total, HD), 1)
    columns = inverse[...].T
    d_proj[:, 0:width] = jnp.zeros((total, width), BF)
    for head in range(heads):
        at = head * HD
        scaled = (d_context[:, at : at + HD].astype(F32) * columns[:, head : head + 1]).astype(BF)
        inner = -jnp.sum(
            scaled.astype(F32) * context[:, at : at + HD].astype(F32), axis=-1, keepdims=True
        )
        high = inner.astype(BF).astype(F32)
        do_ext[head, :, 0:HD] = scaled
        do_ext[head, :, HD : 2 * HD] = jnp.where(
            lanes == 0, high, jnp.where(lanes == 1, inner - high, 0.0)
        ).astype(BF)
    for head in range(heads):
        at = 3 * width + head * HD
        v_ext[head, :, 0:HD] = proj[:, at : at + HD]
        v_ext[head, :, HD : 2 * HD] = jnp.where(lanes < 2, 1.0, 0.0).astype(BF)
    for head in range(heads):
        q_at, k_at, v_at = (part * width + head * HD for part in (1, 2, 3))
        raised = expo[head]
        d_probs = mm_nt(v_ext[head], do_ext[head])
        d_scores = (raised.astype(F32) * d_probs).astype(BF)
        d_queries = mm(proj[:, k_at : k_at + HD].T, d_scores)
        d_keys = mm_nt(proj[:, q_at : q_at + HD].T, d_scores)
        d_values = mm_nt(do_ext[head, :, 0:HD].T, raised)
        d_proj[:, q_at : q_at + HD] = d_queries.astype(BF).T
        d_proj[:, k_at : k_at + HD] = d_keys.astype(BF).T
        d_proj[:, v_at : v_at + HD] = d_values.astype(BF).T
    grad[...] = mm_tn(normed[...], d_proj[...]).astype(BF)
    grad[:, 0:width] = grad_out[...]
    disperse(meta, grad, groups, orders, block_rows)
    through = mm_nt(d_proj[...], weight[...])
    if last:
        through = through + before[...].astype(F32)
        mine[...] = through[0 : 2 * TILE].astype(BF)
        other[...] = through[2 * TILE :].astype(BF)
        first = jnp.sum(through * normed[...].astype(F32), axis=0, keepdims=True) / gain[...]
        end = len(orders[-1]) * block_rows
        groups[-1][end : end + 16, :] = in_two(first, gain_rows[0:1, :])
    else:
        result[...] = through.astype(BF)


def attention_backward(
    meta, heads, block_rows, normed, saved, d_context, grad_out, orders, before=None
):
    last = before is not None
    weight, proj = saved[3:]
    model, width = weight.shape
    total = proj.shape[0]
    rows = jax.ShapeDtypeStruct((total, model), BF)
    in_fast = [*saved, normed, d_context, grad_out]
    scratch = [
        pltpu.VMEM((heads, total, 2 * HD), BF),
        pltpu.VMEM((heads, total, 2 * HD), BF),
        pltpu.VMEM((total, width), BF),
        pltpu.VMEM((model, width), BF),
    ]
    sizes = [len(order) * block_rows for order in orders]
    if last:
        in_fast += [*before[1:], before[0]]
        out_shape = [jax.ShapeDtypeStruct((2 * TILE, model), BF)] * 2
        sizes[-1] += 16
    else:
        out_shape = [rows]
    out_shape += [jax.ShapeDtypeStruct((size, width), BF) for size in sizes]
    return pl.pallas_call(
        functools.partial(backward_kernel, heads, orders, block_rows, last),
        in_specs=[SMEM] + [VMEM] * len(in_fast),
        out_specs=[VMEM] * len(out_shape),
        out_shape=out_shape,
        scratch_shapes=scratch,
        compiler_params=pltpu.CompilerParams(vmem_limit_bytes=BACK_LIMIT),
        cost_estimate=COST,
        name="attention_backward",
    )(meta, *in_fast)


def add(*terms):
    return sum(term.astype(F32) for term in terms)


def hold(values, *others):
    values, others = lax.optimization_barrier((values, others))
    return values, *others


def plus(*terms):
    return sum(term.astype(F32) for term in terms)


def call_local(kernel, out_shape, *operands):
    return pl.pallas_call(
        kernel,
        in_specs=[VMEM] * len(operands),
        out_specs=[VMEM] * len(out_shape),
        out_shape=[jax.ShapeDtypeStruct(shape, kind) for shape, kind in out_shape],
        compiler_params=pltpu.CompilerParams(vmem_limit_bytes=MIDDLE_LIMIT),
        cost_estimate=COST,
        name=kernel.__name__.replace("kernel", "backward"),
    )(*operands)


def join_kernel(own_high, y_high, y_low, xy_low, two, three, y_low_plus):
    rows = two.shape[0]
    for at, dest in ((slice(0, rows), two), (slice(rows, 2 * rows), three)):
        dest[...] = plus(own_high[at, :], y_high[at, :]).astype(BF)
    y_low_plus[...] = plus(y_low[...], xy_low[...]).astype(BF)


def meet_kernel(
    x_low, x_high, both_low, y_high, xy_high, own_low, feed_y, over, one_in, two_in, three_in,
    message, y_high_plus, feed_own, feed_one, feed_over,
):
    half = x_low.shape[0]
    rows = feed_own.shape[0]
    message[0:half, :] = plus(x_low[...], both_low[half:, :]).astype(BF)
    message[half:, :] = x_high[...]
    y_high_plus[...] = plus(y_high[...], xy_high[...]).astype(BF)
    feed_over[...] = plus(over[...], one_in[...], two_in[...], three_in[...]).astype(BF)
    feed_own[...] = plus(own_low[0:rows, :], feed_y[0:rows, :])
    feed_one[...] = plus(own_low[rows:, :], feed_y[rows:, :]).astype(BF)


def fold_kernel(own_low, own_high, x_high, over_x, both_low, y_high, total, gains, *messages):
    rows = total.shape[0]
    end = 4 * rows
    mine = from_two(x_high[2 * rows : 2 * rows + 16, :])
    theirs = from_two(over_x[end : end + 16, :])
    pairs = in_two(*(a + b for a, b in zip(mine, theirs)))
    gains[...] = pairs.astype(F32)
    for index in range(4):
        at = slice((index % 2) * rows, (index % 2 + 1) * rows)
        block = plus(
            (own_low if index < 2 else own_high)[at, :],
            over_x[index * rows : (index + 1) * rows, :],
            (both_low if index < 2 else y_high)[at, :],
        )
        if index == 0:
            total[...] = block
        else:
            messages[index - 1][0:rows, :] = block.astype(BF)
            messages[index - 1][rows:, :] = pairs


class Links:
    def __init__(self, wide, narrow):
        self.wide, self.narrow = wide, narrow
        self.planes = wide // 2
        self.staged = wide == 8

    def y(self, values):
        return lax.ppermute(values, "narrow", [(i, (i + 2) % 4) for i in range(4)])

    def core(self, values):
        return lax.ppermute(values, "narrow", [(i, i ^ 1) for i in range(4)])

    def across(self, values):
        return lax.ppermute(values, "narrow", [(i, (i + 2) % 4 ^ 1) for i in range(4)])

    def x(self, values):
        return lax.ppermute(values, "wide", [(i, i ^ 1) for i in range(self.wide)])

    def z(self, values, ahead):
        turn = lambda i: ((i // 2 + ahead) % self.planes) * 2 + i % 2
        return lax.ppermute(values, "wide", [(i, turn(i)) for i in range(self.wide)])

    def whole_gather(self, piece):
        near = lax.all_gather(piece, "wide", axis=0, tiled=True)
        return [near], [self.y(near)]

    def whole_reduce(self, near, far):
        return lax.psum_scatter(near, "wide", scatter_dimension=0, tiled=True).astype(
            F32
        ) + lax.psum_scatter(self.y(far), "wide", scatter_dimension=0, tiled=True).astype(F32)


def on_device(
    tokens,
    lengths,
    norm_one,
    w_query,
    w_key,
    w_value,
    w_out,
    norm_two,
    w_gate,
    w_up,
    w_down,
    cotangent,
):
    model = tokens.shape[-1]
    wide, narrow = lax.axis_size("wide"), lax.axis_size("narrow")
    links = Links(wide, narrow)
    heads = w_query.shape[1] // HD
    head_width = heads * HD
    units = w_gate.shape[1]
    at_wide, at_narrow = lax.axis_index("wide"), lax.axis_index("narrow")
    y, c = at_narrow >> 1, at_narrow & 1
    x, z = at_wide & 1, at_wide >> 1

    staged = links.staged
    planes = links.planes
    rows = model // wide
    turned = [((z + k) & (planes - 1)) * 2 + (x ^ side) for side in range(2) for k in range(4)]
    blocks = [((y ^ far) * 2 + (c ^ side)) * TILE for side in range(2) for far in range(2)]
    length = lax.dynamic_index_in_dim(lengths, y, 0, keepdims=False)[0]
    numbers = [
        *(spot * rows for spot in turned),
        *blocks,
        length,
    ]
    meta = jnp.stack([jnp.asarray(number, jnp.int32) for number in numbers])
    first_item = y == 0

    gain_one = norm_one.reshape(1, model)
    gain_two = norm_two.reshape(1, model)

    def keep_give(rows):
        flat = rows.reshape(2, TILE, model)
        return (
            lax.dynamic_index_in_dim(flat, y, 0, keepdims=False),
            lax.dynamic_index_in_dim(flat, 1 - y, 0, keepdims=False),
        )

    attn_piece = jnp.concatenate([w_out.T, w_query, w_key, w_value], axis=1)
    feed_piece = jnp.concatenate([w_gate, w_up, w_down.T], axis=1)
    keep, give = keep_give(tokens)
    keep_cot, give_cot = keep_give(cotangent)
    half = planes // 2 * rows
    if staged:
        block_rows = rows
        quarters = ((0, 1), (2, 3), (4, 5), (6, 7))
        attn_near_in = attn_far_in = ((0, 1, 2, 3), (4, 5, 6, 7))
        feed_near_in = ((0,), (4,), (1, 5), (3, 7), (2, 6))
        feed_far_in = ((0, 1, 3), (2, 6), (4, 5, 7))
        feed_near_out = ((0, 1), (2, 3), (4,), (5,), (6,), (7,))
        attn_far_out = ((0, 1, 4, 5), (2, 3), (6, 7))
    else:
        block_rows = model
        quarters = attn_far_out = feed_near_out = ((0,),)
        attn_near_in = attn_far_in = feed_near_in = feed_far_in = ((0,),)

    got = links.y(give)
    if staged:
        feed_x_own = links.x(feed_piece)
        column = [attn_piece] + [links.z(attn_piece, planes - k) for k in range(1, planes)]
        column = jnp.concatenate(column, axis=0)
        over_x, over_y = links.x(column), links.y(column)
        feed_pair = jnp.concatenate([feed_piece, feed_x_own], axis=0)
        feed_pair, column, meta, first_item = hold(feed_pair, column, meta, first_item)
        pair_one = links.z(feed_pair, planes - 1)
        pair_three = links.z(feed_pair, planes - 3)
    else:
        attn_near, attn_far = links.whole_gather(attn_piece)
        feed_near, feed_far = links.whole_gather(feed_piece)
    rows_in = [keep, got, links.core(keep), links.core(got)]
    if staged:
        over_y, rows_in, over_x, feed_pair = hold(over_y, rows_in, over_x, feed_pair)
        give_cot, over_y = hold(give_cot, over_y)
        attn_near = [column, over_x]
        pair_two = links.z(feed_pair, planes - 2)
        attn_far = [over_y, links.x(over_y)]
    got_cot = links.y(give_cot)

    inv_near, context_near, expo_near, *kept_near, normed = attention_forward(
        meta, heads, block_rows, attn_near, attn_near_in, rows_in=rows_in, gain=gain_one
    )
    if staged:
        normed, got_cot, attn_far, pair_one, pair_three = hold(
            normed, got_cot, attn_far, pair_one, pair_three
        )
        feed_y = links.y(
            jnp.concatenate([feed_piece, pair_one[:rows], pair_three[:rows]], axis=0)
        )
    own_cot = jnp.concatenate([keep_cot, got_cot], axis=0)
    cots = [own_cot, links.core(own_cot)]
    inv_far, context_far, expo_far, *kept_far, part_mine = attention_forward(
        meta, heads, block_rows, attn_far, attn_far_in,
        before=(normed, context_near, kept_near[0]),
    )
    if staged:
        part_mine, feed_y, pair_two = hold(part_mine, feed_y, pair_two)
    part_other = links.core(part_mine)
    if staged:
        feed_near = [feed_piece, feed_x_own, pair_one, pair_three, pair_two]
        feed_far = [feed_y, links.y(pair_two), links.x(feed_y)]
    parts = (part_mine, part_other)

    normed_two, down_near, back_near, *near = feed_forward(
        meta, block_rows, cots, feed_near, feed_near_in, feed_near_out, rows_in=rows_in,
        before=(*parts, gain_two),
    )
    if staged:
        own_low, own_high, over, *pieces = near
        over_in = [links.z(pieces[0], 1), None, links.z(pieces[2], 3)]
    mlp_mine, mlp_other, d_mine, *far = feed_forward(
        meta, block_rows, cots, feed_far, feed_far_in, quarters,
        before=(normed_two, down_near, back_near),
    )
    if staged:
        y_low, y_high, xy_low, xy_high = far
        from_xy_high = links.x(xy_high)
    else:
        feed_grad = links.whole_reduce(*near, *far)
    d_other = links.core(d_mine)
    half_rows = 2 * TILE
    output = (
        jnp.concatenate(rows_in[:2], axis=0).astype(F32)
        + part_mine[:half_rows].astype(F32)
        + part_other[half_rows:].astype(F32)
        + mlp_mine.astype(F32)
        + links.core(mlp_other).astype(F32)
    ).astype(BF)
    output_back = links.y(output[TILE:])
    d_middle, d_context_near, d_context_far, out_near, out_far, gain_rows = middle_backward(
        heads,
        rows_in,
        parts,
        gain_two,
        cots,
        (d_mine, d_other),
        (context_near, context_far),
        (kept_near[0], kept_far[0]),
    )
    if staged:
        d_context_far, from_xy_high, output_back, over_in[0], over_in[2] = hold(
            d_context_far, from_xy_high, output_back, over_in[0], over_in[2]
        )
        xy_low, pieces[1], from_xy_high = hold(xy_low, pieces[1], from_xy_high)
        over_in[1] = links.z(pieces[1], 2)
        from_y_high = links.y(add(y_high, from_xy_high).astype(BF))
        from_xy_low = links.x(xy_low)
    d_first, *far = attention_backward(
        meta, heads, block_rows, normed, (inv_far, context_far, expo_far, *kept_far),
        d_context_far, out_far, attn_far_out,
    )
    if staged:
        d_first, from_y_high, from_xy_low, over_in[1] = hold(
            d_first, from_y_high, from_xy_low, over_in[1]
        )
        feed = (rows, feed_piece.shape[1])
        feed_half = (half, feed_piece.shape[1])
        feed_two, feed_three, feed_y_low = call_local(
            join_kernel, [(feed, BF), (feed, BF), (feed_half, BF)],
            own_high, from_y_high, y_low, from_xy_low,
        )
        feed_two = links.z(feed_two, 2)
        feed_low = own_low
        both_low, y_high, xy_high = far
        from_both_low = links.y(both_low)
        from_xy_high = links.x(xy_high)
        from_feed_y = links.y(feed_y_low)
    last_mine, last_other, *near = attention_backward(
        meta, heads, block_rows, normed, (inv_near, context_near, expo_near, *kept_near),
        d_context_near, out_near, quarters, before=(d_first, gain_one, gain_rows),
    )
    if staged:
        last_other, near, from_both_low, from_xy_high, from_feed_y, feed_two = hold(
            last_other, near, from_both_low, from_xy_high, from_feed_y, feed_two
        )
        own_low, own_high, x_low, x_high = near
        width = x_low.shape[1]
        message, y_high, feed_own, feed_one, feed_over = call_local(
            meet_kernel,
            [((2 * half + 16, width), BF), ((half, width), BF), (feed, F32), (feed, BF), (feed, BF)],
            x_low, x_high, from_both_low, y_high, from_xy_high, feed_low, from_feed_y,
            over, *over_in,
        )
        from_x, from_y_high = links.x(message), links.y(y_high)
        feed_parts = [feed_two, links.z(feed_three, 3), links.z(feed_one, 1)]
    else:
        attn_grad = links.whole_reduce(near[0][:model], *far)
        gains = near[0][model:]
    mine, theirs = call_local(
        finish_kernel,
        [((TILE, model), BF)] * 2,
        last_mine, links.core(last_other), *rows_in[:2], d_middle, gain_one,
    )
    if staged:
        from_x, theirs, feed_parts = hold(from_x, theirs, feed_parts)
    back = links.y(theirs)
    if staged:
        attn = (rows, width)
        apart = ((rows + 16, width), BF)
        attn_grad, gains, *messages = call_local(
            fold_kernel, [(attn, F32), ((16, width), F32), apart, apart, apart],
            own_low, own_high, x_high, from_x, from_both_low, from_y_high,
        )
        arrived = [links.z(piece, k + 1) for k, piece in enumerate(messages)]
        feed_over, attn_grad = hold(feed_over, attn_grad)
        feed_parts.append(links.x(feed_over))
        attn_grad = add(attn_grad, *(part[:rows] for part in arrived))
        gains = add(gains, *(part[rows:] for part in arrived))
        feed_grad = add(feed_own, *feed_parts)
        gains, back, feed_grad = hold(gains, back, feed_grad)
    else:
        gains = lax.psum(gains.astype(F32), "wide")
    gains = (gains + links.core(gains)) + (links.y(gains) + links.across(gains))

    def in_order(own, other):
        stacked = jnp.where(first_item, jnp.stack([own, other]), jnp.stack([other, own]))
        return stacked.reshape(tokens.shape)

    return (
        in_order(output[:TILE], output_back),
        in_order(mine, back),
        gains[0] + gains[1],
        attn_grad[:, head_width : 2 * head_width],
        attn_grad[:, 2 * head_width : 3 * head_width],
        attn_grad[:, 3 * head_width :],
        attn_grad[:, :head_width].T,
        gains[2] + gains[3],
        feed_grad[:, :units],
        feed_grad[:, units : 2 * units],
        feed_grad[:, 2 * units :].T,
    )


def solution(mesh):
    in_specs = (
        P(None, "wide", "narrow", None),
        P(None, "wide"),
        P(),
        P("wide", "narrow"),
        P("wide", "narrow"),
        P("wide", "narrow"),
        P("narrow", "wide"),
        P(),
        P("wide", "narrow"),
        P("wide", "narrow"),
        P("narrow", "wide"),
        P(None, "wide", "narrow", None),
    )
    out_specs = (
        P(None, "wide", "narrow", None),
        P(None, "wide", "narrow", None),
        P(),
        P("wide", "narrow"),
        P("wide", "narrow"),
        P("wide", "narrow"),
        P("narrow", "wide"),
        P(),
        P("wide", "narrow"),
        P("wide", "narrow"),
        P("narrow", "wide"),
    )
    return jax.shard_map(
        on_device, mesh=mesh, in_specs=in_specs, out_specs=out_specs, check_vma=False
    )
```

```python
import functools

import jax
import jax.numpy as jnp
from jax import lax
from jax.experimental import pallas as pl
from jax.experimental.pallas import tpu as pltpu
from jax.sharding import PartitionSpec as P

HD = 64
EPSILON = 1e-06
MASKED = -1e30
TILE = 256
FEED_ROWS = 1024
QUERY_ROWS = 1024
MIDDLE_LIMIT = 8 * 1024 * 1024
BACK_LIMIT = 14 * 1024 * 1024
ATTEND_LIMIT = 11 * 1024 * 1024
FEED_LIMIT = 22 * 1024 * 1024
COST = pl.CostEstimate(flops=10**6, bytes_accessed=10**5, transcendentals=0)
BF = jnp.bfloat16
F32 = jnp.float32


def mm(left, right):
    return jnp.dot(left, right, preferred_element_type=F32)


def mm_nt(left, right):
    return lax.dot_general(left, right, (((1,), (1,)), ((), ())), preferred_element_type=F32)


def mm_tn(left, right):
    return lax.dot_general(left, right, (((0,), (0,)), ((), ())), preferred_element_type=F32)


def inverse_rms(features):
    return lax.rsqrt(jnp.mean(features * features, axis=-1, keepdims=True) + EPSILON)


def place(meta, pieces, orders, dest, rows, sems):
    copies = []
    for piece, order in zip(pieces, orders):
        for number, index in enumerate(order):
            at = 0 if rows == dest.shape[0] else pl.multiple_of(meta[index], 16)
            copy = pltpu.make_async_copy(
                piece.at[pl.ds(number * rows, rows), :],
                dest.at[pl.ds(at, rows), :],
                sems.at[len(copies)],
            )
            copy.start()
            copies.append(copy)
    return copies


def wait_all(copies):
    for copy in copies:
        copy.wait()


def blocks_of(orders):
    return sum(len(order) for order in orders)


def disperse(meta, source, groups, orders, rows):
    for group, order in zip(groups, orders):
        for place, index in enumerate(order):
            at = 0 if rows == source.shape[0] else pl.multiple_of(meta[index], 16)
            group[place * rows : (place + 1) * rows, :] = source[pl.ds(at, rows), :]


def row_block(refs, block):
    start = block * TILE
    for ref in refs:
        if start < ref.shape[0]:
            return ref[start : start + TILE, :]
        start -= ref.shape[0]


def forward_kernel(heads, n_rows, orders, block_rows, meta, *refs):
    first = n_rows > 0
    refs = list(refs)
    take = lambda count: [refs.pop(0) for _ in range(count)]
    width = heads * HD
    total = 4 * TILE
    if first:
        (gain,) = take(1)
        sources = take(n_rows)
    else:
        normed, context_first, weight_first = take(3)
    pieces = take(len(orders))
    inverse, context, expo, weight, proj = take(5)
    if first:
        (normed,) = take(1)
    else:
        (partial,) = take(1)
    q_ext, k_ext, v_flip, sems, sems_more = take(5)
    copies = place(meta, pieces, orders, weight, block_rows, sems)
    outs = []

    def carry(source, dest):
        copy = pltpu.make_async_copy(source, dest, sems_more.at[len(outs)])
        copy.start()
        outs.append(copy)

    if first:
        (extra,) = take(1)
        starts = [sum(ref.shape[0] for ref in sources[:k]) for k in range(n_rows)]
        for start, source in zip(starts, sources):
            carry(source, extra.at[pl.ds(start, source.shape[0]), :])
        wait_all(outs)
        for block in range(4):
            rows = slice(block * TILE, (block + 1) * TILE)
            features = extra[rows, :].astype(F32)
            normed[rows, :] = (features * inverse_rms(features) * gain[...]).astype(BF)
    wait_all(copies)
    proj[...] = mm(normed[...], weight[...]).astype(BF)
    lanes = lax.broadcasted_iota(jnp.int32, (TILE, HD), 1)
    index = lax.broadcasted_iota(jnp.int32, (TILE, HD), 0)
    ones = jnp.where(lanes == 0, 1.0, 0.0).astype(BF)
    below = jnp.where(lax.broadcasted_iota(jnp.int32, (16, total), 0) == 0, 1.0, 0.0).astype(BF)
    for block in range(4):
        rows = slice(block * TILE, (block + 1) * TILE)
        usable = meta[8 + block] + index < meta[12]
        bias = jnp.where((lanes == 0) & ~usable, MASKED, 0.0).astype(BF)
        for head in range(heads):
            at = width + head * HD
            q_ext[head, rows, 0:HD] = proj[rows, at : at + HD]
            q_ext[head, rows, HD : 2 * HD] = ones
            at = 2 * width + head * HD
            k_ext[head, rows, 0:HD] = proj[rows, at : at + HD]
            k_ext[head, rows, HD : 2 * HD] = bias
    for head in range(heads):
        at = 3 * width + head * HD
        v_flip[head, 0:HD, :] = proj[:, at : at + HD].T
        v_flip[head, HD : HD + 16, :] = below
    inverse[...] = jnp.ones_like(inverse)
    for head in range(heads):
        for start in range(0, total, QUERY_ROWS):
            rows = slice(start, start + QUERY_ROWS)
            scores = mm_nt(k_ext[head], q_ext[head, rows, :])
            top = jnp.max(scores, axis=0, keepdims=True)
            raised = jnp.exp(scores - top).astype(BF)
            expo[head, :, rows] = raised
            mixed = mm(v_flip[head], raised)
            inv = 1.0 / mixed[HD : HD + 1, :]
            inverse[head : head + 1, rows] = inv
            context[rows, head * HD : (head + 1) * HD] = (mixed[0:HD, :] * inv).astype(BF).T
    if not first:
        partial[...] = (
            mm_nt(context_first[...], weight_first[:, 0:width])
            + mm_nt(context[...], weight[:, 0:width])
        ).astype(BF)


SMEM = pl.BlockSpec(memory_space=pltpu.SMEM)
VMEM = pl.BlockSpec(memory_space=pltpu.VMEM)
HBM = pl.BlockSpec(memory_space=pltpu.HBM)


def attention_forward(meta, heads, block_rows, pieces, orders, rows_in=(), gain=None, before=None):
    width = pieces[0].shape[1]
    model = rows_in[0].shape[1] if rows_in else before[0].shape[1]
    total = 4 * TILE
    rows = jax.ShapeDtypeStruct((total, model), BF)
    numerators = jax.ShapeDtypeStruct((heads, total, total), BF)
    if rows_in:
        in_fast, in_slow = [gain], [*rows_in, *pieces]
        more, extra = [rows], [pltpu.VMEM((total, model), BF)]
    else:
        in_fast, in_slow = [*before], [*pieces]
        more, extra = [rows], []
    return pl.pallas_call(
        functools.partial(forward_kernel, heads, len(rows_in), orders, block_rows),
        in_specs=[SMEM] + [VMEM] * len(in_fast) + [HBM] * len(in_slow),
        out_specs=[VMEM] * 6,
        out_shape=[
            jax.ShapeDtypeStruct((8, total), F32),
            jax.ShapeDtypeStruct((total, heads * HD), BF),
            numerators,
            jax.ShapeDtypeStruct((model, width), BF),
            jax.ShapeDtypeStruct((total, width), BF),
            *more,
        ],
        scratch_shapes=[
            pltpu.VMEM((heads, total, 2 * HD), BF),
            pltpu.VMEM((heads, total, 2 * HD), BF),
            pltpu.VMEM((heads, HD + 16, total), BF),
            pltpu.SemaphoreType.DMA((blocks_of(orders),)),
            pltpu.SemaphoreType.DMA((4,)),
            *extra,
        ],
        compiler_params=pltpu.CompilerParams(vmem_limit_bytes=ATTEND_LIMIT),
        cost_estimate=COST,
        name="attention_forward",
    )(meta, *in_fast, *in_slow)


def gelu_terms(gate):
    scale = 0.7978845608028654
    cube = 0.044715
    square = gate * gate
    bent = jnp.tanh(scale * gate * (1.0 + cube * square))
    half = 0.5 * (1.0 + bent)
    slope = half + 0.5 * gate * (1.0 - bent * bent) * (scale * (1.0 + 3.0 * cube * square))
    return gate * half, slope


def feed_kernel(n_rows, n_cots, in_orders, orders, block_rows, meta, *refs):
    first = n_rows > 0
    refs = list(refs)
    take = lambda count: [refs.pop(0) for _ in range(count)]
    if first:
        rows_in = take(n_rows)
        part_mine, part_other, gain = take(3)
    else:
        normed, result_before, back_before = take(3)
    cots = take(n_cots)
    pieces = take(len(in_orders))
    if first:
        normed, result, back = take(3)
    else:
        mine, other, back = take(3)
    groups = take(len(orders))
    weight, hidden, d_gate, d_up, cot, grad, sems = take(7)
    units = weight.shape[1] // 3
    copies = place(meta, pieces, in_orders, weight, block_rows, sems)
    for block in range(4):
        rows = slice(block * TILE, (block + 1) * TILE)
        cot[rows, :] = row_block(cots, block)
        if first:
            swapped = slice(((block + 2) % 4) * TILE, ((block + 2) % 4 + 1) * TILE)
            features = (
                row_block(rows_in, block).astype(F32)
                + part_mine[rows, :].astype(F32)
                + part_other[swapped, :].astype(F32)
            )
            features = features.astype(BF).astype(F32)
            normed[rows, :] = (features * inverse_rms(features) * gain[...]).astype(BF)
    wait_all(copies)
    for start in range(0, 4 * TILE, FEED_ROWS):
        rows = slice(start, start + FEED_ROWS)
        pre = mm(normed[rows, :], weight[:, 0 : 2 * units])
        act, slope = gelu_terms(pre[:, :units])
        up = pre[:, units:]
        low = (act * up).astype(BF)
        hidden[rows, :] = low
        d_hidden = mm(cot[rows, :], weight[:, 2 * units :])
        gate_low = (d_hidden * up * slope).astype(BF)
        up_low = (d_hidden * act).astype(BF)
        d_gate[rows, :] = gate_low
        d_up[rows, :] = up_low
        down = mm_nt(low, weight[:, 2 * units :])
        through = mm_nt(gate_low, weight[:, 0:units]) + mm_nt(up_low, weight[:, units : 2 * units])
        if first:
            result[rows, :] = down.astype(BF)
            back[rows, :] = through.astype(BF)
        else:
            down = (down + result_before[rows, :].astype(F32)).astype(BF)
            if start < 2 * TILE:
                mine[rows, :] = down[: 2 * TILE - start]
            if start + FEED_ROWS > 2 * TILE:
                begin = max(start - 2 * TILE, 0)
                other[begin : start + FEED_ROWS - 2 * TILE, :] = down[begin + 2 * TILE - start :]
            back[rows, :] = (through + back_before[rows, :].astype(F32)).astype(BF)
    grad[:, 2 * units :] = mm_tn(cot[...], hidden[...]).astype(BF)
    grad[:, 0:units] = mm_tn(normed[...], d_gate[...]).astype(BF)
    grad[:, units : 2 * units] = mm_tn(normed[...], d_up[...]).astype(BF)
    disperse(meta, grad, groups, orders, block_rows)


def feed_forward(meta, block_rows, cots, pieces, in_orders, orders, rows_in=(), before=()):
    width = pieces[0].shape[1]
    model = cots[0].shape[1]
    total = 4 * TILE
    units = width // 3
    full = jax.ShapeDtypeStruct((total, model), BF)
    half = jax.ShapeDtypeStruct((2 * TILE, model), BF)
    operands = [*rows_in, *before, *cots, *pieces]
    out_shape = [full, full, full] if rows_in else [half, half, full]
    out_shape += [
        jax.ShapeDtypeStruct((len(order) * block_rows, width), BF) for order in orders
    ]
    return pl.pallas_call(
        functools.partial(
            feed_kernel, len(rows_in), len(cots), in_orders, orders, block_rows
        ),
        in_specs=[SMEM] + [VMEM] * (len(operands) - len(pieces)) + [HBM] * len(pieces),
        out_specs=[VMEM] * len(out_shape),
        out_shape=out_shape,
        scratch_shapes=[
            pltpu.VMEM((model, width), BF),
            pltpu.VMEM((total, units), BF),
            pltpu.VMEM((total, units), BF),
            pltpu.VMEM((total, units), BF),
            pltpu.VMEM((total, model), BF),
            pltpu.VMEM((model, width), BF),
            pltpu.SemaphoreType.DMA((blocks_of(in_orders),)),
        ],
        compiler_params=pltpu.CompilerParams(vmem_limit_bytes=FEED_LIMIT),
        cost_estimate=COST,
        name="feed_forward",
    )(meta, *operands)


def middle_kernel(heads, n_rows, n_cots, *refs):
    refs = list(refs)
    take = lambda count: [refs.pop(0) for _ in range(count)]
    rows_in = take(n_rows)
    part_mine, part_other, gain = take(3)
    cots = take(n_cots)
    d_mine, d_other, context_near, context_far = take(4)
    weight_near, weight_far = take(2)
    d_middle, d_context_near, d_context_far, grad_near, grad_far, d_gain = take(6)
    (d_all,) = take(1)
    width = heads * HD
    gains = 0.0
    for block in range(4):
        rows = slice(block * TILE, (block + 1) * TILE)
        swapped = slice(((block + 2) % 4) * TILE, ((block + 2) % 4 + 1) * TILE)
        features = (
            row_block(rows_in, block).astype(F32)
            + part_mine[rows, :].astype(F32)
            + part_other[swapped, :].astype(F32)
        )
        features = features.astype(BF).astype(F32)
        inverse = inverse_rms(features)
        back = d_mine[rows, :].astype(F32) + d_other[swapped, :].astype(F32)
        scaled = back * gain[...]
        inner = jnp.mean(scaled * features, axis=-1, keepdims=True)
        result = (
            row_block(cots, block).astype(F32)
            + inverse * scaled
            - features * (inverse * inverse * inverse * inner)
        )
        d_all[rows, :] = result.astype(BF)
        if block < 2:
            d_middle[rows, :] = result
            gains += jnp.sum(back * features * inverse, axis=0, keepdims=True)
    d_gain[...] = jnp.broadcast_to(gains, d_gain.shape)
    d_context_near[...] = mm(d_all[...], weight_near[:, 0:width]).astype(BF)
    d_context_far[...] = mm(d_all[...], weight_far[:, 0:width]).astype(BF)
    grad_near[...] = mm_tn(d_all[...], context_near[...]).astype(BF)
    grad_far[...] = mm_tn(d_all[...], context_far[...]).astype(BF)


def middle_backward(heads, rows_in, parts, gain, cots, d_normed, contexts, weights):
    model = gain.shape[1]
    total = 4 * TILE
    width = heads * HD
    operands = [*rows_in, *parts, gain, *cots, *d_normed, *contexts, *weights]
    return pl.pallas_call(
        functools.partial(middle_kernel, heads, len(rows_in), len(cots)),
        in_specs=[VMEM] * len(operands),
        out_specs=[VMEM] * 6,
        out_shape=[
            jax.ShapeDtypeStruct((2 * TILE, model), F32),
            jax.ShapeDtypeStruct((total, width), BF),
            jax.ShapeDtypeStruct((total, width), BF),
            jax.ShapeDtypeStruct((model, width), BF),
            jax.ShapeDtypeStruct((model, width), BF),
            jax.ShapeDtypeStruct((8, model), F32),
        ],
        scratch_shapes=[
            pltpu.VMEM((total, model), BF),
        ],
        compiler_params=pltpu.CompilerParams(vmem_limit_bytes=MIDDLE_LIMIT),
        cost_estimate=COST,
        name="middle_backward",
    )(*operands)


def in_two(*rows):
    high = [row.astype(BF).astype(F32) for row in rows]
    index = lax.broadcasted_iota(jnp.int32, (16, rows[0].shape[1]), 0)
    result = jnp.zeros((16, rows[0].shape[1]), F32)
    for number, row in enumerate(rows):
        result = jnp.where(index == 2 * number, high[number], result)
        result = jnp.where(index == 2 * number + 1, row - high[number], result)
    return result.astype(BF)


def from_two(rows):
    return [
        rows[2 * k : 2 * k + 1].astype(F32) + rows[2 * k + 1 : 2 * k + 2].astype(F32)
        for k in range(2)
    ]


def finish_kernel(d_mine, d_other, keep, got, d_middle, gain, mine, theirs):
    for number, rows_in in enumerate((keep, got)):
        rows = slice(number * TILE, (number + 1) * TILE)
        features = rows_in[...].astype(F32)
        inverse = inverse_rms(features)
        scaled = (d_mine[rows, :].astype(F32) + d_other[rows, :].astype(F32)) * gain[...]
        inner = jnp.mean(scaled * features, axis=-1, keepdims=True)
        result = (
            d_middle[rows, :] + inverse * scaled - features * (inverse * inverse * inverse * inner)
        ).astype(BF)
        if number == 0:
            mine[...] = result
        else:
            theirs[...] = result


def backward_kernel(heads, orders, block_rows, last, meta, *refs):
    refs = list(refs)
    take = lambda count: [refs.pop(0) for _ in range(count)]
    inverse, context, expo, weight, proj, normed, d_context, grad_out = take(8)
    if last:
        gain, gain_rows = take(2)
    if last:
        (before,) = take(1)
        mine, other = take(2)
    else:
        (result,) = take(1)
    groups = take(len(orders))
    do_ext, v_ext, d_proj, grad = take(4)
    width = heads * HD
    total = 4 * TILE
    lanes = lax.broadcasted_iota(jnp.int32, (total, HD), 1)
    columns = inverse[...].T
    d_proj[:, 0:width] = jnp.zeros((total, width), BF)
    for head in range(heads):
        at = head * HD
        scaled = (d_context[:, at : at + HD].astype(F32) * columns[:, head : head + 1]).astype(BF)
        inner = -jnp.sum(
            scaled.astype(F32) * context[:, at : at + HD].astype(F32), axis=-1, keepdims=True
        )
        high = inner.astype(BF).astype(F32)
        do_ext[head, :, 0:HD] = scaled
        do_ext[head, :, HD : 2 * HD] = jnp.where(
            lanes == 0, high, jnp.where(lanes == 1, inner - high, 0.0)
        ).astype(BF)
    for head in range(heads):
        at = 3 * width + head * HD
        v_ext[head, :, 0:HD] = proj[:, at : at + HD]
        v_ext[head, :, HD : 2 * HD] = jnp.where(lanes < 2, 1.0, 0.0).astype(BF)
    for head in range(heads):
        q_at, k_at, v_at = (part * width + head * HD for part in (1, 2, 3))
        raised = expo[head]
        d_probs = mm_nt(v_ext[head], do_ext[head])
        d_scores = (raised.astype(F32) * d_probs).astype(BF)
        d_queries = mm(proj[:, k_at : k_at + HD].T, d_scores)
        d_keys = mm_nt(proj[:, q_at : q_at + HD].T, d_scores)
        d_values = mm_nt(do_ext[head, :, 0:HD].T, raised)
        d_proj[:, q_at : q_at + HD] = d_queries.astype(BF).T
        d_proj[:, k_at : k_at + HD] = d_keys.astype(BF).T
        d_proj[:, v_at : v_at + HD] = d_values.astype(BF).T
    grad[...] = mm_tn(normed[...], d_proj[...]).astype(BF)
    grad[:, 0:width] = grad_out[...]
    disperse(meta, grad, groups, orders, block_rows)
    through = mm_nt(d_proj[...], weight[...])
    if last:
        through = through + before[...].astype(F32)
        mine[...] = through[0 : 2 * TILE].astype(BF)
        other[...] = through[2 * TILE :].astype(BF)
        first = jnp.sum(through * normed[...].astype(F32), axis=0, keepdims=True) / gain[...]
        end = len(orders[-1]) * block_rows
        groups[-1][end : end + 16, :] = in_two(first, gain_rows[0:1, :])
    else:
        result[...] = through.astype(BF)


def attention_backward(
    meta, heads, block_rows, normed, saved, d_context, grad_out, orders, before=None
):
    last = before is not None
    weight, proj = saved[3:]
    model, width = weight.shape
    total = proj.shape[0]
    rows = jax.ShapeDtypeStruct((total, model), BF)
    in_fast = [*saved, normed, d_context, grad_out]
    scratch = [
        pltpu.VMEM((heads, total, 2 * HD), BF),
        pltpu.VMEM((heads, total, 2 * HD), BF),
        pltpu.VMEM((total, width), BF),
        pltpu.VMEM((model, width), BF),
    ]
    sizes = [len(order) * block_rows for order in orders]
    if last:
        in_fast += [*before[1:], before[0]]
        out_shape = [jax.ShapeDtypeStruct((2 * TILE, model), BF)] * 2
        sizes[-1] += 16
    else:
        out_shape = [rows]
    out_shape += [jax.ShapeDtypeStruct((size, width), BF) for size in sizes]
    return pl.pallas_call(
        functools.partial(backward_kernel, heads, orders, block_rows, last),
        in_specs=[SMEM] + [VMEM] * len(in_fast),
        out_specs=[VMEM] * len(out_shape),
        out_shape=out_shape,
        scratch_shapes=scratch,
        compiler_params=pltpu.CompilerParams(vmem_limit_bytes=BACK_LIMIT),
        cost_estimate=COST,
        name="attention_backward",
    )(meta, *in_fast)


def add(*terms):
    return sum(term.astype(F32) for term in terms)


def hold(values, *others):
    values, others = lax.optimization_barrier((values, others))
    return values, *others


def plus(*terms):
    return sum(term.astype(F32) for term in terms)


def call_local(kernel, out_shape, *operands):
    return pl.pallas_call(
        kernel,
        in_specs=[VMEM] * len(operands),
        out_specs=[VMEM] * len(out_shape),
        out_shape=[jax.ShapeDtypeStruct(shape, kind) for shape, kind in out_shape],
        compiler_params=pltpu.CompilerParams(vmem_limit_bytes=MIDDLE_LIMIT),
        cost_estimate=COST,
        name=kernel.__name__.replace("kernel", "backward"),
    )(*operands)


def join_kernel(own_high, x_high, y_high, y_low, xy_low, two, three, y_low_plus):
    rows = two.shape[0]
    for at, dest in ((slice(0, rows), two), (slice(rows, 2 * rows), three)):
        dest[...] = plus(own_high[at, :], x_high[at, :], y_high[at, :]).astype(BF)
    y_low_plus[...] = plus(y_low[...], xy_low[...]).astype(BF)


def meet_kernel(x_low, x_high, both_low, y_high, xy_high, message, y_high_plus):
    half = x_low.shape[0]
    message[0:half, :] = plus(x_low[...], both_low[half:, :]).astype(BF)
    message[half:, :] = x_high[...]
    y_high_plus[...] = plus(y_high[...], xy_high[...]).astype(BF)


def last_kernel(own_low, feed_x, feed_y, own, one):
    rows = own.shape[0]
    own[...] = plus(own_low[0:rows, :], feed_x[0:rows, :], feed_y[0:rows, :])
    one[...] = plus(own_low[rows:, :], feed_x[rows:, :], feed_y[rows:, :]).astype(BF)


def fold_kernel(own_low, own_high, x_high, over_x, both_low, y_high, total, gains, *messages):
    rows = total.shape[0]
    end = 4 * rows
    mine = from_two(x_high[2 * rows : 2 * rows + 16, :])
    theirs = from_two(over_x[end : end + 16, :])
    pairs = in_two(*(a + b for a, b in zip(mine, theirs)))
    gains[...] = pairs.astype(F32)
    for index in range(4):
        at = slice((index % 2) * rows, (index % 2 + 1) * rows)
        block = plus(
            (own_low if index < 2 else own_high)[at, :],
            over_x[index * rows : (index + 1) * rows, :],
            (both_low if index < 2 else y_high)[at, :],
        )
        if index == 0:
            total[...] = block
        else:
            messages[index - 1][0:rows, :] = block.astype(BF)
            messages[index - 1][rows:, :] = pairs


class Links:
    def __init__(self, wide, narrow):
        self.wide, self.narrow = wide, narrow
        self.planes = wide // 2
        self.staged = wide == 8

    def y(self, values):
        return lax.ppermute(values, "narrow", [(i, (i + 2) % 4) for i in range(4)])

    def core(self, values):
        return lax.ppermute(values, "narrow", [(i, i ^ 1) for i in range(4)])

    def across(self, values):
        return lax.ppermute(values, "narrow", [(i, (i + 2) % 4 ^ 1) for i in range(4)])

    def x(self, values):
        return lax.ppermute(values, "wide", [(i, i ^ 1) for i in range(self.wide)])

    def z(self, values, ahead):
        turn = lambda i: ((i // 2 + ahead) % self.planes) * 2 + i % 2
        return lax.ppermute(values, "wide", [(i, turn(i)) for i in range(self.wide)])

    def whole_gather(self, piece):
        near = lax.all_gather(piece, "wide", axis=0, tiled=True)
        return [near], [self.y(near)]

    def whole_reduce(self, near, far):
        return lax.psum_scatter(near, "wide", scatter_dimension=0, tiled=True).astype(
            F32
        ) + lax.psum_scatter(self.y(far), "wide", scatter_dimension=0, tiled=True).astype(F32)


def on_device(
    tokens,
    lengths,
    norm_one,
    w_query,
    w_key,
    w_value,
    w_out,
    norm_two,
    w_gate,
    w_up,
    w_down,
    cotangent,
):
    model = tokens.shape[-1]
    wide, narrow = lax.axis_size("wide"), lax.axis_size("narrow")
    links = Links(wide, narrow)
    heads = w_query.shape[1] // HD
    head_width = heads * HD
    units = w_gate.shape[1]
    at_wide, at_narrow = lax.axis_index("wide"), lax.axis_index("narrow")
    y, c = at_narrow >> 1, at_narrow & 1
    x, z = at_wide & 1, at_wide >> 1

    staged = links.staged
    planes = links.planes
    rows = model // wide
    turned = [((z + k) & (planes - 1)) * 2 + (x ^ side) for side in range(2) for k in range(4)]
    blocks = [((y ^ far) * 2 + (c ^ side)) * TILE for side in range(2) for far in range(2)]
    length = lax.dynamic_index_in_dim(lengths, y, 0, keepdims=False)[0]
    numbers = [
        *(spot * rows for spot in turned),
        *blocks,
        length,
    ]
    meta = jnp.stack([jnp.asarray(number, jnp.int32) for number in numbers])
    first_item = y == 0

    gain_one = norm_one.reshape(1, model)
    gain_two = norm_two.reshape(1, model)

    def keep_give(rows):
        flat = rows.reshape(2, TILE, model)
        return (
            lax.dynamic_index_in_dim(flat, y, 0, keepdims=False),
            lax.dynamic_index_in_dim(flat, 1 - y, 0, keepdims=False),
        )

    attn_piece = jnp.concatenate([w_out.T, w_query, w_key, w_value], axis=1)
    feed_piece = jnp.concatenate([w_gate, w_up, w_down.T], axis=1)
    keep, give = keep_give(tokens)
    keep_cot, give_cot = keep_give(cotangent)
    half = planes // 2 * rows
    if staged:
        block_rows = rows
        quarters = ((0, 1), (2, 3), (4, 5), (6, 7))
        attn_near_in = attn_far_in = ((0, 1, 2, 3), (4, 5, 6, 7))
        feed_near_in = ((0,), (1,), (3,), (2,), (4, 5, 7), (6,))
        feed_far_in = ((0, 1, 3), (2,), (4, 5), (7, 6))
        attn_far_out = ((0, 1, 4, 5), (2, 3), (6, 7))
    else:
        block_rows = model
        quarters = attn_far_out = ((0,),)
        attn_near_in = attn_far_in = feed_near_in = feed_far_in = ((0,),)

    got = links.y(give)
    if staged:
        column = [attn_piece] + [links.z(attn_piece, planes - k) for k in range(1, planes)]
        column = jnp.concatenate(column, axis=0)
        over_x, over_y = links.x(column), links.y(column)
        feed_piece, column, meta, first_item = hold(feed_piece, column, meta, first_item)
        feed_one = links.z(feed_piece, planes - 1)
        feed_three = links.z(feed_piece, planes - 3)
    else:
        attn_near, attn_far = links.whole_gather(attn_piece)
        feed_near, feed_far = links.whole_gather(feed_piece)
    rows_in = [keep, got, links.core(keep), links.core(got)]
    if staged:
        rows_in, over_y, over_x, feed_one, feed_three = hold(
            rows_in, over_y, over_x, feed_one, feed_three
        )
        give_cot, over_y = hold(give_cot, over_y)
        attn_near = [column, over_x]
        attn_far = [over_y, links.x(over_y)]
        three = jnp.concatenate([feed_piece, feed_one, feed_three], axis=0)
        feed_x = links.x(three)
        feed_y = links.y(three)
        feed_piece, feed_one = hold(feed_piece, feed_one)
        feed_two = links.z(feed_piece, planes - 2)
    got_cot = links.y(give_cot)

    inv_near, context_near, expo_near, *kept_near, normed = attention_forward(
        meta, heads, block_rows, attn_near, attn_near_in, rows_in=rows_in, gain=gain_one
    )
    if staged:
        normed, got_cot, attn_far, feed_two = hold(normed, got_cot, attn_far, feed_two)
        feed_x_two = links.x(feed_two)
        feed_y_two = links.y(feed_two)
    own_cot = jnp.concatenate([keep_cot, got_cot], axis=0)
    cots = [own_cot, links.core(own_cot)]
    inv_far, context_far, expo_far, *kept_far, part_mine = attention_forward(
        meta, heads, block_rows, attn_far, attn_far_in,
        before=(normed, context_near, kept_near[0]),
    )
    if staged:
        part_mine, feed_x, feed_y, feed_x_two, feed_y_two = hold(
            part_mine, feed_x, feed_y, feed_x_two, feed_y_two
        )
    part_other = links.core(part_mine)
    if staged:
        feed_near = [feed_piece, feed_one, feed_three, feed_two, feed_x, feed_x_two]
        feed_far = [
            feed_y,
            feed_y_two,
            links.y(feed_x[: 2 * rows]),
            links.x(jnp.concatenate([feed_y[2 * rows :], feed_y_two], axis=0)),
        ]
    parts = (part_mine, part_other)

    normed_two, down_near, back_near, *near = feed_forward(
        meta, block_rows, cots, feed_near, feed_near_in, quarters, rows_in=rows_in,
        before=(*parts, gain_two),
    )
    if staged:
        own_low, own_high, x_low, x_high = near
        from_x_high = links.x(x_high)
    mlp_mine, mlp_other, d_mine, *far = feed_forward(
        meta, block_rows, cots, feed_far, feed_far_in, quarters,
        before=(normed_two, down_near, back_near),
    )
    if staged:
        mlp_other, from_x_high = hold(mlp_other, from_x_high)
        y_low, y_high, xy_low, xy_high = far
        from_xy_high = links.x(xy_high)
    else:
        feed_grad = links.whole_reduce(*near, *far)
    d_other = links.core(d_mine)
    half_rows = 2 * TILE
    output = (
        jnp.concatenate(rows_in[:2], axis=0).astype(F32)
        + part_mine[:half_rows].astype(F32)
        + part_other[half_rows:].astype(F32)
        + mlp_mine.astype(F32)
        + links.core(mlp_other).astype(F32)
    ).astype(BF)
    output_back = links.y(output[TILE:])
    d_middle, d_context_near, d_context_far, out_near, out_far, gain_rows = middle_backward(
        heads,
        rows_in,
        parts,
        gain_two,
        cots,
        (d_mine, d_other),
        (context_near, context_far),
        (kept_near[0], kept_far[0]),
    )
    if staged:
        d_context_far, from_xy_high, output_back = hold(d_context_far, from_xy_high, output_back)
        xy_low, from_xy_high = hold(xy_low, from_xy_high)
        from_y_high = links.y(add(y_high, from_xy_high).astype(BF))
        from_xy_low = links.x(xy_low)
    d_first, *far = attention_backward(
        meta, heads, block_rows, normed, (inv_far, context_far, expo_far, *kept_far),
        d_context_far, out_far, attn_far_out,
    )
    if staged:
        d_first, from_y_high, from_xy_low = hold(d_first, from_y_high, from_xy_low)
        x_low, from_xy_low = hold(x_low, from_xy_low)
        feed = (rows, feed_piece.shape[1])
        feed_half = (half, feed_piece.shape[1])
        feed_two, feed_three, feed_y_low = call_local(
            join_kernel, [(feed, BF), (feed, BF), (feed_half, BF)],
            own_high, from_x_high, from_y_high, y_low, from_xy_low,
        )
        feed_two = links.z(feed_two, 2)
        feed_low = own_low
        both_low, y_high, xy_high = far
        from_both_low = links.y(both_low)
        from_xy_high = links.x(xy_high)
        from_feed_x, from_feed_y = links.x(x_low), links.y(feed_y_low)
    last_mine, last_other, *near = attention_backward(
        meta, heads, block_rows, normed, (inv_near, context_near, expo_near, *kept_near),
        d_context_near, out_near, quarters, before=(d_first, gain_one, gain_rows),
    )
    if staged:
        last_other, near, from_both_low, from_xy_high, feed_two = hold(
            last_other, near, from_both_low, from_xy_high, feed_two
        )
        own_low, own_high, x_low, x_high = near
        width = x_low.shape[1]
        message, y_high = call_local(
            meet_kernel, [((2 * half + 16, width), BF), ((half, width), BF)],
            x_low, x_high, from_both_low, y_high, from_xy_high,
        )
        from_x, from_y_high = links.x(message), links.y(y_high)
        feed_parts = [feed_two, links.z(feed_three, 3)]
        last_mine, from_feed_x, from_feed_y = hold(last_mine, from_feed_x, from_feed_y)
    else:
        attn_grad = links.whole_reduce(near[0][:model], *far)
        gains = near[0][model:]
    mine, theirs = call_local(
        finish_kernel,
        [((TILE, model), BF)] * 2,
        last_mine, links.core(last_other), *rows_in[:2], d_middle, gain_one,
    )
    if staged:
        feed_own, feed_one = call_local(
            last_kernel, [(feed, F32), (feed, BF)], feed_low, from_feed_x, from_feed_y
        )
        feed_parts.append(links.z(feed_one, 1))
        from_x, theirs, feed_own = hold(from_x, theirs, feed_own)
    back = links.y(theirs)
    if staged:
        attn = (rows, width)
        apart = ((rows + 16, width), BF)
        attn_grad, gains, *messages = call_local(
            fold_kernel, [(attn, F32), ((16, width), F32), apart, apart, apart],
            own_low, own_high, x_high, from_x, from_both_low, from_y_high,
        )
        arrived = [links.z(piece, k + 1) for k, piece in enumerate(messages)]
        attn_grad = add(attn_grad, *(part[:rows] for part in arrived))
        gains = add(gains, *(part[rows:] for part in arrived))
        gains, back = hold(gains, back)
        feed_grad = add(feed_own, *feed_parts)
    else:
        gains = lax.psum(gains.astype(F32), "wide")
    gains = (gains + links.core(gains)) + (links.y(gains) + links.across(gains))

    def in_order(own, other):
        stacked = jnp.where(first_item, jnp.stack([own, other]), jnp.stack([other, own]))
        return stacked.reshape(tokens.shape)

    return (
        in_order(output[:TILE], output_back),
        in_order(mine, back),
        gains[0] + gains[1],
        attn_grad[:, head_width : 2 * head_width],
        attn_grad[:, 2 * head_width : 3 * head_width],
        attn_grad[:, 3 * head_width :],
        attn_grad[:, :head_width].T,
        gains[2] + gains[3],
        feed_grad[:, :units],
        feed_grad[:, units : 2 * units],
        feed_grad[:, 2 * units :].T,
    )


def solution(mesh):
    in_specs = (
        P(None, "wide", "narrow", None),
        P(None, "wide"),
        P(),
        P("wide", "narrow"),
        P("wide", "narrow"),
        P("wide", "narrow"),
        P("narrow", "wide"),
        P(),
        P("wide", "narrow"),
        P("wide", "narrow"),
        P("narrow", "wide"),
        P(None, "wide", "narrow", None),
    )
    out_specs = (
        P(None, "wide", "narrow", None),
        P(None, "wide", "narrow", None),
        P(),
        P("wide", "narrow"),
        P("wide", "narrow"),
        P("wide", "narrow"),
        P("narrow", "wide"),
        P(),
        P("wide", "narrow"),
        P("wide", "narrow"),
        P("narrow", "wide"),
    )
    return jax.shard_map(
        on_device, mesh=mesh, in_specs=in_specs, out_specs=out_specs, check_vma=False
    )
```

```python
import functools

import jax
import jax.numpy as jnp
from jax import lax
from jax.experimental import pallas as pl
from jax.experimental.pallas import tpu as pltpu
from jax.sharding import PartitionSpec as P

HD = 64
EPSILON = 1e-06
MASKED = -1e30
TILE = 256
FEED_ROWS = 1024
QUERY_ROWS = 1024
MIDDLE_LIMIT = 8 * 1024 * 1024
BACK_LIMIT = 14 * 1024 * 1024
ATTEND_LIMIT = 11 * 1024 * 1024
FEED_LIMIT = 22 * 1024 * 1024
COST = pl.CostEstimate(flops=10**6, bytes_accessed=10**5, transcendentals=0)
BF = jnp.bfloat16
F32 = jnp.float32


def mm(left, right):
    return jnp.dot(left, right, preferred_element_type=F32)


def mm_nt(left, right):
    return lax.dot_general(left, right, (((1,), (1,)), ((), ())), preferred_element_type=F32)


def mm_tn(left, right):
    return lax.dot_general(left, right, (((0,), (0,)), ((), ())), preferred_element_type=F32)


def inverse_rms(features):
    return lax.rsqrt(jnp.mean(features * features, axis=-1, keepdims=True) + EPSILON)


def place(meta, pieces, orders, dest, rows, sems):
    copies = []
    for piece, order in zip(pieces, orders):
        for number, index in enumerate(order):
            at = 0 if rows == dest.shape[0] else pl.multiple_of(meta[index], 16)
            copy = pltpu.make_async_copy(
                piece.at[pl.ds(number * rows, rows), :],
                dest.at[pl.ds(at, rows), :],
                sems.at[len(copies)],
            )
            copy.start()
            copies.append(copy)
    return copies


def wait_all(copies):
    for copy in copies:
        copy.wait()


def blocks_of(orders):
    return sum(len(order) for order in orders)


def disperse(meta, source, groups, orders, rows):
    for group, order in zip(groups, orders):
        for place, index in enumerate(order):
            at = 0 if rows == source.shape[0] else pl.multiple_of(meta[index], 16)
            group[place * rows : (place + 1) * rows, :] = source[pl.ds(at, rows), :]


def row_block(refs, block):
    start = block * TILE
    for ref in refs:
        if start < ref.shape[0]:
            return ref[start : start + TILE, :]
        start -= ref.shape[0]


def forward_kernel(heads, n_rows, orders, block_rows, meta, *refs):
    first = n_rows > 0
    refs = list(refs)
    take = lambda count: [refs.pop(0) for _ in range(count)]
    width = heads * HD
    total = 4 * TILE
    if first:
        (gain,) = take(1)
        sources = take(n_rows)
    else:
        normed, context_first, weight_first = take(3)
    pieces = take(len(orders))
    inverse, context, expo, weight, proj = take(5)
    if first:
        (normed,) = take(1)
    else:
        (partial,) = take(1)
    q_ext, k_ext, v_flip, sems, sems_more = take(5)
    copies = place(meta, pieces, orders, weight, block_rows, sems)
    outs = []

    def carry(source, dest):
        copy = pltpu.make_async_copy(source, dest, sems_more.at[len(outs)])
        copy.start()
        outs.append(copy)

    if first:
        (extra,) = take(1)
        starts = [sum(ref.shape[0] for ref in sources[:k]) for k in range(n_rows)]
        for start, source in zip(starts, sources):
            carry(source, extra.at[pl.ds(start, source.shape[0]), :])
        wait_all(outs)
        for block in range(4):
            rows = slice(block * TILE, (block + 1) * TILE)
            features = extra[rows, :].astype(F32)
            normed[rows, :] = (features * inverse_rms(features) * gain[...]).astype(BF)
    wait_all(copies)
    proj[...] = mm(normed[...], weight[...]).astype(BF)
    lanes = lax.broadcasted_iota(jnp.int32, (TILE, HD), 1)
    index = lax.broadcasted_iota(jnp.int32, (TILE, HD), 0)
    ones = jnp.where(lanes == 0, 1.0, 0.0).astype(BF)
    below = jnp.where(lax.broadcasted_iota(jnp.int32, (16, total), 0) == 0, 1.0, 0.0).astype(BF)
    for block in range(4):
        rows = slice(block * TILE, (block + 1) * TILE)
        usable = meta[8 + block] + index < meta[12]
        bias = jnp.where((lanes == 0) & ~usable, MASKED, 0.0).astype(BF)
        for head in range(heads):
            at = width + head * HD
            q_ext[head, rows, 0:HD] = proj[rows, at : at + HD]
            q_ext[head, rows, HD : 2 * HD] = ones
            at = 2 * width + head * HD
            k_ext[head, rows, 0:HD] = proj[rows, at : at + HD]
            k_ext[head, rows, HD : 2 * HD] = bias
    for head in range(heads):
        at = 3 * width + head * HD
        v_flip[head, 0:HD, :] = proj[:, at : at + HD].T
        v_flip[head, HD : HD + 16, :] = below
    inverse[...] = jnp.ones_like(inverse)
    for head in range(heads):
        for start in range(0, total, QUERY_ROWS):
            rows = slice(start, start + QUERY_ROWS)
            scores = mm_nt(k_ext[head], q_ext[head, rows, :])
            top = jnp.max(scores, axis=0, keepdims=True)
            raised = jnp.exp(scores - top).astype(BF)
            expo[head, :, rows] = raised
            mixed = mm(v_flip[head], raised)
            inv = 1.0 / mixed[HD : HD + 1, :]
            inverse[head : head + 1, rows] = inv
            context[rows, head * HD : (head + 1) * HD] = (mixed[0:HD, :] * inv).astype(BF).T
    if not first:
        partial[...] = (
            mm_nt(context_first[...], weight_first[:, 0:width])
            + mm_nt(context[...], weight[:, 0:width])
        ).astype(BF)


SMEM = pl.BlockSpec(memory_space=pltpu.SMEM)
VMEM = pl.BlockSpec(memory_space=pltpu.VMEM)
HBM = pl.BlockSpec(memory_space=pltpu.HBM)


def attention_forward(meta, heads, block_rows, pieces, orders, rows_in=(), gain=None, before=None):
    width = pieces[0].shape[1]
    model = rows_in[0].shape[1] if rows_in else before[0].shape[1]
    total = 4 * TILE
    rows = jax.ShapeDtypeStruct((total, model), BF)
    numerators = jax.ShapeDtypeStruct((heads, total, total), BF)
    if rows_in:
        in_fast, in_slow = [gain], [*rows_in, *pieces]
        more, extra = [rows], [pltpu.VMEM((total, model), BF)]
    else:
        in_fast, in_slow = [*before], [*pieces]
        more, extra = [rows], []
    return pl.pallas_call(
        functools.partial(forward_kernel, heads, len(rows_in), orders, block_rows),
        in_specs=[SMEM] + [VMEM] * len(in_fast) + [HBM] * len(in_slow),
        out_specs=[VMEM] * 6,
        out_shape=[
            jax.ShapeDtypeStruct((8, total), F32),
            jax.ShapeDtypeStruct((total, heads * HD), BF),
            numerators,
            jax.ShapeDtypeStruct((model, width), BF),
            jax.ShapeDtypeStruct((total, width), BF),
            *more,
        ],
        scratch_shapes=[
            pltpu.VMEM((heads, total, 2 * HD), BF),
            pltpu.VMEM((heads, total, 2 * HD), BF),
            pltpu.VMEM((heads, HD + 16, total), BF),
            pltpu.SemaphoreType.DMA((blocks_of(orders),)),
            pltpu.SemaphoreType.DMA((4,)),
            *extra,
        ],
        compiler_params=pltpu.CompilerParams(vmem_limit_bytes=ATTEND_LIMIT),
        cost_estimate=COST,
        name="attention_forward",
    )(meta, *in_fast, *in_slow)


def gelu_terms(gate):
    scale = 0.7978845608028654
    cube = 0.044715
    square = gate * gate
    bent = jnp.tanh(scale * gate * (1.0 + cube * square))
    half = 0.5 * (1.0 + bent)
    slope = half + 0.5 * gate * (1.0 - bent * bent) * (scale * (1.0 + 3.0 * cube * square))
    return gate * half, slope


def feed_kernel(n_rows, n_cots, in_orders, orders, block_rows, meta, *refs):
    first = n_rows > 0
    refs = list(refs)
    take = lambda count: [refs.pop(0) for _ in range(count)]
    if first:
        rows_in = take(n_rows)
        part_mine, part_other, gain = take(3)
    else:
        normed, result_before, back_before = take(3)
    cots = take(n_cots)
    pieces = take(len(in_orders))
    if first:
        normed, result, back = take(3)
    else:
        mine, other, back = take(3)
    groups = take(len(orders))
    weight, hidden, d_gate, d_up, cot, grad, sems = take(7)
    units = weight.shape[1] // 3
    copies = place(meta, pieces, in_orders, weight, block_rows, sems)
    for block in range(4):
        rows = slice(block * TILE, (block + 1) * TILE)
        cot[rows, :] = row_block(cots, block)
        if first:
            swapped = slice(((block + 2) % 4) * TILE, ((block + 2) % 4 + 1) * TILE)
            features = (
                row_block(rows_in, block).astype(F32)
                + part_mine[rows, :].astype(F32)
                + part_other[swapped, :].astype(F32)
            )
            features = features.astype(BF).astype(F32)
            normed[rows, :] = (features * inverse_rms(features) * gain[...]).astype(BF)
    wait_all(copies)
    for start in range(0, 4 * TILE, FEED_ROWS):
        rows = slice(start, start + FEED_ROWS)
        pre = mm(normed[rows, :], weight[:, 0 : 2 * units])
        act, slope = gelu_terms(pre[:, :units])
        up = pre[:, units:]
        low = (act * up).astype(BF)
        hidden[rows, :] = low
        d_hidden = mm(cot[rows, :], weight[:, 2 * units :])
        gate_low = (d_hidden * up * slope).astype(BF)
        up_low = (d_hidden * act).astype(BF)
        d_gate[rows, :] = gate_low
        d_up[rows, :] = up_low
        down = mm_nt(low, weight[:, 2 * units :])
        through = mm_nt(gate_low, weight[:, 0:units]) + mm_nt(up_low, weight[:, units : 2 * units])
        if first:
            result[rows, :] = down.astype(BF)
            back[rows, :] = through.astype(BF)
        else:
            down = (down + result_before[rows, :].astype(F32)).astype(BF)
            if start < 2 * TILE:
                mine[rows, :] = down[: 2 * TILE - start]
            if start + FEED_ROWS > 2 * TILE:
                begin = max(start - 2 * TILE, 0)
                other[begin : start + FEED_ROWS - 2 * TILE, :] = down[begin + 2 * TILE - start :]
            back[rows, :] = (through + back_before[rows, :].astype(F32)).astype(BF)
    grad[:, 2 * units :] = mm_tn(cot[...], hidden[...]).astype(BF)
    grad[:, 0:units] = mm_tn(normed[...], d_gate[...]).astype(BF)
    grad[:, units : 2 * units] = mm_tn(normed[...], d_up[...]).astype(BF)
    disperse(meta, grad, groups, orders, block_rows)


def feed_forward(meta, block_rows, cots, pieces, in_orders, orders, rows_in=(), before=()):
    width = pieces[0].shape[1]
    model = cots[0].shape[1]
    total = 4 * TILE
    units = width // 3
    full = jax.ShapeDtypeStruct((total, model), BF)
    half = jax.ShapeDtypeStruct((2 * TILE, model), BF)
    operands = [*rows_in, *before, *cots, *pieces]
    out_shape = [full, full, full] if rows_in else [half, half, full]
    out_shape += [
        jax.ShapeDtypeStruct((len(order) * block_rows, width), BF) for order in orders
    ]
    return pl.pallas_call(
        functools.partial(
            feed_kernel, len(rows_in), len(cots), in_orders, orders, block_rows
        ),
        in_specs=[SMEM] + [VMEM] * (len(operands) - len(pieces)) + [HBM] * len(pieces),
        out_specs=[VMEM] * len(out_shape),
        out_shape=out_shape,
        scratch_shapes=[
            pltpu.VMEM((model, width), BF),
            pltpu.VMEM((total, units), BF),
            pltpu.VMEM((total, units), BF),
            pltpu.VMEM((total, units), BF),
            pltpu.VMEM((total, model), BF),
            pltpu.VMEM((model, width), BF),
            pltpu.SemaphoreType.DMA((blocks_of(in_orders),)),
        ],
        compiler_params=pltpu.CompilerParams(vmem_limit_bytes=FEED_LIMIT),
        cost_estimate=COST,
        name="feed_forward",
    )(meta, *operands)


def middle_kernel(heads, n_rows, n_cots, *refs):
    refs = list(refs)
    take = lambda count: [refs.pop(0) for _ in range(count)]
    rows_in = take(n_rows)
    part_mine, part_other, gain = take(3)
    cots = take(n_cots)
    d_mine, d_other, context_near, context_far = take(4)
    weight_near, weight_far = take(2)
    d_middle, d_context_near, d_context_far, grad_near, grad_far, d_gain = take(6)
    (d_all,) = take(1)
    width = heads * HD
    gains = 0.0
    for block in range(4):
        rows = slice(block * TILE, (block + 1) * TILE)
        swapped = slice(((block + 2) % 4) * TILE, ((block + 2) % 4 + 1) * TILE)
        features = (
            row_block(rows_in, block).astype(F32)
            + part_mine[rows, :].astype(F32)
            + part_other[swapped, :].astype(F32)
        )
        features = features.astype(BF).astype(F32)
        inverse = inverse_rms(features)
        back = d_mine[rows, :].astype(F32) + d_other[swapped, :].astype(F32)
        scaled = back * gain[...]
        inner = jnp.mean(scaled * features, axis=-1, keepdims=True)
        result = (
            row_block(cots, block).astype(F32)
            + inverse * scaled
            - features * (inverse * inverse * inverse * inner)
        )
        d_all[rows, :] = result.astype(BF)
        if block < 2:
            d_middle[rows, :] = result
            gains += jnp.sum(back * features * inverse, axis=0, keepdims=True)
    d_gain[...] = jnp.broadcast_to(gains, d_gain.shape)
    d_context_near[...] = mm(d_all[...], weight_near[:, 0:width]).astype(BF)
    d_context_far[...] = mm(d_all[...], weight_far[:, 0:width]).astype(BF)
    grad_near[...] = mm_tn(d_all[...], context_near[...]).astype(BF)
    grad_far[...] = mm_tn(d_all[...], context_far[...]).astype(BF)


def middle_backward(heads, rows_in, parts, gain, cots, d_normed, contexts, weights):
    model = gain.shape[1]
    total = 4 * TILE
    width = heads * HD
    operands = [*rows_in, *parts, gain, *cots, *d_normed, *contexts, *weights]
    return pl.pallas_call(
        functools.partial(middle_kernel, heads, len(rows_in), len(cots)),
        in_specs=[VMEM] * len(operands),
        out_specs=[VMEM] * 6,
        out_shape=[
            jax.ShapeDtypeStruct((2 * TILE, model), F32),
            jax.ShapeDtypeStruct((total, width), BF),
            jax.ShapeDtypeStruct((total, width), BF),
            jax.ShapeDtypeStruct((model, width), BF),
            jax.ShapeDtypeStruct((model, width), BF),
            jax.ShapeDtypeStruct((8, model), F32),
        ],
        scratch_shapes=[
            pltpu.VMEM((total, model), BF),
        ],
        compiler_params=pltpu.CompilerParams(vmem_limit_bytes=MIDDLE_LIMIT),
        cost_estimate=COST,
        name="middle_backward",
    )(*operands)


def in_two(*rows):
    high = [row.astype(BF).astype(F32) for row in rows]
    index = lax.broadcasted_iota(jnp.int32, (16, rows[0].shape[1]), 0)
    result = jnp.zeros((16, rows[0].shape[1]), F32)
    for number, row in enumerate(rows):
        result = jnp.where(index == 2 * number, high[number], result)
        result = jnp.where(index == 2 * number + 1, row - high[number], result)
    return result.astype(BF)


def from_two(rows):
    return [
        rows[2 * k : 2 * k + 1].astype(F32) + rows[2 * k + 1 : 2 * k + 2].astype(F32)
        for k in range(2)
    ]


def finish_kernel(d_mine, d_other, keep, got, d_middle, gain, mine, theirs):
    for number, rows_in in enumerate((keep, got)):
        rows = slice(number * TILE, (number + 1) * TILE)
        features = rows_in[...].astype(F32)
        inverse = inverse_rms(features)
        scaled = (d_mine[rows, :].astype(F32) + d_other[rows, :].astype(F32)) * gain[...]
        inner = jnp.mean(scaled * features, axis=-1, keepdims=True)
        result = (
            d_middle[rows, :] + inverse * scaled - features * (inverse * inverse * inverse * inner)
        ).astype(BF)
        if number == 0:
            mine[...] = result
        else:
            theirs[...] = result


def backward_kernel(heads, orders, block_rows, last, meta, *refs):
    refs = list(refs)
    take = lambda count: [refs.pop(0) for _ in range(count)]
    inverse, context, expo, weight, proj, normed, d_context, grad_out = take(8)
    if last:
        gain, gain_rows = take(2)
    if last:
        (before,) = take(1)
        mine, other = take(2)
    else:
        (result,) = take(1)
    groups = take(len(orders))
    do_ext, v_ext, d_proj, grad = take(4)
    width = heads * HD
    total = 4 * TILE
    lanes = lax.broadcasted_iota(jnp.int32, (total, HD), 1)
    columns = inverse[...].T
    d_proj[:, 0:width] = jnp.zeros((total, width), BF)
    for head in range(heads):
        at = head * HD
        scaled = (d_context[:, at : at + HD].astype(F32) * columns[:, head : head + 1]).astype(BF)
        inner = -jnp.sum(
            scaled.astype(F32) * context[:, at : at + HD].astype(F32), axis=-1, keepdims=True
        )
        high = inner.astype(BF).astype(F32)
        do_ext[head, :, 0:HD] = scaled
        do_ext[head, :, HD : 2 * HD] = jnp.where(
            lanes == 0, high, jnp.where(lanes == 1, inner - high, 0.0)
        ).astype(BF)
    for head in range(heads):
        at = 3 * width + head * HD
        v_ext[head, :, 0:HD] = proj[:, at : at + HD]
        v_ext[head, :, HD : 2 * HD] = jnp.where(lanes < 2, 1.0, 0.0).astype(BF)
    for head in range(heads):
        q_at, k_at, v_at = (part * width + head * HD for part in (1, 2, 3))
        raised = expo[head]
        d_probs = mm_nt(v_ext[head], do_ext[head])
        d_scores = (raised.astype(F32) * d_probs).astype(BF)
        d_queries = mm(proj[:, k_at : k_at + HD].T, d_scores)
        d_keys = mm_nt(proj[:, q_at : q_at + HD].T, d_scores)
        d_values = mm_nt(do_ext[head, :, 0:HD].T, raised)
        d_proj[:, q_at : q_at + HD] = d_queries.astype(BF).T
        d_proj[:, k_at : k_at + HD] = d_keys.astype(BF).T
        d_proj[:, v_at : v_at + HD] = d_values.astype(BF).T
    grad[...] = mm_tn(normed[...], d_proj[...]).astype(BF)
    grad[:, 0:width] = grad_out[...]
    disperse(meta, grad, groups, orders, block_rows)
    through = mm_nt(d_proj[...], weight[...])
    if last:
        through = through + before[...].astype(F32)
        mine[...] = through[0 : 2 * TILE].astype(BF)
        other[...] = through[2 * TILE :].astype(BF)
        first = jnp.sum(through * normed[...].astype(F32), axis=0, keepdims=True) / gain[...]
        end = len(orders[-1]) * block_rows
        groups[-1][end : end + 16, :] = in_two(first, gain_rows[0:1, :])
    else:
        result[...] = through.astype(BF)


def attention_backward(
    meta, heads, block_rows, normed, saved, d_context, grad_out, orders, before=None
):
    last = before is not None
    weight, proj = saved[3:]
    model, width = weight.shape
    total = proj.shape[0]
    rows = jax.ShapeDtypeStruct((total, model), BF)
    in_fast = [*saved, normed, d_context, grad_out]
    scratch = [
        pltpu.VMEM((heads, total, 2 * HD), BF),
        pltpu.VMEM((heads, total, 2 * HD), BF),
        pltpu.VMEM((total, width), BF),
        pltpu.VMEM((model, width), BF),
    ]
    sizes = [len(order) * block_rows for order in orders]
    if last:
        in_fast += [*before[1:], before[0]]
        out_shape = [jax.ShapeDtypeStruct((2 * TILE, model), BF)] * 2
        sizes[-1] += 16
    else:
        out_shape = [rows]
    out_shape += [jax.ShapeDtypeStruct((size, width), BF) for size in sizes]
    return pl.pallas_call(
        functools.partial(backward_kernel, heads, orders, block_rows, last),
        in_specs=[SMEM] + [VMEM] * len(in_fast),
        out_specs=[VMEM] * len(out_shape),
        out_shape=out_shape,
        scratch_shapes=scratch,
        compiler_params=pltpu.CompilerParams(vmem_limit_bytes=BACK_LIMIT),
        cost_estimate=COST,
        name="attention_backward",
    )(meta, *in_fast)


def add(*terms):
    return sum(term.astype(F32) for term in terms)


def hold(values, *others):
    values, others = lax.optimization_barrier((values, others))
    return values, *others


def plus(*terms):
    return sum(term.astype(F32) for term in terms)


def call_local(kernel, out_shape, *operands):
    return pl.pallas_call(
        kernel,
        in_specs=[VMEM] * len(operands),
        out_specs=[VMEM] * len(out_shape),
        out_shape=[jax.ShapeDtypeStruct(shape, kind) for shape, kind in out_shape],
        compiler_params=pltpu.CompilerParams(vmem_limit_bytes=MIDDLE_LIMIT),
        cost_estimate=COST,
        name=kernel.__name__.replace("kernel", "backward"),
    )(*operands)


def join_kernel(own_high, x_high, y_high, y_low, xy_low, two, three, y_low_plus):
    rows = two.shape[0]
    for at, dest in ((slice(0, rows), two), (slice(rows, 2 * rows), three)):
        dest[...] = plus(own_high[at, :], x_high[at, :], y_high[at, :]).astype(BF)
    y_low_plus[...] = plus(y_low[...], xy_low[...]).astype(BF)


def meet_kernel(x_low, x_high, both_low, y_high, xy_high, message, y_high_plus):
    half = x_low.shape[0]
    message[0:half, :] = plus(x_low[...], both_low[half:, :]).astype(BF)
    message[half:, :] = x_high[...]
    y_high_plus[...] = plus(y_high[...], xy_high[...]).astype(BF)


def last_kernel(own_low, feed_x, feed_y, own, one):
    rows = own.shape[0]
    own[...] = plus(own_low[0:rows, :], feed_x[0:rows, :], feed_y[0:rows, :])
    one[...] = plus(own_low[rows:, :], feed_x[rows:, :], feed_y[rows:, :]).astype(BF)


def fold_kernel(own_low, own_high, x_high, over_x, both_low, y_high, total, gains, *messages):
    rows = total.shape[0]
    end = 4 * rows
    mine = from_two(x_high[2 * rows : 2 * rows + 16, :])
    theirs = from_two(over_x[end : end + 16, :])
    pairs = in_two(*(a + b for a, b in zip(mine, theirs)))
    gains[...] = pairs.astype(F32)
    for index in range(4):
        at = slice((index % 2) * rows, (index % 2 + 1) * rows)
        block = plus(
            (own_low if index < 2 else own_high)[at, :],
            over_x[index * rows : (index + 1) * rows, :],
            (both_low if index < 2 else y_high)[at, :],
        )
        if index == 0:
            total[...] = block
        else:
            messages[index - 1][0:rows, :] = block.astype(BF)
            messages[index - 1][rows:, :] = pairs


class Links:
    def __init__(self, wide, narrow):
        self.wide, self.narrow = wide, narrow
        self.planes = wide // 2
        self.staged = wide == 8

    def y(self, values):
        return lax.ppermute(values, "narrow", [(i, (i + 2) % 4) for i in range(4)])

    def core(self, values):
        return lax.ppermute(values, "narrow", [(i, i ^ 1) for i in range(4)])

    def across(self, values):
        return lax.ppermute(values, "narrow", [(i, (i + 2) % 4 ^ 1) for i in range(4)])

    def x(self, values):
        return lax.ppermute(values, "wide", [(i, i ^ 1) for i in range(self.wide)])

    def z(self, values, ahead):
        turn = lambda i: ((i // 2 + ahead) % self.planes) * 2 + i % 2
        return lax.ppermute(values, "wide", [(i, turn(i)) for i in range(self.wide)])

    def whole_gather(self, piece):
        near = lax.all_gather(piece, "wide", axis=0, tiled=True)
        return [near], [self.y(near)]

    def whole_reduce(self, near, far):
        return lax.psum_scatter(near, "wide", scatter_dimension=0, tiled=True).astype(
            F32
        ) + lax.psum_scatter(self.y(far), "wide", scatter_dimension=0, tiled=True).astype(F32)


def on_device(
    tokens,
    lengths,
    norm_one,
    w_query,
    w_key,
    w_value,
    w_out,
    norm_two,
    w_gate,
    w_up,
    w_down,
    cotangent,
):
    model = tokens.shape[-1]
    wide, narrow = lax.axis_size("wide"), lax.axis_size("narrow")
    links = Links(wide, narrow)
    heads = w_query.shape[1] // HD
    head_width = heads * HD
    units = w_gate.shape[1]
    at_wide, at_narrow = lax.axis_index("wide"), lax.axis_index("narrow")
    y, c = at_narrow >> 1, at_narrow & 1
    x, z = at_wide & 1, at_wide >> 1

    staged = links.staged
    planes = links.planes
    rows = model // wide
    turned = [((z + k) & (planes - 1)) * 2 + (x ^ side) for side in range(2) for k in range(4)]
    blocks = [((y ^ far) * 2 + (c ^ side)) * TILE for side in range(2) for far in range(2)]
    length = lax.dynamic_index_in_dim(lengths, y, 0, keepdims=False)[0]
    numbers = [
        *(spot * rows for spot in turned),
        *blocks,
        length,
    ]
    meta = jnp.stack([jnp.asarray(number, jnp.int32) for number in numbers])
    first_item = y == 0

    gain_one = norm_one.reshape(1, model)
    gain_two = norm_two.reshape(1, model)

    def keep_give(rows):
        flat = rows.reshape(2, TILE, model)
        return (
            lax.dynamic_index_in_dim(flat, y, 0, keepdims=False),
            lax.dynamic_index_in_dim(flat, 1 - y, 0, keepdims=False),
        )

    attn_piece = jnp.concatenate([w_out.T, w_query, w_key, w_value], axis=1)
    feed_piece = jnp.concatenate([w_gate, w_up, w_down.T], axis=1)
    keep, give = keep_give(tokens)
    keep_cot, give_cot = keep_give(cotangent)
    half = planes // 2 * rows
    if staged:
        block_rows = rows
        quarters = ((0, 1), (2, 3), (4, 5), (6, 7))
        attn_near_in = attn_far_in = ((0, 1, 2, 3), (4, 5, 6, 7))
        feed_near_in = ((0,), (1,), (3,), (2,), (4, 5, 7), (6,))
        feed_far_in = ((0, 1, 3), (2,), (4, 5), (7, 6))
        attn_far_out = ((0, 1, 4, 5), (2, 3), (6, 7))
    else:
        block_rows = model
        quarters = attn_far_out = ((0,),)
        attn_near_in = attn_far_in = feed_near_in = feed_far_in = ((0,),)

    got = links.y(give)
    if staged:
        column = [attn_piece] + [links.z(attn_piece, planes - k) for k in range(1, planes)]
        column = jnp.concatenate(column, axis=0)
        over_x, over_y = links.x(column), links.y(column)
        feed_piece, column, first_item = hold(feed_piece, column, first_item)
        feed_one = links.z(feed_piece, planes - 1)
        feed_three = links.z(feed_piece, planes - 3)
    else:
        attn_near, attn_far = links.whole_gather(attn_piece)
        feed_near, feed_far = links.whole_gather(feed_piece)
    from_keep = links.core(keep)
    if staged:
        got, feed_one, feed_three = hold(got, feed_one, feed_three)
    rows_in = [keep, got, from_keep, links.core(got)]
    if staged:
        over_y, over_x = hold(over_y, over_x)
        give_cot, over_y = hold(give_cot, over_y)
        attn_near = [column, over_x]
        rows_in, over_y, meta = hold(rows_in, over_y, meta)
        attn_far = [over_y, links.x(over_y)]
        three = jnp.concatenate([feed_piece, feed_one, feed_three], axis=0)
        feed_x = links.x(three)
        feed_y = links.y(three)
        feed_piece, feed_one = hold(feed_piece, feed_one)
        feed_two = links.z(feed_piece, planes - 2)
    got_cot = links.y(give_cot)

    inv_near, context_near, expo_near, *kept_near, normed = attention_forward(
        meta, heads, block_rows, attn_near, attn_near_in, rows_in=rows_in, gain=gain_one
    )
    if staged:
        normed, feed_two, attn_far = hold(normed, feed_two, attn_far)
        feed_x_two = links.x(feed_two)
        feed_y_two = links.y(feed_two)
    inv_far, context_far, expo_far, *kept_far, part_mine = attention_forward(
        meta, heads, block_rows, attn_far, attn_far_in,
        before=(normed, context_near, kept_near[0]),
    )
    if staged:
        part_mine, got_cot, feed_x, feed_y, feed_x_two, feed_y_two = hold(
            part_mine, got_cot, feed_x, feed_y, feed_x_two, feed_y_two
        )
    part_other = links.core(part_mine)
    own_cot = jnp.concatenate([keep_cot, got_cot], axis=0)
    cots = [own_cot, links.core(own_cot)]
    if staged:
        feed_near = [feed_piece, feed_one, feed_three, feed_two, feed_x, feed_x_two]
        feed_far = [
            feed_y,
            feed_y_two,
            links.y(feed_x[: 2 * rows]),
            links.x(jnp.concatenate([feed_y[2 * rows :], feed_y_two], axis=0)),
        ]
    parts = (part_mine, part_other)

    normed_two, down_near, back_near, *near = feed_forward(
        meta, block_rows, cots, feed_near, feed_near_in, quarters, rows_in=rows_in,
        before=(*parts, gain_two),
    )
    if staged:
        own_low, own_high, x_low, x_high = near
        from_x_high = links.x(x_high)
    mlp_mine, mlp_other, d_mine, *far = feed_forward(
        meta, block_rows, cots, feed_far, feed_far_in, quarters,
        before=(normed_two, down_near, back_near),
    )
    if staged:
        mlp_other, from_x_high = hold(mlp_other, from_x_high)
        y_low, y_high, xy_low, xy_high = far
        from_xy_high = links.x(xy_high)
    else:
        feed_grad = links.whole_reduce(*near, *far)
    d_other = links.core(d_mine)
    half_rows = 2 * TILE
    output = (
        jnp.concatenate(rows_in[:2], axis=0).astype(F32)
        + part_mine[:half_rows].astype(F32)
        + part_other[half_rows:].astype(F32)
        + mlp_mine.astype(F32)
        + links.core(mlp_other).astype(F32)
    ).astype(BF)
    output_back = links.y(output[TILE:])
    d_middle, d_context_near, d_context_far, out_near, out_far, gain_rows = middle_backward(
        heads,
        rows_in,
        parts,
        gain_two,
        cots,
        (d_mine, d_other),
        (context_near, context_far),
        (kept_near[0], kept_far[0]),
    )
    if staged:
        d_context_far, from_xy_high, output_back = hold(d_context_far, from_xy_high, output_back)
        xy_low, from_xy_high = hold(xy_low, from_xy_high)
        from_y_high = links.y(add(y_high, from_xy_high).astype(BF))
        from_xy_low = links.x(xy_low)
    d_first, *far = attention_backward(
        meta, heads, block_rows, normed, (inv_far, context_far, expo_far, *kept_far),
        d_context_far, out_far, attn_far_out,
    )
    if staged:
        d_first, from_y_high, from_xy_low = hold(d_first, from_y_high, from_xy_low)
        x_low, from_xy_low = hold(x_low, from_xy_low)
        feed = (rows, feed_piece.shape[1])
        feed_half = (half, feed_piece.shape[1])
        feed_two, feed_three, feed_y_low = call_local(
            join_kernel, [(feed, BF), (feed, BF), (feed_half, BF)],
            own_high, from_x_high, from_y_high, y_low, from_xy_low,
        )
        feed_two = links.z(feed_two, 2)
        feed_low = own_low
        both_low, y_high, xy_high = far
        from_both_low = links.y(both_low)
        from_xy_high = links.x(xy_high)
        from_feed_x, from_feed_y = links.x(x_low), links.y(feed_y_low)
    last_mine, last_other, *near = attention_backward(
        meta, heads, block_rows, normed, (inv_near, context_near, expo_near, *kept_near),
        d_context_near, out_near, quarters, before=(d_first, gain_one, gain_rows),
    )
    if staged:
        last_other, near, from_both_low, from_xy_high, feed_two = hold(
            last_other, near, from_both_low, from_xy_high, feed_two
        )
        own_low, own_high, x_low, x_high = near
        width = x_low.shape[1]
        message, y_high = call_local(
            meet_kernel, [((2 * half + 16, width), BF), ((half, width), BF)],
            x_low, x_high, from_both_low, y_high, from_xy_high,
        )
        from_x, from_y_high = links.x(message), links.y(y_high)
        feed_parts = [feed_two, links.z(feed_three, 3)]
        last_mine, from_feed_x, from_feed_y = hold(last_mine, from_feed_x, from_feed_y)
    else:
        attn_grad = links.whole_reduce(near[0][:model], *far)
        gains = near[0][model:]
    mine, theirs = call_local(
        finish_kernel,
        [((TILE, model), BF)] * 2,
        last_mine, links.core(last_other), *rows_in[:2], d_middle, gain_one,
    )
    if staged:
        feed_own, feed_one = call_local(
            last_kernel, [(feed, F32), (feed, BF)], feed_low, from_feed_x, from_feed_y
        )
        feed_parts.append(links.z(feed_one, 1))
        from_x, theirs, feed_own = hold(from_x, theirs, feed_own)
    back = links.y(theirs)
    if staged:
        attn = (rows, width)
        apart = ((rows + 16, width), BF)
        attn_grad, gains, *messages = call_local(
            fold_kernel, [(attn, F32), ((16, width), F32), apart, apart, apart],
            own_low, own_high, x_high, from_x, from_both_low, from_y_high,
        )
        arrived = [links.z(piece, k + 1) for k, piece in enumerate(messages)]
        attn_grad = add(attn_grad, *(part[:rows] for part in arrived))
        gains = add(gains, *(part[rows:] for part in arrived))
        gains, back = hold(gains, back)
        feed_grad = add(feed_own, *feed_parts)
    else:
        gains = lax.psum(gains.astype(F32), "wide")
    gains = (gains + links.core(gains)) + (links.y(gains) + links.across(gains))

    def in_order(own, other):
        stacked = jnp.where(first_item, jnp.stack([own, other]), jnp.stack([other, own]))
        return stacked.reshape(tokens.shape)

    return (
        in_order(output[:TILE], output_back),
        in_order(mine, back),
        gains[0] + gains[1],
        attn_grad[:, head_width : 2 * head_width],
        attn_grad[:, 2 * head_width : 3 * head_width],
        attn_grad[:, 3 * head_width :],
        attn_grad[:, :head_width].T,
        gains[2] + gains[3],
        feed_grad[:, :units],
        feed_grad[:, units : 2 * units],
        feed_grad[:, 2 * units :].T,
    )


def solution(mesh):
    in_specs = (
        P(None, "wide", "narrow", None),
        P(None, "wide"),
        P(),
        P("wide", "narrow"),
        P("wide", "narrow"),
        P("wide", "narrow"),
        P("narrow", "wide"),
        P(),
        P("wide", "narrow"),
        P("wide", "narrow"),
        P("narrow", "wide"),
        P(None, "wide", "narrow", None),
    )
    out_specs = (
        P(None, "wide", "narrow", None),
        P(None, "wide", "narrow", None),
        P(),
        P("wide", "narrow"),
        P("wide", "narrow"),
        P("wide", "narrow"),
        P("narrow", "wide"),
        P(),
        P("wide", "narrow"),
        P("wide", "narrow"),
        P("narrow", "wide"),
    )
    return jax.shard_map(
        on_device, mesh=mesh, in_specs=in_specs, out_specs=out_specs, check_vma=False
    )
```

```python
import functools

import jax
import jax.numpy as jnp
from jax import lax
from jax.experimental import pallas as pl
from jax.experimental.pallas import tpu as pltpu
from jax.sharding import PartitionSpec as P

HD = 64
EPSILON = 1e-06
MASKED = -1e30
TILE = 256
FEED_ROWS = 1024
QUERY_ROWS = 1024
MIDDLE_LIMIT = 8 * 1024 * 1024
BACK_LIMIT = 14 * 1024 * 1024
ATTEND_LIMIT = 11 * 1024 * 1024
FEED_LIMIT = 22 * 1024 * 1024
COST = pl.CostEstimate(flops=10**6, bytes_accessed=10**5, transcendentals=0)
BF = jnp.bfloat16
F32 = jnp.float32


def mm(left, right):
    return jnp.dot(left, right, preferred_element_type=F32)


def mm_nt(left, right):
    return lax.dot_general(left, right, (((1,), (1,)), ((), ())), preferred_element_type=F32)


def mm_tn(left, right):
    return lax.dot_general(left, right, (((0,), (0,)), ((), ())), preferred_element_type=F32)


def inverse_rms(features):
    return lax.rsqrt(jnp.mean(features * features, axis=-1, keepdims=True) + EPSILON)


def place(meta, pieces, orders, dest, rows, sems):
    copies = []
    for piece, order in zip(pieces, orders):
        for number, index in enumerate(order):
            at = 0 if rows == dest.shape[0] else pl.multiple_of(meta[index], 16)
            copy = pltpu.make_async_copy(
                piece.at[pl.ds(number * rows, rows), :],
                dest.at[pl.ds(at, rows), :],
                sems.at[len(copies)],
            )
            copy.start()
            copies.append(copy)
    return copies


def wait_all(copies):
    for copy in copies:
        copy.wait()


def blocks_of(orders):
    return sum(len(order) for order in orders)


def disperse(meta, source, groups, orders, rows):
    for group, order in zip(groups, orders):
        for place, index in enumerate(order):
            at = 0 if rows == source.shape[0] else pl.multiple_of(meta[index], 16)
            group[place * rows : (place + 1) * rows, :] = source[pl.ds(at, rows), :]


def row_block(refs, block):
    start = block * TILE
    for ref in refs:
        if start < ref.shape[0]:
            return ref[start : start + TILE, :]
        start -= ref.shape[0]


def forward_kernel(heads, n_rows, orders, block_rows, meta, *refs):
    first = n_rows > 0
    refs = list(refs)
    take = lambda count: [refs.pop(0) for _ in range(count)]
    width = heads * HD
    total = 4 * TILE
    if first:
        (gain,) = take(1)
        sources = take(n_rows)
    else:
        normed, context_first, weight_first = take(3)
    pieces = take(len(orders))
    inverse, context, expo, weight, proj = take(5)
    if first:
        (normed,) = take(1)
    else:
        (partial,) = take(1)
    q_ext, k_ext, v_flip, sems, sems_more = take(5)
    copies = place(meta, pieces, orders, weight, block_rows, sems)
    outs = []

    def carry(source, dest):
        copy = pltpu.make_async_copy(source, dest, sems_more.at[len(outs)])
        copy.start()
        outs.append(copy)

    if first:
        (extra,) = take(1)
        starts = [sum(ref.shape[0] for ref in sources[:k]) for k in range(n_rows)]
        for start, source in zip(starts, sources):
            carry(source, extra.at[pl.ds(start, source.shape[0]), :])
        wait_all(outs)
        for block in range(4):
            rows = slice(block * TILE, (block + 1) * TILE)
            features = extra[rows, :].astype(F32)
            normed[rows, :] = (features * inverse_rms(features) * gain[...]).astype(BF)
    wait_all(copies)
    proj[...] = mm(normed[...], weight[...]).astype(BF)
    lanes = lax.broadcasted_iota(jnp.int32, (TILE, HD), 1)
    index = lax.broadcasted_iota(jnp.int32, (TILE, HD), 0)
    ones = jnp.where(lanes == 0, 1.0, 0.0).astype(BF)
    below = jnp.where(lax.broadcasted_iota(jnp.int32, (16, total), 0) == 0, 1.0, 0.0).astype(BF)
    for block in range(4):
        rows = slice(block * TILE, (block + 1) * TILE)
        usable = meta[8 + block] + index < meta[12]
        bias = jnp.where((lanes == 0) & ~usable, MASKED, 0.0).astype(BF)
        for head in range(heads):
            at = width + head * HD
            q_ext[head, rows, 0:HD] = proj[rows, at : at + HD]
            q_ext[head, rows, HD : 2 * HD] = ones
            at = 2 * width + head * HD
            k_ext[head, rows, 0:HD] = proj[rows, at : at + HD]
            k_ext[head, rows, HD : 2 * HD] = bias
    for head in range(heads):
        at = 3 * width + head * HD
        v_flip[head, 0:HD, :] = proj[:, at : at + HD].T
        v_flip[head, HD : HD + 16, :] = below
    inverse[...] = jnp.ones_like(inverse)
    for head in range(heads):
        for start in range(0, total, QUERY_ROWS):
            rows = slice(start, start + QUERY_ROWS)
            scores = mm_nt(k_ext[head], q_ext[head, rows, :])
            top = jnp.max(scores, axis=0, keepdims=True)
            raised = jnp.exp(scores - top).astype(BF)
            expo[head, :, rows] = raised
            mixed = mm(v_flip[head], raised)
            inv = 1.0 / mixed[HD : HD + 1, :]
            inverse[head : head + 1, rows] = inv
            context[rows, head * HD : (head + 1) * HD] = (mixed[0:HD, :] * inv).astype(BF).T
    if not first:
        partial[...] = (
            mm_nt(context_first[...], weight_first[:, 0:width])
            + mm_nt(context[...], weight[:, 0:width])
        ).astype(BF)


SMEM = pl.BlockSpec(memory_space=pltpu.SMEM)
VMEM = pl.BlockSpec(memory_space=pltpu.VMEM)
HBM = pl.BlockSpec(memory_space=pltpu.HBM)


def attention_forward(meta, heads, block_rows, pieces, orders, rows_in=(), gain=None, before=None):
    width = pieces[0].shape[1]
    model = rows_in[0].shape[1] if rows_in else before[0].shape[1]
    total = 4 * TILE
    rows = jax.ShapeDtypeStruct((total, model), BF)
    numerators = jax.ShapeDtypeStruct((heads, total, total), BF)
    if rows_in:
        in_fast, in_slow = [gain], [*rows_in, *pieces]
        more, extra = [rows], [pltpu.VMEM((total, model), BF)]
    else:
        in_fast, in_slow = [*before], [*pieces]
        more, extra = [rows], []
    return pl.pallas_call(
        functools.partial(forward_kernel, heads, len(rows_in), orders, block_rows),
        in_specs=[SMEM] + [VMEM] * len(in_fast) + [HBM] * len(in_slow),
        out_specs=[VMEM] * 6,
        out_shape=[
            jax.ShapeDtypeStruct((8, total), F32),
            jax.ShapeDtypeStruct((total, heads * HD), BF),
            numerators,
            jax.ShapeDtypeStruct((model, width), BF),
            jax.ShapeDtypeStruct((total, width), BF),
            *more,
        ],
        scratch_shapes=[
            pltpu.VMEM((heads, total, 2 * HD), BF),
            pltpu.VMEM((heads, total, 2 * HD), BF),
            pltpu.VMEM((heads, HD + 16, total), BF),
            pltpu.SemaphoreType.DMA((blocks_of(orders),)),
            pltpu.SemaphoreType.DMA((4,)),
            *extra,
        ],
        compiler_params=pltpu.CompilerParams(vmem_limit_bytes=ATTEND_LIMIT),
        cost_estimate=COST,
        name="attention_forward",
    )(meta, *in_fast, *in_slow)


def gelu_terms(gate):
    scale = 0.7978845608028654
    cube = 0.044715
    square = gate * gate
    bent = jnp.tanh(scale * gate * (1.0 + cube * square))
    half = 0.5 * (1.0 + bent)
    slope = half + 0.5 * gate * (1.0 - bent * bent) * (scale * (1.0 + 3.0 * cube * square))
    return gate * half, slope


def feed_kernel(n_rows, n_cots, in_orders, orders, block_rows, meta, *refs):
    first = n_rows > 0
    refs = list(refs)
    take = lambda count: [refs.pop(0) for _ in range(count)]
    if first:
        rows_in = take(n_rows)
        part_mine, part_other, gain = take(3)
    else:
        normed, result_before, back_before = take(3)
    cots = take(n_cots)
    pieces = take(len(in_orders))
    if first:
        normed, result, back = take(3)
    else:
        mine, other, back = take(3)
    groups = take(len(orders))
    weight, hidden, d_gate, d_up, cot, grad, sems = take(7)
    units = weight.shape[1] // 3
    copies = place(meta, pieces, in_orders, weight, block_rows, sems)
    for block in range(4):
        rows = slice(block * TILE, (block + 1) * TILE)
        cot[rows, :] = row_block(cots, block)
        if first:
            swapped = slice(((block + 2) % 4) * TILE, ((block + 2) % 4 + 1) * TILE)
            features = (
                row_block(rows_in, block).astype(F32)
                + part_mine[rows, :].astype(F32)
                + part_other[swapped, :].astype(F32)
            )
            features = features.astype(BF).astype(F32)
            normed[rows, :] = (features * inverse_rms(features) * gain[...]).astype(BF)
    wait_all(copies)
    for start in range(0, 4 * TILE, FEED_ROWS):
        rows = slice(start, start + FEED_ROWS)
        pre = mm(normed[rows, :], weight[:, 0 : 2 * units])
        act, slope = gelu_terms(pre[:, :units])
        up = pre[:, units:]
        low = (act * up).astype(BF)
        hidden[rows, :] = low
        d_hidden = mm(cot[rows, :], weight[:, 2 * units :])
        gate_low = (d_hidden * up * slope).astype(BF)
        up_low = (d_hidden * act).astype(BF)
        d_gate[rows, :] = gate_low
        d_up[rows, :] = up_low
        down = mm_nt(low, weight[:, 2 * units :])
        through = mm_nt(gate_low, weight[:, 0:units]) + mm_nt(up_low, weight[:, units : 2 * units])
        if first:
            result[rows, :] = down.astype(BF)
            back[rows, :] = through.astype(BF)
        else:
            down = (down + result_before[rows, :].astype(F32)).astype(BF)
            if start < 2 * TILE:
                mine[rows, :] = down[: 2 * TILE - start]
            if start + FEED_ROWS > 2 * TILE:
                begin = max(start - 2 * TILE, 0)
                other[begin : start + FEED_ROWS - 2 * TILE, :] = down[begin + 2 * TILE - start :]
            back[rows, :] = (through + back_before[rows, :].astype(F32)).astype(BF)
    grad[:, 2 * units :] = mm_tn(cot[...], hidden[...]).astype(BF)
    grad[:, 0:units] = mm_tn(normed[...], d_gate[...]).astype(BF)
    grad[:, units : 2 * units] = mm_tn(normed[...], d_up[...]).astype(BF)
    disperse(meta, grad, groups, orders, block_rows)


def feed_forward(meta, block_rows, cots, pieces, in_orders, orders, rows_in=(), before=()):
    width = pieces[0].shape[1]
    model = cots[0].shape[1]
    total = 4 * TILE
    units = width // 3
    full = jax.ShapeDtypeStruct((total, model), BF)
    half = jax.ShapeDtypeStruct((2 * TILE, model), BF)
    operands = [*rows_in, *before, *cots, *pieces]
    out_shape = [full, full, full] if rows_in else [half, half, full]
    out_shape += [
        jax.ShapeDtypeStruct((len(order) * block_rows, width), BF) for order in orders
    ]
    return pl.pallas_call(
        functools.partial(
            feed_kernel, len(rows_in), len(cots), in_orders, orders, block_rows
        ),
        in_specs=[SMEM] + [VMEM] * (len(operands) - len(pieces)) + [HBM] * len(pieces),
        out_specs=[VMEM] * len(out_shape),
        out_shape=out_shape,
        scratch_shapes=[
            pltpu.VMEM((model, width), BF),
            pltpu.VMEM((total, units), BF),
            pltpu.VMEM((total, units), BF),
            pltpu.VMEM((total, units), BF),
            pltpu.VMEM((total, model), BF),
            pltpu.VMEM((model, width), BF),
            pltpu.SemaphoreType.DMA((blocks_of(in_orders),)),
        ],
        compiler_params=pltpu.CompilerParams(vmem_limit_bytes=FEED_LIMIT),
        cost_estimate=COST,
        name="feed_forward",
    )(meta, *operands)


def middle_kernel(heads, n_rows, n_cots, *refs):
    refs = list(refs)
    take = lambda count: [refs.pop(0) for _ in range(count)]
    rows_in = take(n_rows)
    part_mine, part_other, gain = take(3)
    cots = take(n_cots)
    d_mine, d_other, context_near, context_far = take(4)
    weight_near, weight_far = take(2)
    d_middle, d_context_near, d_context_far, grad_near, grad_far, d_gain = take(6)
    (d_all,) = take(1)
    width = heads * HD
    gains = 0.0
    for block in range(4):
        rows = slice(block * TILE, (block + 1) * TILE)
        swapped = slice(((block + 2) % 4) * TILE, ((block + 2) % 4 + 1) * TILE)
        features = (
            row_block(rows_in, block).astype(F32)
            + part_mine[rows, :].astype(F32)
            + part_other[swapped, :].astype(F32)
        )
        features = features.astype(BF).astype(F32)
        inverse = inverse_rms(features)
        back = d_mine[rows, :].astype(F32) + d_other[swapped, :].astype(F32)
        scaled = back * gain[...]
        inner = jnp.mean(scaled * features, axis=-1, keepdims=True)
        result = (
            row_block(cots, block).astype(F32)
            + inverse * scaled
            - features * (inverse * inverse * inverse * inner)
        )
        d_all[rows, :] = result.astype(BF)
        if block < 2:
            d_middle[rows, :] = result
            gains += jnp.sum(back * features * inverse, axis=0, keepdims=True)
    d_gain[...] = jnp.broadcast_to(gains, d_gain.shape)
    d_context_near[...] = mm(d_all[...], weight_near[:, 0:width]).astype(BF)
    d_context_far[...] = mm(d_all[...], weight_far[:, 0:width]).astype(BF)
    grad_near[...] = mm_tn(d_all[...], context_near[...]).astype(BF)
    grad_far[...] = mm_tn(d_all[...], context_far[...]).astype(BF)


def middle_backward(heads, rows_in, parts, gain, cots, d_normed, contexts, weights):
    model = gain.shape[1]
    total = 4 * TILE
    width = heads * HD
    operands = [*rows_in, *parts, gain, *cots, *d_normed, *contexts, *weights]
    return pl.pallas_call(
        functools.partial(middle_kernel, heads, len(rows_in), len(cots)),
        in_specs=[VMEM] * len(operands),
        out_specs=[VMEM] * 6,
        out_shape=[
            jax.ShapeDtypeStruct((2 * TILE, model), F32),
            jax.ShapeDtypeStruct((total, width), BF),
            jax.ShapeDtypeStruct((total, width), BF),
            jax.ShapeDtypeStruct((model, width), BF),
            jax.ShapeDtypeStruct((model, width), BF),
            jax.ShapeDtypeStruct((8, model), F32),
        ],
        scratch_shapes=[
            pltpu.VMEM((total, model), BF),
        ],
        compiler_params=pltpu.CompilerParams(vmem_limit_bytes=MIDDLE_LIMIT),
        cost_estimate=COST,
        name="middle_backward",
    )(*operands)


def in_two(*rows):
    high = [row.astype(BF).astype(F32) for row in rows]
    index = lax.broadcasted_iota(jnp.int32, (16, rows[0].shape[1]), 0)
    result = jnp.zeros((16, rows[0].shape[1]), F32)
    for number, row in enumerate(rows):
        result = jnp.where(index == 2 * number, high[number], result)
        result = jnp.where(index == 2 * number + 1, row - high[number], result)
    return result.astype(BF)


def from_two(rows):
    return [
        rows[2 * k : 2 * k + 1].astype(F32) + rows[2 * k + 1 : 2 * k + 2].astype(F32)
        for k in range(2)
    ]


def finish_kernel(d_mine, d_other, keep, got, d_middle, gain, mine, theirs):
    for number, rows_in in enumerate((keep, got)):
        rows = slice(number * TILE, (number + 1) * TILE)
        features = rows_in[...].astype(F32)
        inverse = inverse_rms(features)
        scaled = (d_mine[rows, :].astype(F32) + d_other[rows, :].astype(F32)) * gain[...]
        inner = jnp.mean(scaled * features, axis=-1, keepdims=True)
        result = (
            d_middle[rows, :] + inverse * scaled - features * (inverse * inverse * inverse * inner)
        ).astype(BF)
        if number == 0:
            mine[...] = result
        else:
            theirs[...] = result


def backward_kernel(heads, orders, block_rows, last, meta, *refs):
    refs = list(refs)
    take = lambda count: [refs.pop(0) for _ in range(count)]
    inverse, context, expo, weight, proj, normed, d_context, grad_out = take(8)
    if last:
        gain, gain_rows = take(2)
    if last:
        (before,) = take(1)
        mine, other = take(2)
    else:
        (result,) = take(1)
    groups = take(len(orders))
    do_ext, v_ext, d_proj, grad = take(4)
    width = heads * HD
    total = 4 * TILE
    lanes = lax.broadcasted_iota(jnp.int32, (total, HD), 1)
    columns = inverse[...].T
    d_proj[:, 0:width] = jnp.zeros((total, width), BF)
    for head in range(heads):
        at = head * HD
        scaled = (d_context[:, at : at + HD].astype(F32) * columns[:, head : head + 1]).astype(BF)
        inner = -jnp.sum(
            scaled.astype(F32) * context[:, at : at + HD].astype(F32), axis=-1, keepdims=True
        )
        high = inner.astype(BF).astype(F32)
        do_ext[head, :, 0:HD] = scaled
        do_ext[head, :, HD : 2 * HD] = jnp.where(
            lanes == 0, high, jnp.where(lanes == 1, inner - high, 0.0)
        ).astype(BF)
    for head in range(heads):
        at = 3 * width + head * HD
        v_ext[head, :, 0:HD] = proj[:, at : at + HD]
        v_ext[head, :, HD : 2 * HD] = jnp.where(lanes < 2, 1.0, 0.0).astype(BF)
    for head in range(heads):
        q_at, k_at, v_at = (part * width + head * HD for part in (1, 2, 3))
        raised = expo[head]
        d_probs = mm_nt(v_ext[head], do_ext[head])
        d_scores = (raised.astype(F32) * d_probs).astype(BF)
        d_queries = mm(proj[:, k_at : k_at + HD].T, d_scores)
        d_keys = mm_nt(proj[:, q_at : q_at + HD].T, d_scores)
        d_values = mm_nt(do_ext[head, :, 0:HD].T, raised)
        d_proj[:, q_at : q_at + HD] = d_queries.astype(BF).T
        d_proj[:, k_at : k_at + HD] = d_keys.astype(BF).T
        d_proj[:, v_at : v_at + HD] = d_values.astype(BF).T
    grad[...] = mm_tn(normed[...], d_proj[...]).astype(BF)
    grad[:, 0:width] = grad_out[...]
    disperse(meta, grad, groups, orders, block_rows)
    through = mm_nt(d_proj[...], weight[...])
    if last:
        through = through + before[...].astype(F32)
        mine[...] = through[0 : 2 * TILE].astype(BF)
        other[...] = through[2 * TILE :].astype(BF)
        first = jnp.sum(through * normed[...].astype(F32), axis=0, keepdims=True) / gain[...]
        end = len(orders[-1]) * block_rows
        groups[-1][end : end + 16, :] = in_two(first, gain_rows[0:1, :])
    else:
        result[...] = through.astype(BF)


def attention_backward(
    meta, heads, block_rows, normed, saved, d_context, grad_out, orders, before=None
):
    last = before is not None
    weight, proj = saved[3:]
    model, width = weight.shape
    total = proj.shape[0]
    rows = jax.ShapeDtypeStruct((total, model), BF)
    in_fast = [*saved, normed, d_context, grad_out]
    scratch = [
        pltpu.VMEM((heads, total, 2 * HD), BF),
        pltpu.VMEM((heads, total, 2 * HD), BF),
        pltpu.VMEM((total, width), BF),
        pltpu.VMEM((model, width), BF),
    ]
    sizes = [len(order) * block_rows for order in orders]
    if last:
        in_fast += [*before[1:], before[0]]
        out_shape = [jax.ShapeDtypeStruct((2 * TILE, model), BF)] * 2
        sizes[-1] += 16
    else:
        out_shape = [rows]
    out_shape += [jax.ShapeDtypeStruct((size, width), BF) for size in sizes]
    return pl.pallas_call(
        functools.partial(backward_kernel, heads, orders, block_rows, last),
        in_specs=[SMEM] + [VMEM] * len(in_fast),
        out_specs=[VMEM] * len(out_shape),
        out_shape=out_shape,
        scratch_shapes=scratch,
        compiler_params=pltpu.CompilerParams(vmem_limit_bytes=BACK_LIMIT),
        cost_estimate=COST,
        name="attention_backward",
    )(meta, *in_fast)


def add(*terms):
    return sum(term.astype(F32) for term in terms)


def hold(values, *others):
    values, others = lax.optimization_barrier((values, others))
    return values, *others


def plus(*terms):
    return sum(term.astype(F32) for term in terms)


def call_local(kernel, out_shape, *operands):
    return pl.pallas_call(
        kernel,
        in_specs=[VMEM] * len(operands),
        out_specs=[VMEM] * len(out_shape),
        out_shape=[jax.ShapeDtypeStruct(shape, kind) for shape, kind in out_shape],
        compiler_params=pltpu.CompilerParams(vmem_limit_bytes=MIDDLE_LIMIT),
        cost_estimate=COST,
        name=kernel.__name__.replace("kernel", "backward"),
    )(*operands)


def join_kernel(
    own_high, y_high, y_low, xy_low, over, one_in, two_in, three_in,
    two, three, y_low_plus, over_plus,
):
    rows = two.shape[0]
    for at, dest in ((slice(0, rows), two), (slice(rows, 2 * rows), three)):
        dest[...] = plus(own_high[at, :], y_high[at, :]).astype(BF)
    y_low_plus[...] = plus(y_low[...], xy_low[...]).astype(BF)
    over_plus[...] = plus(over[...], one_in[...], two_in[...], three_in[...]).astype(BF)


def meet_kernel(x_low, x_high, both_low, y_high, xy_high, message, y_high_plus):
    half = x_low.shape[0]
    message[0:half, :] = plus(x_low[...], both_low[half:, :]).astype(BF)
    message[half:, :] = x_high[...]
    y_high_plus[...] = plus(y_high[...], xy_high[...]).astype(BF)


def last_kernel(own_low, feed_y, own, one):
    rows = own.shape[0]
    own[...] = plus(own_low[0:rows, :], feed_y[0:rows, :])
    one[...] = plus(own_low[rows:, :], feed_y[rows:, :]).astype(BF)


def fold_kernel(own_low, own_high, x_high, over_x, both_low, y_high, total, gains, *messages):
    rows = total.shape[0]
    end = 4 * rows
    mine = from_two(x_high[2 * rows : 2 * rows + 16, :])
    theirs = from_two(over_x[end : end + 16, :])
    pairs = in_two(*(a + b for a, b in zip(mine, theirs)))
    gains[...] = pairs.astype(F32)
    for index in range(4):
        at = slice((index % 2) * rows, (index % 2 + 1) * rows)
        block = plus(
            (own_low if index < 2 else own_high)[at, :],
            over_x[index * rows : (index + 1) * rows, :],
            (both_low if index < 2 else y_high)[at, :],
        )
        if index == 0:
            total[...] = block
        else:
            messages[index - 1][0:rows, :] = block.astype(BF)
            messages[index - 1][rows:, :] = pairs


class Links:
    def __init__(self, wide, narrow):
        self.wide, self.narrow = wide, narrow
        self.planes = wide // 2
        self.staged = wide == 8

    def y(self, values):
        return lax.ppermute(values, "narrow", [(i, (i + 2) % 4) for i in range(4)])

    def core(self, values):
        return lax.ppermute(values, "narrow", [(i, i ^ 1) for i in range(4)])

    def across(self, values):
        return lax.ppermute(values, "narrow", [(i, (i + 2) % 4 ^ 1) for i in range(4)])

    def x(self, values):
        return lax.ppermute(values, "wide", [(i, i ^ 1) for i in range(self.wide)])

    def z(self, values, ahead):
        turn = lambda i: ((i // 2 + ahead) % self.planes) * 2 + i % 2
        return lax.ppermute(values, "wide", [(i, turn(i)) for i in range(self.wide)])

    def whole_gather(self, piece):
        near = lax.all_gather(piece, "wide", axis=0, tiled=True)
        return [near], [self.y(near)]

    def whole_reduce(self, near, far):
        return lax.psum_scatter(near, "wide", scatter_dimension=0, tiled=True).astype(
            F32
        ) + lax.psum_scatter(self.y(far), "wide", scatter_dimension=0, tiled=True).astype(F32)


def on_device(
    tokens,
    lengths,
    norm_one,
    w_query,
    w_key,
    w_value,
    w_out,
    norm_two,
    w_gate,
    w_up,
    w_down,
    cotangent,
):
    model = tokens.shape[-1]
    wide, narrow = lax.axis_size("wide"), lax.axis_size("narrow")
    links = Links(wide, narrow)
    heads = w_query.shape[1] // HD
    head_width = heads * HD
    units = w_gate.shape[1]
    at_wide, at_narrow = lax.axis_index("wide"), lax.axis_index("narrow")
    y, c = at_narrow >> 1, at_narrow & 1
    x, z = at_wide & 1, at_wide >> 1

    staged = links.staged
    planes = links.planes
    rows = model // wide
    turned = [((z + k) & (planes - 1)) * 2 + (x ^ side) for side in range(2) for k in range(4)]
    blocks = [((y ^ far) * 2 + (c ^ side)) * TILE for side in range(2) for far in range(2)]
    length = lax.dynamic_index_in_dim(lengths, y, 0, keepdims=False)[0]
    numbers = [
        *(spot * rows for spot in turned),
        *blocks,
        length,
    ]
    meta = jnp.stack([jnp.asarray(number, jnp.int32) for number in numbers])
    first_item = y == 0

    gain_one = norm_one.reshape(1, model)
    gain_two = norm_two.reshape(1, model)

    def keep_give(rows):
        flat = rows.reshape(2, TILE, model)
        return (
            lax.dynamic_index_in_dim(flat, y, 0, keepdims=False),
            lax.dynamic_index_in_dim(flat, 1 - y, 0, keepdims=False),
        )

    attn_piece = jnp.concatenate([w_out.T, w_query, w_key, w_value], axis=1)
    feed_piece = jnp.concatenate([w_gate, w_up, w_down.T], axis=1)
    keep, give = keep_give(tokens)
    keep_cot, give_cot = keep_give(cotangent)
    half = planes // 2 * rows
    if staged:
        block_rows = rows
        quarters = ((0, 1), (2, 3), (4, 5), (6, 7))
        attn_near_in = attn_far_in = ((0, 1, 2, 3), (4, 5, 6, 7))
        feed_near_in = ((0,), (1,), (3,), (2,), (4, 5, 7), (6,))
        feed_far_in = ((0, 1, 3), (2,), (4, 5), (7, 6))
        attn_far_out = ((0, 1, 4, 5), (2, 3), (6, 7))
        feed_near_out = ((0, 1), (2, 3), (4,), (5,), (6,), (7,))
    else:
        block_rows = model
        quarters = attn_far_out = feed_near_out = ((0,),)
        attn_near_in = attn_far_in = feed_near_in = feed_far_in = ((0,),)

    got = links.y(give)
    if staged:
        column = [attn_piece] + [links.z(attn_piece, planes - k) for k in range(1, planes)]
        column = jnp.concatenate(column, axis=0)
        over_x, over_y = links.x(column), links.y(column)
        feed_piece, column, first_item = hold(feed_piece, column, first_item)
        feed_one = links.z(feed_piece, planes - 1)
        feed_three = links.z(feed_piece, planes - 3)
    else:
        attn_near, attn_far = links.whole_gather(attn_piece)
        feed_near, feed_far = links.whole_gather(feed_piece)
    from_keep = links.core(keep)
    if staged:
        got, feed_one, feed_three = hold(got, feed_one, feed_three)
    rows_in = [keep, got, from_keep, links.core(got)]
    if staged:
        over_y, over_x = hold(over_y, over_x)
        give_cot, over_y = hold(give_cot, over_y)
        attn_near = [column, over_x]
        rows_in, over_y, meta = hold(rows_in, over_y, meta)
        attn_far = [over_y, links.x(over_y)]
        three = jnp.concatenate([feed_piece, feed_one, feed_three], axis=0)
        feed_x = links.x(three)
        feed_y = links.y(three)
        feed_piece, feed_one = hold(feed_piece, feed_one)
        feed_two = links.z(feed_piece, planes - 2)
    got_cot = links.y(give_cot)

    inv_near, context_near, expo_near, *kept_near, normed = attention_forward(
        meta, heads, block_rows, attn_near, attn_near_in, rows_in=rows_in, gain=gain_one
    )
    if staged:
        normed, feed_two, attn_far = hold(normed, feed_two, attn_far)
        feed_x_two = links.x(feed_two)
        feed_y_two = links.y(feed_two)
    inv_far, context_far, expo_far, *kept_far, part_mine = attention_forward(
        meta, heads, block_rows, attn_far, attn_far_in,
        before=(normed, context_near, kept_near[0]),
    )
    if staged:
        part_mine, got_cot, feed_x, feed_y, feed_x_two, feed_y_two = hold(
            part_mine, got_cot, feed_x, feed_y, feed_x_two, feed_y_two
        )
    part_other = links.core(part_mine)
    own_cot = jnp.concatenate([keep_cot, got_cot], axis=0)
    cots = [own_cot, links.core(own_cot)]
    if staged:
        feed_near = [feed_piece, feed_one, feed_three, feed_two, feed_x, feed_x_two]
        feed_far = [
            feed_y,
            feed_y_two,
            links.y(feed_x[: 2 * rows]),
            links.x(jnp.concatenate([feed_y[2 * rows :], feed_y_two], axis=0)),
        ]
    parts = (part_mine, part_other)

    normed_two, down_near, back_near, *near = feed_forward(
        meta, block_rows, cots, feed_near, feed_near_in, feed_near_out, rows_in=rows_in,
        before=(*parts, gain_two),
    )
    if staged:
        own_low, own_high, over, *pieces = near
        over_one = links.z(pieces[0], 1)
    mlp_mine, mlp_other, d_mine, *far = feed_forward(
        meta, block_rows, cots, feed_far, feed_far_in, quarters,
        before=(normed_two, down_near, back_near),
    )
    if staged:
        mlp_other, over_one = hold(mlp_other, over_one)
        over_three = links.z(pieces[2], 3)
        y_low, y_high, xy_low, xy_high = far
        from_xy_high = links.x(xy_high)
    else:
        feed_grad = links.whole_reduce(*near, *far)
    d_other = links.core(d_mine)
    half_rows = 2 * TILE
    output = (
        jnp.concatenate(rows_in[:2], axis=0).astype(F32)
        + part_mine[:half_rows].astype(F32)
        + part_other[half_rows:].astype(F32)
        + mlp_mine.astype(F32)
        + links.core(mlp_other).astype(F32)
    ).astype(BF)
    output_back = links.y(output[TILE:])
    d_middle, d_context_near, d_context_far, out_near, out_far, gain_rows = middle_backward(
        heads,
        rows_in,
        parts,
        gain_two,
        cots,
        (d_mine, d_other),
        (context_near, context_far),
        (kept_near[0], kept_far[0]),
    )
    if staged:
        d_context_far, from_xy_high, output_back, over_three = hold(
            d_context_far, from_xy_high, output_back, over_three
        )
        xy_low, over_two, from_xy_high = hold(xy_low, pieces[1], from_xy_high)
        over_two = links.z(over_two, 2)
        from_y_high = links.y(add(y_high, from_xy_high).astype(BF))
        from_xy_low = links.x(xy_low)
    d_first, *far = attention_backward(
        meta, heads, block_rows, normed, (inv_far, context_far, expo_far, *kept_far),
        d_context_far, out_far, attn_far_out,
    )
    if staged:
        d_first, from_y_high, from_xy_low, over_two = hold(
            d_first, from_y_high, from_xy_low, over_two
        )
        feed = (rows, feed_piece.shape[1])
        feed_half = (half, feed_piece.shape[1])
        feed_two, feed_three, feed_y_low, feed_over = call_local(
            join_kernel, [(feed, BF), (feed, BF), (feed_half, BF), (feed, BF)],
            own_high, from_y_high, y_low, from_xy_low, over, over_one, over_two, over_three,
        )
        feed_two = links.z(feed_two, 2)
        feed_low = own_low
        both_low, y_high, xy_high = far
        from_both_low = links.y(both_low)
        from_xy_high = links.x(xy_high)
        from_feed_x, from_feed_y = links.x(feed_over), links.y(feed_y_low)
    last_mine, last_other, *near = attention_backward(
        meta, heads, block_rows, normed, (inv_near, context_near, expo_near, *kept_near),
        d_context_near, out_near, quarters, before=(d_first, gain_one, gain_rows),
    )
    if staged:
        last_other, near, from_both_low, from_xy_high, from_feed_x, feed_two = hold(
            last_other, near, from_both_low, from_xy_high, from_feed_x, feed_two
        )
        own_low, own_high, x_low, x_high = near
        width = x_low.shape[1]
        message, y_high = call_local(
            meet_kernel, [((2 * half + 16, width), BF), ((half, width), BF)],
            x_low, x_high, from_both_low, y_high, from_xy_high,
        )
        from_x, from_y_high = links.x(message), links.y(y_high)
        feed_parts = [feed_two, links.z(feed_three, 3)]
        last_mine, from_feed_y = hold(last_mine, from_feed_y)
    else:
        attn_grad = links.whole_reduce(near[0][:model], *far)
        gains = near[0][model:]
    mine, theirs = call_local(
        finish_kernel,
        [((TILE, model), BF)] * 2,
        last_mine, links.core(last_other), *rows_in[:2], d_middle, gain_one,
    )
    if staged:
        feed_own, feed_one = call_local(
            last_kernel, [(feed, F32), (feed, BF)], feed_low, from_feed_y
        )
        feed_parts += [from_feed_x, links.z(feed_one, 1)]
        from_x, theirs, feed_own = hold(from_x, theirs, feed_own)
    back = links.y(theirs)
    if staged:
        attn = (rows, width)
        apart = ((rows + 16, width), BF)
        attn_grad, gains, *messages = call_local(
            fold_kernel, [(attn, F32), ((16, width), F32), apart, apart, apart],
            own_low, own_high, x_high, from_x, from_both_low, from_y_high,
        )
        arrived = [links.z(piece, k + 1) for k, piece in enumerate(messages)]
        attn_grad = add(attn_grad, *(part[:rows] for part in arrived))
        gains = add(gains, *(part[rows:] for part in arrived))
        gains, back = hold(gains, back)
        feed_grad = add(feed_own, *feed_parts)
    else:
        gains = lax.psum(gains.astype(F32), "wide")
    gains = (gains + links.core(gains)) + (links.y(gains) + links.across(gains))

    def in_order(own, other):
        stacked = jnp.where(first_item, jnp.stack([own, other]), jnp.stack([other, own]))
        return stacked.reshape(tokens.shape)

    return (
        in_order(output[:TILE], output_back),
        in_order(mine, back),
        gains[0] + gains[1],
        attn_grad[:, head_width : 2 * head_width],
        attn_grad[:, 2 * head_width : 3 * head_width],
        attn_grad[:, 3 * head_width :],
        attn_grad[:, :head_width].T,
        gains[2] + gains[3],
        feed_grad[:, :units],
        feed_grad[:, units : 2 * units],
        feed_grad[:, 2 * units :].T,
    )


def solution(mesh):
    in_specs = (
        P(None, "wide", "narrow", None),
        P(None, "wide"),
        P(),
        P("wide", "narrow"),
        P("wide", "narrow"),
        P("wide", "narrow"),
        P("narrow", "wide"),
        P(),
        P("wide", "narrow"),
        P("wide", "narrow"),
        P("narrow", "wide"),
        P(None, "wide", "narrow", None),
    )
    out_specs = (
        P(None, "wide", "narrow", None),
        P(None, "wide", "narrow", None),
        P(),
        P("wide", "narrow"),
        P("wide", "narrow"),
        P("wide", "narrow"),
        P("narrow", "wide"),
        P(),
        P("wide", "narrow"),
        P("wide", "narrow"),
        P("narrow", "wide"),
    )
    return jax.shard_map(
        on_device, mesh=mesh, in_specs=in_specs, out_specs=out_specs, check_vma=False
    )
```

```python
import functools

import jax
import jax.numpy as jnp
from jax import lax
from jax.experimental import pallas as pl
from jax.experimental.pallas import tpu as pltpu
from jax.sharding import PartitionSpec as P

HD = 64
EPSILON = 1e-06
MASKED = -1e30
TILE = 256
FEED_ROWS = 1024
QUERY_ROWS = 1024
MIDDLE_LIMIT = 8 * 1024 * 1024
BACK_LIMIT = 14 * 1024 * 1024
ATTEND_LIMIT = 11 * 1024 * 1024
FEED_LIMIT = 22 * 1024 * 1024
COST = pl.CostEstimate(flops=10**6, bytes_accessed=10**5, transcendentals=0)
BF = jnp.bfloat16
F32 = jnp.float32


def mm(left, right):
    return jnp.dot(left, right, preferred_element_type=F32)


def mm_nt(left, right):
    return lax.dot_general(left, right, (((1,), (1,)), ((), ())), preferred_element_type=F32)


def mm_tn(left, right):
    return lax.dot_general(left, right, (((0,), (0,)), ((), ())), preferred_element_type=F32)


def inverse_rms(features):
    return lax.rsqrt(jnp.mean(features * features, axis=-1, keepdims=True) + EPSILON)


def place(meta, pieces, orders, dest, rows, sems):
    copies = []
    for piece, order in zip(pieces, orders):
        for number, index in enumerate(order):
            at = 0 if rows == dest.shape[0] else pl.multiple_of(meta[index], 16)
            copy = pltpu.make_async_copy(
                piece.at[pl.ds(number * rows, rows), :],
                dest.at[pl.ds(at, rows), :],
                sems.at[len(copies)],
            )
            copy.start()
            copies.append(copy)
    return copies


def wait_all(copies):
    for copy in copies:
        copy.wait()


def blocks_of(orders):
    return sum(len(order) for order in orders)


def disperse(meta, source, groups, orders, rows):
    for group, order in zip(groups, orders):
        for place, index in enumerate(order):
            at = 0 if rows == source.shape[0] else pl.multiple_of(meta[index], 16)
            group[place * rows : (place + 1) * rows, :] = source[pl.ds(at, rows), :]


def row_block(refs, block):
    start = block * TILE
    for ref in refs:
        if start < ref.shape[0]:
            return ref[start : start + TILE, :]
        start -= ref.shape[0]


def forward_kernel(heads, n_rows, orders, block_rows, meta, *refs):
    first = n_rows > 0
    refs = list(refs)
    take = lambda count: [refs.pop(0) for _ in range(count)]
    width = heads * HD
    total = 4 * TILE
    if first:
        (gain,) = take(1)
        sources = take(n_rows)
    else:
        normed, context_first, weight_first = take(3)
    pieces = take(len(orders))
    inverse, context, expo, weight, proj = take(5)
    if first:
        (normed,) = take(1)
    else:
        (partial,) = take(1)
    q_ext, k_ext, v_flip, sems, sems_more = take(5)
    copies = place(meta, pieces, orders, weight, block_rows, sems)
    outs = []

    def carry(source, dest):
        copy = pltpu.make_async_copy(source, dest, sems_more.at[len(outs)])
        copy.start()
        outs.append(copy)

    if first:
        (extra,) = take(1)
        starts = [sum(ref.shape[0] for ref in sources[:k]) for k in range(n_rows)]
        for start, source in zip(starts, sources):
            carry(source, extra.at[pl.ds(start, source.shape[0]), :])
        wait_all(outs)
        for block in range(4):
            rows = slice(block * TILE, (block + 1) * TILE)
            features = extra[rows, :].astype(F32)
            normed[rows, :] = (features * inverse_rms(features) * gain[...]).astype(BF)
    wait_all(copies)
    proj[...] = mm(normed[...], weight[...]).astype(BF)
    lanes = lax.broadcasted_iota(jnp.int32, (TILE, HD), 1)
    index = lax.broadcasted_iota(jnp.int32, (TILE, HD), 0)
    ones = jnp.where(lanes == 0, 1.0, 0.0).astype(BF)
    below = jnp.where(lax.broadcasted_iota(jnp.int32, (16, total), 0) == 0, 1.0, 0.0).astype(BF)
    for block in range(4):
        rows = slice(block * TILE, (block + 1) * TILE)
        usable = meta[8 + block] + index < meta[12]
        bias = jnp.where((lanes == 0) & ~usable, MASKED, 0.0).astype(BF)
        for head in range(heads):
            at = width + head * HD
            q_ext[head, rows, 0:HD] = proj[rows, at : at + HD]
            q_ext[head, rows, HD : 2 * HD] = ones
            at = 2 * width + head * HD
            k_ext[head, rows, 0:HD] = proj[rows, at : at + HD]
            k_ext[head, rows, HD : 2 * HD] = bias
    for head in range(heads):
        at = 3 * width + head * HD
        v_flip[head, 0:HD, :] = proj[:, at : at + HD].T
        v_flip[head, HD : HD + 16, :] = below
    inverse[...] = jnp.ones_like(inverse)
    for head in range(heads):
        for start in range(0, total, QUERY_ROWS):
            rows = slice(start, start + QUERY_ROWS)
            scores = mm_nt(k_ext[head], q_ext[head, rows, :])
            top = jnp.max(scores, axis=0, keepdims=True)
            raised = jnp.exp(scores - top).astype(BF)
            expo[head, :, rows] = raised
            mixed = mm(v_flip[head], raised)
            inv = 1.0 / mixed[HD : HD + 1, :]
            inverse[head : head + 1, rows] = inv
            context[rows, head * HD : (head + 1) * HD] = (mixed[0:HD, :] * inv).astype(BF).T
    if not first:
        partial[...] = (
            mm_nt(context_first[...], weight_first[:, 0:width])
            + mm_nt(context[...], weight[:, 0:width])
        ).astype(BF)


SMEM = pl.BlockSpec(memory_space=pltpu.SMEM)
VMEM = pl.BlockSpec(memory_space=pltpu.VMEM)
HBM = pl.BlockSpec(memory_space=pltpu.HBM)


def attention_forward(meta, heads, block_rows, pieces, orders, rows_in=(), gain=None, before=None):
    width = pieces[0].shape[1]
    model = rows_in[0].shape[1] if rows_in else before[0].shape[1]
    total = 4 * TILE
    rows = jax.ShapeDtypeStruct((total, model), BF)
    numerators = jax.ShapeDtypeStruct((heads, total, total), BF)
    if rows_in:
        in_fast, in_slow = [gain], [*rows_in, *pieces]
        more, extra = [rows], [pltpu.VMEM((total, model), BF)]
    else:
        in_fast, in_slow = [*before], [*pieces]
        more, extra = [rows], []
    return pl.pallas_call(
        functools.partial(forward_kernel, heads, len(rows_in), orders, block_rows),
        in_specs=[SMEM] + [VMEM] * len(in_fast) + [HBM] * len(in_slow),
        out_specs=[VMEM] * 6,
        out_shape=[
            jax.ShapeDtypeStruct((8, total), F32),
            jax.ShapeDtypeStruct((total, heads * HD), BF),
            numerators,
            jax.ShapeDtypeStruct((model, width), BF),
            jax.ShapeDtypeStruct((total, width), BF),
            *more,
        ],
        scratch_shapes=[
            pltpu.VMEM((heads, total, 2 * HD), BF),
            pltpu.VMEM((heads, total, 2 * HD), BF),
            pltpu.VMEM((heads, HD + 16, total), BF),
            pltpu.SemaphoreType.DMA((blocks_of(orders),)),
            pltpu.SemaphoreType.DMA((4,)),
            *extra,
        ],
        compiler_params=pltpu.CompilerParams(vmem_limit_bytes=ATTEND_LIMIT),
        cost_estimate=COST,
        name="attention_forward",
    )(meta, *in_fast, *in_slow)


def gelu_terms(gate):
    scale = 0.7978845608028654
    cube = 0.044715
    square = gate * gate
    bent = jnp.tanh(scale * gate * (1.0 + cube * square))
    half = 0.5 * (1.0 + bent)
    slope = half + 0.5 * gate * (1.0 - bent * bent) * (scale * (1.0 + 3.0 * cube * square))
    return gate * half, slope


def feed_kernel(n_rows, n_cots, in_orders, orders, block_rows, meta, *refs):
    first = n_rows > 0
    refs = list(refs)
    take = lambda count: [refs.pop(0) for _ in range(count)]
    if first:
        rows_in = take(n_rows)
        part_mine, part_other, gain = take(3)
    else:
        normed, result_before, back_before = take(3)
    cots = take(n_cots)
    pieces = take(len(in_orders))
    if first:
        normed, result, back = take(3)
    else:
        mine, other, back = take(3)
    groups = take(len(orders))
    weight, hidden, d_gate, d_up, cot, grad, sems = take(7)
    units = weight.shape[1] // 3
    copies = place(meta, pieces, in_orders, weight, block_rows, sems)
    for block in range(4):
        rows = slice(block * TILE, (block + 1) * TILE)
        cot[rows, :] = row_block(cots, block)
        if first:
            swapped = slice(((block + 2) % 4) * TILE, ((block + 2) % 4 + 1) * TILE)
            features = (
                row_block(rows_in, block).astype(F32)
                + part_mine[rows, :].astype(F32)
                + part_other[swapped, :].astype(F32)
            )
            features = features.astype(BF).astype(F32)
            normed[rows, :] = (features * inverse_rms(features) * gain[...]).astype(BF)
    wait_all(copies)
    for start in range(0, 4 * TILE, FEED_ROWS):
        rows = slice(start, start + FEED_ROWS)
        pre = mm(normed[rows, :], weight[:, 0 : 2 * units])
        act, slope = gelu_terms(pre[:, :units])
        up = pre[:, units:]
        low = (act * up).astype(BF)
        hidden[rows, :] = low
        d_hidden = mm(cot[rows, :], weight[:, 2 * units :])
        gate_low = (d_hidden * up * slope).astype(BF)
        up_low = (d_hidden * act).astype(BF)
        d_gate[rows, :] = gate_low
        d_up[rows, :] = up_low
        down = mm_nt(low, weight[:, 2 * units :])
        through = mm_nt(gate_low, weight[:, 0:units]) + mm_nt(up_low, weight[:, units : 2 * units])
        if first:
            result[rows, :] = down.astype(BF)
            back[rows, :] = through.astype(BF)
        else:
            down = (down + result_before[rows, :].astype(F32)).astype(BF)
            if start < 2 * TILE:
                mine[rows, :] = down[: 2 * TILE - start]
            if start + FEED_ROWS > 2 * TILE:
                begin = max(start - 2 * TILE, 0)
                other[begin : start + FEED_ROWS - 2 * TILE, :] = down[begin + 2 * TILE - start :]
            back[rows, :] = (through + back_before[rows, :].astype(F32)).astype(BF)
    grad[:, 2 * units :] = mm_tn(cot[...], hidden[...]).astype(BF)
    grad[:, 0:units] = mm_tn(normed[...], d_gate[...]).astype(BF)
    grad[:, units : 2 * units] = mm_tn(normed[...], d_up[...]).astype(BF)
    disperse(meta, grad, groups, orders, block_rows)


def feed_forward(meta, block_rows, cots, pieces, in_orders, orders, rows_in=(), before=()):
    width = pieces[0].shape[1]
    model = cots[0].shape[1]
    total = 4 * TILE
    units = width // 3
    full = jax.ShapeDtypeStruct((total, model), BF)
    half = jax.ShapeDtypeStruct((2 * TILE, model), BF)
    operands = [*rows_in, *before, *cots, *pieces]
    out_shape = [full, full, full] if rows_in else [half, half, full]
    out_shape += [
        jax.ShapeDtypeStruct((len(order) * block_rows, width), BF) for order in orders
    ]
    return pl.pallas_call(
        functools.partial(
            feed_kernel, len(rows_in), len(cots), in_orders, orders, block_rows
        ),
        in_specs=[SMEM] + [VMEM] * (len(operands) - len(pieces)) + [HBM] * len(pieces),
        out_specs=[VMEM] * len(out_shape),
        out_shape=out_shape,
        scratch_shapes=[
            pltpu.VMEM((model, width), BF),
            pltpu.VMEM((total, units), BF),
            pltpu.VMEM((total, units), BF),
            pltpu.VMEM((total, units), BF),
            pltpu.VMEM((total, model), BF),
            pltpu.VMEM((model, width), BF),
            pltpu.SemaphoreType.DMA((blocks_of(in_orders),)),
        ],
        compiler_params=pltpu.CompilerParams(vmem_limit_bytes=FEED_LIMIT),
        cost_estimate=COST,
        name="feed_forward",
    )(meta, *operands)


def middle_kernel(heads, n_rows, n_cots, *refs):
    refs = list(refs)
    take = lambda count: [refs.pop(0) for _ in range(count)]
    rows_in = take(n_rows)
    part_mine, part_other, gain = take(3)
    cots = take(n_cots)
    d_mine, d_other, context_near, context_far = take(4)
    weight_near, weight_far = take(2)
    d_middle, d_context_near, d_context_far, grad_near, grad_far, d_gain = take(6)
    (d_all,) = take(1)
    width = heads * HD
    gains = 0.0
    for block in range(4):
        rows = slice(block * TILE, (block + 1) * TILE)
        swapped = slice(((block + 2) % 4) * TILE, ((block + 2) % 4 + 1) * TILE)
        features = (
            row_block(rows_in, block).astype(F32)
            + part_mine[rows, :].astype(F32)
            + part_other[swapped, :].astype(F32)
        )
        features = features.astype(BF).astype(F32)
        inverse = inverse_rms(features)
        back = d_mine[rows, :].astype(F32) + d_other[swapped, :].astype(F32)
        scaled = back * gain[...]
        inner = jnp.mean(scaled * features, axis=-1, keepdims=True)
        result = (
            row_block(cots, block).astype(F32)
            + inverse * scaled
            - features * (inverse * inverse * inverse * inner)
        )
        d_all[rows, :] = result.astype(BF)
        if block < 2:
            d_middle[rows, :] = result
            gains += jnp.sum(back * features * inverse, axis=0, keepdims=True)
    d_gain[...] = jnp.broadcast_to(gains, d_gain.shape)
    d_context_near[...] = mm(d_all[...], weight_near[:, 0:width]).astype(BF)
    d_context_far[...] = mm(d_all[...], weight_far[:, 0:width]).astype(BF)
    grad_near[...] = mm_tn(d_all[...], context_near[...]).astype(BF)
    grad_far[...] = mm_tn(d_all[...], context_far[...]).astype(BF)


def middle_backward(heads, rows_in, parts, gain, cots, d_normed, contexts, weights):
    model = gain.shape[1]
    total = 4 * TILE
    width = heads * HD
    operands = [*rows_in, *parts, gain, *cots, *d_normed, *contexts, *weights]
    return pl.pallas_call(
        functools.partial(middle_kernel, heads, len(rows_in), len(cots)),
        in_specs=[VMEM] * len(operands),
        out_specs=[VMEM] * 6,
        out_shape=[
            jax.ShapeDtypeStruct((2 * TILE, model), F32),
            jax.ShapeDtypeStruct((total, width), BF),
            jax.ShapeDtypeStruct((total, width), BF),
            jax.ShapeDtypeStruct((model, width), BF),
            jax.ShapeDtypeStruct((model, width), BF),
            jax.ShapeDtypeStruct((8, model), F32),
        ],
        scratch_shapes=[
            pltpu.VMEM((total, model), BF),
        ],
        compiler_params=pltpu.CompilerParams(vmem_limit_bytes=MIDDLE_LIMIT),
        cost_estimate=COST,
        name="middle_backward",
    )(*operands)


def in_two(*rows):
    high = [row.astype(BF).astype(F32) for row in rows]
    index = lax.broadcasted_iota(jnp.int32, (16, rows[0].shape[1]), 0)
    result = jnp.zeros((16, rows[0].shape[1]), F32)
    for number, row in enumerate(rows):
        result = jnp.where(index == 2 * number, high[number], result)
        result = jnp.where(index == 2 * number + 1, row - high[number], result)
    return result.astype(BF)


def from_two(rows):
    return [
        rows[2 * k : 2 * k + 1].astype(F32) + rows[2 * k + 1 : 2 * k + 2].astype(F32)
        for k in range(2)
    ]


def finish_kernel(d_mine, d_other, keep, got, d_middle, gain, mine, theirs):
    for number, rows_in in enumerate((keep, got)):
        rows = slice(number * TILE, (number + 1) * TILE)
        features = rows_in[...].astype(F32)
        inverse = inverse_rms(features)
        scaled = (d_mine[rows, :].astype(F32) + d_other[rows, :].astype(F32)) * gain[...]
        inner = jnp.mean(scaled * features, axis=-1, keepdims=True)
        result = (
            d_middle[rows, :] + inverse * scaled - features * (inverse * inverse * inverse * inner)
        ).astype(BF)
        if number == 0:
            mine[...] = result
        else:
            theirs[...] = result


def backward_kernel(heads, orders, block_rows, last, meta, *refs):
    refs = list(refs)
    take = lambda count: [refs.pop(0) for _ in range(count)]
    inverse, context, expo, weight, proj, normed, d_context, grad_out = take(8)
    if last:
        gain, gain_rows = take(2)
    if last:
        (before,) = take(1)
        mine, other = take(2)
    else:
        (result,) = take(1)
    groups = take(len(orders))
    do_ext, v_ext, d_proj, grad = take(4)
    width = heads * HD
    total = 4 * TILE
    lanes = lax.broadcasted_iota(jnp.int32, (total, HD), 1)
    columns = inverse[...].T
    d_proj[:, 0:width] = jnp.zeros((total, width), BF)
    for head in range(heads):
        at = head * HD
        scaled = (d_context[:, at : at + HD].astype(F32) * columns[:, head : head + 1]).astype(BF)
        inner = -jnp.sum(
            scaled.astype(F32) * context[:, at : at + HD].astype(F32), axis=-1, keepdims=True
        )
        high = inner.astype(BF).astype(F32)
        do_ext[head, :, 0:HD] = scaled
        do_ext[head, :, HD : 2 * HD] = jnp.where(
            lanes == 0, high, jnp.where(lanes == 1, inner - high, 0.0)
        ).astype(BF)
    for head in range(heads):
        at = 3 * width + head * HD
        v_ext[head, :, 0:HD] = proj[:, at : at + HD]
        v_ext[head, :, HD : 2 * HD] = jnp.where(lanes < 2, 1.0, 0.0).astype(BF)
    for head in range(heads):
        q_at, k_at, v_at = (part * width + head * HD for part in (1, 2, 3))
        raised = expo[head]
        d_probs = mm_nt(v_ext[head], do_ext[head])
        d_scores = (raised.astype(F32) * d_probs).astype(BF)
        d_queries = mm(proj[:, k_at : k_at + HD].T, d_scores)
        d_keys = mm_nt(proj[:, q_at : q_at + HD].T, d_scores)
        d_values = mm_nt(do_ext[head, :, 0:HD].T, raised)
        d_proj[:, q_at : q_at + HD] = d_queries.astype(BF).T
        d_proj[:, k_at : k_at + HD] = d_keys.astype(BF).T
        d_proj[:, v_at : v_at + HD] = d_values.astype(BF).T
    grad[...] = mm_tn(normed[...], d_proj[...]).astype(BF)
    grad[:, 0:width] = grad_out[...]
    disperse(meta, grad, groups, orders, block_rows)
    through = mm_nt(d_proj[...], weight[...])
    if last:
        through = through + before[...].astype(F32)
        mine[...] = through[0 : 2 * TILE].astype(BF)
        other[0 : 2 * TILE, :] = through[2 * TILE :].astype(BF)
        first = jnp.sum(through * normed[...].astype(F32), axis=0, keepdims=True) / gain[...]
        other[2 * TILE :, :] = in_two(first, gain_rows[0:1, :])
    else:
        result[...] = through.astype(BF)


def attention_backward(
    meta, heads, block_rows, normed, saved, d_context, grad_out, orders, before=None
):
    last = before is not None
    weight, proj = saved[3:]
    model, width = weight.shape
    total = proj.shape[0]
    rows = jax.ShapeDtypeStruct((total, model), BF)
    in_fast = [*saved, normed, d_context, grad_out]
    scratch = [
        pltpu.VMEM((heads, total, 2 * HD), BF),
        pltpu.VMEM((heads, total, 2 * HD), BF),
        pltpu.VMEM((total, width), BF),
        pltpu.VMEM((model, width), BF),
    ]
    sizes = [len(order) * block_rows for order in orders]
    if last:
        in_fast += [*before[1:], before[0]]
        out_shape = [
            jax.ShapeDtypeStruct((2 * TILE + extra, model), BF) for extra in (0, 16)
        ]
    else:
        out_shape = [rows]
    out_shape += [jax.ShapeDtypeStruct((size, width), BF) for size in sizes]
    return pl.pallas_call(
        functools.partial(backward_kernel, heads, orders, block_rows, last),
        in_specs=[SMEM] + [VMEM] * len(in_fast),
        out_specs=[VMEM] * len(out_shape),
        out_shape=out_shape,
        scratch_shapes=scratch,
        compiler_params=pltpu.CompilerParams(vmem_limit_bytes=BACK_LIMIT),
        cost_estimate=COST,
        name="attention_backward",
    )(meta, *in_fast)


def add(*terms):
    return sum(term.astype(F32) for term in terms)


def hold(values, *others):
    values, others = lax.optimization_barrier((values, others))
    return values, *others


def plus(*terms):
    return sum(term.astype(F32) for term in terms)


def call_local(kernel, out_shape, *operands):
    return pl.pallas_call(
        kernel,
        in_specs=[VMEM] * len(operands),
        out_specs=[VMEM] * len(out_shape),
        out_shape=[jax.ShapeDtypeStruct(shape, kind) for shape, kind in out_shape],
        compiler_params=pltpu.CompilerParams(vmem_limit_bytes=MIDDLE_LIMIT),
        cost_estimate=COST,
        name=kernel.__name__.replace("kernel", "backward"),
    )(*operands)


def join_kernel(
    own_high, y_high, y_low, xy_low, over, one_in, two_in, three_in,
    two, three, y_low_plus, over_plus,
):
    rows = two.shape[0]
    for at, dest in ((slice(0, rows), two), (slice(rows, 2 * rows), three)):
        dest[...] = plus(own_high[at, :], y_high[at, :]).astype(BF)
    y_low_plus[...] = plus(y_low[...], xy_low[...]).astype(BF)
    over_plus[...] = plus(over[...], one_in[...], two_in[...], three_in[...]).astype(BF)


def meet_kernel(y_all, xy_all, result):
    result[...] = plus(y_all[...], xy_all[...]).astype(BF)


def last_kernel(own_low, feed_y, own, one):
    rows = own.shape[0]
    own[...] = plus(own_low[0:rows, :], feed_y[0:rows, :])
    one[...] = plus(own_low[rows:, :], feed_y[rows:, :]).astype(BF)


def fold_kernel(own, over_x, over_y, mine, theirs, total, gains, *messages):
    rows = total.shape[0]
    sums = mine[...] + theirs[...]
    gains[...] = sums
    pairs = in_two(*from_two(sums))
    for index in range(4):
        at = slice(index * rows, (index + 1) * rows)
        block = plus(own[at, :], over_x[at, :], over_y[at, :])
        if index == 0:
            total[...] = block
        else:
            messages[index - 1][0:rows, :] = block.astype(BF)
            messages[index - 1][rows:, :] = pairs


class Links:
    def __init__(self, wide, narrow):
        self.wide, self.narrow = wide, narrow
        self.planes = wide // 2
        self.staged = wide == 8

    def y(self, values):
        return lax.ppermute(values, "narrow", [(i, (i + 2) % 4) for i in range(4)])

    def core(self, values):
        return lax.ppermute(values, "narrow", [(i, i ^ 1) for i in range(4)])

    def x(self, values):
        return lax.ppermute(values, "wide", [(i, i ^ 1) for i in range(self.wide)])

    def z(self, values, ahead):
        turn = lambda i: ((i // 2 + ahead) % self.planes) * 2 + i % 2
        return lax.ppermute(values, "wide", [(i, turn(i)) for i in range(self.wide)])

    def whole_gather(self, piece):
        near = lax.all_gather(piece, "wide", axis=0, tiled=True)
        return [near], [self.y(near)]

    def whole_reduce(self, near, far):
        return lax.psum_scatter(near, "wide", scatter_dimension=0, tiled=True).astype(
            F32
        ) + lax.psum_scatter(self.y(far), "wide", scatter_dimension=0, tiled=True).astype(F32)


def on_device(
    tokens,
    lengths,
    norm_one,
    w_query,
    w_key,
    w_value,
    w_out,
    norm_two,
    w_gate,
    w_up,
    w_down,
    cotangent,
):
    model = tokens.shape[-1]
    wide, narrow = lax.axis_size("wide"), lax.axis_size("narrow")
    links = Links(wide, narrow)
    heads = w_query.shape[1] // HD
    head_width = heads * HD
    units = w_gate.shape[1]
    at_wide, at_narrow = lax.axis_index("wide"), lax.axis_index("narrow")
    y, c = at_narrow >> 1, at_narrow & 1
    x, z = at_wide & 1, at_wide >> 1

    staged = links.staged
    planes = links.planes
    rows = model // wide
    turned = [((z + k) & (planes - 1)) * 2 + (x ^ side) for side in range(2) for k in range(4)]
    blocks = [((y ^ far) * 2 + (c ^ side)) * TILE for side in range(2) for far in range(2)]
    length = lax.dynamic_index_in_dim(lengths, y, 0, keepdims=False)[0]
    numbers = [
        *(spot * rows for spot in turned),
        *blocks,
        length,
    ]
    meta = jnp.stack([jnp.asarray(number, jnp.int32) for number in numbers])
    first_item = y == 0

    gain_one = norm_one.reshape(1, model)
    gain_two = norm_two.reshape(1, model)

    def keep_give(rows):
        flat = rows.reshape(2, TILE, model)
        return (
            lax.dynamic_index_in_dim(flat, y, 0, keepdims=False),
            lax.dynamic_index_in_dim(flat, 1 - y, 0, keepdims=False),
        )

    attn_piece = jnp.concatenate([w_out.T, w_query, w_key, w_value], axis=1)
    feed_piece = jnp.concatenate([w_gate, w_up, w_down.T], axis=1)
    keep, give = keep_give(tokens)
    keep_cot, give_cot = keep_give(cotangent)
    half = planes // 2 * rows
    if staged:
        block_rows = rows
        quarters = ((0, 1), (2, 3), (4, 5), (6, 7))
        attn_near_in = attn_far_in = ((0, 1, 2, 3), (4, 5, 6, 7))
        feed_near_in = ((0,), (1,), (3,), (2,), (4, 5, 7), (6,))
        feed_far_in = ((0, 1, 3), (2,), (4, 5), (7, 6))
        attn_out = ((0, 1, 2, 3), (4, 5, 6, 7))
        feed_near_out = ((0, 1), (2, 3), (4,), (5,), (6,), (7,))
    else:
        block_rows = model
        quarters = attn_out = feed_near_out = ((0,),)
        attn_near_in = attn_far_in = feed_near_in = feed_far_in = ((0,),)

    got = links.y(give)
    if staged:
        column = [attn_piece] + [links.z(attn_piece, planes - k) for k in range(1, planes)]
        column = jnp.concatenate(column, axis=0)
        over_x, over_y = links.x(column), links.y(column)
        feed_piece, column, first_item = hold(feed_piece, column, first_item)
        feed_one = links.z(feed_piece, planes - 1)
        feed_three = links.z(feed_piece, planes - 3)
    else:
        attn_near, attn_far = links.whole_gather(attn_piece)
        feed_near, feed_far = links.whole_gather(feed_piece)
    from_keep = links.core(keep)
    if staged:
        got, feed_one, feed_three = hold(got, feed_one, feed_three)
    rows_in = [keep, got, from_keep, links.core(got)]
    if staged:
        over_y, over_x = hold(over_y, over_x)
        give_cot, over_y = hold(give_cot, over_y)
        attn_near = [column, over_x]
        rows_in, over_y, meta = hold(rows_in, over_y, meta)
        attn_far = [over_y, links.x(over_y)]
        three = jnp.concatenate([feed_piece, feed_one, feed_three], axis=0)
        feed_x = links.x(three)
        feed_y = links.y(three)
        feed_piece, feed_one = hold(feed_piece, feed_one)
        feed_two = links.z(feed_piece, planes - 2)
    got_cot = links.y(give_cot)

    inv_near, context_near, expo_near, *kept_near, normed = attention_forward(
        meta, heads, block_rows, attn_near, attn_near_in, rows_in=rows_in, gain=gain_one
    )
    if staged:
        normed, feed_two, attn_far = hold(normed, feed_two, attn_far)
        feed_x_two = links.x(feed_two)
        feed_y_two = links.y(feed_two)
    inv_far, context_far, expo_far, *kept_far, part_mine = attention_forward(
        meta, heads, block_rows, attn_far, attn_far_in,
        before=(normed, context_near, kept_near[0]),
    )
    if staged:
        part_mine, got_cot, feed_x, feed_y, feed_x_two, feed_y_two = hold(
            part_mine, got_cot, feed_x, feed_y, feed_x_two, feed_y_two
        )
    part_other = links.core(part_mine)
    own_cot = jnp.concatenate([keep_cot, got_cot], axis=0)
    cots = [own_cot, links.core(own_cot)]
    if staged:
        feed_near = [feed_piece, feed_one, feed_three, feed_two, feed_x, feed_x_two]
        feed_far = [
            feed_y,
            feed_y_two,
            links.y(feed_x[: 2 * rows]),
            links.x(jnp.concatenate([feed_y[2 * rows :], feed_y_two], axis=0)),
        ]
    parts = (part_mine, part_other)

    normed_two, down_near, back_near, *near = feed_forward(
        meta, block_rows, cots, feed_near, feed_near_in, feed_near_out, rows_in=rows_in,
        before=(*parts, gain_two),
    )
    if staged:
        own_low, own_high, over, *pieces = near
        over_one = links.z(pieces[0], 1)
    mlp_mine, mlp_other, d_mine, *far = feed_forward(
        meta, block_rows, cots, feed_far, feed_far_in, quarters,
        before=(normed_two, down_near, back_near),
    )
    if staged:
        mlp_other, over_one = hold(mlp_other, over_one)
        over_three = links.z(pieces[2], 3)
        y_low, y_high, xy_low, xy_high = far
        from_xy_high = links.x(xy_high)
    else:
        feed_grad = links.whole_reduce(*near, *far)
    d_other = links.core(d_mine)
    half_rows = 2 * TILE
    output = (
        jnp.concatenate(rows_in[:2], axis=0).astype(F32)
        + part_mine[:half_rows].astype(F32)
        + part_other[half_rows:].astype(F32)
        + mlp_mine.astype(F32)
        + links.core(mlp_other).astype(F32)
    ).astype(BF)
    output_back = links.y(output[TILE:])
    d_middle, d_context_near, d_context_far, out_near, out_far, gain_rows = middle_backward(
        heads,
        rows_in,
        parts,
        gain_two,
        cots,
        (d_mine, d_other),
        (context_near, context_far),
        (kept_near[0], kept_far[0]),
    )
    if staged:
        d_context_far, from_xy_high, output_back, over_three = hold(
            d_context_far, from_xy_high, output_back, over_three
        )
        xy_low, over_two, from_xy_high = hold(xy_low, pieces[1], from_xy_high)
        over_two = links.z(over_two, 2)
        from_y_high = links.y(add(y_high, from_xy_high).astype(BF))
        from_xy_low = links.x(xy_low)
    d_first, *far = attention_backward(
        meta, heads, block_rows, normed, (inv_far, context_far, expo_far, *kept_far),
        d_context_far, out_far, attn_out,
    )
    if staged:
        d_first, from_y_high, from_xy_low, over_two = hold(
            d_first, from_y_high, from_xy_low, over_two
        )
        feed = (rows, feed_piece.shape[1])
        feed_half = (half, feed_piece.shape[1])
        feed_two, feed_three, feed_y_low, feed_over = call_local(
            join_kernel, [(feed, BF), (feed, BF), (feed_half, BF), (feed, BF)],
            own_high, from_y_high, y_low, from_xy_low, over, over_one, over_two, over_three,
        )
        feed_two = links.z(feed_two, 2)
        feed_low = own_low
        y_all, xy_all = far
        from_xy = links.x(xy_all)
        from_feed_y = links.y(feed_y_low)
    last_mine, last_other, *near = attention_backward(
        meta, heads, block_rows, normed, (inv_near, context_near, expo_near, *kept_near),
        d_context_near, out_near, attn_out, before=(d_first, gain_one, gain_rows),
    )
    if staged:
        last_other, near, from_xy, feed_two, from_feed_y = hold(
            last_other, near, from_xy, feed_two, from_feed_y
        )
        own_all, x_all = near
        (y_all,) = call_local(meet_kernel, [(y_all.shape, BF)], y_all, from_xy)
        from_x, from_y = links.x(x_all), links.y(y_all)
        feed_parts = [feed_two, links.z(feed_three, 3)]
    else:
        attn_grad = links.whole_reduce(*near, *far)
    got_other = links.core(last_other)
    sums = add(last_other[half_rows:], got_other[half_rows:])
    sums = sums + links.y(sums)
    mine, theirs = call_local(
        finish_kernel,
        [((TILE, model), BF)] * 2,
        last_mine, got_other, *rows_in[:2], d_middle, gain_one,
    )
    if staged:
        feed_own, feed_one = call_local(
            last_kernel, [(feed, F32), (feed, BF)], feed_low, from_feed_y
        )
        feed_parts.append(links.z(feed_one, 1))
        from_x, theirs, feed_own, feed_parts = hold(from_x, theirs, feed_own, feed_parts)
    back = links.y(theirs)
    if staged:
        width = own_all.shape[1]
        apart = ((rows + 16, width), BF)
        attn_grad, gains, *messages = call_local(
            fold_kernel, [((rows, width), F32), ((16, width), F32), apart, apart, apart],
            own_all, from_x, from_y, sums, links.x(sums),
        )
        feed_over, attn_grad = hold(feed_over, attn_grad)
        feed_parts.append(links.x(feed_over))
        arrived = [links.z(piece, k + 1) for k, piece in enumerate(messages)]
        attn_grad = add(attn_grad, *(part[:rows] for part in arrived))
        gains = add(gains, *(part[rows:] for part in arrived))
        feed_grad = add(feed_own, *feed_parts)
    else:
        gains = lax.psum(sums, "wide")

    def in_order(own, other):
        stacked = jnp.where(first_item, jnp.stack([own, other]), jnp.stack([other, own]))
        return stacked.reshape(tokens.shape)

    return (
        in_order(output[:TILE], output_back),
        in_order(mine, back),
        gains[0] + gains[1],
        attn_grad[:, head_width : 2 * head_width],
        attn_grad[:, 2 * head_width : 3 * head_width],
        attn_grad[:, 3 * head_width :],
        attn_grad[:, :head_width].T,
        gains[2] + gains[3],
        feed_grad[:, :units],
        feed_grad[:, units : 2 * units],
        feed_grad[:, 2 * units :].T,
    )


def solution(mesh):
    in_specs = (
        P(None, "wide", "narrow", None),
        P(None, "wide"),
        P(),
        P("wide", "narrow"),
        P("wide", "narrow"),
        P("wide", "narrow"),
        P("narrow", "wide"),
        P(),
        P("wide", "narrow"),
        P("wide", "narrow"),
        P("narrow", "wide"),
        P(None, "wide", "narrow", None),
    )
    out_specs = (
        P(None, "wide", "narrow", None),
        P(None, "wide", "narrow", None),
        P(),
        P("wide", "narrow"),
        P("wide", "narrow"),
        P("wide", "narrow"),
        P("narrow", "wide"),
        P(),
        P("wide", "narrow"),
        P("wide", "narrow"),
        P("narrow", "wide"),
    )
    return jax.shard_map(
        on_device, mesh=mesh, in_specs=in_specs, out_specs=out_specs, check_vma=False
    )
```

```python
import functools

import jax
import jax.numpy as jnp
from jax import lax
from jax.experimental import pallas as pl
from jax.experimental.pallas import tpu as pltpu
from jax.sharding import PartitionSpec as P

HD = 64
EPSILON = 1e-06
MASKED = -1e30
TILE = 256
FEED_ROWS = 1024
QUERY_ROWS = 1024
MIDDLE_LIMIT = 8 * 1024 * 1024
BACK_LIMIT = 14 * 1024 * 1024
ATTEND_LIMIT = 11 * 1024 * 1024
FEED_LIMIT = 22 * 1024 * 1024
COST = pl.CostEstimate(flops=10**6, bytes_accessed=10**5, transcendentals=0)
BF = jnp.bfloat16
F32 = jnp.float32


def mm(left, right):
    return jnp.dot(left, right, preferred_element_type=F32)


def mm_nt(left, right):
    return lax.dot_general(left, right, (((1,), (1,)), ((), ())), preferred_element_type=F32)


def mm_tn(left, right):
    return lax.dot_general(left, right, (((0,), (0,)), ((), ())), preferred_element_type=F32)


def inverse_rms(features):
    return lax.rsqrt(jnp.mean(features * features, axis=-1, keepdims=True) + EPSILON)


def place(meta, pieces, orders, dest, rows, sems):
    copies = []
    for piece, order in zip(pieces, orders):
        for number, index in enumerate(order):
            at = 0 if rows == dest.shape[0] else pl.multiple_of(meta[index], 16)
            copy = pltpu.make_async_copy(
                piece.at[pl.ds(number * rows, rows), :],
                dest.at[pl.ds(at, rows), :],
                sems.at[len(copies)],
            )
            copy.start()
            copies.append(copy)
    return copies


def wait_all(copies):
    for copy in copies:
        copy.wait()


def blocks_of(orders):
    return sum(len(order) for order in orders)


def disperse(meta, source, groups, orders, rows):
    for group, order in zip(groups, orders):
        for place, index in enumerate(order):
            at = 0 if rows == source.shape[0] else pl.multiple_of(meta[index], 16)
            group[place * rows : (place + 1) * rows, :] = source[pl.ds(at, rows), :]


def row_block(refs, block):
    start = block * TILE
    for ref in refs:
        if start < ref.shape[0]:
            return ref[start : start + TILE, :]
        start -= ref.shape[0]


def forward_kernel(heads, n_rows, orders, block_rows, meta, *refs):
    first = n_rows > 0
    refs = list(refs)
    take = lambda count: [refs.pop(0) for _ in range(count)]
    width = heads * HD
    total = 4 * TILE
    if first:
        (gain,) = take(1)
        sources = take(n_rows)
    else:
        normed, context_first, weight_first = take(3)
    pieces = take(len(orders))
    inverse, context, expo, weight, proj = take(5)
    if first:
        (normed,) = take(1)
    else:
        (partial,) = take(1)
    q_ext, k_ext, v_flip, sems, sems_more = take(5)
    copies = place(meta, pieces, orders, weight, block_rows, sems)
    outs = []

    def carry(source, dest):
        copy = pltpu.make_async_copy(source, dest, sems_more.at[len(outs)])
        copy.start()
        outs.append(copy)

    if first:
        (extra,) = take(1)
        starts = [sum(ref.shape[0] for ref in sources[:k]) for k in range(n_rows)]
        for start, source in zip(starts, sources):
            carry(source, extra.at[pl.ds(start, source.shape[0]), :])
        wait_all(outs)
        for block in range(4):
            rows = slice(block * TILE, (block + 1) * TILE)
            features = extra[rows, :].astype(F32)
            normed[rows, :] = (features * inverse_rms(features) * gain[...]).astype(BF)
    wait_all(copies)
    proj[...] = mm(normed[...], weight[...]).astype(BF)
    lanes = lax.broadcasted_iota(jnp.int32, (TILE, HD), 1)
    index = lax.broadcasted_iota(jnp.int32, (TILE, HD), 0)
    ones = jnp.where(lanes == 0, 1.0, 0.0).astype(BF)
    below = jnp.where(lax.broadcasted_iota(jnp.int32, (16, total), 0) == 0, 1.0, 0.0).astype(BF)
    for block in range(4):
        rows = slice(block * TILE, (block + 1) * TILE)
        usable = meta[8 + block] + index < meta[12]
        bias = jnp.where((lanes == 0) & ~usable, MASKED, 0.0).astype(BF)
        for head in range(heads):
            at = width + head * HD
            q_ext[head, rows, 0:HD] = proj[rows, at : at + HD]
            q_ext[head, rows, HD : 2 * HD] = ones
            at = 2 * width + head * HD
            k_ext[head, rows, 0:HD] = proj[rows, at : at + HD]
            k_ext[head, rows, HD : 2 * HD] = bias
    for head in range(heads):
        at = 3 * width + head * HD
        v_flip[head, 0:HD, :] = proj[:, at : at + HD].T
        v_flip[head, HD : HD + 16, :] = below
    inverse[...] = jnp.ones_like(inverse)
    for head in range(heads):
        for start in range(0, total, QUERY_ROWS):
            rows = slice(start, start + QUERY_ROWS)
            scores = mm_nt(k_ext[head], q_ext[head, rows, :])
            top = jnp.max(scores, axis=0, keepdims=True)
            raised = jnp.exp(scores - top).astype(BF)
            expo[head, :, rows] = raised
            mixed = mm(v_flip[head], raised)
            inv = 1.0 / mixed[HD : HD + 1, :]
            inverse[head : head + 1, rows] = inv
            context[rows, head * HD : (head + 1) * HD] = (mixed[0:HD, :] * inv).astype(BF).T
    if not first:
        partial[...] = (
            mm_nt(context_first[...], weight_first[:, 0:width])
            + mm_nt(context[...], weight[:, 0:width])
        ).astype(BF)


SMEM = pl.BlockSpec(memory_space=pltpu.SMEM)
VMEM = pl.BlockSpec(memory_space=pltpu.VMEM)
HBM = pl.BlockSpec(memory_space=pltpu.HBM)


def attention_forward(meta, heads, block_rows, pieces, orders, rows_in=(), gain=None, before=None):
    width = pieces[0].shape[1]
    model = rows_in[0].shape[1] if rows_in else before[0].shape[1]
    total = 4 * TILE
    rows = jax.ShapeDtypeStruct((total, model), BF)
    numerators = jax.ShapeDtypeStruct((heads, total, total), BF)
    if rows_in:
        in_fast, in_slow = [gain], [*rows_in, *pieces]
        more, extra = [rows], [pltpu.VMEM((total, model), BF)]
    else:
        in_fast, in_slow = [*before], [*pieces]
        more, extra = [rows], []
    return pl.pallas_call(
        functools.partial(forward_kernel, heads, len(rows_in), orders, block_rows),
        in_specs=[SMEM] + [VMEM] * len(in_fast) + [HBM] * len(in_slow),
        out_specs=[VMEM] * 6,
        out_shape=[
            jax.ShapeDtypeStruct((8, total), F32),
            jax.ShapeDtypeStruct((total, heads * HD), BF),
            numerators,
            jax.ShapeDtypeStruct((model, width), BF),
            jax.ShapeDtypeStruct((total, width), BF),
            *more,
        ],
        scratch_shapes=[
            pltpu.VMEM((heads, total, 2 * HD), BF),
            pltpu.VMEM((heads, total, 2 * HD), BF),
            pltpu.VMEM((heads, HD + 16, total), BF),
            pltpu.SemaphoreType.DMA((blocks_of(orders),)),
            pltpu.SemaphoreType.DMA((4,)),
            *extra,
        ],
        compiler_params=pltpu.CompilerParams(vmem_limit_bytes=ATTEND_LIMIT),
        cost_estimate=COST,
        name="attention_forward",
    )(meta, *in_fast, *in_slow)


def gelu_terms(gate):
    scale = 0.7978845608028654
    cube = 0.044715
    square = gate * gate
    bent = jnp.tanh(scale * gate * (1.0 + cube * square))
    half = 0.5 * (1.0 + bent)
    slope = half + 0.5 * gate * (1.0 - bent * bent) * (scale * (1.0 + 3.0 * cube * square))
    return gate * half, slope


def feed_kernel(n_rows, n_cots, in_orders, orders, block_rows, meta, *refs):
    first = n_rows > 0
    refs = list(refs)
    take = lambda count: [refs.pop(0) for _ in range(count)]
    if first:
        rows_in = take(n_rows)
        part_mine, part_other, gain = take(3)
    else:
        normed, result_before, back_before = take(3)
    cots = take(n_cots)
    pieces = take(len(in_orders))
    if first:
        normed, result, back = take(3)
    else:
        mine, other, back = take(3)
    groups = take(len(orders))
    weight, hidden, d_gate, d_up, cot, grad, sems = take(7)
    units = weight.shape[1] // 3
    copies = place(meta, pieces, in_orders, weight, block_rows, sems)
    for block in range(4):
        rows = slice(block * TILE, (block + 1) * TILE)
        cot[rows, :] = row_block(cots, block)
        if first:
            swapped = slice(((block + 2) % 4) * TILE, ((block + 2) % 4 + 1) * TILE)
            features = (
                row_block(rows_in, block).astype(F32)
                + part_mine[rows, :].astype(F32)
                + part_other[swapped, :].astype(F32)
            )
            features = features.astype(BF).astype(F32)
            normed[rows, :] = (features * inverse_rms(features) * gain[...]).astype(BF)
    wait_all(copies)
    for start in range(0, 4 * TILE, FEED_ROWS):
        rows = slice(start, start + FEED_ROWS)
        pre = mm(normed[rows, :], weight[:, 0 : 2 * units])
        act, slope = gelu_terms(pre[:, :units])
        up = pre[:, units:]
        low = (act * up).astype(BF)
        hidden[rows, :] = low
        d_hidden = mm(cot[rows, :], weight[:, 2 * units :])
        gate_low = (d_hidden * up * slope).astype(BF)
        up_low = (d_hidden * act).astype(BF)
        d_gate[rows, :] = gate_low
        d_up[rows, :] = up_low
        down = mm_nt(low, weight[:, 2 * units :])
        through = mm_nt(gate_low, weight[:, 0:units]) + mm_nt(up_low, weight[:, units : 2 * units])
        if first:
            result[rows, :] = down.astype(BF)
            back[rows, :] = through.astype(BF)
        else:
            down = (down + result_before[rows, :].astype(F32)).astype(BF)
            if start < 2 * TILE:
                mine[rows, :] = down[: 2 * TILE - start]
            if start + FEED_ROWS > 2 * TILE:
                begin = max(start - 2 * TILE, 0)
                other[begin : start + FEED_ROWS - 2 * TILE, :] = down[begin + 2 * TILE - start :]
            back[rows, :] = (through + back_before[rows, :].astype(F32)).astype(BF)
    grad[:, 2 * units :] = mm_tn(cot[...], hidden[...]).astype(BF)
    grad[:, 0:units] = mm_tn(normed[...], d_gate[...]).astype(BF)
    grad[:, units : 2 * units] = mm_tn(normed[...], d_up[...]).astype(BF)
    disperse(meta, grad, groups, orders, block_rows)


def feed_forward(meta, block_rows, cots, pieces, in_orders, orders, rows_in=(), before=()):
    width = pieces[0].shape[1]
    model = cots[0].shape[1]
    total = 4 * TILE
    units = width // 3
    full = jax.ShapeDtypeStruct((total, model), BF)
    half = jax.ShapeDtypeStruct((2 * TILE, model), BF)
    operands = [*rows_in, *before, *cots, *pieces]
    out_shape = [full, full, full] if rows_in else [half, half, full]
    out_shape += [
        jax.ShapeDtypeStruct((len(order) * block_rows, width), BF) for order in orders
    ]
    return pl.pallas_call(
        functools.partial(
            feed_kernel, len(rows_in), len(cots), in_orders, orders, block_rows
        ),
        in_specs=[SMEM] + [VMEM] * (len(operands) - len(pieces)) + [HBM] * len(pieces),
        out_specs=[VMEM] * len(out_shape),
        out_shape=out_shape,
        scratch_shapes=[
            pltpu.VMEM((model, width), BF),
            pltpu.VMEM((total, units), BF),
            pltpu.VMEM((total, units), BF),
            pltpu.VMEM((total, units), BF),
            pltpu.VMEM((total, model), BF),
            pltpu.VMEM((model, width), BF),
            pltpu.SemaphoreType.DMA((blocks_of(in_orders),)),
        ],
        compiler_params=pltpu.CompilerParams(vmem_limit_bytes=FEED_LIMIT),
        cost_estimate=COST,
        name="feed_forward",
    )(meta, *operands)


def middle_kernel(heads, n_rows, n_cots, *refs):
    refs = list(refs)
    take = lambda count: [refs.pop(0) for _ in range(count)]
    rows_in = take(n_rows)
    part_mine, part_other, gain = take(3)
    cots = take(n_cots)
    d_mine, d_other, context_near, context_far = take(4)
    weight_near, weight_far = take(2)
    d_middle, d_context_near, d_context_far, grad_near, grad_far, d_gain = take(6)
    (d_all,) = take(1)
    width = heads * HD
    gains = 0.0
    for block in range(4):
        rows = slice(block * TILE, (block + 1) * TILE)
        swapped = slice(((block + 2) % 4) * TILE, ((block + 2) % 4 + 1) * TILE)
        features = (
            row_block(rows_in, block).astype(F32)
            + part_mine[rows, :].astype(F32)
            + part_other[swapped, :].astype(F32)
        )
        features = features.astype(BF).astype(F32)
        inverse = inverse_rms(features)
        back = d_mine[rows, :].astype(F32) + d_other[swapped, :].astype(F32)
        scaled = back * gain[...]
        inner = jnp.mean(scaled * features, axis=-1, keepdims=True)
        result = (
            row_block(cots, block).astype(F32)
            + inverse * scaled
            - features * (inverse * inverse * inverse * inner)
        )
        d_all[rows, :] = result.astype(BF)
        if block < 2:
            d_middle[rows, :] = result
            gains += jnp.sum(back * features * inverse, axis=0, keepdims=True)
    d_gain[...] = jnp.broadcast_to(gains, d_gain.shape)
    d_context_near[...] = mm(d_all[...], weight_near[:, 0:width]).astype(BF)
    d_context_far[...] = mm(d_all[...], weight_far[:, 0:width]).astype(BF)
    grad_near[...] = mm_tn(d_all[...], context_near[...]).astype(BF)
    grad_far[...] = mm_tn(d_all[...], context_far[...]).astype(BF)


def middle_backward(heads, rows_in, parts, gain, cots, d_normed, contexts, weights):
    model = gain.shape[1]
    total = 4 * TILE
    width = heads * HD
    operands = [*rows_in, *parts, gain, *cots, *d_normed, *contexts, *weights]
    return pl.pallas_call(
        functools.partial(middle_kernel, heads, len(rows_in), len(cots)),
        in_specs=[VMEM] * len(operands),
        out_specs=[VMEM] * 6,
        out_shape=[
            jax.ShapeDtypeStruct((2 * TILE, model), F32),
            jax.ShapeDtypeStruct((total, width), BF),
            jax.ShapeDtypeStruct((total, width), BF),
            jax.ShapeDtypeStruct((model, width), BF),
            jax.ShapeDtypeStruct((model, width), BF),
            jax.ShapeDtypeStruct((8, model), F32),
        ],
        scratch_shapes=[
            pltpu.VMEM((total, model), BF),
        ],
        compiler_params=pltpu.CompilerParams(vmem_limit_bytes=MIDDLE_LIMIT),
        cost_estimate=COST,
        name="middle_backward",
    )(*operands)


def in_two(*rows):
    high = [row.astype(BF).astype(F32) for row in rows]
    index = lax.broadcasted_iota(jnp.int32, (16, rows[0].shape[1]), 0)
    result = jnp.zeros((16, rows[0].shape[1]), F32)
    for number, row in enumerate(rows):
        result = jnp.where(index == 2 * number, high[number], result)
        result = jnp.where(index == 2 * number + 1, row - high[number], result)
    return result.astype(BF)


def from_two(rows):
    return [
        rows[2 * k : 2 * k + 1].astype(F32) + rows[2 * k + 1 : 2 * k + 2].astype(F32)
        for k in range(2)
    ]


def finish_kernel(d_mine, d_other, keep, got, d_middle, gain, mine, theirs):
    for number, rows_in in enumerate((keep, got)):
        rows = slice(number * TILE, (number + 1) * TILE)
        features = rows_in[...].astype(F32)
        inverse = inverse_rms(features)
        scaled = (d_mine[rows, :].astype(F32) + d_other[rows, :].astype(F32)) * gain[...]
        inner = jnp.mean(scaled * features, axis=-1, keepdims=True)
        result = (
            d_middle[rows, :] + inverse * scaled - features * (inverse * inverse * inverse * inner)
        ).astype(BF)
        if number == 0:
            mine[...] = result
        else:
            theirs[...] = result


def backward_kernel(heads, orders, block_rows, last, meta, *refs):
    refs = list(refs)
    take = lambda count: [refs.pop(0) for _ in range(count)]
    inverse, context, expo, weight, proj, normed, d_context, grad_out = take(8)
    if last:
        gain, gain_rows = take(2)
    if last:
        (before,) = take(1)
        mine, other = take(2)
    else:
        (result,) = take(1)
    groups = take(len(orders))
    do_ext, v_ext, d_proj, grad = take(4)
    width = heads * HD
    total = 4 * TILE
    lanes = lax.broadcasted_iota(jnp.int32, (total, HD), 1)
    columns = inverse[...].T
    d_proj[:, 0:width] = jnp.zeros((total, width), BF)
    for head in range(heads):
        at = head * HD
        scaled = (d_context[:, at : at + HD].astype(F32) * columns[:, head : head + 1]).astype(BF)
        inner = -jnp.sum(
            scaled.astype(F32) * context[:, at : at + HD].astype(F32), axis=-1, keepdims=True
        )
        high = inner.astype(BF).astype(F32)
        do_ext[head, :, 0:HD] = scaled
        do_ext[head, :, HD : 2 * HD] = jnp.where(
            lanes == 0, high, jnp.where(lanes == 1, inner - high, 0.0)
        ).astype(BF)
    for head in range(heads):
        at = 3 * width + head * HD
        v_ext[head, :, 0:HD] = proj[:, at : at + HD]
        v_ext[head, :, HD : 2 * HD] = jnp.where(lanes < 2, 1.0, 0.0).astype(BF)
    for head in range(heads):
        q_at, k_at, v_at = (part * width + head * HD for part in (1, 2, 3))
        raised = expo[head]
        d_probs = mm_nt(v_ext[head], do_ext[head])
        d_scores = (raised.astype(F32) * d_probs).astype(BF)
        d_queries = mm(proj[:, k_at : k_at + HD].T, d_scores)
        d_keys = mm_nt(proj[:, q_at : q_at + HD].T, d_scores)
        d_values = mm_nt(do_ext[head, :, 0:HD].T, raised)
        d_proj[:, q_at : q_at + HD] = d_queries.astype(BF).T
        d_proj[:, k_at : k_at + HD] = d_keys.astype(BF).T
        d_proj[:, v_at : v_at + HD] = d_values.astype(BF).T
    grad[...] = mm_tn(normed[...], d_proj[...]).astype(BF)
    grad[:, 0:width] = grad_out[...]
    disperse(meta, grad, groups, orders, block_rows)
    through = mm_nt(d_proj[...], weight[...])
    if last:
        through = through + before[...].astype(F32)
        mine[...] = through[0 : 2 * TILE].astype(BF)
        other[...] = through[2 * TILE :].astype(BF)
        first = jnp.sum(through * normed[...].astype(F32), axis=0, keepdims=True) / gain[...]
        end = len(orders[-1]) * block_rows
        groups[-1][end : end + 16, :] = in_two(first, gain_rows[0:1, :])
    else:
        result[...] = through.astype(BF)


def attention_backward(
    meta, heads, block_rows, normed, saved, d_context, grad_out, orders, before=None
):
    last = before is not None
    weight, proj = saved[3:]
    model, width = weight.shape
    total = proj.shape[0]
    rows = jax.ShapeDtypeStruct((total, model), BF)
    in_fast = [*saved, normed, d_context, grad_out]
    scratch = [
        pltpu.VMEM((heads, total, 2 * HD), BF),
        pltpu.VMEM((heads, total, 2 * HD), BF),
        pltpu.VMEM((total, width), BF),
        pltpu.VMEM((model, width), BF),
    ]
    sizes = [len(order) * block_rows for order in orders]
    if last:
        in_fast += [*before[1:], before[0]]
        out_shape = [jax.ShapeDtypeStruct((2 * TILE, model), BF)] * 2
        sizes[-1] += 16
    else:
        out_shape = [rows]
    out_shape += [jax.ShapeDtypeStruct((size, width), BF) for size in sizes]
    return pl.pallas_call(
        functools.partial(backward_kernel, heads, orders, block_rows, last),
        in_specs=[SMEM] + [VMEM] * len(in_fast),
        out_specs=[VMEM] * len(out_shape),
        out_shape=out_shape,
        scratch_shapes=scratch,
        compiler_params=pltpu.CompilerParams(vmem_limit_bytes=BACK_LIMIT),
        cost_estimate=COST,
        name="attention_backward",
    )(meta, *in_fast)


def add(*terms):
    return sum(term.astype(F32) for term in terms)


def hold(values, *others):
    values, others = lax.optimization_barrier((values, others))
    return values, *others


def plus(*terms):
    return sum(term.astype(F32) for term in terms)


def call_local(kernel, out_shape, *operands):
    return pl.pallas_call(
        kernel,
        in_specs=[VMEM] * len(operands),
        out_specs=[VMEM] * len(out_shape),
        out_shape=[jax.ShapeDtypeStruct(shape, kind) for shape, kind in out_shape],
        compiler_params=pltpu.CompilerParams(vmem_limit_bytes=MIDDLE_LIMIT),
        cost_estimate=COST,
        name=kernel.__name__.replace("kernel", "backward"),
    )(*operands)


def join_kernel(
    own_high, y_high, y_low, xy_low, over, one_in, two_in, three_in,
    two, three, y_low_plus, over_plus,
):
    rows = two.shape[0]
    for at, dest in ((slice(0, rows), two), (slice(rows, 2 * rows), three)):
        dest[...] = plus(own_high[at, :], y_high[at, :]).astype(BF)
    y_low_plus[...] = plus(y_low[...], xy_low[...]).astype(BF)
    over_plus[...] = plus(over[...], one_in[...], two_in[...], three_in[...]).astype(BF)


def meet_kernel(y_all, xy_all, result):
    result[...] = plus(y_all[...], xy_all[...]).astype(BF)


def last_kernel(own_low, feed_y, own, one):
    rows = own.shape[0]
    own[...] = plus(own_low[0:rows, :], feed_y[0:rows, :])
    one[...] = plus(own_low[rows:, :], feed_y[rows:, :]).astype(BF)


def fold_kernel(own, sent, over_x, over_y, total, gains, *messages):
    rows = total.shape[0]
    end = 4 * rows
    mine, theirs = from_two(sent[end : end + 16, :]), from_two(over_x[end : end + 16, :])
    pairs = in_two(*(a + b for a, b in zip(mine, theirs)))
    gains[...] = pairs.astype(F32)
    for index in range(4):
        at = slice(index * rows, (index + 1) * rows)
        block = plus(own[at, :], over_x[at, :], over_y[at, :])
        if index == 0:
            total[...] = block
        else:
            messages[index - 1][0:rows, :] = block.astype(BF)
            messages[index - 1][rows:, :] = pairs


class Links:
    def __init__(self, wide, narrow):
        self.wide, self.narrow = wide, narrow
        self.planes = wide // 2
        self.staged = wide == 8

    def y(self, values):
        return lax.ppermute(values, "narrow", [(i, (i + 2) % 4) for i in range(4)])

    def core(self, values):
        return lax.ppermute(values, "narrow", [(i, i ^ 1) for i in range(4)])

    def across(self, values):
        return lax.ppermute(values, "narrow", [(i, (i + 2) % 4 ^ 1) for i in range(4)])

    def x(self, values):
        return lax.ppermute(values, "wide", [(i, i ^ 1) for i in range(self.wide)])

    def z(self, values, ahead):
        turn = lambda i: ((i // 2 + ahead) % self.planes) * 2 + i % 2
        return lax.ppermute(values, "wide", [(i, turn(i)) for i in range(self.wide)])

    def whole_gather(self, piece):
        near = lax.all_gather(piece, "wide", axis=0, tiled=True)
        return [near], [self.y(near)]

    def whole_reduce(self, near, far):
        return lax.psum_scatter(near, "wide", scatter_dimension=0, tiled=True).astype(
            F32
        ) + lax.psum_scatter(self.y(far), "wide", scatter_dimension=0, tiled=True).astype(F32)


def on_device(
    tokens,
    lengths,
    norm_one,
    w_query,
    w_key,
    w_value,
    w_out,
    norm_two,
    w_gate,
    w_up,
    w_down,
    cotangent,
):
    model = tokens.shape[-1]
    wide, narrow = lax.axis_size("wide"), lax.axis_size("narrow")
    links = Links(wide, narrow)
    heads = w_query.shape[1] // HD
    head_width = heads * HD
    units = w_gate.shape[1]
    at_wide, at_narrow = lax.axis_index("wide"), lax.axis_index("narrow")
    y, c = at_narrow >> 1, at_narrow & 1
    x, z = at_wide & 1, at_wide >> 1

    staged = links.staged
    planes = links.planes
    rows = model // wide
    turned = [((z + k) & (planes - 1)) * 2 + (x ^ side) for side in range(2) for k in range(4)]
    blocks = [((y ^ far) * 2 + (c ^ side)) * TILE for side in range(2) for far in range(2)]
    length = lax.dynamic_index_in_dim(lengths, y, 0, keepdims=False)[0]
    numbers = [
        *(spot * rows for spot in turned),
        *blocks,
        length,
    ]
    meta = jnp.stack([jnp.asarray(number, jnp.int32) for number in numbers])
    first_item = y == 0

    gain_one = norm_one.reshape(1, model)
    gain_two = norm_two.reshape(1, model)

    def keep_give(rows):
        flat = rows.reshape(2, TILE, model)
        return (
            lax.dynamic_index_in_dim(flat, y, 0, keepdims=False),
            lax.dynamic_index_in_dim(flat, 1 - y, 0, keepdims=False),
        )

    attn_piece = jnp.concatenate([w_out.T, w_query, w_key, w_value], axis=1)
    feed_piece = jnp.concatenate([w_gate, w_up, w_down.T], axis=1)
    keep, give = keep_give(tokens)
    keep_cot, give_cot = keep_give(cotangent)
    half = planes // 2 * rows
    if staged:
        block_rows = rows
        quarters = ((0, 1), (2, 3), (4, 5), (6, 7))
        attn_near_in = attn_far_in = ((0, 1, 2, 3), (4, 5, 6, 7))
        feed_near_in = ((0,), (1,), (3,), (2,), (4, 5, 7), (6,))
        feed_far_in = ((0, 1, 3), (2,), (4, 5), (7, 6))
        attn_out = ((0, 1, 2, 3), (4, 5, 6, 7))
        feed_near_out = ((0, 1), (2, 3), (4,), (5,), (6,), (7,))
    else:
        block_rows = model
        quarters = attn_out = feed_near_out = ((0,),)
        attn_near_in = attn_far_in = feed_near_in = feed_far_in = ((0,),)

    got = links.y(give)
    if staged:
        column = [attn_piece] + [links.z(attn_piece, planes - k) for k in range(1, planes)]
        column = jnp.concatenate(column, axis=0)
        over_x, over_y = links.x(column), links.y(column)
        feed_piece, column, first_item = hold(feed_piece, column, first_item)
        feed_one = links.z(feed_piece, planes - 1)
        feed_three = links.z(feed_piece, planes - 3)
    else:
        attn_near, attn_far = links.whole_gather(attn_piece)
        feed_near, feed_far = links.whole_gather(feed_piece)
    from_keep = links.core(keep)
    if staged:
        got, feed_one, feed_three = hold(got, feed_one, feed_three)
    rows_in = [keep, got, from_keep, links.core(got)]
    if staged:
        over_y, over_x = hold(over_y, over_x)
        give_cot, over_y = hold(give_cot, over_y)
        attn_near = [column, over_x]
        rows_in, over_y, meta = hold(rows_in, over_y, meta)
        attn_far = [over_y, links.x(over_y)]
        three = jnp.concatenate([feed_piece, feed_one, feed_three], axis=0)
        feed_x = links.x(three)
        feed_y = links.y(three)
        feed_piece, feed_one = hold(feed_piece, feed_one)
        feed_two = links.z(feed_piece, planes - 2)
    got_cot = links.y(give_cot)

    inv_near, context_near, expo_near, *kept_near, normed = attention_forward(
        meta, heads, block_rows, attn_near, attn_near_in, rows_in=rows_in, gain=gain_one
    )
    if staged:
        normed, feed_two, attn_far = hold(normed, feed_two, attn_far)
        feed_x_two = links.x(feed_two)
        feed_y_two = links.y(feed_two)
    inv_far, context_far, expo_far, *kept_far, part_mine = attention_forward(
        meta, heads, block_rows, attn_far, attn_far_in,
        before=(normed, context_near, kept_near[0]),
    )
    if staged:
        part_mine, got_cot, feed_x, feed_y, feed_x_two, feed_y_two = hold(
            part_mine, got_cot, feed_x, feed_y, feed_x_two, feed_y_two
        )
    part_other = links.core(part_mine)
    own_cot = jnp.concatenate([keep_cot, got_cot], axis=0)
    cots = [own_cot, links.core(own_cot)]
    if staged:
        feed_near = [feed_piece, feed_one, feed_three, feed_two, feed_x, feed_x_two]
        feed_far = [
            feed_y,
            feed_y_two,
            links.y(feed_x[: 2 * rows]),
            links.x(jnp.concatenate([feed_y[2 * rows :], feed_y_two], axis=0)),
        ]
    parts = (part_mine, part_other)

    normed_two, down_near, back_near, *near = feed_forward(
        meta, block_rows, cots, feed_near, feed_near_in, feed_near_out, rows_in=rows_in,
        before=(*parts, gain_two),
    )
    if staged:
        own_low, own_high, over, *pieces = near
        over_one = links.z(pieces[0], 1)
    mlp_mine, mlp_other, d_mine, *far = feed_forward(
        meta, block_rows, cots, feed_far, feed_far_in, quarters,
        before=(normed_two, down_near, back_near),
    )
    if staged:
        mlp_other, over_one = hold(mlp_other, over_one)
        over_three = links.z(pieces[2], 3)
        y_low, y_high, xy_low, xy_high = far
        from_xy_high = links.x(xy_high)
    else:
        feed_grad = links.whole_reduce(*near, *far)
    d_other = links.core(d_mine)
    half_rows = 2 * TILE
    output = (
        jnp.concatenate(rows_in[:2], axis=0).astype(F32)
        + part_mine[:half_rows].astype(F32)
        + part_other[half_rows:].astype(F32)
        + mlp_mine.astype(F32)
        + links.core(mlp_other).astype(F32)
    ).astype(BF)
    output_back = links.y(output[TILE:])
    d_middle, d_context_near, d_context_far, out_near, out_far, gain_rows = middle_backward(
        heads,
        rows_in,
        parts,
        gain_two,
        cots,
        (d_mine, d_other),
        (context_near, context_far),
        (kept_near[0], kept_far[0]),
    )
    if staged:
        d_context_far, from_xy_high, output_back, over_three = hold(
            d_context_far, from_xy_high, output_back, over_three
        )
        xy_low, over_two, from_xy_high = hold(xy_low, pieces[1], from_xy_high)
        over_two = links.z(over_two, 2)
        from_y_high = links.y(add(y_high, from_xy_high).astype(BF))
        from_xy_low = links.x(xy_low)
    d_first, *far = attention_backward(
        meta, heads, block_rows, normed, (inv_far, context_far, expo_far, *kept_far),
        d_context_far, out_far, attn_out,
    )
    if staged:
        d_first, from_y_high, from_xy_low, over_two = hold(
            d_first, from_y_high, from_xy_low, over_two
        )
        feed = (rows, feed_piece.shape[1])
        feed_half = (half, feed_piece.shape[1])
        feed_two, feed_three, feed_y_low, feed_over = call_local(
            join_kernel, [(feed, BF), (feed, BF), (feed_half, BF), (feed, BF)],
            own_high, from_y_high, y_low, from_xy_low, over, over_one, over_two, over_three,
        )
        feed_two = links.z(feed_two, 2)
        feed_low = own_low
        y_all, xy_all = far
        from_xy = links.x(xy_all)
        from_feed_y = links.y(feed_y_low)
    last_mine, last_other, *near = attention_backward(
        meta, heads, block_rows, normed, (inv_near, context_near, expo_near, *kept_near),
        d_context_near, out_near, attn_out, before=(d_first, gain_one, gain_rows),
    )
    if staged:
        last_other, near, from_xy, from_feed_y = hold(last_other, near, from_xy, from_feed_y)
        own_all, x_all = near
        (y_all,) = call_local(meet_kernel, [(y_all.shape, BF)], y_all, from_xy)
        y_all, feed_two = hold(y_all, feed_two)
        from_x, from_y = links.x(x_all), links.y(y_all)
        feed_parts = [feed_two, links.z(feed_three, 3)]
    else:
        attn_grad = links.whole_reduce(near[0][:model], *far)
        gains = lax.psum(near[0][model:].astype(F32), "wide")
    got_other = links.core(last_other)
    mine, theirs = call_local(
        finish_kernel,
        [((TILE, model), BF)] * 2,
        last_mine, got_other, *rows_in[:2], d_middle, gain_one,
    )
    if staged:
        feed_own, feed_one = call_local(
            last_kernel, [(feed, F32), (feed, BF)], feed_low, from_feed_y
        )
        feed_parts.append(links.z(feed_one, 1))
        from_x, theirs, feed_own, feed_parts = hold(from_x, theirs, feed_own, feed_parts)
    back = links.y(theirs)
    if staged:
        width = own_all.shape[1]
        apart = ((rows + 16, width), BF)
        attn_grad, gains, *messages = call_local(
            fold_kernel, [((rows, width), F32), ((16, width), F32), apart, apart, apart],
            own_all, x_all, from_x, from_y,
        )
        feed_over, attn_grad = hold(feed_over, attn_grad)
        feed_parts.append(links.x(feed_over))
        arrived = [links.z(piece, k + 1) for k, piece in enumerate(messages)]
        attn_grad = add(attn_grad, *(part[:rows] for part in arrived))
        gains = add(gains, *(part[rows:] for part in arrived))
        feed_grad = add(feed_own, *feed_parts)
    gains = (gains + links.core(gains)) + (links.y(gains) + links.across(gains))

    def in_order(own, other):
        stacked = jnp.where(first_item, jnp.stack([own, other]), jnp.stack([other, own]))
        return stacked.reshape(tokens.shape)

    return (
        in_order(output[:TILE], output_back),
        in_order(mine, back),
        gains[0] + gains[1],
        attn_grad[:, head_width : 2 * head_width],
        attn_grad[:, 2 * head_width : 3 * head_width],
        attn_grad[:, 3 * head_width :],
        attn_grad[:, :head_width].T,
        gains[2] + gains[3],
        feed_grad[:, :units],
        feed_grad[:, units : 2 * units],
        feed_grad[:, 2 * units :].T,
    )


def solution(mesh):
    in_specs = (
        P(None, "wide", "narrow", None),
        P(None, "wide"),
        P(),
        P("wide", "narrow"),
        P("wide", "narrow"),
        P("wide", "narrow"),
        P("narrow", "wide"),
        P(),
        P("wide", "narrow"),
        P("wide", "narrow"),
        P("narrow", "wide"),
        P(None, "wide", "narrow", None),
    )
    out_specs = (
        P(None, "wide", "narrow", None),
        P(None, "wide", "narrow", None),
        P(),
        P("wide", "narrow"),
        P("wide", "narrow"),
        P("wide", "narrow"),
        P("narrow", "wide"),
        P(),
        P("wide", "narrow"),
        P("wide", "narrow"),
        P("narrow", "wide"),
    )
    return jax.shard_map(
        on_device, mesh=mesh, in_specs=in_specs, out_specs=out_specs, check_vma=False
    )
```

```python
import functools

import jax
import jax.numpy as jnp
from jax import lax
from jax.experimental import pallas as pl
from jax.experimental.pallas import tpu as pltpu
from jax.sharding import PartitionSpec as P

HD = 64
EPSILON = 1e-06
MASKED = -1e30
TILE = 256
FEED_ROWS = 1024
QUERY_ROWS = 1024
MIDDLE_LIMIT = 8 * 1024 * 1024
BACK_LIMIT = 14 * 1024 * 1024
ATTEND_LIMIT = 11 * 1024 * 1024
FEED_LIMIT = 22 * 1024 * 1024
COST = pl.CostEstimate(flops=10**6, bytes_accessed=10**5, transcendentals=0)
BF = jnp.bfloat16
F32 = jnp.float32


def mm(left, right):
    return jnp.dot(left, right, preferred_element_type=F32)


def mm_nt(left, right):
    return lax.dot_general(left, right, (((1,), (1,)), ((), ())), preferred_element_type=F32)


def mm_tn(left, right):
    return lax.dot_general(left, right, (((0,), (0,)), ((), ())), preferred_element_type=F32)


def inverse_rms(features):
    return lax.rsqrt(jnp.mean(features * features, axis=-1, keepdims=True) + EPSILON)


def place(meta, pieces, orders, dest, rows):
    for piece, order in zip(pieces, orders):
        for number, index in enumerate(order):
            at = 0 if rows == dest.shape[0] else pl.multiple_of(meta[index], 16)
            dest[pl.ds(at, rows), :] = piece[number * rows : (number + 1) * rows, :]


def disperse(meta, source, groups, orders, rows):
    for group, order in zip(groups, orders):
        for place, index in enumerate(order):
            at = 0 if rows == source.shape[0] else pl.multiple_of(meta[index], 16)
            group[place * rows : (place + 1) * rows, :] = source[pl.ds(at, rows), :]


def row_block(refs, block):
    start = block * TILE
    for ref in refs:
        if start < ref.shape[0]:
            return ref[start : start + TILE, :]
        start -= ref.shape[0]


def forward_kernel(heads, n_rows, orders, block_rows, meta, *refs):
    first = n_rows > 0
    refs = list(refs)
    take = lambda count: [refs.pop(0) for _ in range(count)]
    width = heads * HD
    total = 4 * TILE
    if first:
        (gain,) = take(1)
        sources = take(n_rows)
    else:
        normed, context_first, weight_first = take(3)
    pieces = take(len(orders))
    inverse, context, expo, weight, proj = take(5)
    if first:
        (normed,) = take(1)
    else:
        (partial,) = take(1)
    q_ext, k_ext, v_flip = take(3)
    place(meta, pieces, orders, weight, block_rows)
    if first:
        for block in range(4):
            rows = slice(block * TILE, (block + 1) * TILE)
            features = row_block(sources, block).astype(F32)
            normed[rows, :] = (features * inverse_rms(features) * gain[...]).astype(BF)
    proj[...] = mm(normed[...], weight[...]).astype(BF)
    lanes = lax.broadcasted_iota(jnp.int32, (TILE, HD), 1)
    index = lax.broadcasted_iota(jnp.int32, (TILE, HD), 0)
    ones = jnp.where(lanes == 0, 1.0, 0.0).astype(BF)
    below = jnp.where(lax.broadcasted_iota(jnp.int32, (16, total), 0) == 0, 1.0, 0.0).astype(BF)
    for block in range(4):
        rows = slice(block * TILE, (block + 1) * TILE)
        usable = meta[8 + block] + index < meta[12]
        bias = jnp.where((lanes == 0) & ~usable, MASKED, 0.0).astype(BF)
        for head in range(heads):
            at = width + head * HD
            q_ext[head, rows, 0:HD] = proj[rows, at : at + HD]
            q_ext[head, rows, HD : 2 * HD] = ones
            at = 2 * width + head * HD
            k_ext[head, rows, 0:HD] = proj[rows, at : at + HD]
            k_ext[head, rows, HD : 2 * HD] = bias
    for head in range(heads):
        at = 3 * width + head * HD
        v_flip[head, 0:HD, :] = proj[:, at : at + HD].T
        v_flip[head, HD : HD + 16, :] = below
    inverse[...] = jnp.ones_like(inverse)
    for head in range(heads):
        for start in range(0, total, QUERY_ROWS):
            rows = slice(start, start + QUERY_ROWS)
            scores = mm_nt(k_ext[head], q_ext[head, rows, :])
            top = jnp.max(scores, axis=0, keepdims=True)
            raised = jnp.exp(scores - top).astype(BF)
            expo[head, :, rows] = raised
            mixed = mm(v_flip[head], raised)
            inv = 1.0 / mixed[HD : HD + 1, :]
            inverse[head : head + 1, rows] = inv
            context[rows, head * HD : (head + 1) * HD] = (mixed[0:HD, :] * inv).astype(BF).T
    if not first:
        partial[...] = (
            mm_nt(context_first[...], weight_first[:, 0:width])
            + mm_nt(context[...], weight[:, 0:width])
        ).astype(BF)


SMEM = pl.BlockSpec(memory_space=pltpu.SMEM)
VMEM = pl.BlockSpec(memory_space=pltpu.VMEM)


def attention_forward(meta, heads, block_rows, pieces, orders, rows_in=(), gain=None, before=None):
    width = pieces[0].shape[1]
    model = rows_in[0].shape[1] if rows_in else before[0].shape[1]
    total = 4 * TILE
    rows = jax.ShapeDtypeStruct((total, model), BF)
    numerators = jax.ShapeDtypeStruct((heads, total, total), BF)
    operands = [gain, *rows_in] if rows_in else [*before]
    operands += pieces
    return pl.pallas_call(
        functools.partial(forward_kernel, heads, len(rows_in), orders, block_rows),
        in_specs=[SMEM] + [VMEM] * len(operands),
        out_specs=[VMEM] * 6,
        out_shape=[
            jax.ShapeDtypeStruct((8, total), F32),
            jax.ShapeDtypeStruct((total, heads * HD), BF),
            numerators,
            jax.ShapeDtypeStruct((model, width), BF),
            jax.ShapeDtypeStruct((total, width), BF),
            rows,
        ],
        scratch_shapes=[
            pltpu.VMEM((heads, total, 2 * HD), BF),
            pltpu.VMEM((heads, total, 2 * HD), BF),
            pltpu.VMEM((heads, HD + 16, total), BF),
        ],
        compiler_params=pltpu.CompilerParams(vmem_limit_bytes=ATTEND_LIMIT),
        cost_estimate=COST,
        name="attention_forward",
    )(meta, *operands)


def gelu_terms(gate):
    scale = 0.7978845608028654
    cube = 0.044715
    square = gate * gate
    bent = jnp.tanh(scale * gate * (1.0 + cube * square))
    half = 0.5 * (1.0 + bent)
    slope = half + 0.5 * gate * (1.0 - bent * bent) * (scale * (1.0 + 3.0 * cube * square))
    return gate * half, slope


def feed_kernel(n_rows, n_cots, in_orders, orders, block_rows, meta, *refs):
    first = n_rows > 0
    refs = list(refs)
    take = lambda count: [refs.pop(0) for _ in range(count)]
    if first:
        rows_in = take(n_rows)
        part_mine, part_other, gain = take(3)
    else:
        normed, result_before, back_before = take(3)
    cots = take(n_cots)
    pieces = take(len(in_orders))
    if first:
        normed, result, back = take(3)
    else:
        mine, other, back = take(3)
    groups = take(len(orders))
    weight, hidden, d_gate, d_up, cot, grad = take(6)
    units = weight.shape[1] // 3
    place(meta, pieces, in_orders, weight, block_rows)
    for block in range(4):
        rows = slice(block * TILE, (block + 1) * TILE)
        cot[rows, :] = row_block(cots, block)
        if first:
            swapped = slice(((block + 2) % 4) * TILE, ((block + 2) % 4 + 1) * TILE)
            features = (
                row_block(rows_in, block).astype(F32)
                + part_mine[rows, :].astype(F32)
                + part_other[swapped, :].astype(F32)
            )
            features = features.astype(BF).astype(F32)
            normed[rows, :] = (features * inverse_rms(features) * gain[...]).astype(BF)
    for start in range(0, 4 * TILE, FEED_ROWS):
        rows = slice(start, start + FEED_ROWS)
        pre = mm(normed[rows, :], weight[:, 0 : 2 * units])
        act, slope = gelu_terms(pre[:, :units])
        up = pre[:, units:]
        low = (act * up).astype(BF)
        hidden[rows, :] = low
        d_hidden = mm(cot[rows, :], weight[:, 2 * units :])
        gate_low = (d_hidden * up * slope).astype(BF)
        up_low = (d_hidden * act).astype(BF)
        d_gate[rows, :] = gate_low
        d_up[rows, :] = up_low
        down = mm_nt(low, weight[:, 2 * units :])
        through = mm_nt(gate_low, weight[:, 0:units]) + mm_nt(up_low, weight[:, units : 2 * units])
        if first:
            result[rows, :] = down.astype(BF)
            back[rows, :] = through.astype(BF)
        else:
            down = (down + result_before[rows, :].astype(F32)).astype(BF)
            if start < 2 * TILE:
                mine[rows, :] = down[: 2 * TILE - start]
            if start + FEED_ROWS > 2 * TILE:
                begin = max(start - 2 * TILE, 0)
                other[begin : start + FEED_ROWS - 2 * TILE, :] = down[begin + 2 * TILE - start :]
            back[rows, :] = (through + back_before[rows, :].astype(F32)).astype(BF)
    grad[:, 2 * units :] = mm_tn(cot[...], hidden[...]).astype(BF)
    grad[:, 0:units] = mm_tn(normed[...], d_gate[...]).astype(BF)
    grad[:, units : 2 * units] = mm_tn(normed[...], d_up[...]).astype(BF)
    disperse(meta, grad, groups, orders, block_rows)


def feed_forward(meta, block_rows, cots, pieces, in_orders, orders, rows_in=(), before=()):
    width = pieces[0].shape[1]
    model = cots[0].shape[1]
    total = 4 * TILE
    units = width // 3
    full = jax.ShapeDtypeStruct((total, model), BF)
    half = jax.ShapeDtypeStruct((2 * TILE, model), BF)
    operands = [*rows_in, *before, *cots, *pieces]
    out_shape = [full, full, full] if rows_in else [half, half, full]
    out_shape += [
        jax.ShapeDtypeStruct((len(order) * block_rows, width), BF) for order in orders
    ]
    return pl.pallas_call(
        functools.partial(
            feed_kernel, len(rows_in), len(cots), in_orders, orders, block_rows
        ),
        in_specs=[SMEM] + [VMEM] * len(operands),
        out_specs=[VMEM] * len(out_shape),
        out_shape=out_shape,
        scratch_shapes=[
            pltpu.VMEM((model, width), BF),
            pltpu.VMEM((total, units), BF),
            pltpu.VMEM((total, units), BF),
            pltpu.VMEM((total, units), BF),
            pltpu.VMEM((total, model), BF),
            pltpu.VMEM((model, width), BF),
        ],
        compiler_params=pltpu.CompilerParams(vmem_limit_bytes=FEED_LIMIT),
        cost_estimate=COST,
        name="feed_forward",
    )(meta, *operands)


def middle_kernel(heads, n_rows, n_cots, *refs):
    refs = list(refs)
    take = lambda count: [refs.pop(0) for _ in range(count)]
    rows_in = take(n_rows)
    part_mine, part_other, gain = take(3)
    cots = take(n_cots)
    d_mine, d_other, context_near, context_far = take(4)
    weight_near, weight_far = take(2)
    d_middle, d_context_near, d_context_far, grad_near, grad_far, d_gain = take(6)
    (d_all,) = take(1)
    width = heads * HD
    gains = 0.0
    for block in range(4):
        rows = slice(block * TILE, (block + 1) * TILE)
        swapped = slice(((block + 2) % 4) * TILE, ((block + 2) % 4 + 1) * TILE)
        features = (
            row_block(rows_in, block).astype(F32)
            + part_mine[rows, :].astype(F32)
            + part_other[swapped, :].astype(F32)
        )
        features = features.astype(BF).astype(F32)
        inverse = inverse_rms(features)
        back = d_mine[rows, :].astype(F32) + d_other[swapped, :].astype(F32)
        scaled = back * gain[...]
        inner = jnp.mean(scaled * features, axis=-1, keepdims=True)
        result = (
            row_block(cots, block).astype(F32)
            + inverse * scaled
            - features * (inverse * inverse * inverse * inner)
        )
        d_all[rows, :] = result.astype(BF)
        if block < 2:
            d_middle[rows, :] = result
            gains += jnp.sum(back * features * inverse, axis=0, keepdims=True)
    d_gain[...] = jnp.broadcast_to(gains, d_gain.shape)
    d_context_near[...] = mm(d_all[...], weight_near[:, 0:width]).astype(BF)
    d_context_far[...] = mm(d_all[...], weight_far[:, 0:width]).astype(BF)
    grad_near[...] = mm_tn(d_all[...], context_near[...]).astype(BF)
    grad_far[...] = mm_tn(d_all[...], context_far[...]).astype(BF)


def middle_backward(heads, rows_in, parts, gain, cots, d_normed, contexts, weights):
    model = gain.shape[1]
    total = 4 * TILE
    width = heads * HD
    operands = [*rows_in, *parts, gain, *cots, *d_normed, *contexts, *weights]
    return pl.pallas_call(
        functools.partial(middle_kernel, heads, len(rows_in), len(cots)),
        in_specs=[VMEM] * len(operands),
        out_specs=[VMEM] * 6,
        out_shape=[
            jax.ShapeDtypeStruct((2 * TILE, model), F32),
            jax.ShapeDtypeStruct((total, width), BF),
            jax.ShapeDtypeStruct((total, width), BF),
            jax.ShapeDtypeStruct((model, width), BF),
            jax.ShapeDtypeStruct((model, width), BF),
            jax.ShapeDtypeStruct((8, model), F32),
        ],
        scratch_shapes=[
            pltpu.VMEM((total, model), BF),
        ],
        compiler_params=pltpu.CompilerParams(vmem_limit_bytes=MIDDLE_LIMIT),
        cost_estimate=COST,
        name="middle_backward",
    )(*operands)


def in_two(*rows):
    high = [row.astype(BF).astype(F32) for row in rows]
    index = lax.broadcasted_iota(jnp.int32, (16, rows[0].shape[1]), 0)
    result = jnp.zeros((16, rows[0].shape[1]), F32)
    for number, row in enumerate(rows):
        result = jnp.where(index == 2 * number, high[number], result)
        result = jnp.where(index == 2 * number + 1, row - high[number], result)
    return result.astype(BF)


def from_two(rows):
    return [
        rows[2 * k : 2 * k + 1].astype(F32) + rows[2 * k + 1 : 2 * k + 2].astype(F32)
        for k in range(2)
    ]


def finish_kernel(d_mine, d_other, keep, got, d_middle, gain, mine, theirs):
    for number, rows_in in enumerate((keep, got)):
        rows = slice(number * TILE, (number + 1) * TILE)
        features = rows_in[...].astype(F32)
        inverse = inverse_rms(features)
        scaled = (d_mine[rows, :].astype(F32) + d_other[rows, :].astype(F32)) * gain[...]
        inner = jnp.mean(scaled * features, axis=-1, keepdims=True)
        result = (
            d_middle[rows, :] + inverse * scaled - features * (inverse * inverse * inverse * inner)
        ).astype(BF)
        if number == 0:
            mine[...] = result
        else:
            theirs[...] = result


def backward_kernel(heads, orders, block_rows, last, meta, *refs):
    refs = list(refs)
    take = lambda count: [refs.pop(0) for _ in range(count)]
    inverse, context, expo, weight, proj, normed, d_context, grad_out = take(8)
    if last:
        gain, gain_rows = take(2)
    if last:
        (before,) = take(1)
        mine, other = take(2)
    else:
        (result,) = take(1)
    groups = take(len(orders))
    do_ext, v_ext, d_proj, grad = take(4)
    width = heads * HD
    total = 4 * TILE
    lanes = lax.broadcasted_iota(jnp.int32, (total, HD), 1)
    columns = inverse[...].T
    d_proj[:, 0:width] = jnp.zeros((total, width), BF)
    for head in range(heads):
        at = head * HD
        scaled = (d_context[:, at : at + HD].astype(F32) * columns[:, head : head + 1]).astype(BF)
        inner = -jnp.sum(
            scaled.astype(F32) * context[:, at : at + HD].astype(F32), axis=-1, keepdims=True
        )
        high = inner.astype(BF).astype(F32)
        do_ext[head, :, 0:HD] = scaled
        do_ext[head, :, HD : 2 * HD] = jnp.where(
            lanes == 0, high, jnp.where(lanes == 1, inner - high, 0.0)
        ).astype(BF)
    for head in range(heads):
        at = 3 * width + head * HD
        v_ext[head, :, 0:HD] = proj[:, at : at + HD]
        v_ext[head, :, HD : 2 * HD] = jnp.where(lanes < 2, 1.0, 0.0).astype(BF)
    for head in range(heads):
        q_at, k_at, v_at = (part * width + head * HD for part in (1, 2, 3))
        raised = expo[head]
        d_probs = mm_nt(v_ext[head], do_ext[head])
        d_scores = (raised.astype(F32) * d_probs).astype(BF)
        d_queries = mm(proj[:, k_at : k_at + HD].T, d_scores)
        d_keys = mm_nt(proj[:, q_at : q_at + HD].T, d_scores)
        d_values = mm_nt(do_ext[head, :, 0:HD].T, raised)
        d_proj[:, q_at : q_at + HD] = d_queries.astype(BF).T
        d_proj[:, k_at : k_at + HD] = d_keys.astype(BF).T
        d_proj[:, v_at : v_at + HD] = d_values.astype(BF).T
    grad[...] = mm_tn(normed[...], d_proj[...]).astype(BF)
    grad[:, 0:width] = grad_out[...]
    disperse(meta, grad, groups, orders, block_rows)
    through = mm_nt(d_proj[...], weight[...])
    if last:
        through = through + before[...].astype(F32)
        mine[...] = through[0 : 2 * TILE].astype(BF)
        other[...] = through[2 * TILE :].astype(BF)
        first = jnp.sum(through * normed[...].astype(F32), axis=0, keepdims=True) / gain[...]
        end = len(orders[-1]) * block_rows
        groups[-1][end : end + 16, :] = in_two(first, gain_rows[0:1, :])
    else:
        result[...] = through.astype(BF)


def attention_backward(
    meta, heads, block_rows, normed, saved, d_context, grad_out, orders, before=None
):
    last = before is not None
    weight, proj = saved[3:]
    model, width = weight.shape
    total = proj.shape[0]
    rows = jax.ShapeDtypeStruct((total, model), BF)
    in_fast = [*saved, normed, d_context, grad_out]
    scratch = [
        pltpu.VMEM((heads, total, 2 * HD), BF),
        pltpu.VMEM((heads, total, 2 * HD), BF),
        pltpu.VMEM((total, width), BF),
        pltpu.VMEM((model, width), BF),
    ]
    sizes = [len(order) * block_rows for order in orders]
    if last:
        in_fast += [*before[1:], before[0]]
        out_shape = [jax.ShapeDtypeStruct((2 * TILE, model), BF)] * 2
        sizes[-1] += 16
    else:
        out_shape = [rows]
    out_shape += [jax.ShapeDtypeStruct((size, width), BF) for size in sizes]
    return pl.pallas_call(
        functools.partial(backward_kernel, heads, orders, block_rows, last),
        in_specs=[SMEM] + [VMEM] * len(in_fast),
        out_specs=[VMEM] * len(out_shape),
        out_shape=out_shape,
        scratch_shapes=scratch,
        compiler_params=pltpu.CompilerParams(vmem_limit_bytes=BACK_LIMIT),
        cost_estimate=COST,
        name="attention_backward",
    )(meta, *in_fast)


def add(*terms):
    return sum(term.astype(F32) for term in terms)


def hold(values, *others):
    values, others = lax.optimization_barrier((values, others))
    return values, *others


def plus(*terms):
    return sum(term.astype(F32) for term in terms)


def call_local(kernel, out_shape, *operands):
    return pl.pallas_call(
        kernel,
        in_specs=[VMEM] * len(operands),
        out_specs=[VMEM] * len(out_shape),
        out_shape=[jax.ShapeDtypeStruct(shape, kind) for shape, kind in out_shape],
        compiler_params=pltpu.CompilerParams(vmem_limit_bytes=MIDDLE_LIMIT),
        cost_estimate=COST,
        name=kernel.__name__.replace("kernel", "backward"),
    )(*operands)


def join_kernel(
    own_high, y_high, y_low, xy_low, over, one_in, two_in, three_in,
    two, three, y_low_plus, over_plus,
):
    rows = two.shape[0]
    for at, dest in ((slice(0, rows), two), (slice(rows, 2 * rows), three)):
        dest[...] = plus(own_high[at, :], y_high[at, :]).astype(BF)
    y_low_plus[...] = plus(y_low[...], xy_low[...]).astype(BF)
    over_plus[...] = plus(over[...], one_in[...], two_in[...], three_in[...]).astype(BF)


def meet_kernel(x_low, x_high, both_low, y_high, xy_high, message, y_high_plus):
    half = x_low.shape[0]
    message[0:half, :] = plus(x_low[...], both_low[half:, :]).astype(BF)
    message[half:, :] = x_high[...]
    y_high_plus[...] = plus(y_high[...], xy_high[...]).astype(BF)


def last_kernel(own_low, feed_y, own, one):
    rows = own.shape[0]
    own[...] = plus(own_low[0:rows, :], feed_y[0:rows, :])
    one[...] = plus(own_low[rows:, :], feed_y[rows:, :]).astype(BF)


def fold_kernel(own_low, own_high, x_high, over_x, both_low, y_high, total, gains, *messages):
    rows = total.shape[0]
    end = 4 * rows
    mine = from_two(x_high[2 * rows : 2 * rows + 16, :])
    theirs = from_two(over_x[end : end + 16, :])
    pairs = in_two(*(a + b for a, b in zip(mine, theirs)))
    gains[...] = pairs.astype(F32)
    for index in range(4):
        at = slice((index % 2) * rows, (index % 2 + 1) * rows)
        block = plus(
            (own_low if index < 2 else own_high)[at, :],
            over_x[index * rows : (index + 1) * rows, :],
            (both_low if index < 2 else y_high)[at, :],
        )
        if index == 0:
            total[...] = block
        else:
            messages[index - 1][0:rows, :] = block.astype(BF)
            messages[index - 1][rows:, :] = pairs


class Links:
    def __init__(self, wide, narrow):
        self.wide, self.narrow = wide, narrow
        self.planes = wide // 2
        self.staged = wide == 8

    def y(self, values):
        return lax.ppermute(values, "narrow", [(i, (i + 2) % 4) for i in range(4)])

    def core(self, values):
        return lax.ppermute(values, "narrow", [(i, i ^ 1) for i in range(4)])

    def across(self, values):
        return lax.ppermute(values, "narrow", [(i, (i + 2) % 4 ^ 1) for i in range(4)])

    def x(self, values):
        return lax.ppermute(values, "wide", [(i, i ^ 1) for i in range(self.wide)])

    def z(self, values, ahead):
        turn = lambda i: ((i // 2 + ahead) % self.planes) * 2 + i % 2
        return lax.ppermute(values, "wide", [(i, turn(i)) for i in range(self.wide)])

    def whole_gather(self, piece):
        near = lax.all_gather(piece, "wide", axis=0, tiled=True)
        return [near], [self.y(near)]

    def whole_reduce(self, near, far):
        return lax.psum_scatter(near, "wide", scatter_dimension=0, tiled=True).astype(
            F32
        ) + lax.psum_scatter(self.y(far), "wide", scatter_dimension=0, tiled=True).astype(F32)


def on_device(
    tokens,
    lengths,
    norm_one,
    w_query,
    w_key,
    w_value,
    w_out,
    norm_two,
    w_gate,
    w_up,
    w_down,
    cotangent,
):
    model = tokens.shape[-1]
    wide, narrow = lax.axis_size("wide"), lax.axis_size("narrow")
    links = Links(wide, narrow)
    heads = w_query.shape[1] // HD
    head_width = heads * HD
    units = w_gate.shape[1]
    at_wide, at_narrow = lax.axis_index("wide"), lax.axis_index("narrow")
    y, c = at_narrow >> 1, at_narrow & 1
    x, z = at_wide & 1, at_wide >> 1

    staged = links.staged
    planes = links.planes
    rows = model // wide
    turned = [((z + k) & (planes - 1)) * 2 + (x ^ side) for side in range(2) for k in range(4)]
    blocks = [((y ^ far) * 2 + (c ^ side)) * TILE for side in range(2) for far in range(2)]
    length = lax.dynamic_index_in_dim(lengths, y, 0, keepdims=False)[0]
    numbers = [
        *(spot * rows for spot in turned),
        *blocks,
        length,
    ]
    meta = jnp.stack([jnp.asarray(number, jnp.int32) for number in numbers])
    first_item = y == 0

    gain_one = norm_one.reshape(1, model)
    gain_two = norm_two.reshape(1, model)

    def keep_give(rows):
        flat = rows.reshape(2, TILE, model)
        return (
            lax.dynamic_index_in_dim(flat, y, 0, keepdims=False),
            lax.dynamic_index_in_dim(flat, 1 - y, 0, keepdims=False),
        )

    attn_piece = jnp.concatenate([w_out.T, w_query, w_key, w_value], axis=1)
    feed_piece = jnp.concatenate([w_gate, w_up, w_down.T], axis=1)
    keep, give = keep_give(tokens)
    keep_cot, give_cot = keep_give(cotangent)
    half = planes // 2 * rows
    if staged:
        block_rows = rows
        quarters = ((0, 1), (2, 3), (4, 5), (6, 7))
        attn_near_in = attn_far_in = ((0, 1, 2, 3), (4, 5, 6, 7))
        feed_near_in = ((0,), (1,), (3,), (2,), (4, 5, 7), (6,))
        feed_far_in = ((0, 1, 3), (2,), (4, 5), (7, 6))
        attn_far_out = ((0, 1, 4, 5), (2, 3), (6, 7))
        feed_near_out = ((0, 1), (2, 3), (4,), (5,), (6,), (7,))
    else:
        block_rows = model
        quarters = attn_far_out = feed_near_out = ((0,),)
        attn_near_in = attn_far_in = feed_near_in = feed_far_in = ((0,),)

    got = links.y(give)
    if staged:
        column = [attn_piece] + [links.z(attn_piece, planes - k) for k in range(1, planes)]
        column = jnp.concatenate(column, axis=0)
        over_x, over_y = links.x(column), links.y(column)
        feed_piece, column, first_item = hold(feed_piece, column, first_item)
        feed_one = links.z(feed_piece, planes - 1)
        feed_three = links.z(feed_piece, planes - 3)
    else:
        attn_near, attn_far = links.whole_gather(attn_piece)
        feed_near, feed_far = links.whole_gather(feed_piece)
    from_keep = links.core(keep)
    if staged:
        got, feed_one, feed_three = hold(got, feed_one, feed_three)
    rows_in = [keep, got, from_keep, links.core(got)]
    if staged:
        over_y, over_x = hold(over_y, over_x)
        give_cot, over_y = hold(give_cot, over_y)
        attn_near = [column, over_x]
        rows_in, over_y, meta = hold(rows_in, over_y, meta)
        attn_far = [over_y, links.x(over_y)]
        three = jnp.concatenate([feed_piece, feed_one, feed_three], axis=0)
        feed_x = links.x(three)
        feed_y = links.y(three)
        feed_piece, feed_one = hold(feed_piece, feed_one)
        feed_two = links.z(feed_piece, planes - 2)
    got_cot = links.y(give_cot)

    inv_near, context_near, expo_near, *kept_near, normed = attention_forward(
        meta, heads, block_rows, attn_near, attn_near_in, rows_in=rows_in, gain=gain_one
    )
    if staged:
        normed, feed_two, attn_far = hold(normed, feed_two, attn_far)
        feed_x_two = links.x(feed_two)
        feed_y_two = links.y(feed_two)
    inv_far, context_far, expo_far, *kept_far, part_mine = attention_forward(
        meta, heads, block_rows, attn_far, attn_far_in,
        before=(normed, context_near, kept_near[0]),
    )
    if staged:
        part_mine, got_cot, feed_x, feed_y, feed_x_two, feed_y_two = hold(
            part_mine, got_cot, feed_x, feed_y, feed_x_two, feed_y_two
        )
    part_other = links.core(part_mine)
    own_cot = jnp.concatenate([keep_cot, got_cot], axis=0)
    cots = [own_cot, links.core(own_cot)]
    if staged:
        feed_near = [feed_piece, feed_one, feed_three, feed_two, feed_x, feed_x_two]
        feed_far = [
            feed_y,
            feed_y_two,
            links.y(feed_x[: 2 * rows]),
            links.x(jnp.concatenate([feed_y[2 * rows :], feed_y_two], axis=0)),
        ]
    parts = (part_mine, part_other)

    normed_two, down_near, back_near, *near = feed_forward(
        meta, block_rows, cots, feed_near, feed_near_in, feed_near_out, rows_in=rows_in,
        before=(*parts, gain_two),
    )
    if staged:
        own_low, own_high, over, *pieces = near
        over_one = links.z(pieces[0], 1)
    mlp_mine, mlp_other, d_mine, *far = feed_forward(
        meta, block_rows, cots, feed_far, feed_far_in, quarters,
        before=(normed_two, down_near, back_near),
    )
    if staged:
        mlp_other, over_one = hold(mlp_other, over_one)
        over_three = links.z(pieces[2], 3)
        y_low, y_high, xy_low, xy_high = far
        from_xy_high = links.x(xy_high)
    else:
        feed_grad = links.whole_reduce(*near, *far)
    d_other = links.core(d_mine)
    half_rows = 2 * TILE
    output = (
        jnp.concatenate(rows_in[:2], axis=0).astype(F32)
        + part_mine[:half_rows].astype(F32)
        + part_other[half_rows:].astype(F32)
        + mlp_mine.astype(F32)
        + links.core(mlp_other).astype(F32)
    ).astype(BF)
    output_back = links.y(output[TILE:])
    d_middle, d_context_near, d_context_far, out_near, out_far, gain_rows = middle_backward(
        heads,
        rows_in,
        parts,
        gain_two,
        cots,
        (d_mine, d_other),
        (context_near, context_far),
        (kept_near[0], kept_far[0]),
    )
    if staged:
        d_context_far, from_xy_high, output_back, over_three = hold(
            d_context_far, from_xy_high, output_back, over_three
        )
        xy_low, over_two, from_xy_high = hold(xy_low, pieces[1], from_xy_high)
        over_two = links.z(over_two, 2)
        from_y_high = links.y(add(y_high, from_xy_high).astype(BF))
        from_xy_low = links.x(xy_low)
    d_first, *far = attention_backward(
        meta, heads, block_rows, normed, (inv_far, context_far, expo_far, *kept_far),
        d_context_far, out_far, attn_far_out,
    )
    if staged:
        d_first, from_y_high, from_xy_low, over_two = hold(
            d_first, from_y_high, from_xy_low, over_two
        )
        feed = (rows, feed_piece.shape[1])
        feed_half = (half, feed_piece.shape[1])
        feed_two, feed_three, feed_y_low, feed_over = call_local(
            join_kernel, [(feed, BF), (feed, BF), (feed_half, BF), (feed, BF)],
            own_high, from_y_high, y_low, from_xy_low, over, over_one, over_two, over_three,
        )
        feed_two = links.z(feed_two, 2)
        feed_low = own_low
        both_low, y_high, xy_high = far
        from_both_low = links.y(both_low)
        from_xy_high = links.x(xy_high)
        from_feed_x, from_feed_y = links.x(feed_over), links.y(feed_y_low)
    last_mine, last_other, *near = attention_backward(
        meta, heads, block_rows, normed, (inv_near, context_near, expo_near, *kept_near),
        d_context_near, out_near, quarters, before=(d_first, gain_one, gain_rows),
    )
    if staged:
        last_other, near, from_both_low, from_xy_high, from_feed_x, feed_two = hold(
            last_other, near, from_both_low, from_xy_high, from_feed_x, feed_two
        )
        own_low, own_high, x_low, x_high = near
        width = x_low.shape[1]
        message, y_high = call_local(
            meet_kernel, [((2 * half + 16, width), BF), ((half, width), BF)],
            x_low, x_high, from_both_low, y_high, from_xy_high,
        )
        from_x, from_y_high = links.x(message), links.y(y_high)
        feed_parts = [feed_two, links.z(feed_three, 3)]
        last_mine, from_feed_y = hold(last_mine, from_feed_y)
    else:
        attn_grad = links.whole_reduce(near[0][:model], *far)
        gains = near[0][model:]
    mine, theirs = call_local(
        finish_kernel,
        [((TILE, model), BF)] * 2,
        last_mine, links.core(last_other), *rows_in[:2], d_middle, gain_one,
    )
    if staged:
        feed_own, feed_one = call_local(
            last_kernel, [(feed, F32), (feed, BF)], feed_low, from_feed_y
        )
        feed_parts += [from_feed_x, links.z(feed_one, 1)]
        from_x, theirs, feed_own = hold(from_x, theirs, feed_own)
    back = links.y(theirs)
    if staged:
        attn = (rows, width)
        apart = ((rows + 16, width), BF)
        attn_grad, gains, *messages = call_local(
            fold_kernel, [(attn, F32), ((16, width), F32), apart, apart, apart],
            own_low, own_high, x_high, from_x, from_both_low, from_y_high,
        )
        arrived = [links.z(piece, k + 1) for k, piece in enumerate(messages)]
        attn_grad = add(attn_grad, *(part[:rows] for part in arrived))
        gains = add(gains, *(part[rows:] for part in arrived))
        gains, back = hold(gains, back)
        feed_grad = add(feed_own, *feed_parts)
    else:
        gains = lax.psum(gains.astype(F32), "wide")
    gains = (gains + links.core(gains)) + (links.y(gains) + links.across(gains))

    def in_order(own, other):
        stacked = jnp.where(first_item, jnp.stack([own, other]), jnp.stack([other, own]))
        return stacked.reshape(tokens.shape)

    return (
        in_order(output[:TILE], output_back),
        in_order(mine, back),
        gains[0] + gains[1],
        attn_grad[:, head_width : 2 * head_width],
        attn_grad[:, 2 * head_width : 3 * head_width],
        attn_grad[:, 3 * head_width :],
        attn_grad[:, :head_width].T,
        gains[2] + gains[3],
        feed_grad[:, :units],
        feed_grad[:, units : 2 * units],
        feed_grad[:, 2 * units :].T,
    )


def solution(mesh):
    in_specs = (
        P(None, "wide", "narrow", None),
        P(None, "wide"),
        P(),
        P("wide", "narrow"),
        P("wide", "narrow"),
        P("wide", "narrow"),
        P("narrow", "wide"),
        P(),
        P("wide", "narrow"),
        P("wide", "narrow"),
        P("narrow", "wide"),
        P(None, "wide", "narrow", None),
    )
    out_specs = (
        P(None, "wide", "narrow", None),
        P(None, "wide", "narrow", None),
        P(),
        P("wide", "narrow"),
        P("wide", "narrow"),
        P("wide", "narrow"),
        P("narrow", "wide"),
        P(),
        P("wide", "narrow"),
        P("wide", "narrow"),
        P("narrow", "wide"),
    )
    return jax.shard_map(
        on_device, mesh=mesh, in_specs=in_specs, out_specs=out_specs, check_vma=False
    )
```
